32 devices in a mesh: dp: 8 (over y, x, core), shard: 4 (over z).
Axes of the slice: x: 2, y: 2, z: 4, core: 2. Of those that a mesh axis runs over, the one named last changes fastest.
Arguments:
- queries: bfloat16 [4096, 2048], P(('dp', 'shard')), may hold values from -6 to 6
- keys_in: bfloat16 [4096, 2048], P(('dp', 'shard')), may hold values from -6 to 6
- values: bfloat16 [4096, 2048], P(('dp', 'shard')), may hold values from -6 to 6
- out_grad: bfloat16 [4096, 2048], P(('dp', 'shard')), may hold values from -48 to 48
- out_weight: bfloat16 [2048, 2048], P('shard'), may hold values from -0.125 to 0.125
- block_lists: int32 [8, 4, 4], P('dp'), may hold values from 0 to 3, as said below
- voxel_count: int32 [8], P('dp'), may hold values from 256 to 512
Outputs:
- grad_query: bfloat16 [4096, 2048], P(('dp', 'shard'))
- grad_key: bfloat16 [4096, 2048], P(('dp', 'shard'))
- grad_value: bfloat16 [4096, 2048], P(('dp', 'shard'))
- grad_weight: bfloat16 [2048, 2048], P('shard')
The draws below stay inside these ranges and needn't reach their ends.
Inputs may be any that keep to these rules, and one draw needn't show every extreme that they name: `block_lists`: entry 0 of row b of a scene's list is b itself; the 4 entries of a row are different blocks of that scene.
All inputs are finite; a program needn't handle non-finite values.
Results may differ from the reference program's by a relative error of at most 0.0095.
Values may be sent and summed in bfloat16 or wider, within the bound.
No kernel may reach another device: no remote copies, remote signals or barrier semaphores. Data moves between devices by JAX's collectives and lax.ppermute only.
A program may use at most 128 MiB of HBM per device.

```python
import math
import jax
import jax.numpy as jnp
from jax import lax

HEADS = 16
HDIM = 128
OUTW = 2048
BLOCK = 128
NB = 4
SCENE_TOK = 512
NBLK = 4
SCENES = 8
TOKENS = 4096


def draw_queries(key, part):
    key = jax.random.fold_in(key, 11)
    return jnp.clip(jax.random.normal(key, (TOKENS, HEADS * HDIM)), -4.0, 4.0).astype(jnp.bfloat16)


def draw_keys_in(key, part):
    key = jax.random.fold_in(key, 13)
    return jnp.clip(jax.random.normal(key, (TOKENS, HEADS * HDIM)), -4.0, 4.0).astype(jnp.bfloat16)


def draw_block_lists(key, part):
    key = jax.random.fold_in(key, 17)
    picks = jax.random.randint(key, (SCENES, NBLK, NBLK - 1), 0, 2 ** 20) * NBLK + jnp.arange(NBLK - 1, dtype=jnp.int32)
    unused, offsets = lax.top_k(picks, NB - 1)
    own_block = jnp.broadcast_to(jnp.arange(NBLK, dtype=jnp.int32)[None, :, None], (SCENES, NBLK, 1))
    others = (own_block + offsets.astype(jnp.int32) + 1) % NBLK
    return jnp.concatenate([own_block, others], axis=-1).astype(jnp.int32)


def touch_ends(entries, rng, smallest, high):
    index_at = [jax.random.randint(jax.random.fold_in(rng, axis), (), 0, length) for axis, length in enumerate(entries.shape)]
    main_axis = entries.shape.index(max(entries.shape))
    beside = index_at[:main_axis] + [(index_at[main_axis] + 1) % entries.shape[main_axis]] + index_at[main_axis + 1:]
    return entries.at[tuple(index_at)].set(smallest).at[tuple(beside)].set(high)


def block_scale(key, dims, shards, low, high):
    gain = 1.0
    for dim, parts in shards:
        draws = jax.random.uniform(jax.random.fold_in(jax.random.fold_in(key, 6), dim), (parts,), jnp.float32, low / len(shards), high / len(shards))
        gain = gain * jnp.repeat(jnp.exp(draws), dims[dim] // parts).reshape((-1,) + (1,) * (len(dims) - 1 - dim))
    return gain


def scatter_about(stream_key, shape, deviation, limit, cuts=(), kind=jnp.bfloat16):
    level = block_scale(stream_key, shape, cuts, -0.22, 0.18) if cuts else 1.0
    entries = jax.random.normal(stream_key, shape, jnp.float32) * deviation * level
    return jnp.minimum(jnp.maximum(entries, -limit), limit).astype(kind)


def setup_inputs(seed: int = 0) -> dict:
    streams_of = jax.random.split(jax.random.key(seed), 8)
    return {
        "queries": draw_queries(jax.random.fold_in(streams_of[7], 71), 0),
        "keys_in": draw_keys_in(jax.random.fold_in(streams_of[7], 71), 0),
        "values": scatter_about(streams_of[2], (TOKENS, HEADS * HDIM), 1.0, 6.0, ((0, 32),)),
        "out_grad": scatter_about(streams_of[3], (TOKENS, OUTW), 8.0, 48.0, ((0, 32),)),
        "out_weight": scatter_about(streams_of[4], (HEADS * HDIM, OUTW), (HEADS * HDIM) ** -0.5, 0.125, ((0, 4),)),
        "block_lists": draw_block_lists(jax.random.fold_in(streams_of[7], 71), 0),
        "voxel_count": touch_ends(jax.random.randint(streams_of[6], (SCENES,), SCENE_TOK // 2, SCENE_TOK + 1), jax.random.fold_in(streams_of[6], 1), SCENE_TOK // 2, SCENE_TOK).astype(jnp.int32),
    }


def attend(queries, keys_in, values, block_ids, live_count):
    row_count, width_all = queries.shape
    head_count = width_all // HDIM
    block_count = row_count // BLOCK
    score_scale = 1.0 / math.sqrt(HDIM)
    query_blk = queries.reshape(block_count, BLOCK, head_count, HDIM).astype(jnp.float32)
    key_blk = keys_in.reshape(block_count, BLOCK, head_count, HDIM)[block_ids].reshape(block_count, NB * BLOCK, head_count, HDIM).astype(jnp.float32)
    value_blk = values.reshape(block_count, BLOCK, head_count, HDIM)[block_ids].reshape(block_count, NB * BLOCK, head_count, HDIM).astype(jnp.float32)
    query_pos = jnp.arange(row_count, dtype=jnp.int32).reshape(block_count, BLOCK)
    key_pos = (block_ids[:, :, None] * BLOCK + jnp.arange(BLOCK, dtype=jnp.int32)[None, None, :]).reshape(block_count, NB * BLOCK)
    allowed = (key_pos[:, None, :] < live_count) | (query_pos[:, :, None] >= live_count)
    scores = jnp.einsum('bqhd,bkhd->bhqk', query_blk, key_blk) * score_scale
    scores = jnp.where(allowed[:, None], scores, -jnp.inf)
    peak = lax.optimization_barrier(jnp.max(scores, axis=-1, keepdims=True))
    weights = jnp.exp(scores - peak)
    probs = weights / lax.optimization_barrier(jnp.sum(weights, axis=-1, keepdims=True))
    return (query_blk, key_blk, value_blk, probs)

def scene_pass(queries, keys_in, values, grad_out, out_weight, block_ids, live_count):
    row_count, width_all = queries.shape
    head_count = width_all // HDIM
    block_count = row_count // BLOCK
    score_scale = 1.0 / math.sqrt(HDIM)
    is_live = jnp.arange(row_count, dtype=jnp.int32) < live_count
    grad_live = jnp.where(is_live[:, None], grad_out, jnp.zeros_like(grad_out))
    query_blk, key_blk, value_blk, probs = attend(queries, keys_in, values, block_ids, live_count)
    prob_bf = lax.optimization_barrier(probs.astype(jnp.bfloat16)).astype(jnp.float32)
    heads_out = jnp.einsum('bhqk,bkhd->bqhd', prob_bf, value_blk).reshape(row_count, width_all).astype(jnp.bfloat16)
    grad_attn = jnp.dot(grad_live, out_weight.T, preferred_element_type=jnp.float32).astype(jnp.bfloat16)
    weight_sum = jnp.dot(heads_out.T, grad_live, preferred_element_type=jnp.float32)
    grad_o = lax.optimization_barrier(grad_attn).reshape(block_count, BLOCK, head_count, HDIM).astype(jnp.float32)
    grad_prob = jnp.einsum('bqhd,bkhd->bhqk', grad_o, value_blk)
    row_delta = lax.optimization_barrier(jnp.sum(probs * grad_prob, axis=-1, keepdims=True))
    dscore = (probs * (grad_prob - row_delta) * score_scale).astype(jnp.bfloat16)
    dscore = lax.optimization_barrier(dscore).astype(jnp.float32)
    grad_query = jnp.einsum('bhqk,bkhd->bqhd', dscore, key_blk).reshape(row_count, width_all).astype(jnp.bfloat16)
    onehot = (block_ids[:, :, None] == jnp.arange(block_count, dtype=jnp.int32)[None, None, :]).astype(jnp.float32)
    key_parts = jnp.einsum('bhqk,bqhd->bkhd', dscore, query_blk).reshape(block_count, NB, BLOCK, width_all)
    value_parts = jnp.einsum('bhqk,bqhd->bkhd', prob_bf, grad_o).reshape(block_count, NB, BLOCK, width_all)
    grad_key = jnp.einsum('bjc,bjrx->crx', onehot, key_parts, precision=lax.Precision.HIGHEST).reshape(row_count, width_all).astype(jnp.bfloat16)
    grad_value = jnp.einsum('bjc,bjrx->crx', onehot, value_parts, precision=lax.Precision.HIGHEST).reshape(row_count, width_all).astype(jnp.bfloat16)
    return (grad_query, grad_key, grad_value, weight_sum)

def reference(queries, keys_in, values, out_grad, out_weight, block_lists, voxel_count):
    scene_shape = (SCENES, SCENE_TOK, -1)
    stacked = (queries.reshape(scene_shape), keys_in.reshape(scene_shape), values.reshape(scene_shape), out_grad.reshape(scene_shape), block_lists, voxel_count)

    def scene_step(running, scene_item):
        query_s, key_s, value_s, grad_s, ids_s, count_s = scene_item
        grad_query, grad_key, grad_value, weight_sum = scene_pass(query_s, key_s, value_s, grad_s, out_weight, ids_s, count_s)
        return (running + weight_sum, (grad_query, grad_key, grad_value))
    start_sum = jnp.zeros((HEADS * HDIM, OUTW), jnp.float32)
    running, (grad_query, grad_key, grad_value) = lax.scan(scene_step, start_sum, stacked)
    flat_shape = (TOKENS, HEADS * HDIM)
    grad_weight = (running / SCENES).astype(jnp.bfloat16)
    return (grad_query.reshape(flat_shape), grad_key.reshape(flat_shape), grad_value.reshape(flat_shape), grad_weight)
```

```python
import functools
import math

import jax
import jax.numpy as jnp
from jax import lax
from jax.experimental import pallas as pl
from jax.experimental.pallas import tpu as pltpu
from jax.sharding import PartitionSpec as P

HDIM = 128
BLOCK = 128
NB = 4
GROUPS = 1
VMEM_BYTES = 48 * 1024 * 1024

f32 = jnp.float32
bf16 = jnp.bfloat16


def dot(a, b, ca, cb):
    return lax.dot_general(a, b, (((ca,), (cb,)), ((), ())), preferred_element_type=f32)


def sds(shape, dtype):
    return jax.ShapeDtypeStruct(shape, dtype)


def params():
    return pltpu.CompilerParams(vmem_limit_bytes=VMEM_BYTES)


def swap(x, axis, size, flip):
    return lax.ppermute(x, axis, [(i, i ^ flip) for i in range(size)])


def pack_kernel(meta, q_ref, k_ref, v_ref, *outs):
    z = meta[0]
    width = q_ref.shape[1] // 4
    part = width // GROUPS
    for g in range(GROUPS):
        for k in range(4):
            start = pl.multiple_of((z ^ k) * width + g * part, 128)
            for i, ref in enumerate((q_ref, k_ref, v_ref)):
                outs[g * 4 + k][i] = ref[:, pl.ds(start, part)]


def pack(meta, queries, keys_in, values):
    rows, width = queries.shape
    part = width // 4 // GROUPS
    return pl.pallas_call(
        pack_kernel,
        out_shape=[sds((3, rows, part), bf16)] * (4 * GROUPS),
        in_specs=[pl.BlockSpec(memory_space=pltpu.SMEM)]
        + [pl.BlockSpec(memory_space=pltpu.VMEM)] * 3,
        out_specs=[pl.BlockSpec(memory_space=pltpu.VMEM)] * (4 * GROUPS),
        compiler_params=params(),
        cost_estimate=pl.CostEstimate(flops=0, bytes_accessed=12 * rows * width, transcendentals=0),
        name="pack_heads",
    )(meta, queries, keys_in, values)


def token_pos(shape, dim, z):
    return lax.broadcasted_iota(jnp.int32, shape, dim) ^ (z * BLOCK)


def grad_attn_kernel(meta, g0, g1, g2, g3, w_ref, out_ref):
    z, count = meta[0], meta[1]
    grad = jnp.concatenate([g0[...], g1[...], g2[...], g3[...]], axis=0)
    live = token_pos((grad.shape[0], 1), 0, z) < count
    product = dot(grad, w_ref[...], 1, 1)
    out_ref[...] = jnp.where(live, product, 0.0).astype(bf16)


def grad_attn(meta, grads, weight):
    rows, outw = grads[0].shape
    width = weight.shape[0]
    tile = 256
    return pl.pallas_call(
        grad_attn_kernel,
        out_shape=sds((4 * rows, width), bf16),
        grid=(width // tile,),
        in_specs=[pl.BlockSpec(memory_space=pltpu.SMEM)]
        + [pl.BlockSpec((rows, outw), lambda i: (0, 0))] * 4
        + [pl.BlockSpec((tile, outw), lambda i: (i, 0))],
        out_specs=pl.BlockSpec((4 * rows, tile), lambda i: (0, i)),
        compiler_params=params(),
        cost_estimate=pl.CostEstimate(
            flops=8 * rows * width * outw, bytes_accessed=8 * rows * outw + 2 * width * outw, transcendentals=0
        ),
        name="grad_attn",
    )(meta, *grads, weight)


def attend_kernel(meta, p0, p1, p2, p3, do_ref, ot_ref, b0, b1, b2, b3):
    z, count = meta[0], meta[1]
    pieces, backs = (p0, p1, p2, p3), (b0, b1, b2, b3)
    rows = p0.shape[1]
    total = 4 * rows
    tile = 2 * rows
    scale = 1.0 / math.sqrt(HDIM)
    key_live = token_pos((total, 1), 0, z) < count
    query_live = token_pos((1, total), 1, z) < count
    for h in range(p0.shape[2] // HDIM):
        cols = slice(h * HDIM, (h + 1) * HDIM)
        query, key, value = (jnp.concatenate([p[i, :, cols] for p in pieces], axis=0) for i in range(3))
        grad = do_ref[:, cols]
        grad_key = grad_value = jnp.zeros((total, HDIM), f32)
        for t in range(2):
            part = slice(t * tile, (t + 1) * tile)
            live = query_live[:, part]
            scores = dot(key, query[part], 1, 1) * scale
            scores = jnp.where(key_live | ~live, scores, -jnp.inf)
            weights = jnp.exp(scores - jnp.max(scores, axis=0, keepdims=True))
            probs = weights * (1.0 / jnp.sum(weights, axis=0, keepdims=True))
            prob_bf = probs.astype(bf16)
            heads = dot(value, prob_bf, 0, 0)
            ot_ref[cols, part] = jnp.where(live, heads, 0.0).astype(bf16)
            grad_prob = dot(value, grad[part], 1, 1)
            row_delta = jnp.sum(probs * grad_prob, axis=0, keepdims=True)
            dscore = (probs * (grad_prob - row_delta) * scale).astype(bf16)
            grad_query = dot(key, dscore, 0, 0).T.astype(bf16)
            backs[2 * t][0, :, cols] = grad_query[:rows]
            backs[2 * t + 1][0, :, cols] = grad_query[rows:]
            grad_key += dot(dscore, query[part], 1, 0)
            grad_value += dot(prob_bf, grad[part], 1, 0)
        for k in range(4):
            mine = slice(k * rows, (k + 1) * rows)
            backs[k][1, :, cols] = grad_key[mine].astype(bf16)
            backs[k][2, :, cols] = grad_value[mine].astype(bf16)


def attend(meta, pieces, grad, group):
    _, rows, width = pieces[0].shape
    step = min(width, 2 * HDIM)
    piece = pl.BlockSpec((3, rows, step), lambda i: (0, 0, i))
    pairs = 16 * rows * rows * width
    return pl.pallas_call(
        attend_kernel,
        out_shape=[sds((width, 4 * rows), bf16)] + [sds((3, rows, width), bf16)] * 4,
        grid=(width // step,),
        in_specs=[pl.BlockSpec(memory_space=pltpu.SMEM)]
        + [piece] * 4
        + [pl.BlockSpec((4 * rows, step), lambda i: (0, group * (width // step) + i))],
        out_specs=[pl.BlockSpec((step, 4 * rows), lambda i: (i, 0))] + [piece] * 4,
        compiler_params=params(),
        cost_estimate=pl.CostEstimate(
            flops=12 * pairs, bytes_accessed=56 * rows * width, transcendentals=pairs // HDIM
        ),
        name="attend",
    )(meta, *pieces, grad)


def weight_kernel(half, heads_ref, g0, g1, g2, g3, out_ref):
    grad = jnp.concatenate([g0[...], g1[...], g2[...], g3[...]], axis=0)
    out_ref[...] = dot(heads_ref[...], grad, 1, 0).astype(out_ref.dtype)


def weight_half(half, heads, grads, dtype):
    rows, outw = grads[0].shape
    width = heads.shape[0] // 2
    tile = 512
    return pl.pallas_call(
        weight_kernel,
        out_shape=sds((width, outw), dtype),
        grid_spec=pltpu.PrefetchScalarGridSpec(
            num_scalar_prefetch=1,
            grid=(outw // tile,),
            in_specs=[pl.BlockSpec((width, 4 * rows), lambda i, half: (half[0], 0))]
            + [pl.BlockSpec((rows, tile), lambda i, half: (0, i))] * 4,
            out_specs=pl.BlockSpec((width, tile), lambda i, half: (0, i)),
        ),
        compiler_params=params(),
        cost_estimate=pl.CostEstimate(
            flops=8 * rows * width * outw, bytes_accessed=8 * rows * outw + 4 * width * outw, transcendentals=0
        ),
        name="weight_half",
    )(half, heads, *grads)


def split_kernel(chip, keep_ref, recv_ref, own_ref, *sends):
    size = own_ref.shape[0]
    for j in range(4):
        at = pl.ds(pl.multiple_of((chip[0] ^ j) * size, size), size)
        total = keep_ref[at, :] + recv_ref[at, :].astype(f32)
        if j:
            sends[j - 1][...] = total.astype(bf16)
        else:
            own_ref[...] = total


def split(chip, keep, recv):
    rows, outw = keep.shape
    size = rows // 4
    return pl.pallas_call(
        split_kernel,
        out_shape=[sds((size, outw), f32)] + [sds((size, outw), bf16)] * 3,
        in_specs=[pl.BlockSpec(memory_space=pltpu.SMEM)] + [pl.BlockSpec(memory_space=pltpu.VMEM)] * 2,
        out_specs=[pl.BlockSpec(memory_space=pltpu.VMEM)] * 4,
        compiler_params=params(),
        cost_estimate=pl.CostEstimate(flops=rows * outw, bytes_accessed=9 * rows * outw, transcendentals=0),
        name="split_sum",
    )(chip, keep, recv)


def total_kernel(scale, own_ref, r1, r2, r3, out_ref):
    total = own_ref[...] + r1[...].astype(f32) + r2[...].astype(f32) + r3[...].astype(f32)
    out_ref[...] = (total * scale).astype(bf16)


def total_of(own, parts, scale):
    return pl.pallas_call(
        functools.partial(total_kernel, scale),
        out_shape=sds(own.shape, bf16),
        in_specs=[pl.BlockSpec(memory_space=pltpu.VMEM)] * 4,
        out_specs=pl.BlockSpec(memory_space=pltpu.VMEM),
        compiler_params=params(),
        cost_estimate=pl.CostEstimate(flops=3 * own.size, bytes_accessed=12 * own.size, transcendentals=0),
        name="scene_total",
    )(own, *parts)


def join_weight_kernel(place, *refs):
    out_ref = refs[-1]
    size = refs[0].shape[0]
    count = len(refs) - 1
    for n, ref in enumerate(refs[:-1]):
        g, j = divmod(n, 8)
        at = ((place[0] ^ (j // 4)) * 4 + (place[1] ^ (j % 4)) + g * 8) * size
        out_ref[pl.ds(pl.multiple_of(at, size), size), :] = ref[...]


def join_weight(place, parts):
    size, outw = parts[0].shape
    rows = size * len(parts)
    return pl.pallas_call(
        join_weight_kernel,
        out_shape=sds((rows, outw), bf16),
        in_specs=[pl.BlockSpec(memory_space=pltpu.SMEM)] + [pl.BlockSpec(memory_space=pltpu.VMEM)] * len(parts),
        out_specs=pl.BlockSpec(memory_space=pltpu.VMEM),
        compiler_params=params(),
        cost_estimate=pl.CostEstimate(flops=0, bytes_accessed=4 * rows * outw, transcendentals=0),
        name="join_weight",
    )(place, *parts)


def join_kernel(meta, *refs):
    z = meta[0]
    outs = refs[-3:]
    width = outs[0].shape[1] // 4
    part = width // GROUPS
    for g in range(GROUPS):
        for k in range(4):
            start = pl.multiple_of((z ^ k) * width + g * part, 128)
            for i, out_ref in enumerate(outs):
                out_ref[:, pl.ds(start, part)] = refs[g * 4 + k][i]


def join(meta, backs):
    _, rows, part = backs[0].shape
    width = part * GROUPS * 4
    return pl.pallas_call(
        join_kernel,
        out_shape=[sds((rows, width), bf16)] * 3,
        in_specs=[pl.BlockSpec(memory_space=pltpu.SMEM)] + [pl.BlockSpec(memory_space=pltpu.VMEM)] * len(backs),
        out_specs=[pl.BlockSpec(memory_space=pltpu.VMEM)] * 3,
        compiler_params=params(),
        cost_estimate=pl.CostEstimate(flops=0, bytes_accessed=12 * rows * width, transcendentals=0),
        name="join_heads",
    )(meta, *backs)


def dense_body(queries, keys_in, values, out_grad, out_weight, voxel_count):
    z = lax.axis_index("shard")
    dp = lax.axis_index("dp")
    core, chip = dp & 1, dp >> 1
    meta = jnp.stack([z, voxel_count[0]]).astype(jnp.int32)

    across = swap(out_grad, "shard", 4, 2)
    beside = swap(out_grad, "shard", 4, 1)
    packed = pack(meta, queries, keys_in, values)
    pieces = []
    for g in range(GROUPS):
        mine = packed[4 * g : 4 * g + 4]
        pieces.append([mine[0]] + [swap(mine[k], "shard", 4, k) for k in (1, 2, 3)])
    corner = swap(across, "shard", 4, 1)
    grads = (out_grad, beside, across, corner)
    grad = grad_attn(meta, grads, out_weight)

    backs, weight_parts = [], []
    for g in range(GROUPS):
        heads, *mine = attend(meta, pieces[g], grad, g)
        backs += [mine[0]] + [swap(mine[k], "shard", 4, k) for k in (1, 2, 3)]
        send = weight_half(jnp.reshape(1 - core, (1,)), heads, grads, bf16)
        recv = swap(send, "dp", 8, 1)
        keep = weight_half(jnp.reshape(core, (1,)), heads, grads, f32)
        own, *sends = split(jnp.reshape(chip, (1,)), keep, recv)
        arrived = [swap(sends[j - 1], "dp", 8, 2 * j) for j in (1, 2, 3)]
        done = total_of(own, arrived, 1.0 / 8)
        near = [done] + [swap(done, "dp", 8, 2 * j) for j in (1, 2, 3)]
        weight_parts += near + [swap(part, "dp", 8, 1) for part in near]
    grad_weight = join_weight(jnp.stack([core, chip]).astype(jnp.int32), weight_parts)
    return (*join(meta, backs), grad_weight)


def attend_listed(queries, keys_in, values, block_ids, live_count):
    row_count, width_all = queries.shape
    head_count = width_all // HDIM
    block_count = row_count // BLOCK
    score_scale = 1.0 / math.sqrt(HDIM)
    query_blk = queries.reshape(block_count, BLOCK, head_count, HDIM)
    key_blk = keys_in.reshape(block_count, BLOCK, head_count, HDIM)[block_ids].reshape(
        block_count, NB * BLOCK, head_count, HDIM
    )
    value_blk = values.reshape(block_count, BLOCK, head_count, HDIM)[block_ids].reshape(
        block_count, NB * BLOCK, head_count, HDIM
    )
    query_pos = jnp.arange(row_count, dtype=jnp.int32).reshape(block_count, BLOCK)
    key_pos = (
        block_ids[:, :, None] * BLOCK + jnp.arange(BLOCK, dtype=jnp.int32)[None, None, :]
    ).reshape(block_count, NB * BLOCK)
    allowed = (key_pos[:, None, :] < live_count) | (query_pos[:, :, None] >= live_count)
    scores = (
        jnp.einsum("bqhd,bkhd->bhqk", query_blk, key_blk, preferred_element_type=jnp.float32)
        * score_scale
    )
    scores = jnp.where(allowed[:, None], scores, -jnp.inf)
    peak = jnp.max(scores, axis=-1, keepdims=True)
    weights = jnp.exp(scores - peak)
    probs = weights / jnp.sum(weights, axis=-1, keepdims=True)
    return (query_blk, key_blk, value_blk, probs)


def listed_body(queries, keys_in, values, out_grad, out_weight, block_lists, voxel_count):
    local_rows = queries.shape[0]
    live_count = voxel_count[0]
    block_ids = block_lists[0]
    positions = lax.axis_index("shard") * local_rows + jnp.arange(local_rows, dtype=jnp.int32)
    grad_live = jnp.where((positions < live_count)[:, None], out_grad, jnp.zeros_like(out_grad))
    query_head, key_head, value_head = (
        lax.all_to_all(queries, "shard", split_axis=1, concat_axis=0, tiled=True),
        lax.all_to_all(keys_in, "shard", split_axis=1, concat_axis=0, tiled=True),
        lax.all_to_all(values, "shard", split_axis=1, concat_axis=0, tiled=True),
    )
    row_count, width_all = query_head.shape
    head_count = width_all // HDIM
    block_count = row_count // BLOCK
    score_scale = 1.0 / math.sqrt(HDIM)
    query_blk, key_blk, value_blk, probs = attend_listed(
        query_head, key_head, value_head, block_ids, live_count
    )
    prob_bf = probs.astype(jnp.bfloat16)
    heads_out = (
        jnp.einsum("bhqk,bkhd->bqhd", prob_bf, value_blk, preferred_element_type=jnp.float32)
        .reshape(row_count, width_all)
        .astype(jnp.bfloat16)
    )
    row_piece = lax.all_gather(grad_live, "shard", axis=0, tiled=True)
    acc_now = jnp.einsum("rw,ro->wo", heads_out, row_piece, preferred_element_type=jnp.float32)
    product = jnp.einsum("ro,wo->rw", row_piece, out_weight, preferred_element_type=jnp.float32)
    grad_o = product.astype(jnp.bfloat16).reshape(block_count, BLOCK, head_count, HDIM)
    grad_prob = jnp.einsum("bqhd,bkhd->bhqk", grad_o, value_blk, preferred_element_type=jnp.float32)
    row_delta = jnp.sum(probs * grad_prob, axis=-1, keepdims=True)
    dscore = (probs * (grad_prob - row_delta) * score_scale).astype(jnp.bfloat16)
    grad_query = (
        jnp.einsum("bhqk,bkhd->bqhd", dscore, key_blk, preferred_element_type=jnp.float32)
        .reshape(row_count, width_all)
        .astype(jnp.bfloat16)
    )
    onehot = (
        block_ids[:, :, None] == jnp.arange(block_count, dtype=jnp.int32)[None, None, :]
    ).astype(jnp.float32)
    key_parts = jnp.einsum(
        "bhqk,bqhd->bkhd", dscore, query_blk, preferred_element_type=jnp.float32
    ).reshape(block_count, NB, BLOCK, width_all)
    value_parts = jnp.einsum(
        "bhqk,bqhd->bkhd", prob_bf, grad_o, preferred_element_type=jnp.float32
    ).reshape(block_count, NB, BLOCK, width_all)
    grad_key = (
        jnp.einsum("bjc,bjrx->crx", onehot, key_parts, precision=lax.Precision.HIGHEST)
        .reshape(row_count, width_all)
        .astype(jnp.bfloat16)
    )
    grad_value = (
        jnp.einsum("bjc,bjrx->crx", onehot, value_parts, precision=lax.Precision.HIGHEST)
        .reshape(row_count, width_all)
        .astype(jnp.bfloat16)
    )
    query_back, key_back, value_back = (
        lax.all_to_all(grad_query, "shard", split_axis=0, concat_axis=1, tiled=True),
        lax.all_to_all(grad_key, "shard", split_axis=0, concat_axis=1, tiled=True),
        lax.all_to_all(grad_value, "shard", split_axis=0, concat_axis=1, tiled=True),
    )
    scene_total = lax.axis_size("dp")
    summed = lax.psum(acc_now, "dp")
    grad_weight = (summed / scene_total).astype(jnp.bfloat16)
    return (query_back, key_back, value_back, grad_weight)


def body(queries, keys_in, values, out_grad, out_weight, block_lists, voxel_count):
    dense = block_lists.shape[1] == NB and queries.shape[0] == BLOCK
    if dense and lax.axis_size("shard") == 4 and lax.axis_size("dp") == 8:
        return dense_body(queries, keys_in, values, out_grad, out_weight, voxel_count)
    return listed_body(queries, keys_in, values, out_grad, out_weight, block_lists, voxel_count)


def solution(mesh):
    return jax.shard_map(
        body,
        mesh=mesh,
        in_specs=(
            P(("dp", "shard"), None),
            P(("dp", "shard"), None),
            P(("dp", "shard"), None),
            P(("dp", "shard"), None),
            P("shard", None),
            P("dp", None, None),
            P("dp"),
        ),
        out_specs=(
            P(("dp", "shard"), None),
            P(("dp", "shard"), None),
            P(("dp", "shard"), None),
            P("shard", None),
        ),
        check_vma=False,
    )
```

```python
import functools
import math

import jax
import jax.numpy as jnp
from jax import lax
from jax.experimental import pallas as pl
from jax.experimental.pallas import tpu as pltpu
from jax.sharding import PartitionSpec as P

HDIM = 128
BLOCK = 128
NB = 4
GROUPS = 2
MIB = 1024 * 1024
DP = ("chips", "core")

NO_COST = pl.CostEstimate(flops=0, bytes_accessed=1024, transcendentals=0)

f32 = jnp.float32
bf16 = jnp.bfloat16


def dot(a, b, ca, cb):
    return lax.dot_general(a, b, (((ca,), (cb,)), ((), ())), preferred_element_type=f32)


def sds(shape, dtype):
    return jax.ShapeDtypeStruct(shape, dtype)


def params(mib=8):
    return pltpu.CompilerParams(vmem_limit_bytes=mib * MIB)


def swap(x, axis, size, flip):
    return lax.ppermute(x, axis, [(i, i ^ flip) for i in range(size)])


def after(x, *earlier):
    return lax.optimization_barrier((x, *earlier))[0]


def pack_kernel(meta, q_ref, k_ref, v_ref, *outs):
    z = meta[0]
    width = q_ref.shape[1] // 4
    part = width // GROUPS
    for g in range(GROUPS):
        for k in range(4):
            start = pl.multiple_of((z ^ k) * width + g * part, 128)
            for i, ref in enumerate((q_ref, k_ref, v_ref)):
                outs[g * 4 + k][i] = ref[:, pl.ds(start, part)]


def pack(meta, queries, keys_in, values):
    rows, width = queries.shape
    part = width // 4 // GROUPS
    return pl.pallas_call(
        pack_kernel,
        out_shape=[sds((3, rows, part), bf16)] * (4 * GROUPS),
        in_specs=[pl.BlockSpec(memory_space=pltpu.SMEM)]
        + [pl.BlockSpec(memory_space=pltpu.VMEM)] * 3,
        out_specs=[pl.BlockSpec(memory_space=pltpu.VMEM)] * (4 * GROUPS),
        compiler_params=params(),
        cost_estimate=NO_COST,
        name="pack_heads",
    )(meta, queries, keys_in, values)


def token_pos(shape, dim, z):
    return lax.broadcasted_iota(jnp.int32, shape, dim) ^ (z * BLOCK)


def grad_attn_kernel(meta, g0, g1, g2, g3, w_ref, out_ref):
    z, count = meta[0], meta[1]
    grad = jnp.concatenate([g0[...], g1[...], g2[...], g3[...]], axis=0)
    live = token_pos((grad.shape[0], 1), 0, z) < count
    product = dot(grad, w_ref[...], 1, 1)
    out_ref[...] = jnp.where(live, product, 0.0).astype(bf16)


def grad_attn(meta, grads, weight):
    rows, outw = grads[0].shape
    width = weight.shape[0]
    tile = 256
    return pl.pallas_call(
        grad_attn_kernel,
        out_shape=sds((4 * rows, width), bf16),
        grid=(width // tile,),
        in_specs=[pl.BlockSpec(memory_space=pltpu.SMEM)]
        + [pl.BlockSpec((rows, outw), lambda i: (0, 0))] * 4
        + [pl.BlockSpec((tile, outw), lambda i: (i, 0))],
        out_specs=pl.BlockSpec((4 * rows, tile), lambda i: (0, i)),
        compiler_params=params(16),
        cost_estimate=NO_COST,
        name="grad_attn",
    )(meta, *grads, weight)


def attend_kernel(meta, p0, p1, p2, p3, do_ref, ot_ref, b0, b1, b2, b3):
    z, count = meta[0], meta[1]
    pieces, backs = (p0, p1, p2, p3), (b0, b1, b2, b3)
    rows = p0.shape[1]
    total = 4 * rows
    tile = 2 * rows
    scale = 1.0 / math.sqrt(HDIM)
    key_live = token_pos((total, 1), 0, z) < count
    query_live = token_pos((1, total), 1, z) < count
    for h in range(p0.shape[2] // HDIM):
        cols = slice(h * HDIM, (h + 1) * HDIM)
        query, key, value = (jnp.concatenate([p[i, :, cols] for p in pieces], axis=0) for i in range(3))
        grad = do_ref[:, cols]
        grad_key = grad_value = jnp.zeros((total, HDIM), f32)
        for t in range(2):
            part = slice(t * tile, (t + 1) * tile)
            live = query_live[:, part]
            scores = dot(key, query[part], 1, 1) * scale
            scores = jnp.where(key_live | ~live, scores, -jnp.inf)
            weights = jnp.exp(scores - jnp.max(scores, axis=0, keepdims=True))
            probs = weights * (1.0 / jnp.sum(weights, axis=0, keepdims=True))
            prob_bf = probs.astype(bf16)
            heads = dot(value, prob_bf, 0, 0)
            ot_ref[cols, part] = jnp.where(live, heads, 0.0).astype(bf16)
            grad_prob = dot(value, grad[part], 1, 1)
            row_delta = jnp.sum(probs * grad_prob, axis=0, keepdims=True)
            dscore = (probs * (grad_prob - row_delta) * scale).astype(bf16)
            grad_query = dot(key, dscore, 0, 0).T.astype(bf16)
            backs[2 * t][0, :, cols] = grad_query[:rows]
            backs[2 * t + 1][0, :, cols] = grad_query[rows:]
            grad_key += dot(dscore, query[part], 1, 0)
            grad_value += dot(prob_bf, grad[part], 1, 0)
        for k in range(4):
            mine = slice(k * rows, (k + 1) * rows)
            backs[k][1, :, cols] = grad_key[mine].astype(bf16)
            backs[k][2, :, cols] = grad_value[mine].astype(bf16)


def attend(meta, pieces, grad, group):
    _, rows, width = pieces[0].shape
    step = min(width, 2 * HDIM)
    piece = pl.BlockSpec((3, rows, step), lambda i: (0, 0, i))
    return pl.pallas_call(
        attend_kernel,
        out_shape=[sds((width, 4 * rows), bf16)] + [sds((3, rows, width), bf16)] * 4,
        grid=(width // step,),
        in_specs=[pl.BlockSpec(memory_space=pltpu.SMEM)]
        + [piece] * 4
        + [pl.BlockSpec((4 * rows, step), lambda i: (0, group * (width // step) + i))],
        out_specs=[pl.BlockSpec((step, 4 * rows), lambda i: (i, 0))] + [piece] * 4,
        compiler_params=params(16),
        cost_estimate=NO_COST,
        name="attend",
    )(meta, *pieces, grad)


def weight_kernel(half, *refs):
    *heads, g0, g1, g2, g3, out_ref = refs
    grad = jnp.concatenate([g0[...], g1[...], g2[...], g3[...]], axis=0)
    rows = out_ref.shape[0] // len(heads)
    for n, ref in enumerate(heads):
        out_ref[n * rows : (n + 1) * rows, :] = dot(ref[...], grad, 1, 0).astype(out_ref.dtype)


def weight_half(half, heads, grads, dtype):
    rows, outw = grads[0].shape
    part = heads[0].shape[0] // 2
    width = part * len(heads)
    tile = 512
    return pl.pallas_call(
        weight_kernel,
        out_shape=sds((width, outw), dtype),
        grid_spec=pltpu.PrefetchScalarGridSpec(
            num_scalar_prefetch=1,
            grid=(outw // tile,),
            in_specs=[pl.BlockSpec((part, 4 * rows), lambda i, half: (half[0], 0))] * len(heads)
            + [pl.BlockSpec((rows, tile), lambda i, half: (0, i))] * 4,
            out_specs=pl.BlockSpec((width, tile), lambda i, half: (0, i)),
        ),
        compiler_params=params(16),
        cost_estimate=NO_COST,
        name="weight_half",
    )(half, *heads, *grads)


def whole(kernel, out_shape, operands, name, scalars=0):
    return pl.pallas_call(
        kernel,
        out_shape=out_shape,
        in_specs=[pl.BlockSpec(memory_space=pltpu.SMEM)] * scalars
        + [pl.BlockSpec(memory_space=pltpu.VMEM)] * (len(operands) - scalars),
        out_specs=jax.tree.map(lambda _: pl.BlockSpec(memory_space=pltpu.VMEM), out_shape),
        compiler_params=params(),
        cost_estimate=NO_COST,
        name=name,
    )(*operands)


def add_kernel(keep_ref, given_ref, out_ref):
    out_ref[...] = (keep_ref[...] + given_ref[...].astype(f32)).astype(bf16)


def add_parts(keep, given):
    return whole(add_kernel, sds(keep.shape, bf16), (keep, given), "add_parts")


def scale_kernel(scale, in_ref, out_ref):
    out_ref[...] = (in_ref[...].astype(f32) * scale).astype(bf16)


def scaled(x, scale):
    return whole(functools.partial(scale_kernel, scale), sds(x.shape, bf16), (x,), "scene_mean")


def pair_kernel(core, own_ref, other_ref, out_ref):
    rows = own_ref.shape[0] // GROUPS
    for g in range(GROUPS):
        part = slice(g * rows, (g + 1) * rows)
        for other, ref in enumerate((own_ref, other_ref)):
            at = pl.multiple_of((core[0] ^ other) * rows + 2 * g * rows, rows)
            out_ref[pl.ds(at, rows), :] = ref[part, :]


def pair(core, own, other):
    rows, outw = own.shape
    return whole(pair_kernel, sds((2 * rows, outw), bf16), (core, own, other), "pair_halves", 1)


def join_kernel(meta, *refs):
    z = meta[0]
    outs = refs[-3:]
    width = outs[0].shape[1] // 4
    part = width // GROUPS
    for g in range(GROUPS):
        for k in range(4):
            start = pl.multiple_of((z ^ k) * width + g * part, 128)
            for i, out_ref in enumerate(outs):
                out_ref[:, pl.ds(start, part)] = refs[g * 4 + k][i]


def join(meta, backs):
    _, rows, part = backs[0].shape
    width = part * GROUPS * 4
    return pl.pallas_call(
        join_kernel,
        out_shape=[sds((rows, width), bf16)] * 3,
        in_specs=[pl.BlockSpec(memory_space=pltpu.SMEM)] + [pl.BlockSpec(memory_space=pltpu.VMEM)] * len(backs),
        out_specs=[pl.BlockSpec(memory_space=pltpu.VMEM)] * 3,
        compiler_params=params(),
        cost_estimate=NO_COST,
        name="join_heads",
    )(meta, *backs)


def dense_body(queries, keys_in, values, out_grad, out_weight, voxel_count):
    z = lax.axis_index("shard")
    meta = jnp.stack([z, voxel_count[0]]).astype(jnp.int32)

    def send(x, k, *earlier):
        return swap(after(x, *earlier) if earlier else x, "shard", 4, k)

    across = send(out_grad, 2)
    beside = send(out_grad, 1)
    packed = pack(meta, queries, keys_in, values)
    first, second = packed[:4], packed[4:]
    first3 = send(first[3], 3)
    first1 = send(first[1], 1, beside)
    first2 = send(first[2], 2, across)
    corner = send(across, 1, first3)
    second3 = send(second[3], 3, first3, across)
    second2 = send(second[2], 2, first2)
    second1 = send(second[1], 1, first1, corner)
    grads = (out_grad, beside, across, corner)
    grad = grad_attn(meta, grads, out_weight)

    pieces = ((first[0], first1, first2, first3), (second[0], second1, second2, second3))
    backs, heads = [], []
    last = pieces[1]
    for g in range(GROUPS):
        head, *mine = attend(meta, pieces[g], grad, g)
        heads.append(head)
        last = [mine[0]] + [send(mine[k], k, last[k]) for k in (1, 2, 3)]
        backs += last

    core = lax.axis_index("core").astype(jnp.int32).reshape(1)
    ready = [after(heads[0], backs[1]), heads[1]]
    given = swap(weight_half(1 - core, ready, grads, bf16), "core", 2, 1)
    part = add_parts(weight_half(core, ready, grads, f32), after(given, *backs[2:4]))
    total = after(lax.psum(part, "chips"), *backs[5:8])
    total = scaled(total, 1.0 / (lax.axis_size("chips") * lax.axis_size("core")))
    grad_weight = pair(core, total, swap(total, "core", 2, 1))
    return (*join(meta, backs), grad_weight)


def attend_listed(queries, keys_in, values, block_ids, live_count):
    row_count, width_all = queries.shape
    head_count = width_all // HDIM
    block_count = row_count // BLOCK
    score_scale = 1.0 / math.sqrt(HDIM)
    query_blk = queries.reshape(block_count, BLOCK, head_count, HDIM)
    key_blk = keys_in.reshape(block_count, BLOCK, head_count, HDIM)[block_ids].reshape(
        block_count, NB * BLOCK, head_count, HDIM
    )
    value_blk = values.reshape(block_count, BLOCK, head_count, HDIM)[block_ids].reshape(
        block_count, NB * BLOCK, head_count, HDIM
    )
    query_pos = jnp.arange(row_count, dtype=jnp.int32).reshape(block_count, BLOCK)
    key_pos = (
        block_ids[:, :, None] * BLOCK + jnp.arange(BLOCK, dtype=jnp.int32)[None, None, :]
    ).reshape(block_count, NB * BLOCK)
    allowed = (key_pos[:, None, :] < live_count) | (query_pos[:, :, None] >= live_count)
    scores = (
        jnp.einsum("bqhd,bkhd->bhqk", query_blk, key_blk, preferred_element_type=jnp.float32)
        * score_scale
    )
    scores = jnp.where(allowed[:, None], scores, -jnp.inf)
    peak = jnp.max(scores, axis=-1, keepdims=True)
    weights = jnp.exp(scores - peak)
    probs = weights / jnp.sum(weights, axis=-1, keepdims=True)
    return (query_blk, key_blk, value_blk, probs)


def listed_body(queries, keys_in, values, out_grad, out_weight, block_lists, voxel_count):
    local_rows = queries.shape[0]
    live_count = voxel_count[0]
    block_ids = block_lists[0]
    positions = lax.axis_index("shard") * local_rows + jnp.arange(local_rows, dtype=jnp.int32)
    grad_live = jnp.where((positions < live_count)[:, None], out_grad, jnp.zeros_like(out_grad))
    query_head, key_head, value_head = (
        lax.all_to_all(queries, "shard", split_axis=1, concat_axis=0, tiled=True),
        lax.all_to_all(keys_in, "shard", split_axis=1, concat_axis=0, tiled=True),
        lax.all_to_all(values, "shard", split_axis=1, concat_axis=0, tiled=True),
    )
    row_count, width_all = query_head.shape
    head_count = width_all // HDIM
    block_count = row_count // BLOCK
    score_scale = 1.0 / math.sqrt(HDIM)
    query_blk, key_blk, value_blk, probs = attend_listed(
        query_head, key_head, value_head, block_ids, live_count
    )
    prob_bf = probs.astype(jnp.bfloat16)
    heads_out = (
        jnp.einsum("bhqk,bkhd->bqhd", prob_bf, value_blk, preferred_element_type=jnp.float32)
        .reshape(row_count, width_all)
        .astype(jnp.bfloat16)
    )
    row_piece = lax.all_gather(grad_live, "shard", axis=0, tiled=True)
    acc_now = jnp.einsum("rw,ro->wo", heads_out, row_piece, preferred_element_type=jnp.float32)
    product = jnp.einsum("ro,wo->rw", row_piece, out_weight, preferred_element_type=jnp.float32)
    grad_o = product.astype(jnp.bfloat16).reshape(block_count, BLOCK, head_count, HDIM)
    grad_prob = jnp.einsum("bqhd,bkhd->bhqk", grad_o, value_blk, preferred_element_type=jnp.float32)
    row_delta = jnp.sum(probs * grad_prob, axis=-1, keepdims=True)
    dscore = (probs * (grad_prob - row_delta) * score_scale).astype(jnp.bfloat16)
    grad_query = (
        jnp.einsum("bhqk,bkhd->bqhd", dscore, key_blk, preferred_element_type=jnp.float32)
        .reshape(row_count, width_all)
        .astype(jnp.bfloat16)
    )
    onehot = (
        block_ids[:, :, None] == jnp.arange(block_count, dtype=jnp.int32)[None, None, :]
    ).astype(jnp.float32)
    key_parts = jnp.einsum(
        "bhqk,bqhd->bkhd", dscore, query_blk, preferred_element_type=jnp.float32
    ).reshape(block_count, NB, BLOCK, width_all)
    value_parts = jnp.einsum(
        "bhqk,bqhd->bkhd", prob_bf, grad_o, preferred_element_type=jnp.float32
    ).reshape(block_count, NB, BLOCK, width_all)
    grad_key = (
        jnp.einsum("bjc,bjrx->crx", onehot, key_parts, precision=lax.Precision.HIGHEST)
        .reshape(row_count, width_all)
        .astype(jnp.bfloat16)
    )
    grad_value = (
        jnp.einsum("bjc,bjrx->crx", onehot, value_parts, precision=lax.Precision.HIGHEST)
        .reshape(row_count, width_all)
        .astype(jnp.bfloat16)
    )
    query_back, key_back, value_back = (
        lax.all_to_all(grad_query, "shard", split_axis=0, concat_axis=1, tiled=True),
        lax.all_to_all(grad_key, "shard", split_axis=0, concat_axis=1, tiled=True),
        lax.all_to_all(grad_value, "shard", split_axis=0, concat_axis=1, tiled=True),
    )
    scene_total = lax.axis_size(DP)
    summed = lax.psum(acc_now, DP)
    grad_weight = (summed / scene_total).astype(jnp.bfloat16)
    return (query_back, key_back, value_back, grad_weight)


def body(queries, keys_in, values, out_grad, out_weight, block_lists, voxel_count):
    dense = block_lists.shape[1] == NB and queries.shape[0] == BLOCK
    if dense and lax.axis_size("shard") == 4:
        return dense_body(queries, keys_in, values, out_grad, out_weight, voxel_count)
    return listed_body(queries, keys_in, values, out_grad, out_weight, block_lists, voxel_count)


def solution(mesh):
    chips = mesh.shape["dp"] // 2
    mesh = jax.sharding.Mesh(mesh.devices.reshape(chips, 2, -1), ("chips", "core", "shard"))
    return jax.shard_map(
        body,
        mesh=mesh,
        in_specs=(
            P((*DP, "shard"), None),
            P((*DP, "shard"), None),
            P((*DP, "shard"), None),
            P((*DP, "shard"), None),
            P("shard", None),
            P(DP, None, None),
            P(DP),
        ),
        out_specs=(
            P((*DP, "shard"), None),
            P((*DP, "shard"), None),
            P((*DP, "shard"), None),
            P("shard", None),
        ),
        check_vma=False,
    )
```

```python
import functools
import math

import jax
import jax.numpy as jnp
from jax import lax
from jax.experimental import pallas as pl
from jax.experimental.pallas import tpu as pltpu
from jax.sharding import PartitionSpec as P

HDIM = 128
BLOCK = 128
NB = 4
MIB = 1024 * 1024
DP = ("chips", "core")

Z, COUNT, CORE, CHIP = range(4)

NO_COST = pl.CostEstimate(flops=0, bytes_accessed=1024, transcendentals=0)

f32 = jnp.float32
bf16 = jnp.bfloat16


def dot(a, b, ca, cb):
    return lax.dot_general(a, b, (((ca,), (cb,)), ((), ())), preferred_element_type=f32)


def sds(shape, dtype):
    return jax.ShapeDtypeStruct(shape, dtype)


def params(mib=8):
    return pltpu.CompilerParams(vmem_limit_bytes=mib * MIB)


def swap(x, axis, size, flip):
    return lax.ppermute(x, axis, [(i, i ^ flip) for i in range(size)])


def after(x, *earlier):
    return lax.optimization_barrier((x, *earlier))[0]


def run_all(copies):
    for copy in copies:
        copy.start()
    for copy in copies:
        copy.wait()


def pack_kernel(meta, q_ref, k_ref, v_ref, *refs):
    *outs, sems = refs
    width = outs[0].shape[2]
    copies = []
    for k, out_ref in enumerate(outs):
        start = pl.multiple_of((meta[Z] ^ k) * width, 128)
        for i, ref in enumerate((q_ref, k_ref, v_ref)):
            copies.append(pltpu.make_async_copy(ref.at[:, pl.ds(start, width)], out_ref.at[i], sems.at[3 * k + i]))
    run_all(copies)


def pack(meta, queries, keys_in, values):
    rows, width = queries.shape
    return pl.pallas_call(
        pack_kernel,
        out_shape=[sds((3, rows, width // 4), bf16)] * 4,
        in_specs=[pl.BlockSpec(memory_space=pltpu.SMEM)] + [pl.BlockSpec(memory_space=pl.ANY)] * 3,
        out_specs=[pl.BlockSpec(memory_space=pltpu.VMEM)] * 4,
        scratch_shapes=[pltpu.SemaphoreType.DMA((12,))],
        compiler_params=params(),
        cost_estimate=NO_COST,
        name="pack_heads",
    )(meta, queries, keys_in, values)


def token_pos(shape, dim, z):
    return lax.broadcasted_iota(jnp.int32, shape, dim) ^ (z * BLOCK)


def grad_attn_kernel(meta, *refs):
    *grads, w_ref, out_ref = refs
    grad = jnp.concatenate([g[...] for g in grads], axis=0)
    live = token_pos((grad.shape[0], 1), 0, meta[Z]) < meta[COUNT]
    product = dot(grad, w_ref[...], 1, 1)
    out_ref[...] = jnp.where(live, product, 0.0).astype(bf16)


def grad_attn(meta, grads, weight):
    rows = sum(g.shape[0] for g in grads)
    width, outw = weight.shape
    tile = 256
    return pl.pallas_call(
        grad_attn_kernel,
        out_shape=sds((rows, width), bf16),
        grid=(width // tile,),
        in_specs=[pl.BlockSpec(memory_space=pltpu.SMEM)]
        + [pl.BlockSpec(g.shape, lambda i: (0, 0)) for g in grads]
        + [pl.BlockSpec((tile, outw), lambda i: (i, 0))],
        out_specs=pl.BlockSpec((rows, tile), lambda i: (0, i)),
        compiler_params=params(16),
        cost_estimate=NO_COST,
        name="grad_attn",
    )(meta, *grads, weight)


def attend_kernel(meta, p0, p1, p2, p3, do_ref, ot_ref, b0, b1, b2, b3):
    z, count = meta[Z], meta[COUNT]
    pieces, backs = (p0, p1, p2, p3), (b0, b1, b2, b3)
    rows = p0.shape[1]
    total = 4 * rows
    tile = 2 * rows
    scale = 1.0 / math.sqrt(HDIM)
    key_live = token_pos((total, 1), 0, z) < count
    query_live = token_pos((1, total), 1, z) < count
    for h in range(p0.shape[2] // HDIM):
        cols = slice(h * HDIM, (h + 1) * HDIM)
        query, key, value = (jnp.concatenate([p[i, :, cols] for p in pieces], axis=0) for i in range(3))
        grad = do_ref[:, cols]
        grad_key = grad_value = jnp.zeros((total, HDIM), f32)
        for t in range(2):
            part = slice(t * tile, (t + 1) * tile)
            live = query_live[:, part]
            scores = dot(key, query[part], 1, 1) * scale
            scores = jnp.where(key_live | ~live, scores, -jnp.inf)
            weights = jnp.exp(scores - jnp.max(scores, axis=0, keepdims=True))
            probs = weights * (1.0 / jnp.sum(weights, axis=0, keepdims=True))
            prob_bf = probs.astype(bf16)
            heads = dot(value, prob_bf, 0, 0)
            ot_ref[cols, part] = jnp.where(live, heads, 0.0).astype(bf16)
            grad_prob = dot(value, grad[part], 1, 1)
            row_delta = jnp.sum(probs * grad_prob, axis=0, keepdims=True)
            dscore = (probs * (grad_prob - row_delta) * scale).astype(bf16)
            grad_query = dot(key, dscore, 0, 0).T.astype(bf16)
            backs[2 * t][0, :, cols] = grad_query[:rows]
            backs[2 * t + 1][0, :, cols] = grad_query[rows:]
            grad_key += dot(dscore, query[part], 1, 0)
            grad_value += dot(prob_bf, grad[part], 1, 0)
        for k in range(4):
            mine = slice(k * rows, (k + 1) * rows)
            backs[k][1, :, cols] = grad_key[mine].astype(bf16)
            backs[k][2, :, cols] = grad_value[mine].astype(bf16)


def attend(meta, pieces, grad):
    _, rows, width = pieces[0].shape
    step = 2 * HDIM
    piece = pl.BlockSpec((3, rows, step), lambda i: (0, 0, i))
    return pl.pallas_call(
        attend_kernel,
        out_shape=[sds((width, 4 * rows), bf16)] + [sds((3, rows, width), bf16)] * 4,
        grid=(width // step,),
        in_specs=[pl.BlockSpec(memory_space=pltpu.SMEM)]
        + [piece] * 4
        + [pl.BlockSpec((4 * rows, step), lambda i: (0, i))],
        out_specs=[pl.BlockSpec((step, 4 * rows), lambda i: (i, 0))] + [piece] * 4,
        compiler_params=params(16),
        cost_estimate=NO_COST,
        name="attend",
    )(meta, *pieces, grad)


def weight_kernel(other, meta, heads_ref, *refs):
    grads, outs = refs[:-4], refs[-4:]
    grad = jnp.concatenate([g[...] for g in grads], axis=0)
    size = outs[0].shape[0]
    lines = []
    for j in range(4):
        at = ((meta[CORE] ^ other) * 4 + (meta[CHIP] ^ j)) * size
        lines.append(heads_ref[pl.ds(pl.multiple_of(at, size), size), :])
    product = dot(jnp.concatenate(lines, axis=0), grad, 1, 0)
    for j, out_ref in enumerate(outs):
        out_ref[...] = product[j * size : (j + 1) * size].astype(out_ref.dtype)


def weight_half(meta, heads, grads, other, dtype):
    outw = grads[0].shape[1]
    size = heads.shape[0] // 8
    tile = 512
    return pl.pallas_call(
        functools.partial(weight_kernel, other),
        out_shape=[sds((size, outw), dtype)] * 4,
        grid=(outw // tile,),
        in_specs=[pl.BlockSpec(memory_space=pltpu.SMEM), pl.BlockSpec(heads.shape, lambda i: (0, 0))]
        + [pl.BlockSpec((g.shape[0], tile), lambda i: (0, i)) for g in grads],
        out_specs=[pl.BlockSpec((size, tile), lambda i: (0, i))] * 4,
        compiler_params=params(16),
        cost_estimate=NO_COST,
        name="weight_half",
    )(meta, heads, *grads)


def whole(kernel, out_shape, operands, name, scalars=0):
    return pl.pallas_call(
        kernel,
        out_shape=out_shape,
        in_specs=[pl.BlockSpec(memory_space=pltpu.SMEM)] * scalars
        + [pl.BlockSpec(memory_space=pltpu.VMEM)] * (len(operands) - scalars),
        out_specs=jax.tree.map(lambda _: pl.BlockSpec(memory_space=pltpu.VMEM), out_shape),
        compiler_params=params(),
        cost_estimate=NO_COST,
        name=name,
    )(*operands)


def add_kernel(*refs):
    keeps, recvs, outs = refs[:4], refs[4:8], refs[8:]
    for keep, recv, out_ref in zip(keeps, recvs, outs):
        out_ref[...] = (keep[...] + recv[...].astype(f32)).astype(out_ref.dtype)


def add_parts(keeps, recvs):
    shape = keeps[0].shape
    return whole(add_kernel, [sds(shape, f32)] + [sds(shape, bf16)] * 3, (*keeps, *recvs), "add_parts")


def total_kernel(scale, own_ref, r1, r2, r3, out_ref):
    total = own_ref[...] + r1[...].astype(f32) + r2[...].astype(f32) + r3[...].astype(f32)
    out_ref[...] = (total * scale).astype(bf16)


def total_of(own, recvs, scale):
    return whole(functools.partial(total_kernel, scale), sds(own.shape, bf16), (own, *recvs), "scene_mean")


def join_weight_kernel(meta, *refs):
    *parts, out_ref, sems = refs
    size = parts[0].shape[0]
    copies = []
    for n, ref in enumerate(parts):
        at = ((meta[CORE] ^ (n // 4)) * 4 + (meta[CHIP] ^ (n % 4))) * size
        copies.append(pltpu.make_async_copy(ref, out_ref.at[pl.ds(pl.multiple_of(at, size), size), :], sems.at[n]))
    run_all(copies)


def join_weight(meta, parts):
    size, outw = parts[0].shape
    return pl.pallas_call(
        join_weight_kernel,
        out_shape=sds((8 * size, outw), bf16),
        in_specs=[pl.BlockSpec(memory_space=pltpu.SMEM)] + [pl.BlockSpec(memory_space=pl.ANY)] * 8,
        out_specs=pl.BlockSpec(memory_space=pl.ANY),
        scratch_shapes=[pltpu.SemaphoreType.DMA((8,))],
        compiler_params=params(),
        cost_estimate=NO_COST,
        name="join_weight",
    )(meta, *parts)


def join_kernel(meta, *refs):
    *pieces, sems = refs
    pieces, outs = pieces[:4], pieces[4:]
    width = pieces[0].shape[2]
    copies = []
    for k, ref in enumerate(pieces):
        start = pl.multiple_of((meta[Z] ^ k) * width, 128)
        for i, out_ref in enumerate(outs):
            copies.append(pltpu.make_async_copy(ref.at[i], out_ref.at[:, pl.ds(start, width)], sems.at[3 * k + i]))
    run_all(copies)


def join(meta, pieces):
    _, rows, width = pieces[0].shape
    return pl.pallas_call(
        join_kernel,
        out_shape=[sds((rows, 4 * width), bf16)] * 3,
        in_specs=[pl.BlockSpec(memory_space=pltpu.SMEM)] + [pl.BlockSpec(memory_space=pl.ANY)] * 4,
        out_specs=[pl.BlockSpec(memory_space=pl.ANY)] * 3,
        scratch_shapes=[pltpu.SemaphoreType.DMA((12,))],
        compiler_params=params(),
        cost_estimate=NO_COST,
        name="join_heads",
    )(meta, *pieces)


def dense_body(queries, keys_in, values, out_grad, out_weight, voxel_count):
    meta = jnp.stack([lax.axis_index("shard"), voxel_count[0], lax.axis_index("core"), lax.axis_index("chips")])
    meta = meta.astype(jnp.int32)

    def send(x, k, *earlier):
        return swap(after(x, *earlier) if earlier else x, "shard", 4, k)

    across = send(out_grad, 2)
    beside = send(out_grad, 1)
    packed = pack(meta, queries, keys_in, values)
    piece3 = send(packed[3], 3)
    piece1 = send(packed[1], 1)
    piece2 = send(packed[2], 2, beside)
    across_then = after(across, piece3, piece1)
    half = across.shape[0] // 2
    corners = [send(across_then[:half], 1), send(across_then[half:], 1)]
    grads = (out_grad, beside, across, *corners)
    grad = grad_attn(meta, grads, out_weight)
    heads, *mine = attend(meta, (packed[0], piece1, piece2, piece3), grad)
    back2, back3, back1 = (send(mine[k], k) for k in (2, 3, 1))

    sends = weight_half(meta, heads, grads, 1, bf16)
    recvs = [swap(x, "core", 2, 1) for x in sends]
    own, *sends = add_parts(weight_half(meta, heads, grads, 0, f32), recvs)
    recvs = [swap(x, "chips", 4, j + 1) for j, x in enumerate(sends)]
    done = total_of(after(own, back2), recvs, 1.0 / 8)
    near = [done] + [swap(done, "chips", 4, j) for j in (1, 2, 3)]
    *near, back3, back1 = lax.optimization_barrier((*near, back3, back1))
    far = [swap(x, "core", 2, 1) for x in near]
    grad_weight = join_weight(meta, near + far)
    return (*join(meta, (mine[0], back1, back2, back3)), grad_weight)


def attend_listed(queries, keys_in, values, block_ids, live_count):
    row_count, width_all = queries.shape
    head_count = width_all // HDIM
    block_count = row_count // BLOCK
    score_scale = 1.0 / math.sqrt(HDIM)
    query_blk = queries.reshape(block_count, BLOCK, head_count, HDIM)
    key_blk = keys_in.reshape(block_count, BLOCK, head_count, HDIM)[block_ids].reshape(
        block_count, NB * BLOCK, head_count, HDIM
    )
    value_blk = values.reshape(block_count, BLOCK, head_count, HDIM)[block_ids].reshape(
        block_count, NB * BLOCK, head_count, HDIM
    )
    query_pos = jnp.arange(row_count, dtype=jnp.int32).reshape(block_count, BLOCK)
    key_pos = (
        block_ids[:, :, None] * BLOCK + jnp.arange(BLOCK, dtype=jnp.int32)[None, None, :]
    ).reshape(block_count, NB * BLOCK)
    allowed = (key_pos[:, None, :] < live_count) | (query_pos[:, :, None] >= live_count)
    scores = (
        jnp.einsum("bqhd,bkhd->bhqk", query_blk, key_blk, preferred_element_type=jnp.float32)
        * score_scale
    )
    scores = jnp.where(allowed[:, None], scores, -jnp.inf)
    peak = jnp.max(scores, axis=-1, keepdims=True)
    weights = jnp.exp(scores - peak)
    probs = weights / jnp.sum(weights, axis=-1, keepdims=True)
    return (query_blk, key_blk, value_blk, probs)


def listed_body(queries, keys_in, values, out_grad, out_weight, block_lists, voxel_count):
    local_rows = queries.shape[0]
    live_count = voxel_count[0]
    block_ids = block_lists[0]
    positions = lax.axis_index("shard") * local_rows + jnp.arange(local_rows, dtype=jnp.int32)
    grad_live = jnp.where((positions < live_count)[:, None], out_grad, jnp.zeros_like(out_grad))
    query_head, key_head, value_head = (
        lax.all_to_all(queries, "shard", split_axis=1, concat_axis=0, tiled=True),
        lax.all_to_all(keys_in, "shard", split_axis=1, concat_axis=0, tiled=True),
        lax.all_to_all(values, "shard", split_axis=1, concat_axis=0, tiled=True),
    )
    row_count, width_all = query_head.shape
    head_count = width_all // HDIM
    block_count = row_count // BLOCK
    score_scale = 1.0 / math.sqrt(HDIM)
    query_blk, key_blk, value_blk, probs = attend_listed(
        query_head, key_head, value_head, block_ids, live_count
    )
    prob_bf = probs.astype(jnp.bfloat16)
    heads_out = (
        jnp.einsum("bhqk,bkhd->bqhd", prob_bf, value_blk, preferred_element_type=jnp.float32)
        .reshape(row_count, width_all)
        .astype(jnp.bfloat16)
    )
    row_piece = lax.all_gather(grad_live, "shard", axis=0, tiled=True)
    acc_now = jnp.einsum("rw,ro->wo", heads_out, row_piece, preferred_element_type=jnp.float32)
    product = jnp.einsum("ro,wo->rw", row_piece, out_weight, preferred_element_type=jnp.float32)
    grad_o = product.astype(jnp.bfloat16).reshape(block_count, BLOCK, head_count, HDIM)
    grad_prob = jnp.einsum("bqhd,bkhd->bhqk", grad_o, value_blk, preferred_element_type=jnp.float32)
    row_delta = jnp.sum(probs * grad_prob, axis=-1, keepdims=True)
    dscore = (probs * (grad_prob - row_delta) * score_scale).astype(jnp.bfloat16)
    grad_query = (
        jnp.einsum("bhqk,bkhd->bqhd", dscore, key_blk, preferred_element_type=jnp.float32)
        .reshape(row_count, width_all)
        .astype(jnp.bfloat16)
    )
    onehot = (
        block_ids[:, :, None] == jnp.arange(block_count, dtype=jnp.int32)[None, None, :]
    ).astype(jnp.float32)
    key_parts = jnp.einsum(
        "bhqk,bqhd->bkhd", dscore, query_blk, preferred_element_type=jnp.float32
    ).reshape(block_count, NB, BLOCK, width_all)
    value_parts = jnp.einsum(
        "bhqk,bqhd->bkhd", prob_bf, grad_o, preferred_element_type=jnp.float32
    ).reshape(block_count, NB, BLOCK, width_all)
    grad_key = (
        jnp.einsum("bjc,bjrx->crx", onehot, key_parts, precision=lax.Precision.HIGHEST)
        .reshape(row_count, width_all)
        .astype(jnp.bfloat16)
    )
    grad_value = (
        jnp.einsum("bjc,bjrx->crx", onehot, value_parts, precision=lax.Precision.HIGHEST)
        .reshape(row_count, width_all)
        .astype(jnp.bfloat16)
    )
    query_back, key_back, value_back = (
        lax.all_to_all(grad_query, "shard", split_axis=0, concat_axis=1, tiled=True),
        lax.all_to_all(grad_key, "shard", split_axis=0, concat_axis=1, tiled=True),
        lax.all_to_all(grad_value, "shard", split_axis=0, concat_axis=1, tiled=True),
    )
    scene_total = lax.axis_size(DP)
    summed = lax.psum(acc_now, DP)
    grad_weight = (summed / scene_total).astype(jnp.bfloat16)
    return (query_back, key_back, value_back, grad_weight)


def body(queries, keys_in, values, out_grad, out_weight, block_lists, voxel_count):
    dense = block_lists.shape[1] == NB and queries.shape[0] == BLOCK
    if dense and lax.axis_size("shard") == 4 and lax.axis_size("chips") == 4:
        return dense_body(queries, keys_in, values, out_grad, out_weight, voxel_count)
    return listed_body(queries, keys_in, values, out_grad, out_weight, block_lists, voxel_count)


def solution(mesh):
    chips = mesh.shape["dp"] // 2
    mesh = jax.sharding.Mesh(mesh.devices.reshape(chips, 2, -1), ("chips", "core", "shard"))
    return jax.shard_map(
        body,
        mesh=mesh,
        in_specs=(
            P((*DP, "shard"), None),
            P((*DP, "shard"), None),
            P((*DP, "shard"), None),
            P((*DP, "shard"), None),
            P("shard", None),
            P(DP, None, None),
            P(DP),
        ),
        out_specs=(
            P((*DP, "shard"), None),
            P((*DP, "shard"), None),
            P((*DP, "shard"), None),
            P("shard", None),
        ),
        check_vma=False,
    )
```

```python
import functools
import math

import jax
import jax.numpy as jnp
from jax import lax
from jax.experimental import pallas as pl
from jax.experimental.pallas import tpu as pltpu
from jax.sharding import PartitionSpec as P

HDIM = 128
BLOCK = 128
NB = 4
MIB = 1024 * 1024
DP = ("chips", "core")

Z, COUNT, CORE, CHIP = range(4)

NO_COST = pl.CostEstimate(flops=0, bytes_accessed=1024, transcendentals=0)

f32 = jnp.float32
bf16 = jnp.bfloat16


def dot(a, b, ca, cb):
    return lax.dot_general(a, b, (((ca,), (cb,)), ((), ())), preferred_element_type=f32)


def sds(shape, dtype):
    return jax.ShapeDtypeStruct(shape, dtype)


def params(mib=8):
    return pltpu.CompilerParams(vmem_limit_bytes=mib * MIB)


def swap(x, axis, size, flip):
    return lax.ppermute(x, axis, [(i, i ^ flip) for i in range(size)])


def after(x, *earlier):
    return lax.optimization_barrier((x, *earlier))[0]


def run_all(copies):
    for copy in copies:
        copy.start()
    for copy in copies:
        copy.wait()


def pack_kernel(meta, q_ref, k_ref, v_ref, *refs):
    *outs, sems = refs
    width = outs[0].shape[2]
    copies = []
    for k, out_ref in enumerate(outs):
        start = pl.multiple_of((meta[Z] ^ k) * width, 128)
        for i, ref in enumerate((q_ref, k_ref, v_ref)):
            copies.append(pltpu.make_async_copy(ref.at[:, pl.ds(start, width)], out_ref.at[i], sems.at[3 * k + i]))
    run_all(copies)


def pack(meta, queries, keys_in, values):
    rows, width = queries.shape
    return pl.pallas_call(
        pack_kernel,
        out_shape=[sds((3, rows, width // 4), bf16)] * 4,
        in_specs=[pl.BlockSpec(memory_space=pltpu.SMEM)] + [pl.BlockSpec(memory_space=pl.ANY)] * 3,
        out_specs=[pl.BlockSpec(memory_space=pltpu.VMEM)] * 4,
        scratch_shapes=[pltpu.SemaphoreType.DMA((12,))],
        compiler_params=params(),
        cost_estimate=NO_COST,
        name="pack_heads",
    )(meta, queries, keys_in, values)


def token_pos(shape, dim, z):
    return lax.broadcasted_iota(jnp.int32, shape, dim) ^ (z * BLOCK)


def grad_attn_kernel(meta, *refs):
    *grads, w_ref, out_ref = refs
    grad = jnp.concatenate([g[...] for g in grads], axis=0)
    live = token_pos((grad.shape[0], 1), 0, meta[Z]) < meta[COUNT]
    product = dot(grad, w_ref[...], 1, 1)
    out_ref[...] = jnp.where(live, product, 0.0).astype(bf16)


def grad_attn(meta, grads, weight):
    rows = sum(g.shape[0] for g in grads)
    width, outw = weight.shape
    tile = 256
    return pl.pallas_call(
        grad_attn_kernel,
        out_shape=sds((rows, width), bf16),
        grid=(width // tile,),
        in_specs=[pl.BlockSpec(memory_space=pltpu.SMEM)]
        + [pl.BlockSpec(g.shape, lambda i: (0, 0)) for g in grads]
        + [pl.BlockSpec((tile, outw), lambda i: (i, 0))],
        out_specs=pl.BlockSpec((rows, tile), lambda i: (0, i)),
        compiler_params=params(16),
        cost_estimate=NO_COST,
        name="grad_attn",
    )(meta, *grads, weight)


def attend_kernel(meta, p0, p1, p2, p3, do_ref, ot_ref, b0, b1, b2, b3):
    z, count = meta[Z], meta[COUNT]
    pieces, backs = (p0, p1, p2, p3), (b0, b1, b2, b3)
    rows = p0.shape[1]
    total = 4 * rows
    tile = 2 * rows
    scale = 1.0 / math.sqrt(HDIM)
    key_live = token_pos((total, 1), 0, z) < count
    query_live = token_pos((1, total), 1, z) < count
    for h in range(p0.shape[2] // HDIM):
        cols = slice(h * HDIM, (h + 1) * HDIM)
        query, key, value = (jnp.concatenate([p[i, :, cols] for p in pieces], axis=0) for i in range(3))
        grad = do_ref[:, cols]
        grad_key = grad_value = jnp.zeros((total, HDIM), f32)
        for t in range(2):
            part = slice(t * tile, (t + 1) * tile)
            live = query_live[:, part]
            scores = dot(key, query[part], 1, 1) * scale
            scores = jnp.where(key_live | ~live, scores, -jnp.inf)
            weights = jnp.exp(scores - jnp.max(scores, axis=0, keepdims=True))
            probs = weights * (1.0 / jnp.sum(weights, axis=0, keepdims=True))
            prob_bf = probs.astype(bf16)
            heads = dot(value, prob_bf, 0, 0)
            ot_ref[cols, part] = jnp.where(live, heads, 0.0).astype(bf16)
            grad_prob = dot(value, grad[part], 1, 1)
            row_delta = jnp.sum(probs * grad_prob, axis=0, keepdims=True)
            dscore = (probs * (grad_prob - row_delta) * scale).astype(bf16)
            grad_query = dot(key, dscore, 0, 0).T.astype(bf16)
            backs[2 * t][0, :, cols] = grad_query[:rows]
            backs[2 * t + 1][0, :, cols] = grad_query[rows:]
            grad_key += dot(dscore, query[part], 1, 0)
            grad_value += dot(prob_bf, grad[part], 1, 0)
        for k in range(4):
            mine = slice(k * rows, (k + 1) * rows)
            backs[k][1, :, cols] = grad_key[mine].astype(bf16)
            backs[k][2, :, cols] = grad_value[mine].astype(bf16)


def attend(meta, pieces, grad):
    _, rows, width = pieces[0].shape
    step = 2 * HDIM
    piece = pl.BlockSpec((3, rows, step), lambda i: (0, 0, i))
    return pl.pallas_call(
        attend_kernel,
        out_shape=[sds((width, 4 * rows), bf16)] + [sds((3, rows, width), bf16)] * 4,
        grid=(width // step,),
        in_specs=[pl.BlockSpec(memory_space=pltpu.SMEM)]
        + [piece] * 4
        + [pl.BlockSpec((4 * rows, step), lambda i: (0, i))],
        out_specs=[pl.BlockSpec((step, 4 * rows), lambda i: (i, 0))] + [piece] * 4,
        compiler_params=params(16),
        cost_estimate=NO_COST,
        name="attend",
    )(meta, *pieces, grad)


def weight_kernel(other, meta, heads_ref, *refs):
    grads, outs = refs[:-4], refs[-4:]
    grad = jnp.concatenate([g[...] for g in grads], axis=0)
    size = outs[0].shape[0]
    lines = []
    for j in range(4):
        at = ((meta[CORE] ^ other) * 4 + (meta[CHIP] ^ j)) * size
        lines.append(heads_ref[pl.ds(pl.multiple_of(at, size), size), :])
    product = dot(jnp.concatenate(lines, axis=0), grad, 1, 0)
    for j, out_ref in enumerate(outs):
        out_ref[...] = product[j * size : (j + 1) * size].astype(out_ref.dtype)


def weight_half(meta, heads, grads, other, dtype):
    outw = grads[0].shape[1]
    size = heads.shape[0] // 8
    tile = 512
    return pl.pallas_call(
        functools.partial(weight_kernel, other),
        out_shape=[sds((size, outw), dtype)] * 4,
        grid=(outw // tile,),
        in_specs=[pl.BlockSpec(memory_space=pltpu.SMEM), pl.BlockSpec(heads.shape, lambda i: (0, 0))]
        + [pl.BlockSpec((g.shape[0], tile), lambda i: (0, i)) for g in grads],
        out_specs=[pl.BlockSpec((size, tile), lambda i: (0, i))] * 4,
        compiler_params=params(16),
        cost_estimate=NO_COST,
        name="weight_half",
    )(meta, heads, *grads)


def whole(kernel, out_shape, operands, name, scalars=0):
    return pl.pallas_call(
        kernel,
        out_shape=out_shape,
        in_specs=[pl.BlockSpec(memory_space=pltpu.SMEM)] * scalars
        + [pl.BlockSpec(memory_space=pltpu.VMEM)] * (len(operands) - scalars),
        out_specs=jax.tree.map(lambda _: pl.BlockSpec(memory_space=pltpu.VMEM), out_shape),
        compiler_params=params(),
        cost_estimate=NO_COST,
        name=name,
    )(*operands)


def add_kernel(*refs):
    keeps, recvs, outs = refs[:4], refs[4:8], refs[8:]
    for keep, recv, out_ref in zip(keeps, recvs, outs):
        out_ref[...] = (keep[...] + recv[...].astype(f32)).astype(out_ref.dtype)


def add_parts(keeps, recvs):
    shape = keeps[0].shape
    return whole(add_kernel, [sds(shape, f32)] + [sds(shape, bf16)] * 3, (*keeps, *recvs), "add_parts")


def total_kernel(scale, own_ref, r1, r2, r3, out_ref):
    total = own_ref[...] + r1[...].astype(f32) + r2[...].astype(f32) + r3[...].astype(f32)
    out_ref[...] = (total * scale).astype(bf16)


def total_of(own, recvs, scale):
    return whole(functools.partial(total_kernel, scale), sds(own.shape, bf16), (own, *recvs), "scene_mean")


def join_weight_kernel(meta, *refs):
    *parts, out_ref, sems = refs
    size = parts[0].shape[0]
    copies = []
    for n, ref in enumerate(parts):
        at = ((meta[CORE] ^ (n // 4)) * 4 + (meta[CHIP] ^ (n % 4))) * size
        copies.append(pltpu.make_async_copy(ref, out_ref.at[pl.ds(pl.multiple_of(at, size), size), :], sems.at[n]))
    run_all(copies)


def join_weight(meta, parts):
    size, outw = parts[0].shape
    return pl.pallas_call(
        join_weight_kernel,
        out_shape=sds((8 * size, outw), bf16),
        in_specs=[pl.BlockSpec(memory_space=pltpu.SMEM)] + [pl.BlockSpec(memory_space=pl.ANY)] * 8,
        out_specs=pl.BlockSpec(memory_space=pl.ANY),
        scratch_shapes=[pltpu.SemaphoreType.DMA((8,))],
        compiler_params=params(),
        cost_estimate=NO_COST,
        name="join_weight",
    )(meta, *parts)


def join_kernel(meta, *refs):
    *pieces, sems = refs
    pieces, outs = pieces[:4], pieces[4:]
    width = pieces[0].shape[2]
    copies = []
    for k, ref in enumerate(pieces):
        start = pl.multiple_of((meta[Z] ^ k) * width, 128)
        for i, out_ref in enumerate(outs):
            copies.append(pltpu.make_async_copy(ref.at[i], out_ref.at[:, pl.ds(start, width)], sems.at[3 * k + i]))
    run_all(copies)


def join(meta, pieces):
    _, rows, width = pieces[0].shape
    return pl.pallas_call(
        join_kernel,
        out_shape=[sds((rows, 4 * width), bf16)] * 3,
        in_specs=[pl.BlockSpec(memory_space=pltpu.SMEM)] + [pl.BlockSpec(memory_space=pl.ANY)] * 4,
        out_specs=[pl.BlockSpec(memory_space=pl.ANY)] * 3,
        scratch_shapes=[pltpu.SemaphoreType.DMA((12,))],
        compiler_params=params(),
        cost_estimate=NO_COST,
        name="join_heads",
    )(meta, *pieces)


def dense_body(queries, keys_in, values, out_grad, out_weight, voxel_count):
    meta = jnp.stack([lax.axis_index("shard"), voxel_count[0], lax.axis_index("core"), lax.axis_index("chips")])
    meta = meta.astype(jnp.int32)

    def send(x, k, *earlier):
        return swap(after(x, *earlier) if earlier else x, "shard", 4, k)

    across = send(out_grad, 2)
    beside = send(out_grad, 1)
    packed = pack(meta, queries, keys_in, values)
    piece1 = send(packed[1], 1)
    piece3 = send(packed[3], 3, beside)
    piece2 = send(packed[2], 2, across)
    half = across.shape[0] // 2
    corners = [send(across[:half], 1), send(after(across, piece1)[half:], 1)]
    grads = (out_grad, beside, across, *corners)
    grad = grad_attn(meta, grads, out_weight)
    heads, *mine = attend(meta, (packed[0], piece1, piece2, piece3), grad)
    back2 = send(mine[2], 2)

    sends = weight_half(meta, heads, grads, 1, bf16)
    recvs = [swap(x, "core", 2, 1) for x in sends]
    own, *sends = add_parts(weight_half(meta, heads, grads, 0, f32), recvs)
    recvs = [swap(x, "chips", 4, j + 1) for j, x in enumerate(sends)]
    back3 = send(mine[3], 3, recvs[0])
    back1 = send(mine[1], 1, recvs[1])
    done = total_of(after(own, back2), recvs, 1.0 / 8)
    near = [done] + [swap(done, "chips", 4, j) for j in (1, 2, 3)]
    *near, back3, back1 = lax.optimization_barrier((*near, back3, back1))
    far = [swap(x, "core", 2, 1) for x in near]
    grad_weight = join_weight(meta, near + far)
    return (*join(meta, (mine[0], back1, back2, back3)), grad_weight)


def attend_listed(queries, keys_in, values, block_ids, live_count):
    row_count, width_all = queries.shape
    head_count = width_all // HDIM
    block_count = row_count // BLOCK
    score_scale = 1.0 / math.sqrt(HDIM)
    query_blk = queries.reshape(block_count, BLOCK, head_count, HDIM)
    key_blk = keys_in.reshape(block_count, BLOCK, head_count, HDIM)[block_ids].reshape(
        block_count, NB * BLOCK, head_count, HDIM
    )
    value_blk = values.reshape(block_count, BLOCK, head_count, HDIM)[block_ids].reshape(
        block_count, NB * BLOCK, head_count, HDIM
    )
    query_pos = jnp.arange(row_count, dtype=jnp.int32).reshape(block_count, BLOCK)
    key_pos = (
        block_ids[:, :, None] * BLOCK + jnp.arange(BLOCK, dtype=jnp.int32)[None, None, :]
    ).reshape(block_count, NB * BLOCK)
    allowed = (key_pos[:, None, :] < live_count) | (query_pos[:, :, None] >= live_count)
    scores = (
        jnp.einsum("bqhd,bkhd->bhqk", query_blk, key_blk, preferred_element_type=jnp.float32)
        * score_scale
    )
    scores = jnp.where(allowed[:, None], scores, -jnp.inf)
    peak = jnp.max(scores, axis=-1, keepdims=True)
    weights = jnp.exp(scores - peak)
    probs = weights / jnp.sum(weights, axis=-1, keepdims=True)
    return (query_blk, key_blk, value_blk, probs)


def listed_body(queries, keys_in, values, out_grad, out_weight, block_lists, voxel_count):
    local_rows = queries.shape[0]
    live_count = voxel_count[0]
    block_ids = block_lists[0]
    positions = lax.axis_index("shard") * local_rows + jnp.arange(local_rows, dtype=jnp.int32)
    grad_live = jnp.where((positions < live_count)[:, None], out_grad, jnp.zeros_like(out_grad))
    query_head, key_head, value_head = (
        lax.all_to_all(queries, "shard", split_axis=1, concat_axis=0, tiled=True),
        lax.all_to_all(keys_in, "shard", split_axis=1, concat_axis=0, tiled=True),
        lax.all_to_all(values, "shard", split_axis=1, concat_axis=0, tiled=True),
    )
    row_count, width_all = query_head.shape
    head_count = width_all // HDIM
    block_count = row_count // BLOCK
    score_scale = 1.0 / math.sqrt(HDIM)
    query_blk, key_blk, value_blk, probs = attend_listed(
        query_head, key_head, value_head, block_ids, live_count
    )
    prob_bf = probs.astype(jnp.bfloat16)
    heads_out = (
        jnp.einsum("bhqk,bkhd->bqhd", prob_bf, value_blk, preferred_element_type=jnp.float32)
        .reshape(row_count, width_all)
        .astype(jnp.bfloat16)
    )
    row_piece = lax.all_gather(grad_live, "shard", axis=0, tiled=True)
    acc_now = jnp.einsum("rw,ro->wo", heads_out, row_piece, preferred_element_type=jnp.float32)
    product = jnp.einsum("ro,wo->rw", row_piece, out_weight, preferred_element_type=jnp.float32)
    grad_o = product.astype(jnp.bfloat16).reshape(block_count, BLOCK, head_count, HDIM)
    grad_prob = jnp.einsum("bqhd,bkhd->bhqk", grad_o, value_blk, preferred_element_type=jnp.float32)
    row_delta = jnp.sum(probs * grad_prob, axis=-1, keepdims=True)
    dscore = (probs * (grad_prob - row_delta) * score_scale).astype(jnp.bfloat16)
    grad_query = (
        jnp.einsum("bhqk,bkhd->bqhd", dscore, key_blk, preferred_element_type=jnp.float32)
        .reshape(row_count, width_all)
        .astype(jnp.bfloat16)
    )
    onehot = (
        block_ids[:, :, None] == jnp.arange(block_count, dtype=jnp.int32)[None, None, :]
    ).astype(jnp.float32)
    key_parts = jnp.einsum(
        "bhqk,bqhd->bkhd", dscore, query_blk, preferred_element_type=jnp.float32
    ).reshape(block_count, NB, BLOCK, width_all)
    value_parts = jnp.einsum(
        "bhqk,bqhd->bkhd", prob_bf, grad_o, preferred_element_type=jnp.float32
    ).reshape(block_count, NB, BLOCK, width_all)
    grad_key = (
        jnp.einsum("bjc,bjrx->crx", onehot, key_parts, precision=lax.Precision.HIGHEST)
        .reshape(row_count, width_all)
        .astype(jnp.bfloat16)
    )
    grad_value = (
        jnp.einsum("bjc,bjrx->crx", onehot, value_parts, precision=lax.Precision.HIGHEST)
        .reshape(row_count, width_all)
        .astype(jnp.bfloat16)
    )
    query_back, key_back, value_back = (
        lax.all_to_all(grad_query, "shard", split_axis=0, concat_axis=1, tiled=True),
        lax.all_to_all(grad_key, "shard", split_axis=0, concat_axis=1, tiled=True),
        lax.all_to_all(grad_value, "shard", split_axis=0, concat_axis=1, tiled=True),
    )
    scene_total = lax.axis_size(DP)
    summed = lax.psum(acc_now, DP)
    grad_weight = (summed / scene_total).astype(jnp.bfloat16)
    return (query_back, key_back, value_back, grad_weight)


def body(queries, keys_in, values, out_grad, out_weight, block_lists, voxel_count):
    dense = block_lists.shape[1] == NB and queries.shape[0] == BLOCK
    if dense and lax.axis_size("shard") == 4 and lax.axis_size("chips") == 4:
        return dense_body(queries, keys_in, values, out_grad, out_weight, voxel_count)
    return listed_body(queries, keys_in, values, out_grad, out_weight, block_lists, voxel_count)


def solution(mesh):
    chips = mesh.shape["dp"] // 2
    mesh = jax.sharding.Mesh(mesh.devices.reshape(chips, 2, -1), ("chips", "core", "shard"))
    return jax.shard_map(
        body,
        mesh=mesh,
        in_specs=(
            P((*DP, "shard"), None),
            P((*DP, "shard"), None),
            P((*DP, "shard"), None),
            P((*DP, "shard"), None),
            P("shard", None),
            P(DP, None, None),
            P(DP),
        ),
        out_specs=(
            P((*DP, "shard"), None),
            P((*DP, "shard"), None),
            P((*DP, "shard"), None),
            P("shard", None),
        ),
        check_vma=False,
    )
```

```python
import functools
import math

import jax
import jax.numpy as jnp
from jax import lax
from jax.experimental import pallas as pl
from jax.experimental.pallas import tpu as pltpu
from jax.sharding import PartitionSpec as P

HDIM = 128
BLOCK = 128
NB = 4
MIB = 1024 * 1024
DP = ("chips", "core")

Z, COUNT, CORE, CHIP = range(4)

NO_COST = pl.CostEstimate(flops=0, bytes_accessed=1024, transcendentals=0)

f32 = jnp.float32
bf16 = jnp.bfloat16


def dot(a, b, ca, cb):
    return lax.dot_general(a, b, (((ca,), (cb,)), ((), ())), preferred_element_type=f32)


def sds(shape, dtype):
    return jax.ShapeDtypeStruct(shape, dtype)


def params(mib=8):
    return pltpu.CompilerParams(vmem_limit_bytes=mib * MIB)


def swap(x, axis, size, flip):
    return lax.ppermute(x, axis, [(i, i ^ flip) for i in range(size)])


def after(x, *earlier):
    return lax.optimization_barrier((x, *earlier))[0]


def run_all(copies):
    for copy in copies:
        copy.start()
    for copy in copies:
        copy.wait()


def pack_kernel(meta, q_ref, k_ref, v_ref, *refs):
    *outs, sems = refs
    width = outs[0].shape[2]
    copies = []
    for k, out_ref in enumerate(outs):
        start = pl.multiple_of((meta[Z] ^ k) * width, 128)
        for i, ref in enumerate((q_ref, k_ref, v_ref)):
            copies.append(pltpu.make_async_copy(ref.at[:, pl.ds(start, width)], out_ref.at[i], sems.at[3 * k + i]))
    run_all(copies)


def pack(meta, queries, keys_in, values):
    rows, width = queries.shape
    return pl.pallas_call(
        pack_kernel,
        out_shape=[sds((3, rows, width // 4), bf16)] * 4,
        in_specs=[pl.BlockSpec(memory_space=pltpu.SMEM)] + [pl.BlockSpec(memory_space=pl.ANY)] * 3,
        out_specs=[pl.BlockSpec(memory_space=pltpu.VMEM)] * 4,
        scratch_shapes=[pltpu.SemaphoreType.DMA((12,))],
        compiler_params=params(),
        cost_estimate=NO_COST,
        name="pack_heads",
    )(meta, queries, keys_in, values)


def token_pos(shape, dim, z, start=0):
    return (lax.broadcasted_iota(jnp.int32, shape, dim) + start) ^ (z * BLOCK)


def grad_attn_kernel(start, meta, *refs):
    *grads, w_ref, out_ref = refs
    grad = jnp.concatenate([g[...] for g in grads], axis=0)
    live = token_pos((grad.shape[0], 1), 0, meta[Z], start) < meta[COUNT]
    product = dot(grad, w_ref[...], 1, 1)
    out_ref[...] = jnp.where(live, product, 0.0).astype(bf16)


def grad_attn(meta, grads, weight, start):
    rows = sum(g.shape[0] for g in grads)
    width, outw = weight.shape
    tile = 256
    return pl.pallas_call(
        functools.partial(grad_attn_kernel, start),
        out_shape=sds((rows, width), bf16),
        grid=(width // tile,),
        in_specs=[pl.BlockSpec(memory_space=pltpu.SMEM)]
        + [pl.BlockSpec(g.shape, lambda i: (0, 0)) for g in grads]
        + [pl.BlockSpec((tile, outw), lambda i: (i, 0))],
        out_specs=pl.BlockSpec((rows, tile), lambda i: (0, i)),
        compiler_params=params(16),
        cost_estimate=NO_COST,
        name="grad_attn",
    )(meta, *grads, weight)


def forward_kernel(meta, p0, p1, p2, p3, weight_ref, inverse_ref, out_ref, heads_ref, bias_ref):
    pieces = (p0, p1, p2, p3)
    rows = p0.shape[1]
    total = 4 * rows
    tile = 2 * rows
    to_power = math.log2(math.e) / math.sqrt(HDIM)
    query_live = token_pos((1, total), 1, meta[Z]) < meta[COUNT]

    @pl.when(pl.program_id(0) == 0)
    def _():
        key_live = token_pos((total, 1), 0, meta[Z]) < meta[COUNT]
        bias_ref[...] = jnp.where(key_live | ~query_live, 0.0, -jnp.inf)

    for h in range(p0.shape[2] // HDIM):
        cols = slice(h * HDIM, (h + 1) * HDIM)
        query, key, value = (jnp.concatenate([p[i, :, cols] for p in pieces], axis=0) for i in range(3))
        for t in range(2):
            part = slice(t * tile, (t + 1) * tile)
            scores = dot(key, query[part], 1, 1) + bias_ref[:, part]
            peak = jnp.max(scores, axis=0, keepdims=True)
            weights = jnp.exp2((scores - peak) * to_power).astype(bf16)
            weight_ref[h, :, part] = weights
            inverse = 1.0 / jnp.sum(weights.astype(f32), axis=0, keepdims=True)
            inverse_ref[h, :, part] = inverse
            heads = dot(value, weights, 0, 0) * inverse
            out_ref[cols, part] = heads
            heads_ref[cols, part] = jnp.where(query_live[:, part], heads, 0.0).astype(bf16)


def piece_spec(piece, step):
    return pl.BlockSpec((3, piece.shape[1], step), lambda i: (0, 0, i))


def forward(meta, pieces):
    _, rows, width = pieces[0].shape
    total, step = 4 * rows, 2 * HDIM
    wide = pl.BlockSpec((step, total), lambda i: (i, 0))
    return pl.pallas_call(
        forward_kernel,
        out_shape=[
            sds((width // HDIM, total, total), bf16),
            sds((width // HDIM, 1, total), f32),
            sds((width, total), f32),
            sds((width, total), bf16),
        ],
        grid=(width // step,),
        in_specs=[pl.BlockSpec(memory_space=pltpu.SMEM)] + [piece_spec(p, step) for p in pieces],
        out_specs=[
            pl.BlockSpec((2, total, total), lambda i: (i, 0, 0)),
            pl.BlockSpec((2, 1, total), lambda i: (i, 0, 0)),
            wide,
            wide,
        ],
        scratch_shapes=[pltpu.VMEM((total, total), f32)],
        compiler_params=params(20),
        cost_estimate=NO_COST,
        name="attend_forward",
    )(meta, *pieces)


def backward_kernel(p0, p1, p2, p3, early_ref, late_ref, weight_ref, inverse_ref, out_ref, b0, b1, b2, b3):
    pieces, backs = (p0, p1, p2, p3), (b0, b1, b2, b3)
    rows = p0.shape[1]
    total = 4 * rows
    tile = 2 * rows
    scale = 1.0 / math.sqrt(HDIM)
    for h in range(p0.shape[2] // HDIM):
        cols = slice(h * HDIM, (h + 1) * HDIM)
        query, key, value = (jnp.concatenate([p[i, :, cols] for p in pieces], axis=0) for i in range(3))
        grad = jnp.concatenate([early_ref[:, cols], late_ref[:, cols]], axis=0)
        grad_key = grad_value = jnp.zeros((total, HDIM), f32)
        for t in range(2):
            part = slice(t * tile, (t + 1) * tile)
            weights = weight_ref[h, :, part]
            inverse = inverse_ref[h, :, part]
            turned = grad[part].astype(f32).T
            row_delta = jnp.sum(out_ref[cols, part] * turned, axis=0, keepdims=True)
            grad_prob = dot(value, grad[part], 1, 1)
            dscore = (weights.astype(f32) * ((grad_prob - row_delta) * (inverse * scale))).astype(bf16)
            grad_query = dot(key, dscore, 0, 0).T.astype(bf16)
            backs[2 * t][0, :, cols] = grad_query[:rows]
            backs[2 * t + 1][0, :, cols] = grad_query[rows:]
            grad_key += dot(dscore, query[part], 1, 0)
            grad_value += dot(weights, (turned * inverse).T.astype(bf16), 1, 0)
        for k in range(4):
            mine = slice(k * rows, (k + 1) * rows)
            backs[k][1, :, cols] = grad_key[mine].astype(bf16)
            backs[k][2, :, cols] = grad_value[mine].astype(bf16)


def backward(pieces, grads, weights, inverse, outs):
    _, rows, width = pieces[0].shape
    total, step = 4 * rows, 2 * HDIM
    specs = [piece_spec(p, step) for p in pieces]
    return pl.pallas_call(
        backward_kernel,
        out_shape=[sds((3, rows, width), bf16)] * 4,
        grid=(width // step,),
        in_specs=specs
        + [pl.BlockSpec((g.shape[0], step), lambda i: (0, i)) for g in grads]
        + [
            pl.BlockSpec((2, total, total), lambda i: (i, 0, 0)),
            pl.BlockSpec((2, 1, total), lambda i: (i, 0, 0)),
            pl.BlockSpec((step, total), lambda i: (i, 0)),
        ],
        out_specs=specs,
        compiler_params=params(20),
        cost_estimate=NO_COST,
        name="attend_backward",
    )(*pieces, *grads, weights, inverse, outs)


def weight_kernel(other, meta, heads_ref, *refs):
    grads, outs = refs[:-4], refs[-4:]
    grad = jnp.concatenate([g[...] for g in grads], axis=0)
    size = outs[0].shape[0]
    lines = []
    for j in range(4):
        at = ((meta[CORE] ^ other) * 4 + (meta[CHIP] ^ j)) * size
        lines.append(heads_ref[pl.ds(pl.multiple_of(at, size), size), :])
    product = dot(jnp.concatenate(lines, axis=0), grad, 1, 0)
    for j, out_ref in enumerate(outs):
        out_ref[...] = product[j * size : (j + 1) * size].astype(out_ref.dtype)


def weight_half(meta, heads, grads, other, dtype):
    outw = grads[0].shape[1]
    size = heads.shape[0] // 8
    tile = 512
    return pl.pallas_call(
        functools.partial(weight_kernel, other),
        out_shape=[sds((size, outw), dtype)] * 4,
        grid=(outw // tile,),
        in_specs=[pl.BlockSpec(memory_space=pltpu.SMEM), pl.BlockSpec(heads.shape, lambda i: (0, 0))]
        + [pl.BlockSpec((g.shape[0], tile), lambda i: (0, i)) for g in grads],
        out_specs=[pl.BlockSpec((size, tile), lambda i: (0, i))] * 4,
        compiler_params=params(16),
        cost_estimate=NO_COST,
        name="weight_half",
    )(meta, heads, *grads)


def whole(kernel, out_shape, operands, name, scalars=0):
    return pl.pallas_call(
        kernel,
        out_shape=out_shape,
        in_specs=[pl.BlockSpec(memory_space=pltpu.SMEM)] * scalars
        + [pl.BlockSpec(memory_space=pltpu.VMEM)] * (len(operands) - scalars),
        out_specs=jax.tree.map(lambda _: pl.BlockSpec(memory_space=pltpu.VMEM), out_shape),
        compiler_params=params(),
        cost_estimate=NO_COST,
        name=name,
    )(*operands)


def add_kernel(*refs):
    keeps, recvs, outs = refs[:4], refs[4:8], refs[8:]
    for keep, recv, out_ref in zip(keeps, recvs, outs):
        out_ref[...] = (keep[...] + recv[...].astype(f32)).astype(out_ref.dtype)


def add_parts(keeps, recvs):
    shape = keeps[0].shape
    return whole(add_kernel, [sds(shape, f32)] + [sds(shape, bf16)] * 3, (*keeps, *recvs), "add_parts")


def total_kernel(scale, own_ref, r1, r2, r3, out_ref):
    total = own_ref[...] + r1[...].astype(f32) + r2[...].astype(f32) + r3[...].astype(f32)
    out_ref[...] = (total * scale).astype(bf16)


def total_of(own, recvs, scale):
    return whole(functools.partial(total_kernel, scale), sds(own.shape, bf16), (own, *recvs), "scene_mean")


def join_weight_kernel(meta, *refs):
    *parts, out_ref, sems = refs
    size = parts[0].shape[0]
    copies = []
    for n, ref in enumerate(parts):
        at = ((meta[CORE] ^ (n // 4)) * 4 + (meta[CHIP] ^ (n % 4))) * size
        copies.append(pltpu.make_async_copy(ref, out_ref.at[pl.ds(pl.multiple_of(at, size), size), :], sems.at[n]))
    run_all(copies)


def join_weight(meta, parts):
    size, outw = parts[0].shape
    return pl.pallas_call(
        join_weight_kernel,
        out_shape=sds((8 * size, outw), bf16),
        in_specs=[pl.BlockSpec(memory_space=pltpu.SMEM)] + [pl.BlockSpec(memory_space=pl.ANY)] * 8,
        out_specs=pl.BlockSpec(memory_space=pl.ANY),
        scratch_shapes=[pltpu.SemaphoreType.DMA((8,))],
        compiler_params=params(),
        cost_estimate=NO_COST,
        name="join_weight",
    )(meta, *parts)


def join_kernel(meta, *refs):
    *pieces, sems = refs
    pieces, outs = pieces[:4], pieces[4:]
    width = pieces[0].shape[2]
    copies = []
    for k, ref in enumerate(pieces):
        start = pl.multiple_of((meta[Z] ^ k) * width, 128)
        for i, out_ref in enumerate(outs):
            copies.append(pltpu.make_async_copy(ref.at[i], out_ref.at[:, pl.ds(start, width)], sems.at[3 * k + i]))
    run_all(copies)


def join(meta, pieces):
    _, rows, width = pieces[0].shape
    return pl.pallas_call(
        join_kernel,
        out_shape=[sds((rows, 4 * width), bf16)] * 3,
        in_specs=[pl.BlockSpec(memory_space=pltpu.SMEM)] + [pl.BlockSpec(memory_space=pl.ANY)] * 4,
        out_specs=[pl.BlockSpec(memory_space=pl.ANY)] * 3,
        scratch_shapes=[pltpu.SemaphoreType.DMA((12,))],
        compiler_params=params(),
        cost_estimate=NO_COST,
        name="join_heads",
    )(meta, *pieces)


def dense_body(queries, keys_in, values, out_grad, out_weight, voxel_count):
    meta = jnp.stack([lax.axis_index("shard"), voxel_count[0], lax.axis_index("core"), lax.axis_index("chips")])
    meta = meta.astype(jnp.int32)

    def send(x, k, *earlier):
        return swap(after(x, *earlier) if earlier else x, "shard", 4, k)

    across = send(out_grad, 2)
    beside = send(out_grad, 1)
    packed = pack(meta, queries, keys_in, values)
    piece1 = send(packed[1], 1)
    piece3 = send(packed[3], 3, beside)
    piece2 = send(packed[2], 2, across)
    half = across.shape[0] // 2
    corners = [send(across[:half], 1), send(after(across, piece1)[half:], 1)]
    grad_early = grad_attn(meta, (out_grad, beside, across), out_weight, 0)
    pieces = (packed[0], piece1, piece2, piece3)
    weights, inverse, outs, heads = forward(meta, pieces)

    grad_early, heads, *corners = lax.optimization_barrier((grad_early, heads, *corners))
    grads = (out_grad, beside, across, *corners)
    grad_late = grad_attn(meta, grads[3:], out_weight, 3 * BLOCK)
    mine = backward(pieces, (grad_early, grad_late), weights, inverse, outs)
    back2 = send(mine[2], 2)

    sends = weight_half(meta, heads, grads, 1, bf16)
    recvs = [swap(x, "core", 2, 1) for x in sends]
    own, *sends = add_parts(weight_half(meta, heads, grads, 0, f32), recvs)
    recvs = [swap(x, "chips", 4, j + 1) for j, x in enumerate(sends)]
    back3 = send(mine[3], 3, recvs[0])
    back1 = send(mine[1], 1, recvs[1])
    done = total_of(after(own, back2), recvs, 1.0 / 8)
    near = [done] + [swap(done, "chips", 4, j) for j in (1, 2, 3)]
    *near, back3, back1 = lax.optimization_barrier((*near, back3, back1))
    far = [swap(x, "core", 2, 1) for x in near]
    grad_weight = join_weight(meta, near + far)
    return (*join(meta, (mine[0], back1, back2, back3)), grad_weight)


def attend_listed(queries, keys_in, values, block_ids, live_count):
    row_count, width_all = queries.shape
    head_count = width_all // HDIM
    block_count = row_count // BLOCK
    score_scale = 1.0 / math.sqrt(HDIM)
    query_blk = queries.reshape(block_count, BLOCK, head_count, HDIM)
    key_blk = keys_in.reshape(block_count, BLOCK, head_count, HDIM)[block_ids].reshape(
        block_count, NB * BLOCK, head_count, HDIM
    )
    value_blk = values.reshape(block_count, BLOCK, head_count, HDIM)[block_ids].reshape(
        block_count, NB * BLOCK, head_count, HDIM
    )
    query_pos = jnp.arange(row_count, dtype=jnp.int32).reshape(block_count, BLOCK)
    key_pos = (
        block_ids[:, :, None] * BLOCK + jnp.arange(BLOCK, dtype=jnp.int32)[None, None, :]
    ).reshape(block_count, NB * BLOCK)
    allowed = (key_pos[:, None, :] < live_count) | (query_pos[:, :, None] >= live_count)
    scores = (
        jnp.einsum("bqhd,bkhd->bhqk", query_blk, key_blk, preferred_element_type=jnp.float32)
        * score_scale
    )
    scores = jnp.where(allowed[:, None], scores, -jnp.inf)
    peak = jnp.max(scores, axis=-1, keepdims=True)
    weights = jnp.exp(scores - peak)
    probs = weights / jnp.sum(weights, axis=-1, keepdims=True)
    return (query_blk, key_blk, value_blk, probs)


def listed_body(queries, keys_in, values, out_grad, out_weight, block_lists, voxel_count):
    local_rows = queries.shape[0]
    live_count = voxel_count[0]
    block_ids = block_lists[0]
    positions = lax.axis_index("shard") * local_rows + jnp.arange(local_rows, dtype=jnp.int32)
    grad_live = jnp.where((positions < live_count)[:, None], out_grad, jnp.zeros_like(out_grad))
    query_head, key_head, value_head = (
        lax.all_to_all(queries, "shard", split_axis=1, concat_axis=0, tiled=True),
        lax.all_to_all(keys_in, "shard", split_axis=1, concat_axis=0, tiled=True),
        lax.all_to_all(values, "shard", split_axis=1, concat_axis=0, tiled=True),
    )
    row_count, width_all = query_head.shape
    head_count = width_all // HDIM
    block_count = row_count // BLOCK
    score_scale = 1.0 / math.sqrt(HDIM)
    query_blk, key_blk, value_blk, probs = attend_listed(
        query_head, key_head, value_head, block_ids, live_count
    )
    prob_bf = probs.astype(jnp.bfloat16)
    heads_out = (
        jnp.einsum("bhqk,bkhd->bqhd", prob_bf, value_blk, preferred_element_type=jnp.float32)
        .reshape(row_count, width_all)
        .astype(jnp.bfloat16)
    )
    row_piece = lax.all_gather(grad_live, "shard", axis=0, tiled=True)
    acc_now = jnp.einsum("rw,ro->wo", heads_out, row_piece, preferred_element_type=jnp.float32)
    product = jnp.einsum("ro,wo->rw", row_piece, out_weight, preferred_element_type=jnp.float32)
    grad_o = product.astype(jnp.bfloat16).reshape(block_count, BLOCK, head_count, HDIM)
    grad_prob = jnp.einsum("bqhd,bkhd->bhqk", grad_o, value_blk, preferred_element_type=jnp.float32)
    row_delta = jnp.sum(probs * grad_prob, axis=-1, keepdims=True)
    dscore = (probs * (grad_prob - row_delta) * score_scale).astype(jnp.bfloat16)
    grad_query = (
        jnp.einsum("bhqk,bkhd->bqhd", dscore, key_blk, preferred_element_type=jnp.float32)
        .reshape(row_count, width_all)
        .astype(jnp.bfloat16)
    )
    onehot = (
        block_ids[:, :, None] == jnp.arange(block_count, dtype=jnp.int32)[None, None, :]
    ).astype(jnp.float32)
    key_parts = jnp.einsum(
        "bhqk,bqhd->bkhd", dscore, query_blk, preferred_element_type=jnp.float32
    ).reshape(block_count, NB, BLOCK, width_all)
    value_parts = jnp.einsum(
        "bhqk,bqhd->bkhd", prob_bf, grad_o, preferred_element_type=jnp.float32
    ).reshape(block_count, NB, BLOCK, width_all)
    grad_key = (
        jnp.einsum("bjc,bjrx->crx", onehot, key_parts, precision=lax.Precision.HIGHEST)
        .reshape(row_count, width_all)
        .astype(jnp.bfloat16)
    )
    grad_value = (
        jnp.einsum("bjc,bjrx->crx", onehot, value_parts, precision=lax.Precision.HIGHEST)
        .reshape(row_count, width_all)
        .astype(jnp.bfloat16)
    )
    query_back, key_back, value_back = (
        lax.all_to_all(grad_query, "shard", split_axis=0, concat_axis=1, tiled=True),
        lax.all_to_all(grad_key, "shard", split_axis=0, concat_axis=1, tiled=True),
        lax.all_to_all(grad_value, "shard", split_axis=0, concat_axis=1, tiled=True),
    )
    scene_total = lax.axis_size(DP)
    summed = lax.psum(acc_now, DP)
    grad_weight = (summed / scene_total).astype(jnp.bfloat16)
    return (query_back, key_back, value_back, grad_weight)


def body(queries, keys_in, values, out_grad, out_weight, block_lists, voxel_count):
    dense = block_lists.shape[1] == NB and queries.shape[0] == BLOCK
    if dense and lax.axis_size("shard") == 4 and lax.axis_size("chips") == 4:
        return dense_body(queries, keys_in, values, out_grad, out_weight, voxel_count)
    return listed_body(queries, keys_in, values, out_grad, out_weight, block_lists, voxel_count)


def solution(mesh):
    chips = mesh.shape["dp"] // 2
    mesh = jax.sharding.Mesh(mesh.devices.reshape(chips, 2, -1), ("chips", "core", "shard"))
    return jax.shard_map(
        body,
        mesh=mesh,
        in_specs=(
            P((*DP, "shard"), None),
            P((*DP, "shard"), None),
            P((*DP, "shard"), None),
            P((*DP, "shard"), None),
            P("shard", None),
            P(DP, None, None),
            P(DP),
        ),
        out_specs=(
            P((*DP, "shard"), None),
            P((*DP, "shard"), None),
            P((*DP, "shard"), None),
            P("shard", None),
        ),
        check_vma=False,
    )
```

```python
import functools
import math

import jax
import jax.numpy as jnp
from jax import lax
from jax.experimental import pallas as pl
from jax.experimental.pallas import tpu as pltpu
from jax.sharding import PartitionSpec as P

HDIM = 128
BLOCK = 128
NB = 4
MIB = 1024 * 1024
DP = ("chips", "core")

Z, COUNT, CORE, CHIP = range(4)

NO_COST = pl.CostEstimate(flops=0, bytes_accessed=1024, transcendentals=0)

f32 = jnp.float32
bf16 = jnp.bfloat16


def dot(a, b, ca, cb):
    return lax.dot_general(a, b, (((ca,), (cb,)), ((), ())), preferred_element_type=f32)


def sds(shape, dtype):
    return jax.ShapeDtypeStruct(shape, dtype)


def params(mib=8):
    return pltpu.CompilerParams(vmem_limit_bytes=mib * MIB)


def swap(x, axis, size, flip):
    return lax.ppermute(x, axis, [(i, i ^ flip) for i in range(size)])


def after(x, *earlier):
    return lax.optimization_barrier((x, *earlier))[0]


def run_all(copies):
    for copy in copies:
        copy.start()
    for copy in copies:
        copy.wait()


def whole(kernel, out_shape, operands, name, scalars=0, mib=8, scratch=()):
    return pl.pallas_call(
        kernel,
        out_shape=out_shape,
        in_specs=[pl.BlockSpec(memory_space=pltpu.SMEM)] * scalars
        + [pl.BlockSpec(memory_space=pltpu.VMEM)] * (len(operands) - scalars),
        out_specs=jax.tree.map(lambda _: pl.BlockSpec(memory_space=pltpu.VMEM), out_shape),
        scratch_shapes=scratch,
        compiler_params=params(mib),
        cost_estimate=NO_COST,
        name=name,
    )(*operands)


def pack_kernel(meta, q_ref, k_ref, v_ref, *refs):
    *outs, sems = refs
    width = outs[0].shape[2]
    copies = []
    for k, out_ref in enumerate(outs):
        start = pl.multiple_of((meta[Z] ^ k) * width, 128)
        for i, ref in enumerate((q_ref, k_ref, v_ref)):
            copies.append(pltpu.make_async_copy(ref.at[:, pl.ds(start, width)], out_ref.at[i], sems.at[3 * k + i]))
    run_all(copies)


def pack(meta, queries, keys_in, values):
    rows, width = queries.shape
    return pl.pallas_call(
        pack_kernel,
        out_shape=[sds((3, rows, width // 4), bf16)] * 4,
        in_specs=[pl.BlockSpec(memory_space=pltpu.SMEM)] + [pl.BlockSpec(memory_space=pl.ANY)] * 3,
        out_specs=[pl.BlockSpec(memory_space=pltpu.VMEM)] * 4,
        scratch_shapes=[pltpu.SemaphoreType.DMA((12,))],
        compiler_params=params(),
        cost_estimate=NO_COST,
        name="pack_heads",
    )(meta, queries, keys_in, values)


def token_pos(shape, dim, z, start=0):
    return (lax.broadcasted_iota(jnp.int32, shape, dim) + start) ^ (z * BLOCK)


def grad_attn_kernel(start, meta, *refs):
    *grads, w_ref, out_ref = refs
    grad = jnp.concatenate([g[...] for g in grads], axis=0)
    live = token_pos((grad.shape[0], 1), 0, meta[Z], start) < meta[COUNT]
    tile = 2 * HDIM

    @pl.loop(0, w_ref.shape[0] // tile)
    def _(i):
        part = pl.ds(pl.multiple_of(i * tile, tile), tile)
        out_ref[:, part] = jnp.where(live, dot(grad, w_ref[part, :], 1, 1), 0.0).astype(bf16)


def grad_attn(meta, grads, weight, start):
    shape = (sum(g.shape[0] for g in grads), weight.shape[0])
    kernel = functools.partial(grad_attn_kernel, start)
    return whole(kernel, sds(shape, bf16), (meta, *grads, weight), "grad_attn", 1, 16)


def forward_kernel(meta, p0, p1, p2, p3, weight_ref, inverse_ref, out_ref, heads_ref, bias_ref):
    pieces = (p0, p1, p2, p3)
    rows = p0.shape[1]
    total = 4 * rows
    tile = 2 * rows
    to_power = math.log2(math.e) / math.sqrt(HDIM)
    query_live = token_pos((1, total), 1, meta[Z]) < meta[COUNT]

    key_live = token_pos((total, 1), 0, meta[Z]) < meta[COUNT]
    bias_ref[...] = jnp.where(key_live | ~query_live, 0.0, -jnp.inf)

    def head(h):
        cols = pl.ds(pl.multiple_of(h * HDIM, HDIM), HDIM)
        query, key, value = (jnp.concatenate([p[i, :, cols] for p in pieces], axis=0) for i in range(3))
        for t in range(2):
            part = slice(t * tile, (t + 1) * tile)
            scores = dot(key, query[part], 1, 1) + bias_ref[:, part]
            peak = jnp.max(scores, axis=0, keepdims=True)
            weights = jnp.exp2((scores - peak) * to_power).astype(bf16)
            weight_ref[h, :, part] = weights
            inverse = 1.0 / jnp.sum(weights.astype(f32), axis=0, keepdims=True)
            inverse_ref[h, :, part] = inverse
            heads = dot(value, weights, 0, 0) * inverse
            out_ref[cols, part] = heads
            heads_ref[cols, part] = jnp.where(query_live[:, part], heads, 0.0).astype(bf16)

    @pl.loop(0, p0.shape[2] // HDIM // 2)
    def _(i):
        head(2 * i)
        head(2 * i + 1)


def forward(meta, pieces):
    _, rows, width = pieces[0].shape
    total = 4 * rows
    shapes = [
        sds((width // HDIM, total, total), bf16),
        sds((width // HDIM, 1, total), f32),
        sds((width, total), f32),
        sds((width, total), bf16),
    ]
    scratch = [pltpu.VMEM((total, total), f32)]
    return whole(forward_kernel, shapes, (meta, *pieces), "attend_forward", 1, 16, scratch)


def backward_kernel(p0, p1, p2, p3, early_ref, late_ref, weight_ref, inverse_ref, out_ref, b0, b1, b2, b3):
    pieces, backs = (p0, p1, p2, p3), (b0, b1, b2, b3)
    rows = p0.shape[1]
    total = 4 * rows
    tile = 2 * rows
    scale = 1.0 / math.sqrt(HDIM)

    def head(h):
        cols = pl.ds(pl.multiple_of(h * HDIM, HDIM), HDIM)
        query, key, value = (jnp.concatenate([p[i, :, cols] for p in pieces], axis=0) for i in range(3))
        grad = jnp.concatenate([early_ref[:, cols], late_ref[:, cols]], axis=0)
        grad_key = grad_value = jnp.zeros((total, HDIM), f32)
        for t in range(2):
            part = slice(t * tile, (t + 1) * tile)
            weights = weight_ref[h, :, part]
            inverse = inverse_ref[h, :, part]
            turned = grad[part].astype(f32).T
            row_delta = jnp.sum(out_ref[cols, part] * turned, axis=0, keepdims=True)
            grad_prob = dot(value, grad[part], 1, 1)
            dscore = (weights.astype(f32) * ((grad_prob - row_delta) * (inverse * scale))).astype(bf16)
            grad_query = dot(key, dscore, 0, 0).T.astype(bf16)
            backs[2 * t][0, :, cols] = grad_query[:rows]
            backs[2 * t + 1][0, :, cols] = grad_query[rows:]
            grad_key += dot(dscore, query[part], 1, 0)
            grad_value += dot(weights, (turned * inverse).T.astype(bf16), 1, 0)
        for k in range(4):
            mine = slice(k * rows, (k + 1) * rows)
            backs[k][1, :, cols] = grad_key[mine].astype(bf16)
            backs[k][2, :, cols] = grad_value[mine].astype(bf16)

    @pl.loop(0, p0.shape[2] // HDIM // 2)
    def _(i):
        head(2 * i)
        head(2 * i + 1)


def backward(pieces, grads, weights, inverse, outs):
    shapes = [sds(p.shape, bf16) for p in pieces]
    operands = (*pieces, *grads, weights, inverse, outs)
    return whole(backward_kernel, shapes, operands, "attend_backward", 0, 16)


def weight_kernel(meta, heads_ref, *refs):
    *grads, send_ref, keep_ref = refs
    width = heads_ref.shape[0]
    size = width // 8
    lines = []
    for other in (1, 0):
        for j in range(4):
            at = ((meta[CORE] ^ other) * 4 + (meta[CHIP] ^ j)) * size
            lines.append(heads_ref[pl.ds(pl.multiple_of(at, size), size), :])
    lines = jnp.concatenate(lines, axis=0)
    tile = 4 * HDIM

    @pl.loop(0, send_ref.shape[1] // tile)
    def _(i):
        part = pl.ds(pl.multiple_of(i * tile, tile), tile)
        product = dot(lines, jnp.concatenate([g[:, part] for g in grads], axis=0), 1, 0)
        send_ref[:, part] = product[: width // 2].astype(bf16)
        keep_ref[:, part] = product[width // 2 :]


def weight_halves(meta, heads, grads):
    shape = (heads.shape[0] // 2, grads[0].shape[1])
    return whole(weight_kernel, [sds(shape, bf16), sds(shape, f32)], (meta, heads, *grads), "weight_halves", 1, 16)


def add_kernel(keep_ref, recv_ref, *outs):
    size = outs[0].shape[0]
    for j, out_ref in enumerate(outs):
        part = slice(j * size, (j + 1) * size)
        out_ref[...] = (keep_ref[part, :] + recv_ref[part, :].astype(f32)).astype(out_ref.dtype)


def add_parts(keep, recv):
    shape = (keep.shape[0] // 4, keep.shape[1])
    return whole(add_kernel, [sds(shape, f32)] + [sds(shape, bf16)] * 3, (keep, recv), "add_parts")


def total_kernel(scale, own_ref, r1, r2, r3, out_ref):
    total = own_ref[...] + r1[...].astype(f32) + r2[...].astype(f32) + r3[...].astype(f32)
    out_ref[...] = (total * scale).astype(bf16)


def total_of(own, recvs, scale):
    return whole(functools.partial(total_kernel, scale), sds(own.shape, bf16), (own, *recvs), "scene_mean")


def join_weight_kernel(meta, *refs):
    *parts, out_ref, sems = refs
    size = parts[0].shape[0]
    copies = []
    for n, ref in enumerate(parts):
        at = ((meta[CORE] ^ (n // 4)) * 4 + (meta[CHIP] ^ (n % 4))) * size
        copies.append(pltpu.make_async_copy(ref, out_ref.at[pl.ds(pl.multiple_of(at, size), size), :], sems.at[n]))
    run_all(copies)


def join_weight(meta, parts):
    size, outw = parts[0].shape
    return pl.pallas_call(
        join_weight_kernel,
        out_shape=sds((8 * size, outw), bf16),
        in_specs=[pl.BlockSpec(memory_space=pltpu.SMEM)] + [pl.BlockSpec(memory_space=pl.ANY)] * 8,
        out_specs=pl.BlockSpec(memory_space=pl.ANY),
        scratch_shapes=[pltpu.SemaphoreType.DMA((8,))],
        compiler_params=params(),
        cost_estimate=NO_COST,
        name="join_weight",
    )(meta, *parts)


def join_kernel(meta, *refs):
    *pieces, sems = refs
    pieces, outs = pieces[:4], pieces[4:]
    width = pieces[0].shape[2]
    copies = []
    for k, ref in enumerate(pieces):
        start = pl.multiple_of((meta[Z] ^ k) * width, 128)
        for i, out_ref in enumerate(outs):
            copies.append(pltpu.make_async_copy(ref.at[i], out_ref.at[:, pl.ds(start, width)], sems.at[3 * k + i]))
    run_all(copies)


def join(meta, pieces):
    _, rows, width = pieces[0].shape
    return pl.pallas_call(
        join_kernel,
        out_shape=[sds((rows, 4 * width), bf16)] * 3,
        in_specs=[pl.BlockSpec(memory_space=pltpu.SMEM)] + [pl.BlockSpec(memory_space=pl.ANY)] * 4,
        out_specs=[pl.BlockSpec(memory_space=pl.ANY)] * 3,
        scratch_shapes=[pltpu.SemaphoreType.DMA((12,))],
        compiler_params=params(),
        cost_estimate=NO_COST,
        name="join_heads",
    )(meta, *pieces)


def dense_body(queries, keys_in, values, out_grad, out_weight, voxel_count):
    meta = jnp.stack([lax.axis_index("shard"), voxel_count[0], lax.axis_index("core"), lax.axis_index("chips")])
    meta = meta.astype(jnp.int32)

    def send(x, k, *earlier):
        return swap(after(x, *earlier) if earlier else x, "shard", 4, k)

    across = send(out_grad, 2)
    beside = send(out_grad, 1)
    packed = pack(meta, queries, keys_in, values)
    piece1 = send(packed[1], 1)
    piece3 = send(packed[3], 3, beside)
    piece2 = send(packed[2], 2, across)
    half = across.shape[0] // 2
    across_then = after(across, piece1)
    corners = [send(across_then[:half], 1), send(across_then[half:], 1)]
    grad_early = grad_attn(meta, (out_grad, beside, across), out_weight, 0)
    pieces = (packed[0], piece1, piece2, piece3)
    weights, inverse, outs, heads = forward(meta, pieces)

    grad_early, heads, *corners = lax.optimization_barrier((grad_early, heads, *corners))
    grads = (out_grad, beside, across, *corners)
    grad_late = grad_attn(meta, grads[3:], out_weight, 3 * BLOCK)
    mine = backward(pieces, (grad_early, grad_late), weights, inverse, outs)
    back2, back1 = send(mine[2], 2), send(mine[1], 1)

    out, keep = weight_halves(meta, heads, grads)
    own, *sends = add_parts(keep, swap(out, "core", 2, 1))
    recvs = [swap(x, "chips", 4, j + 1) for j, x in enumerate(sends)]
    back3 = send(mine[3], 3, recvs[0])
    done = total_of(after(own, back2, back1), recvs, 1.0 / 8)
    near = [done] + [swap(done, "chips", 4, j) for j in (1, 2, 3)]
    *near, back3 = lax.optimization_barrier((*near, back3))
    far = [swap(x, "core", 2, 1) for x in near]
    grad_weight = join_weight(meta, near + far)
    return (*join(meta, (mine[0], back1, back2, back3)), grad_weight)


def attend_listed(queries, keys_in, values, block_ids, live_count):
    row_count, width_all = queries.shape
    head_count = width_all // HDIM
    block_count = row_count // BLOCK
    score_scale = 1.0 / math.sqrt(HDIM)
    query_blk = queries.reshape(block_count, BLOCK, head_count, HDIM)
    key_blk = keys_in.reshape(block_count, BLOCK, head_count, HDIM)[block_ids].reshape(
        block_count, NB * BLOCK, head_count, HDIM
    )
    value_blk = values.reshape(block_count, BLOCK, head_count, HDIM)[block_ids].reshape(
        block_count, NB * BLOCK, head_count, HDIM
    )
    query_pos = jnp.arange(row_count, dtype=jnp.int32).reshape(block_count, BLOCK)
    key_pos = (
        block_ids[:, :, None] * BLOCK + jnp.arange(BLOCK, dtype=jnp.int32)[None, None, :]
    ).reshape(block_count, NB * BLOCK)
    allowed = (key_pos[:, None, :] < live_count) | (query_pos[:, :, None] >= live_count)
    scores = (
        jnp.einsum("bqhd,bkhd->bhqk", query_blk, key_blk, preferred_element_type=jnp.float32)
        * score_scale
    )
    scores = jnp.where(allowed[:, None], scores, -jnp.inf)
    peak = jnp.max(scores, axis=-1, keepdims=True)
    weights = jnp.exp(scores - peak)
    probs = weights / jnp.sum(weights, axis=-1, keepdims=True)
    return (query_blk, key_blk, value_blk, probs)


def listed_body(queries, keys_in, values, out_grad, out_weight, block_lists, voxel_count):
    local_rows = queries.shape[0]
    live_count = voxel_count[0]
    block_ids = block_lists[0]
    positions = lax.axis_index("shard") * local_rows + jnp.arange(local_rows, dtype=jnp.int32)
    grad_live = jnp.where((positions < live_count)[:, None], out_grad, jnp.zeros_like(out_grad))
    query_head, key_head, value_head = (
        lax.all_to_all(queries, "shard", split_axis=1, concat_axis=0, tiled=True),
        lax.all_to_all(keys_in, "shard", split_axis=1, concat_axis=0, tiled=True),
        lax.all_to_all(values, "shard", split_axis=1, concat_axis=0, tiled=True),
    )
    row_count, width_all = query_head.shape
    head_count = width_all // HDIM
    block_count = row_count // BLOCK
    score_scale = 1.0 / math.sqrt(HDIM)
    query_blk, key_blk, value_blk, probs = attend_listed(
        query_head, key_head, value_head, block_ids, live_count
    )
    prob_bf = probs.astype(jnp.bfloat16)
    heads_out = (
        jnp.einsum("bhqk,bkhd->bqhd", prob_bf, value_blk, preferred_element_type=jnp.float32)
        .reshape(row_count, width_all)
        .astype(jnp.bfloat16)
    )
    row_piece = lax.all_gather(grad_live, "shard", axis=0, tiled=True)
    acc_now = jnp.einsum("rw,ro->wo", heads_out, row_piece, preferred_element_type=jnp.float32)
    product = jnp.einsum("ro,wo->rw", row_piece, out_weight, preferred_element_type=jnp.float32)
    grad_o = product.astype(jnp.bfloat16).reshape(block_count, BLOCK, head_count, HDIM)
    grad_prob = jnp.einsum("bqhd,bkhd->bhqk", grad_o, value_blk, preferred_element_type=jnp.float32)
    row_delta = jnp.sum(probs * grad_prob, axis=-1, keepdims=True)
    dscore = (probs * (grad_prob - row_delta) * score_scale).astype(jnp.bfloat16)
    grad_query = (
        jnp.einsum("bhqk,bkhd->bqhd", dscore, key_blk, preferred_element_type=jnp.float32)
        .reshape(row_count, width_all)
        .astype(jnp.bfloat16)
    )
    onehot = (
        block_ids[:, :, None] == jnp.arange(block_count, dtype=jnp.int32)[None, None, :]
    ).astype(jnp.float32)
    key_parts = jnp.einsum(
        "bhqk,bqhd->bkhd", dscore, query_blk, preferred_element_type=jnp.float32
    ).reshape(block_count, NB, BLOCK, width_all)
    value_parts = jnp.einsum(
        "bhqk,bqhd->bkhd", prob_bf, grad_o, preferred_element_type=jnp.float32
    ).reshape(block_count, NB, BLOCK, width_all)
    grad_key = (
        jnp.einsum("bjc,bjrx->crx", onehot, key_parts, precision=lax.Precision.HIGHEST)
        .reshape(row_count, width_all)
        .astype(jnp.bfloat16)
    )
    grad_value = (
        jnp.einsum("bjc,bjrx->crx", onehot, value_parts, precision=lax.Precision.HIGHEST)
        .reshape(row_count, width_all)
        .astype(jnp.bfloat16)
    )
    query_back, key_back, value_back = (
        lax.all_to_all(grad_query, "shard", split_axis=0, concat_axis=1, tiled=True),
        lax.all_to_all(grad_key, "shard", split_axis=0, concat_axis=1, tiled=True),
        lax.all_to_all(grad_value, "shard", split_axis=0, concat_axis=1, tiled=True),
    )
    scene_total = lax.axis_size(DP)
    summed = lax.psum(acc_now, DP)
    grad_weight = (summed / scene_total).astype(jnp.bfloat16)
    return (query_back, key_back, value_back, grad_weight)


def body(queries, keys_in, values, out_grad, out_weight, block_lists, voxel_count):
    dense = block_lists.shape[1] == NB and queries.shape[0] == BLOCK
    if dense and lax.axis_size("shard") == 4 and lax.axis_size("chips") == 4:
        return dense_body(queries, keys_in, values, out_grad, out_weight, voxel_count)
    return listed_body(queries, keys_in, values, out_grad, out_weight, block_lists, voxel_count)


def solution(mesh):
    chips = mesh.shape["dp"] // 2
    mesh = jax.sharding.Mesh(mesh.devices.reshape(chips, 2, -1), ("chips", "core", "shard"))
    return jax.shard_map(
        body,
        mesh=mesh,
        in_specs=(
            P((*DP, "shard"), None),
            P((*DP, "shard"), None),
            P((*DP, "shard"), None),
            P((*DP, "shard"), None),
            P("shard", None),
            P(DP, None, None),
            P(DP),
        ),
        out_specs=(
            P((*DP, "shard"), None),
            P((*DP, "shard"), None),
            P((*DP, "shard"), None),
            P("shard", None),
        ),
        check_vma=False,
    )
```

```python
import functools
import math

import jax
import jax.numpy as jnp
from jax import lax
from jax.experimental import pallas as pl
from jax.experimental.pallas import tpu as pltpu
from jax.sharding import PartitionSpec as P

HDIM = 128
BLOCK = 128
NB = 4
MIB = 1024 * 1024
DP = ("chips", "core")

Z, COUNT, CORE, CHIP = range(4)

EARLY = 2

NO_COST = pl.CostEstimate(flops=0, bytes_accessed=1024, transcendentals=0)

f32 = jnp.float32
bf16 = jnp.bfloat16


def dot(a, b, ca, cb):
    return lax.dot_general(a, b, (((ca,), (cb,)), ((), ())), preferred_element_type=f32)


def sds(shape, dtype):
    return jax.ShapeDtypeStruct(shape, dtype)


def params(mib=8):
    return pltpu.CompilerParams(vmem_limit_bytes=mib * MIB)


def swap(x, axis, size, flip):
    return lax.ppermute(x, axis, [(i, i ^ flip) for i in range(size)])


def after(x, *earlier):
    return lax.optimization_barrier((x, *earlier))[0]


def run_all(copies):
    for copy in copies:
        copy.start()
    for copy in copies:
        copy.wait()


def whole(kernel, out_shape, operands, name, scalars=0, mib=8, scratch=()):
    return pl.pallas_call(
        kernel,
        out_shape=out_shape,
        in_specs=[pl.BlockSpec(memory_space=pltpu.SMEM)] * scalars
        + [pl.BlockSpec(memory_space=pltpu.VMEM)] * (len(operands) - scalars),
        out_specs=jax.tree.map(lambda _: pl.BlockSpec(memory_space=pltpu.VMEM), out_shape),
        scratch_shapes=scratch,
        compiler_params=params(mib),
        cost_estimate=NO_COST,
        name=name,
    )(*operands)


def pack_kernel(meta, q_ref, k_ref, v_ref, *refs):
    *outs, sems = refs
    width = outs[0].shape[2]
    copies = []
    for n, out_ref in enumerate(outs):
        k, first = (n, 0) if n < 2 else (n // 2 + 1, n % 2 * EARLY * HDIM)
        start = pl.multiple_of((meta[Z] ^ k) * width + first, 128)
        for i, ref in enumerate((q_ref, k_ref, v_ref)):
            part = ref.at[:, pl.ds(start, out_ref.shape[2])]
            copies.append(pltpu.make_async_copy(part, out_ref.at[i], sems.at[3 * n + i]))
    run_all(copies)


def pack(meta, queries, keys_in, values):
    rows, width = queries.shape
    part, early = width // 4, EARLY * HDIM
    shapes = [sds((3, rows, n), bf16) for n in (part, part, early, part - early, early, part - early)]
    return pl.pallas_call(
        pack_kernel,
        out_shape=shapes,
        in_specs=[pl.BlockSpec(memory_space=pltpu.SMEM)] + [pl.BlockSpec(memory_space=pl.ANY)] * 3,
        out_specs=[pl.BlockSpec(memory_space=pltpu.VMEM)] * len(shapes),
        scratch_shapes=[pltpu.SemaphoreType.DMA((3 * len(shapes),))],
        compiler_params=params(),
        cost_estimate=NO_COST,
        name="pack_heads",
    )(meta, queries, keys_in, values)


def token_pos(shape, dim, z, start=0):
    return (lax.broadcasted_iota(jnp.int32, shape, dim) + start) ^ (z * BLOCK)


def grad_attn_kernel(start, meta, *refs):
    *grads, w_ref, out_ref = refs
    grad = jnp.concatenate([g[...] for g in grads], axis=0)
    live = token_pos((grad.shape[0], 1), 0, meta[Z], start) < meta[COUNT]
    tile = 2 * HDIM

    @pl.loop(0, w_ref.shape[0] // tile)
    def _(i):
        part = pl.ds(pl.multiple_of(i * tile, tile), tile)
        out_ref[:, part] = jnp.where(live, dot(grad, w_ref[part, :], 1, 1), 0.0).astype(bf16)


def grad_attn(meta, grads, weight, start):
    shape = (sum(g.shape[0] for g in grads), weight.shape[0])
    kernel = functools.partial(grad_attn_kernel, start)
    return whole(kernel, sds(shape, bf16), (meta, *grads, weight), "grad_attn", 1, 16)


def head_of(pieces, group, h):
    part = pieces[-1].shape[2]
    parts = []
    for p in pieces:
        start = (group * EARLY * HDIM if p.shape[2] > part else 0) + h * HDIM
        parts.append([p[i, :, start : start + HDIM] for i in range(3)])
    return (jnp.concatenate(x, axis=0) for x in zip(*parts))


def forward_kernel(group, meta, p0, p1, p2, p3, weight_ref, inverse_ref, out_ref, heads_ref, bias_ref):
    pieces = (p0, p1, p2, p3)
    rows = p0.shape[1]
    total = 4 * rows
    tile = 2 * rows
    to_power = math.log2(math.e) / math.sqrt(HDIM)
    query_live = token_pos((1, total), 1, meta[Z]) < meta[COUNT]
    key_live = token_pos((total, 1), 0, meta[Z]) < meta[COUNT]
    bias_ref[...] = jnp.where(key_live | ~query_live, 0.0, -jnp.inf)
    for h in range(p3.shape[2] // HDIM):
        cols = slice(h * HDIM, (h + 1) * HDIM)
        query, key, value = head_of(pieces, group, h)
        for t in range(2):
            part = slice(t * tile, (t + 1) * tile)
            scores = dot(key, query[part], 1, 1) + bias_ref[:, part]
            peak = jnp.max(scores, axis=0, keepdims=True)
            weights = jnp.exp2((scores - peak) * to_power).astype(bf16)
            weight_ref[h, :, part] = weights
            inverse = 1.0 / jnp.sum(weights.astype(f32), axis=0, keepdims=True)
            inverse_ref[h, :, part] = inverse
            heads = dot(value, weights, 0, 0) * inverse
            out_ref[cols, part] = heads
            heads_ref[cols, part] = jnp.where(query_live[:, part], heads, 0.0).astype(bf16)


def forward(meta, pieces, group):
    _, rows, width = pieces[-1].shape
    total = 4 * rows
    shapes = [
        sds((width // HDIM, total, total), bf16),
        sds((width // HDIM, 1, total), f32),
        sds((width, total), f32),
        sds((width, total), bf16),
    ]
    scratch = [pltpu.VMEM((total, total), f32)]
    kernel = functools.partial(forward_kernel, group)
    return whole(kernel, shapes, (meta, *pieces), "attend_forward", 1, 16, scratch)


def backward_kernel(group, *refs):
    pieces, backs = refs[:4], refs[-4:]
    early_ref, late_ref, weight_ref, inverse_ref, out_ref, *others = refs[4:-4]
    rows = pieces[0].shape[1]
    total = 4 * rows
    tile = 2 * rows
    part = pieces[-1].shape[2]
    scale = 1.0 / math.sqrt(HDIM)
    first = EARLY * HDIM if others else 0
    for other_ref, back_ref in zip(others, backs):
        back_ref[:, :, :first] = other_ref[...]
    for h in range(part // HDIM):
        start = group * EARLY * HDIM + h * HDIM
        query, key, value = head_of(pieces, group, h)
        grad = jnp.concatenate([ref[:, start : start + HDIM] for ref in (early_ref, late_ref)], axis=0)
        grad_key = grad_value = jnp.zeros((total, HDIM), f32)
        here = slice(h * HDIM, (h + 1) * HDIM)
        cols = slice(first + h * HDIM, first + (h + 1) * HDIM)
        for t in range(2):
            span = slice(t * tile, (t + 1) * tile)
            weights = weight_ref[h, :, span]
            inverse = inverse_ref[h, :, span]
            turned = grad[span].astype(f32).T
            row_delta = jnp.sum(out_ref[here, span] * turned, axis=0, keepdims=True)
            grad_prob = dot(value, grad[span], 1, 1)
            dscore = (weights.astype(f32) * ((grad_prob - row_delta) * (inverse * scale))).astype(bf16)
            grad_query = dot(key, dscore, 0, 0).T.astype(bf16)
            backs[2 * t][0, :, cols] = grad_query[:rows]
            backs[2 * t + 1][0, :, cols] = grad_query[rows:]
            grad_key += dot(dscore, query[span], 1, 0)
            grad_value += dot(weights, (turned * inverse).T.astype(bf16), 1, 0)
        for k in range(4):
            mine = slice(k * rows, (k + 1) * rows)
            backs[k][1, :, cols] = grad_key[mine].astype(bf16)
            backs[k][2, :, cols] = grad_value[mine].astype(bf16)


def backward(pieces, grads, saved, group, others=()):
    _, rows, part = pieces[-1].shape
    shapes = [sds((3, rows, part + sum(x.shape[2] for x in others[:1])), bf16)] * 4
    kernel = functools.partial(backward_kernel, group)
    return whole(kernel, shapes, (*pieces, *grads, *saved, *others), "attend_backward", 0, 16)


LINE = HDIM // 8


def line_at(meta, head, other, j):
    at = head * HDIM + ((meta[CORE] ^ other) * 4 + (meta[CHIP] ^ j)) * LINE
    return pl.ds(pl.multiple_of(at, LINE), LINE)


def weight_kernel(meta, heads_ref, *refs):
    *grads, send_ref, keep_ref = refs
    width = heads_ref.shape[0]
    lines = []
    for other in (1, 0):
        for j in range(4):
            lines += [heads_ref[line_at(meta, h, other, j), :] for h in range(width // HDIM)]
    lines = jnp.concatenate(lines, axis=0)
    tile = 4 * HDIM

    @pl.loop(0, send_ref.shape[1] // tile)
    def _(i):
        part = pl.ds(pl.multiple_of(i * tile, tile), tile)
        product = dot(lines, jnp.concatenate([g[:, part] for g in grads], axis=0), 1, 0)
        send_ref[:, part] = product[: width // 2].astype(bf16)
        keep_ref[:, part] = product[width // 2 :]


def weight_halves(meta, heads, grads):
    shape = (heads.shape[0] // 2, grads[0].shape[1])
    return whole(weight_kernel, [sds(shape, bf16), sds(shape, f32)], (meta, heads, *grads), "weight_halves", 1, 16)


def add_kernel(*refs):
    keeps, recvs, outs = refs[:2], refs[2:4], refs[4:]
    for j, out_ref in enumerate(outs):
        start = 0
        for keep_ref, recv_ref in zip(keeps, recvs):
            size = keep_ref.shape[0] // 4
            part = slice(j * size, (j + 1) * size)
            total = keep_ref[part, :] + recv_ref[part, :].astype(f32)
            out_ref[start : start + size, :] = total.astype(out_ref.dtype)
            start += size


def add_parts(keeps, recvs):
    shape = (sum(x.shape[0] for x in keeps) // 4, keeps[0].shape[1])
    return whole(add_kernel, [sds(shape, f32)] + [sds(shape, bf16)] * 3, (*keeps, *recvs), "add_parts")


def total_kernel(scale, own_ref, r1, r2, r3, out_ref):
    total = own_ref[...] + r1[...].astype(f32) + r2[...].astype(f32) + r3[...].astype(f32)
    out_ref[...] = (total * scale).astype(bf16)


def total_of(own, recvs, scale):
    return whole(functools.partial(total_kernel, scale), sds(own.shape, bf16), (own, *recvs), "scene_mean")


def join_weight_kernel(meta, *refs):
    *parts, out_ref, sems = refs
    copies = []
    for n, ref in enumerate(parts):
        for h in range(ref.shape[0] // LINE):
            line = out_ref.at[line_at(meta, h, n // 4, n % 4), :]
            part = ref.at[pl.ds(h * LINE, LINE), :]
            copies.append(pltpu.make_async_copy(part, line, sems.at[len(copies)]))
    run_all(copies)


def join_weight(meta, parts):
    size, outw = parts[0].shape
    return pl.pallas_call(
        join_weight_kernel,
        out_shape=sds((8 * size, outw), bf16),
        in_specs=[pl.BlockSpec(memory_space=pltpu.SMEM)] + [pl.BlockSpec(memory_space=pl.ANY)] * 8,
        out_specs=pl.BlockSpec(memory_space=pl.ANY),
        scratch_shapes=[pltpu.SemaphoreType.DMA((8 * size // LINE,))],
        compiler_params=params(),
        cost_estimate=NO_COST,
        name="join_weight",
    )(meta, *parts)


def join_kernel(meta, *refs):
    *pieces, sems = refs
    pieces, outs = pieces[:4], pieces[4:]
    width = pieces[0].shape[2]
    copies = []
    for k, ref in enumerate(pieces):
        start = pl.multiple_of((meta[Z] ^ k) * width, 128)
        for i, out_ref in enumerate(outs):
            copies.append(pltpu.make_async_copy(ref.at[i], out_ref.at[:, pl.ds(start, width)], sems.at[3 * k + i]))
    run_all(copies)


def join(meta, pieces):
    _, rows, width = pieces[0].shape
    return pl.pallas_call(
        join_kernel,
        out_shape=[sds((rows, 4 * width), bf16)] * 3,
        in_specs=[pl.BlockSpec(memory_space=pltpu.SMEM)] + [pl.BlockSpec(memory_space=pl.ANY)] * 4,
        out_specs=[pl.BlockSpec(memory_space=pl.ANY)] * 3,
        scratch_shapes=[pltpu.SemaphoreType.DMA((12,))],
        compiler_params=params(),
        cost_estimate=NO_COST,
        name="join_heads",
    )(meta, *pieces)


def dense_body(queries, keys_in, values, out_grad, out_weight, voxel_count):
    meta = jnp.stack([lax.axis_index("shard"), voxel_count[0], lax.axis_index("core"), lax.axis_index("chips")])
    meta = meta.astype(jnp.int32)

    def send(x, k, *earlier):
        return swap(after(x, *earlier) if earlier else x, "shard", 4, k)

    across = send(out_grad, 2)
    beside = send(out_grad, 1)
    own, near1, far2a, far2b, far3a, far3b = pack(meta, queries, keys_in, values)
    piece1 = send(near1, 1)
    piece3a = send(far3a, 3, beside)
    piece2a = send(far2a, 2, across)
    piece3b = send(far3b, 3, piece3a)
    piece2b = send(far2b, 2, piece2a)
    half = across.shape[0] // 2
    across_then = after(across, piece1)
    corners = [send(across_then[:half], 1), send(across_then[half:], 1)]
    grad_early = grad_attn(meta, (out_grad, beside, across), out_weight, 0)

    pieces = (own, piece1, piece2a, piece3a)
    *saved, heads = forward(meta, pieces, 0)
    grad_early, heads, *corners = lax.optimization_barrier((grad_early, heads, *corners))
    grads = (out_grad, beside, across, *corners)
    grad_heads = (grad_early, grad_attn(meta, grads[3:], out_weight, 3 * BLOCK))
    mine = backward(pieces, grad_heads, saved, 0)
    out_a, keep_a = weight_halves(meta, heads, grads)
    recv_a = swap(out_a, "core", 2, 1)
    *mine, keep_a, piece2b, piece3b = lax.optimization_barrier((*mine, keep_a, piece2b, piece3b))
    pieces = (own, piece1, piece2b, piece3b)
    *saved, heads = forward(meta, pieces, 1)
    mine = backward(pieces, grad_heads, saved, 1, mine)
    back2 = send(mine[2], 2)

    out_b, keep_b = weight_halves(meta, heads, grads)
    own_part, *sends = add_parts((keep_a, keep_b), (recv_a, swap(out_b, "core", 2, 1)))
    recvs = [swap(x, "chips", 4, j + 1) for j, x in enumerate(sends)]
    back3 = send(mine[3], 3, recvs[1])
    back1 = send(mine[1], 1, recvs[0])
    done = total_of(after(own_part, back2), recvs, 1.0 / 8)
    near = [done] + [swap(done, "chips", 4, j) for j in (1, 2, 3)]
    *near, back3, back1 = lax.optimization_barrier((*near, back3, back1))
    far = [swap(x, "core", 2, 1) for x in near]
    grad_weight = join_weight(meta, near + far)
    return (*join(meta, (mine[0], back1, back2, back3)), grad_weight)


def attend_listed(queries, keys_in, values, block_ids, live_count):
    row_count, width_all = queries.shape
    head_count = width_all // HDIM
    block_count = row_count // BLOCK
    score_scale = 1.0 / math.sqrt(HDIM)
    query_blk = queries.reshape(block_count, BLOCK, head_count, HDIM)
    key_blk = keys_in.reshape(block_count, BLOCK, head_count, HDIM)[block_ids].reshape(
        block_count, NB * BLOCK, head_count, HDIM
    )
    value_blk = values.reshape(block_count, BLOCK, head_count, HDIM)[block_ids].reshape(
        block_count, NB * BLOCK, head_count, HDIM
    )
    query_pos = jnp.arange(row_count, dtype=jnp.int32).reshape(block_count, BLOCK)
    key_pos = (
        block_ids[:, :, None] * BLOCK + jnp.arange(BLOCK, dtype=jnp.int32)[None, None, :]
    ).reshape(block_count, NB * BLOCK)
    allowed = (key_pos[:, None, :] < live_count) | (query_pos[:, :, None] >= live_count)
    scores = (
        jnp.einsum("bqhd,bkhd->bhqk", query_blk, key_blk, preferred_element_type=jnp.float32)
        * score_scale
    )
    scores = jnp.where(allowed[:, None], scores, -jnp.inf)
    peak = jnp.max(scores, axis=-1, keepdims=True)
    weights = jnp.exp(scores - peak)
    probs = weights / jnp.sum(weights, axis=-1, keepdims=True)
    return (query_blk, key_blk, value_blk, probs)


def listed_body(queries, keys_in, values, out_grad, out_weight, block_lists, voxel_count):
    local_rows = queries.shape[0]
    live_count = voxel_count[0]
    block_ids = block_lists[0]
    positions = lax.axis_index("shard") * local_rows + jnp.arange(local_rows, dtype=jnp.int32)
    grad_live = jnp.where((positions < live_count)[:, None], out_grad, jnp.zeros_like(out_grad))
    query_head, key_head, value_head = (
        lax.all_to_all(queries, "shard", split_axis=1, concat_axis=0, tiled=True),
        lax.all_to_all(keys_in, "shard", split_axis=1, concat_axis=0, tiled=True),
        lax.all_to_all(values, "shard", split_axis=1, concat_axis=0, tiled=True),
    )
    row_count, width_all = query_head.shape
    head_count = width_all // HDIM
    block_count = row_count // BLOCK
    score_scale = 1.0 / math.sqrt(HDIM)
    query_blk, key_blk, value_blk, probs = attend_listed(
        query_head, key_head, value_head, block_ids, live_count
    )
    prob_bf = probs.astype(jnp.bfloat16)
    heads_out = (
        jnp.einsum("bhqk,bkhd->bqhd", prob_bf, value_blk, preferred_element_type=jnp.float32)
        .reshape(row_count, width_all)
        .astype(jnp.bfloat16)
    )
    row_piece = lax.all_gather(grad_live, "shard", axis=0, tiled=True)
    acc_now = jnp.einsum("rw,ro->wo", heads_out, row_piece, preferred_element_type=jnp.float32)
    product = jnp.einsum("ro,wo->rw", row_piece, out_weight, preferred_element_type=jnp.float32)
    grad_o = product.astype(jnp.bfloat16).reshape(block_count, BLOCK, head_count, HDIM)
    grad_prob = jnp.einsum("bqhd,bkhd->bhqk", grad_o, value_blk, preferred_element_type=jnp.float32)
    row_delta = jnp.sum(probs * grad_prob, axis=-1, keepdims=True)
    dscore = (probs * (grad_prob - row_delta) * score_scale).astype(jnp.bfloat16)
    grad_query = (
        jnp.einsum("bhqk,bkhd->bqhd", dscore, key_blk, preferred_element_type=jnp.float32)
        .reshape(row_count, width_all)
        .astype(jnp.bfloat16)
    )
    onehot = (
        block_ids[:, :, None] == jnp.arange(block_count, dtype=jnp.int32)[None, None, :]
    ).astype(jnp.float32)
    key_parts = jnp.einsum(
        "bhqk,bqhd->bkhd", dscore, query_blk, preferred_element_type=jnp.float32
    ).reshape(block_count, NB, BLOCK, width_all)
    value_parts = jnp.einsum(
        "bhqk,bqhd->bkhd", prob_bf, grad_o, preferred_element_type=jnp.float32
    ).reshape(block_count, NB, BLOCK, width_all)
    grad_key = (
        jnp.einsum("bjc,bjrx->crx", onehot, key_parts, precision=lax.Precision.HIGHEST)
        .reshape(row_count, width_all)
        .astype(jnp.bfloat16)
    )
    grad_value = (
        jnp.einsum("bjc,bjrx->crx", onehot, value_parts, precision=lax.Precision.HIGHEST)
        .reshape(row_count, width_all)
        .astype(jnp.bfloat16)
    )
    query_back, key_back, value_back = (
        lax.all_to_all(grad_query, "shard", split_axis=0, concat_axis=1, tiled=True),
        lax.all_to_all(grad_key, "shard", split_axis=0, concat_axis=1, tiled=True),
        lax.all_to_all(grad_value, "shard", split_axis=0, concat_axis=1, tiled=True),
    )
    scene_total = lax.axis_size(DP)
    summed = lax.psum(acc_now, DP)
    grad_weight = (summed / scene_total).astype(jnp.bfloat16)
    return (query_back, key_back, value_back, grad_weight)


def body(queries, keys_in, values, out_grad, out_weight, block_lists, voxel_count):
    dense = block_lists.shape[1] == NB and queries.shape[0] == BLOCK
    if dense and lax.axis_size("shard") == 4 and lax.axis_size("chips") == 4:
        return dense_body(queries, keys_in, values, out_grad, out_weight, voxel_count)
    return listed_body(queries, keys_in, values, out_grad, out_weight, block_lists, voxel_count)


def solution(mesh):
    chips = mesh.shape["dp"] // 2
    mesh = jax.sharding.Mesh(mesh.devices.reshape(chips, 2, -1), ("chips", "core", "shard"))
    return jax.shard_map(
        body,
        mesh=mesh,
        in_specs=(
            P((*DP, "shard"), None),
            P((*DP, "shard"), None),
            P((*DP, "shard"), None),
            P((*DP, "shard"), None),
            P("shard", None),
            P(DP, None, None),
            P(DP),
        ),
        out_specs=(
            P((*DP, "shard"), None),
            P((*DP, "shard"), None),
            P((*DP, "shard"), None),
            P("shard", None),
        ),
        check_vma=False,
    )
```

```python
import functools
import math

import jax
import jax.numpy as jnp
from jax import lax
from jax.experimental import pallas as pl
from jax.experimental.pallas import tpu as pltpu
from jax.sharding import PartitionSpec as P

HDIM = 128
BLOCK = 128
NB = 4
MIB = 1024 * 1024
DP = ("chips", "core")

Z, COUNT, CORE, CHIP = range(4)

EARLY = 2

NO_COST = pl.CostEstimate(flops=0, bytes_accessed=1024, transcendentals=0)

f32 = jnp.float32
bf16 = jnp.bfloat16


def dot(a, b, ca, cb):
    return lax.dot_general(a, b, (((ca,), (cb,)), ((), ())), preferred_element_type=f32)


def sds(shape, dtype):
    return jax.ShapeDtypeStruct(shape, dtype)


def params(mib=8):
    return pltpu.CompilerParams(vmem_limit_bytes=mib * MIB)


def swap(x, axis, size, flip):
    return lax.ppermute(x, axis, [(i, i ^ flip) for i in range(size)])


def after(x, *earlier):
    return lax.optimization_barrier((x, *earlier))[0]


def run_all(copies):
    for copy in copies:
        copy.start()
    for copy in copies:
        copy.wait()


def whole(kernel, out_shape, operands, name, scalars=0, mib=8, scratch=()):
    return pl.pallas_call(
        kernel,
        out_shape=out_shape,
        in_specs=[pl.BlockSpec(memory_space=pltpu.SMEM)] * scalars
        + [pl.BlockSpec(memory_space=pltpu.VMEM)] * (len(operands) - scalars),
        out_specs=jax.tree.map(lambda _: pl.BlockSpec(memory_space=pltpu.VMEM), out_shape),
        scratch_shapes=scratch,
        compiler_params=params(mib),
        cost_estimate=NO_COST,
        name=name,
    )(*operands)


def pack_kernel(meta, q_ref, k_ref, v_ref, *refs):
    *outs, sems = refs
    width = outs[0].shape[2]
    copies = []
    for n, out_ref in enumerate(outs):
        k, first = (n, 0) if n < 2 else (n // 2 + 1, n % 2 * EARLY * HDIM)
        start = pl.multiple_of((meta[Z] ^ k) * width + first, 128)
        for i, ref in enumerate((q_ref, k_ref, v_ref)):
            part = ref.at[:, pl.ds(start, out_ref.shape[2])]
            copies.append(pltpu.make_async_copy(part, out_ref.at[i], sems.at[3 * n + i]))
    run_all(copies)


def pack(meta, queries, keys_in, values):
    rows, width = queries.shape
    part, early = width // 4, EARLY * HDIM
    shapes = [sds((3, rows, n), bf16) for n in (part, part, early, part - early, early, part - early)]
    return pl.pallas_call(
        pack_kernel,
        out_shape=shapes,
        in_specs=[pl.BlockSpec(memory_space=pltpu.SMEM)] + [pl.BlockSpec(memory_space=pl.ANY)] * 3,
        out_specs=[pl.BlockSpec(memory_space=pltpu.VMEM)] * len(shapes),
        scratch_shapes=[pltpu.SemaphoreType.DMA((3 * len(shapes),))],
        compiler_params=params(),
        cost_estimate=NO_COST,
        name="pack_heads",
    )(meta, queries, keys_in, values)


def token_pos(shape, dim, z, start=0):
    return (lax.broadcasted_iota(jnp.int32, shape, dim) + start) ^ (z * BLOCK)


def grad_attn_kernel(start, meta, *refs):
    *grads, w_ref, out_ref = refs
    grad = jnp.concatenate([g[...] for g in grads], axis=0)
    live = token_pos((grad.shape[0], 1), 0, meta[Z], start) < meta[COUNT]
    tile = 2 * HDIM

    @pl.loop(0, w_ref.shape[0] // tile)
    def _(i):
        part = pl.ds(pl.multiple_of(i * tile, tile), tile)
        out_ref[:, part] = jnp.where(live, dot(grad, w_ref[part, :], 1, 1), 0.0).astype(bf16)


def grad_attn(meta, grads, weight, start):
    shape = (sum(g.shape[0] for g in grads), weight.shape[0])
    kernel = functools.partial(grad_attn_kernel, start)
    return whole(kernel, sds(shape, bf16), (meta, *grads, weight), "grad_attn", 1, 16)


def head_of(pieces, group, h):
    part = pieces[-1].shape[2]
    parts = []
    for p in pieces:
        start = (group * EARLY * HDIM if p.shape[2] > part else 0) + h * HDIM
        parts.append([p[i, :, start : start + HDIM] for i in range(3)])
    return (jnp.concatenate(x, axis=0) for x in zip(*parts))


def forward_kernel(group, meta, p0, p1, p2, p3, weight_ref, inverse_ref, out_ref, heads_ref, bias_ref):
    pieces = (p0, p1, p2, p3)
    rows = p0.shape[1]
    total = 4 * rows
    tile = 2 * rows
    to_power = math.log2(math.e) / math.sqrt(HDIM)
    query_live = token_pos((1, total), 1, meta[Z]) < meta[COUNT]
    key_live = token_pos((total, 1), 0, meta[Z]) < meta[COUNT]
    bias_ref[...] = jnp.where(key_live | ~query_live, 0.0, -jnp.inf)
    for h in range(p3.shape[2] // HDIM):
        cols = slice(h * HDIM, (h + 1) * HDIM)
        query, key, value = head_of(pieces, group, h)
        for t in range(2):
            part = slice(t * tile, (t + 1) * tile)
            scores = dot(key, query[part], 1, 1) + bias_ref[:, part]
            peak = jnp.max(scores, axis=0, keepdims=True)
            weights = jnp.exp2((scores - peak) * to_power).astype(bf16)
            weight_ref[h, :, part] = weights
            inverse = 1.0 / jnp.sum(weights.astype(f32), axis=0, keepdims=True)
            inverse_ref[h, :, part] = inverse
            heads = dot(value, weights, 0, 0) * inverse
            out_ref[cols, part] = heads
            heads_ref[cols, part] = jnp.where(query_live[:, part], heads, 0.0).astype(bf16)


def forward(meta, pieces, group):
    _, rows, width = pieces[-1].shape
    total = 4 * rows
    shapes = [
        sds((width // HDIM, total, total), bf16),
        sds((width // HDIM, 1, total), f32),
        sds((width, total), f32),
        sds((width, total), bf16),
    ]
    scratch = [pltpu.VMEM((total, total), f32)]
    kernel = functools.partial(forward_kernel, group)
    return whole(kernel, shapes, (meta, *pieces), "attend_forward", 1, 16, scratch)


def backward_kernel(meta, own, near, far2a, far3a, far2b, far3b, early_ref, late_ref, *refs):
    saved, back_ref = (refs[:3], refs[3:6]), refs[6]
    rows = own.shape[1]
    total = 4 * rows
    tile = 2 * rows
    scale = 1.0 / math.sqrt(HDIM)
    places = [meta[Z] ^ k for k in range(4)]
    for n in range(own.shape[2] // HDIM):
        group, h = divmod(n, EARLY)
        query, key, value = head_of(((own, near, far2a, far3a), (own, near, far2b, far3b))[group], group, h)
        weight_ref, inverse_ref, out_ref = saved[group]
        here = slice(h * HDIM, (h + 1) * HDIM)
        cols = slice(n * HDIM, (n + 1) * HDIM)
        grad = jnp.concatenate([early_ref[:, cols], late_ref[:, cols]], axis=0)
        grad_key = grad_value = jnp.zeros((total, HDIM), f32)
        for t in range(2):
            span = slice(t * tile, (t + 1) * tile)
            weights = weight_ref[h, :, span]
            inverse = inverse_ref[h, :, span]
            turned = grad[span].astype(f32).T
            row_delta = jnp.sum(out_ref[here, span] * turned, axis=0, keepdims=True)
            grad_prob = dot(value, grad[span], 1, 1)
            dscore = (weights.astype(f32) * ((grad_prob - row_delta) * (inverse * scale))).astype(bf16)
            grad_query = dot(key, dscore, 0, 0).T.astype(bf16)
            back_ref[places[2 * t], 0, :, cols] = grad_query[:rows]
            back_ref[places[2 * t + 1], 0, :, cols] = grad_query[rows:]
            grad_key += dot(dscore, query[span], 1, 0)
            grad_value += dot(weights, (turned * inverse).T.astype(bf16), 1, 0)
        for k in range(4):
            mine = slice(k * rows, (k + 1) * rows)
            back_ref[places[k], 1, :, cols] = grad_key[mine].astype(bf16)
            back_ref[places[k], 2, :, cols] = grad_value[mine].astype(bf16)


def backward(meta, pieces, grads, saved):
    shape = (4, *pieces[0].shape)
    return whole(backward_kernel, sds(shape, bf16), (meta, *pieces, *grads, *saved), "attend_backward", 1, 16)


LINE = HDIM // 8


def line_at(meta, head, other, j):
    at = head * HDIM + ((meta[CORE] ^ other) * 4 + (meta[CHIP] ^ j)) * LINE
    return pl.ds(pl.multiple_of(at, LINE), LINE)


def weight_kernel(meta, heads_a, heads_b, *refs):
    *grads, send_ref, keep_ref = refs
    width = heads_a.shape[0] + heads_b.shape[0]
    lines = []
    for other in (1, 0):
        for j in range(4):
            for ref in (heads_a, heads_b):
                lines += [ref[line_at(meta, h, other, j), :] for h in range(ref.shape[0] // HDIM)]
    lines = jnp.concatenate(lines, axis=0)
    tile = 4 * HDIM

    @pl.loop(0, send_ref.shape[1] // tile)
    def _(i):
        part = pl.ds(pl.multiple_of(i * tile, tile), tile)
        product = dot(lines, jnp.concatenate([g[:, part] for g in grads], axis=0), 1, 0)
        send_ref[:, part] = product[: width // 2].astype(bf16)
        keep_ref[:, part] = product[width // 2 :]


def weight_halves(meta, heads, grads):
    shape = (sum(x.shape[0] for x in heads) // 2, grads[0].shape[1])
    return whole(weight_kernel, [sds(shape, bf16), sds(shape, f32)], (meta, *heads, *grads), "weight_halves", 1, 16)


def add_kernel(keep_ref, recv_ref, *outs):
    size = outs[0].shape[0]
    for j, out_ref in enumerate(outs):
        part = slice(j * size, (j + 1) * size)
        out_ref[...] = (keep_ref[part, :] + recv_ref[part, :].astype(f32)).astype(out_ref.dtype)


def add_parts(keep, recv):
    shape = (keep.shape[0] // 4, keep.shape[1])
    return whole(add_kernel, [sds(shape, f32)] + [sds(shape, bf16)] * 3, (keep, recv), "add_parts")


def total_kernel(scale, own_ref, r1, r2, r3, out_ref):
    total = own_ref[...] + r1[...].astype(f32) + r2[...].astype(f32) + r3[...].astype(f32)
    out_ref[...] = (total * scale).astype(bf16)


def total_of(own, recvs, scale):
    return whole(functools.partial(total_kernel, scale), sds(own.shape, bf16), (own, *recvs), "scene_mean")


def join_weight_kernel(meta, *refs):
    *parts, out_ref, sems = refs
    copies = []
    for n, ref in enumerate(parts):
        for h in range(ref.shape[0] // LINE):
            line = out_ref.at[line_at(meta, h, n // 4, n % 4), :]
            part = ref.at[pl.ds(h * LINE, LINE), :]
            copies.append(pltpu.make_async_copy(part, line, sems.at[len(copies)]))
    run_all(copies)


def join_weight(meta, parts):
    size, outw = parts[0].shape
    return pl.pallas_call(
        join_weight_kernel,
        out_shape=sds((8 * size, outw), bf16),
        in_specs=[pl.BlockSpec(memory_space=pltpu.SMEM)] + [pl.BlockSpec(memory_space=pl.ANY)] * 8,
        out_specs=pl.BlockSpec(memory_space=pl.ANY),
        scratch_shapes=[pltpu.SemaphoreType.DMA((8 * size // LINE,))],
        compiler_params=params(),
        cost_estimate=NO_COST,
        name="join_weight",
    )(meta, *parts)


def join_kernel(back_ref, *refs):
    *outs, sems = refs
    width = back_ref.shape[3]
    copies = []
    for j in range(4):
        for i, out_ref in enumerate(outs):
            cols = out_ref.at[:, pl.ds(j * width, width)]
            copies.append(pltpu.make_async_copy(back_ref.at[j, i], cols, sems.at[len(copies)]))
    run_all(copies)


def join(back):
    _, _, rows, width = back.shape
    return pl.pallas_call(
        join_kernel,
        out_shape=[sds((rows, 4 * width), bf16)] * 3,
        in_specs=[pl.BlockSpec(memory_space=pl.ANY)],
        out_specs=[pl.BlockSpec(memory_space=pl.ANY)] * 3,
        scratch_shapes=[pltpu.SemaphoreType.DMA((12,))],
        compiler_params=params(),
        cost_estimate=NO_COST,
        name="join_heads",
    )(back)


def dense_body(queries, keys_in, values, out_grad, out_weight, voxel_count):
    meta = jnp.stack([lax.axis_index("shard"), voxel_count[0], lax.axis_index("core"), lax.axis_index("chips")])
    meta = meta.astype(jnp.int32)

    def send(x, k, *earlier):
        return swap(after(x, *earlier) if earlier else x, "shard", 4, k)

    across = send(out_grad, 2)
    beside = send(out_grad, 1)
    own, near1, far2a, far2b, far3a, far3b = pack(meta, queries, keys_in, values)
    piece1 = send(near1, 1)
    piece3a = send(far3a, 3, beside)
    piece2a = send(far2a, 2, across)
    piece3b = send(far3b, 3, piece3a)
    piece2b = send(far2b, 2, piece2a)
    half = across.shape[0] // 2
    across_then = after(across, piece1)
    corners = [send(across_then[:half], 1), send(across_then[half:], 1)]
    grad_early = grad_attn(meta, (out_grad, beside, across), out_weight, 0)

    *saved_a, heads_a = forward(meta, (own, piece1, piece2a, piece3a), 0)
    heads_a, piece2b, piece3b = lax.optimization_barrier((heads_a, piece2b, piece3b))
    *saved_b, heads_b = forward(meta, (own, piece1, piece2b, piece3b), 1)
    grad_early, heads_b, *corners = lax.optimization_barrier((grad_early, heads_b, *corners))
    grads = (out_grad, beside, across, *corners)
    grad_heads = (grad_early, grad_attn(meta, grads[3:], out_weight, 3 * BLOCK))
    pieces = (own, piece1, piece2a, piece3a, piece2b, piece3b)
    back = backward(meta, pieces, grad_heads, (*saved_a, *saved_b))
    back_all = lax.all_to_all(back, "shard", split_axis=0, concat_axis=0, tiled=True)

    out, keep = weight_halves(meta, (heads_a, after(heads_b, back)), grads)
    own_part, *sends = add_parts(keep, swap(out, "core", 2, 1))
    recvs = [swap(x, "chips", 4, j + 1) for j, x in enumerate(sends)]
    done = total_of(own_part, recvs, 1.0 / 8)
    near = [done] + [swap(done, "chips", 4, j) for j in (1, 2, 3)]
    far = [swap(x, "core", 2, 1) for x in near]
    grad_weight = join_weight(meta, near + far)
    return (*join(back_all), grad_weight)


def attend_listed(queries, keys_in, values, block_ids, live_count):
    row_count, width_all = queries.shape
    head_count = width_all // HDIM
    block_count = row_count // BLOCK
    score_scale = 1.0 / math.sqrt(HDIM)
    query_blk = queries.reshape(block_count, BLOCK, head_count, HDIM)
    key_blk = keys_in.reshape(block_count, BLOCK, head_count, HDIM)[block_ids].reshape(
        block_count, NB * BLOCK, head_count, HDIM
    )
    value_blk = values.reshape(block_count, BLOCK, head_count, HDIM)[block_ids].reshape(
        block_count, NB * BLOCK, head_count, HDIM
    )
    query_pos = jnp.arange(row_count, dtype=jnp.int32).reshape(block_count, BLOCK)
    key_pos = (
        block_ids[:, :, None] * BLOCK + jnp.arange(BLOCK, dtype=jnp.int32)[None, None, :]
    ).reshape(block_count, NB * BLOCK)
    allowed = (key_pos[:, None, :] < live_count) | (query_pos[:, :, None] >= live_count)
    scores = (
        jnp.einsum("bqhd,bkhd->bhqk", query_blk, key_blk, preferred_element_type=jnp.float32)
        * score_scale
    )
    scores = jnp.where(allowed[:, None], scores, -jnp.inf)
    peak = jnp.max(scores, axis=-1, keepdims=True)
    weights = jnp.exp(scores - peak)
    probs = weights / jnp.sum(weights, axis=-1, keepdims=True)
    return (query_blk, key_blk, value_blk, probs)


def listed_body(queries, keys_in, values, out_grad, out_weight, block_lists, voxel_count):
    local_rows = queries.shape[0]
    live_count = voxel_count[0]
    block_ids = block_lists[0]
    positions = lax.axis_index("shard") * local_rows + jnp.arange(local_rows, dtype=jnp.int32)
    grad_live = jnp.where((positions < live_count)[:, None], out_grad, jnp.zeros_like(out_grad))
    query_head, key_head, value_head = (
        lax.all_to_all(queries, "shard", split_axis=1, concat_axis=0, tiled=True),
        lax.all_to_all(keys_in, "shard", split_axis=1, concat_axis=0, tiled=True),
        lax.all_to_all(values, "shard", split_axis=1, concat_axis=0, tiled=True),
    )
    row_count, width_all = query_head.shape
    head_count = width_all // HDIM
    block_count = row_count // BLOCK
    score_scale = 1.0 / math.sqrt(HDIM)
    query_blk, key_blk, value_blk, probs = attend_listed(
        query_head, key_head, value_head, block_ids, live_count
    )
    prob_bf = probs.astype(jnp.bfloat16)
    heads_out = (
        jnp.einsum("bhqk,bkhd->bqhd", prob_bf, value_blk, preferred_element_type=jnp.float32)
        .reshape(row_count, width_all)
        .astype(jnp.bfloat16)
    )
    row_piece = lax.all_gather(grad_live, "shard", axis=0, tiled=True)
    acc_now = jnp.einsum("rw,ro->wo", heads_out, row_piece, preferred_element_type=jnp.float32)
    product = jnp.einsum("ro,wo->rw", row_piece, out_weight, preferred_element_type=jnp.float32)
    grad_o = product.astype(jnp.bfloat16).reshape(block_count, BLOCK, head_count, HDIM)
    grad_prob = jnp.einsum("bqhd,bkhd->bhqk", grad_o, value_blk, preferred_element_type=jnp.float32)
    row_delta = jnp.sum(probs * grad_prob, axis=-1, keepdims=True)
    dscore = (probs * (grad_prob - row_delta) * score_scale).astype(jnp.bfloat16)
    grad_query = (
        jnp.einsum("bhqk,bkhd->bqhd", dscore, key_blk, preferred_element_type=jnp.float32)
        .reshape(row_count, width_all)
        .astype(jnp.bfloat16)
    )
    onehot = (
        block_ids[:, :, None] == jnp.arange(block_count, dtype=jnp.int32)[None, None, :]
    ).astype(jnp.float32)
    key_parts = jnp.einsum(
        "bhqk,bqhd->bkhd", dscore, query_blk, preferred_element_type=jnp.float32
    ).reshape(block_count, NB, BLOCK, width_all)
    value_parts = jnp.einsum(
        "bhqk,bqhd->bkhd", prob_bf, grad_o, preferred_element_type=jnp.float32
    ).reshape(block_count, NB, BLOCK, width_all)
    grad_key = (
        jnp.einsum("bjc,bjrx->crx", onehot, key_parts, precision=lax.Precision.HIGHEST)
        .reshape(row_count, width_all)
        .astype(jnp.bfloat16)
    )
    grad_value = (
        jnp.einsum("bjc,bjrx->crx", onehot, value_parts, precision=lax.Precision.HIGHEST)
        .reshape(row_count, width_all)
        .astype(jnp.bfloat16)
    )
    query_back, key_back, value_back = (
        lax.all_to_all(grad_query, "shard", split_axis=0, concat_axis=1, tiled=True),
        lax.all_to_all(grad_key, "shard", split_axis=0, concat_axis=1, tiled=True),
        lax.all_to_all(grad_value, "shard", split_axis=0, concat_axis=1, tiled=True),
    )
    scene_total = lax.axis_size(DP)
    summed = lax.psum(acc_now, DP)
    grad_weight = (summed / scene_total).astype(jnp.bfloat16)
    return (query_back, key_back, value_back, grad_weight)


def body(queries, keys_in, values, out_grad, out_weight, block_lists, voxel_count):
    dense = block_lists.shape[1] == NB and queries.shape[0] == BLOCK
    if dense and lax.axis_size("shard") == 4 and lax.axis_size("chips") == 4:
        return dense_body(queries, keys_in, values, out_grad, out_weight, voxel_count)
    return listed_body(queries, keys_in, values, out_grad, out_weight, block_lists, voxel_count)


def solution(mesh):
    chips = mesh.shape["dp"] // 2
    mesh = jax.sharding.Mesh(mesh.devices.reshape(chips, 2, -1), ("chips", "core", "shard"))
    return jax.shard_map(
        body,
        mesh=mesh,
        in_specs=(
            P((*DP, "shard"), None),
            P((*DP, "shard"), None),
            P((*DP, "shard"), None),
            P((*DP, "shard"), None),
            P("shard", None),
            P(DP, None, None),
            P(DP),
        ),
        out_specs=(
            P((*DP, "shard"), None),
            P((*DP, "shard"), None),
            P((*DP, "shard"), None),
            P("shard", None),
        ),
        check_vma=False,
    )
```

```python
import functools
import math

import jax
import jax.numpy as jnp
from jax import lax
from jax.experimental import pallas as pl
from jax.experimental.pallas import tpu as pltpu
from jax.sharding import PartitionSpec as P

HDIM = 128
BLOCK = 128
NB = 4
MIB = 1024 * 1024
DP = ("chips", "core")

Z, COUNT, CORE, CHIP = range(4)

EARLY = 2

NO_COST = pl.CostEstimate(flops=0, bytes_accessed=1024, transcendentals=0)

f32 = jnp.float32
bf16 = jnp.bfloat16


def dot(a, b, ca, cb):
    return lax.dot_general(a, b, (((ca,), (cb,)), ((), ())), preferred_element_type=f32)


def sds(shape, dtype):
    return jax.ShapeDtypeStruct(shape, dtype)


def params(mib=8):
    return pltpu.CompilerParams(vmem_limit_bytes=mib * MIB)


def swap(x, axis, size, flip):
    flip_of = flip if callable(flip) else lambda i: flip
    return lax.ppermute(x, axis, [(i, i ^ flip_of(i)) for i in range(size)])


def after(x, *earlier):
    return lax.optimization_barrier((x, *earlier))[0]


def run_all(copies):
    for copy in copies:
        copy.start()
    for copy in copies:
        copy.wait()


def whole(kernel, out_shape, operands, name, scalars=0, mib=8, scratch=()):
    return pl.pallas_call(
        kernel,
        out_shape=out_shape,
        in_specs=[pl.BlockSpec(memory_space=pltpu.SMEM)] * scalars
        + [pl.BlockSpec(memory_space=pltpu.VMEM)] * (len(operands) - scalars),
        out_specs=jax.tree.map(lambda _: pl.BlockSpec(memory_space=pltpu.VMEM), out_shape),
        scratch_shapes=scratch,
        compiler_params=params(mib),
        cost_estimate=NO_COST,
        name=name,
    )(*operands)


def pack_kernel(meta, q_ref, k_ref, v_ref, *refs):
    *outs, sems = refs
    width = outs[0].shape[2]
    copies = []
    for n, out_ref in enumerate(outs):
        k, first = (n, 0) if n < 2 else (n // 2 + 1, n % 2 * EARLY * HDIM)
        start = pl.multiple_of((meta[Z] ^ k) * width + first, 128)
        for i, ref in enumerate((q_ref, k_ref, v_ref)):
            part = ref.at[:, pl.ds(start, out_ref.shape[2])]
            copies.append(pltpu.make_async_copy(part, out_ref.at[i], sems.at[3 * n + i]))
    run_all(copies)


def pack(meta, queries, keys_in, values):
    rows, width = queries.shape
    part, early = width // 4, EARLY * HDIM
    shapes = [sds((3, rows, n), bf16) for n in (part, part, early, part - early, early, part - early)]
    return pl.pallas_call(
        pack_kernel,
        out_shape=shapes,
        in_specs=[pl.BlockSpec(memory_space=pltpu.SMEM)] + [pl.BlockSpec(memory_space=pl.ANY)] * 3,
        out_specs=[pl.BlockSpec(memory_space=pltpu.VMEM)] * len(shapes),
        scratch_shapes=[pltpu.SemaphoreType.DMA((3 * len(shapes),))],
        compiler_params=params(),
        cost_estimate=NO_COST,
        name="pack_heads",
    )(meta, queries, keys_in, values)


def token_pos(shape, dim, z, start=0):
    return (lax.broadcasted_iota(jnp.int32, shape, dim) + start) ^ (z * BLOCK)


def grad_attn_kernel(start, meta, *refs):
    *grads, w_ref, out_ref = refs
    grad = jnp.concatenate([g[...] for g in grads], axis=0)
    live = token_pos((grad.shape[0], 1), 0, meta[Z], start) < meta[COUNT]
    tile = 2 * HDIM

    @pl.loop(0, w_ref.shape[0] // tile)
    def _(i):
        part = pl.ds(pl.multiple_of(i * tile, tile), tile)
        out_ref[:, part] = jnp.where(live, dot(grad, w_ref[part, :], 1, 1), 0.0).astype(bf16)


def grad_attn(meta, grads, weight, start):
    shape = (sum(g.shape[0] for g in grads), weight.shape[0])
    kernel = functools.partial(grad_attn_kernel, start)
    return whole(kernel, sds(shape, bf16), (meta, *grads, weight), "grad_attn", 1, 16)


def head_of(pieces, group, h):
    part = pieces[-1].shape[2]
    parts = []
    for p in pieces:
        start = (group * EARLY * HDIM if p.shape[2] > part else 0) + h * HDIM
        parts.append([p[i, :, start : start + HDIM] for i in range(3)])
    return (jnp.concatenate(x, axis=0) for x in zip(*parts))


def forward_kernel(group, meta, p0, p1, p2, p3, weight_ref, inverse_ref, out_ref, heads_ref, bias_ref):
    pieces = (p0, p1, p2, p3)
    rows = p0.shape[1]
    total = 4 * rows
    tile = 2 * rows
    to_power = math.log2(math.e) / math.sqrt(HDIM)
    query_live = token_pos((1, total), 1, meta[Z]) < meta[COUNT]
    key_live = token_pos((total, 1), 0, meta[Z]) < meta[COUNT]
    bias_ref[...] = jnp.where(key_live | ~query_live, 0.0, -jnp.inf)
    for h in range(p3.shape[2] // HDIM):
        cols = slice(h * HDIM, (h + 1) * HDIM)
        query, key, value = head_of(pieces, group, h)
        for t in range(2):
            part = slice(t * tile, (t + 1) * tile)
            scores = dot(key, query[part], 1, 1) + bias_ref[:, part]
            peak = jnp.max(scores, axis=0, keepdims=True)
            weights = jnp.exp2((scores - peak) * to_power).astype(bf16)
            weight_ref[h, :, part] = weights
            inverse = 1.0 / jnp.sum(weights.astype(f32), axis=0, keepdims=True)
            inverse_ref[h, :, part] = inverse
            heads = dot(value, weights, 0, 0) * inverse
            out_ref[cols, part] = heads
            heads_ref[cols, part] = jnp.where(query_live[:, part], heads, 0.0).astype(bf16)


def forward(meta, pieces, group):
    _, rows, width = pieces[-1].shape
    total = 4 * rows
    shapes = [
        sds((width // HDIM, total, total), bf16),
        sds((width // HDIM, 1, total), f32),
        sds((width, total), f32),
        sds((width, total), bf16),
    ]
    scratch = [pltpu.VMEM((total, total), f32)]
    kernel = functools.partial(forward_kernel, group)
    return whole(kernel, shapes, (meta, *pieces), "attend_forward", 1, 16, scratch)


def backward_kernel(group, meta, p0, p1, p2, p3, early_ref, late_ref, weight_ref, inverse_ref, out_ref, back_ref):
    pieces = (p0, p1, p2, p3)
    rows = p0.shape[1]
    total = 4 * rows
    tile = 2 * rows
    scale = 1.0 / math.sqrt(HDIM)
    places = [meta[Z] ^ k for k in range(4)]
    for h in range(p3.shape[2] // HDIM):
        query, key, value = head_of(pieces, group, h)
        cols = slice(h * HDIM, (h + 1) * HDIM)
        start = (group * EARLY + h) * HDIM
        grad = jnp.concatenate([ref[:, start : start + HDIM] for ref in (early_ref, late_ref)], axis=0)
        grad_key = grad_value = jnp.zeros((total, HDIM), f32)
        for t in range(2):
            span = slice(t * tile, (t + 1) * tile)
            weights = weight_ref[h, :, span]
            inverse = inverse_ref[h, :, span]
            turned = grad[span].astype(f32).T
            row_delta = jnp.sum(out_ref[cols, span] * turned, axis=0, keepdims=True)
            grad_prob = dot(value, grad[span], 1, 1)
            dscore = (weights.astype(f32) * ((grad_prob - row_delta) * (inverse * scale))).astype(bf16)
            grad_query = dot(key, dscore, 0, 0).T.astype(bf16)
            back_ref[places[2 * t], 0, :, cols] = grad_query[:rows]
            back_ref[places[2 * t + 1], 0, :, cols] = grad_query[rows:]
            grad_key += dot(dscore, query[span], 1, 0)
            grad_value += dot(weights, (turned * inverse).T.astype(bf16), 1, 0)
        for k in range(4):
            mine = slice(k * rows, (k + 1) * rows)
            back_ref[places[k], 1, :, cols] = grad_key[mine].astype(bf16)
            back_ref[places[k], 2, :, cols] = grad_value[mine].astype(bf16)


def backward(meta, pieces, grads, saved, group):
    shape = (4, *pieces[-1].shape)
    kernel = functools.partial(backward_kernel, group)
    return whole(kernel, sds(shape, bf16), (meta, *pieces, *grads, *saved), "attend_backward", 1, 16)


LINE = HDIM // 8


def first_flip(i):
    return 4 if i & 1 else 2


def second_flip(i):
    return 2 if i & 1 else 4


def line_at(meta, head, other, n):
    core = meta[CORE] ^ other
    flip = (0, 2 - core, 1 + core, 3)[n]
    at = head * HDIM + (core * 4 + (meta[CHIP] ^ flip)) * LINE
    return pl.ds(pl.multiple_of(at, LINE), LINE)


def weight_kernel(meta, heads_ref, *refs):
    *grads, send_ref, keep_ref = refs
    width = heads_ref.shape[0]
    lines = []
    for other in (1, 0):
        for n in range(4):
            lines += [heads_ref[line_at(meta, h, other, n), :] for h in range(width // HDIM)]
    lines = jnp.concatenate(lines, axis=0)
    tile = 4 * HDIM

    @pl.loop(0, send_ref.shape[1] // tile)
    def _(i):
        part = pl.ds(pl.multiple_of(i * tile, tile), tile)
        product = dot(lines, jnp.concatenate([g[:, part] for g in grads], axis=0), 1, 0)
        send_ref[:, part] = product[: width // 2].astype(bf16)
        keep_ref[:, part] = product[width // 2 :]


def weight_halves(meta, heads, grads):
    shape = (heads.shape[0] // 2, grads[0].shape[1])
    return whole(weight_kernel, [sds(shape, bf16), sds(shape, f32)], (meta, heads, *grads), "weight_halves", 1, 16)


def merge_kernel(*refs):
    keeps, recvs, outs = refs[:2], refs[2:4], refs[4:]
    starts = [0, 0]
    for n in range(4):
        out_ref = outs[n // 2]
        for keep_ref, recv_ref in zip(keeps, recvs):
            size = keep_ref.shape[0] // 4
            total = keep_ref[n * size : (n + 1) * size, :] + recv_ref[n * size : (n + 1) * size, :].astype(f32)
            at = starts[n // 2]
            out_ref[at : at + size, :] = total.astype(out_ref.dtype)
            starts[n // 2] += size


def merge_split(keeps, recvs):
    shape = (sum(x.shape[0] for x in keeps) // 2, keeps[0].shape[1])
    return whole(merge_kernel, [sds(shape, f32), sds(shape, bf16)], (*keeps, *recvs), "merge_split")


def split_kernel(keep_ref, recv_ref, own_ref, send_ref):
    size = own_ref.shape[0]
    own_ref[...] = keep_ref[:size, :] + recv_ref[:size, :].astype(f32)
    send_ref[...] = (keep_ref[size:, :] + recv_ref[size:, :].astype(f32)).astype(bf16)


def split(keep, recv):
    shape = (keep.shape[0] // 2, keep.shape[1])
    return whole(split_kernel, [sds(shape, f32), sds(shape, bf16)], (keep, recv), "split_sum")


def total_kernel(scale, own_ref, recv_ref, out_ref):
    out_ref[...] = ((own_ref[...] + recv_ref[...].astype(f32)) * scale).astype(bf16)


def total_of(own, recv, scale):
    return whole(functools.partial(total_kernel, scale), sds(own.shape, bf16), (own, recv), "scene_mean")


def stack_kernel(first_ref, second_ref, out_ref):
    size = first_ref.shape[0]
    out_ref[:size, :] = first_ref[...]
    out_ref[size:, :] = second_ref[...]


def stack(first, second):
    return whole(stack_kernel, sds((2 * first.shape[0], first.shape[1]), bf16), (first, second), "stack")


def join_weight_kernel(meta, *refs):
    *parts, out_ref, sems = refs
    copies = []
    for p, ref in enumerate(parts):
        other, upper = divmod(p, 2)
        heads = ref.shape[0] // (2 * LINE)
        for m in range(2 * heads):
            lower, h = divmod(m, heads)
            line = out_ref.at[line_at(meta, h, other, 2 * upper + lower), :]
            part = ref.at[pl.ds(m * LINE, LINE), :]
            copies.append(pltpu.make_async_copy(part, line, sems.at[len(copies)]))
    run_all(copies)


def join_weight(meta, parts):
    rows, outw = sum(p.shape[0] for p in parts), parts[0].shape[1]
    return pl.pallas_call(
        join_weight_kernel,
        out_shape=sds((rows, outw), bf16),
        in_specs=[pl.BlockSpec(memory_space=pltpu.SMEM)] + [pl.BlockSpec(memory_space=pl.ANY)] * len(parts),
        out_specs=pl.BlockSpec(memory_space=pl.ANY),
        scratch_shapes=[pltpu.SemaphoreType.DMA((rows // LINE,))],
        compiler_params=params(),
        cost_estimate=NO_COST,
        name="join_weight",
    )(meta, *parts)


def join_kernel(a_ref, b_ref, *refs):
    *outs, sems = refs
    copies = []
    for j in range(4):
        start = j * (a_ref.shape[3] + b_ref.shape[3])
        for ref in (a_ref, b_ref):
            for i, out_ref in enumerate(outs):
                cols = out_ref.at[:, pl.ds(start, ref.shape[3])]
                copies.append(pltpu.make_async_copy(ref.at[j, i], cols, sems.at[len(copies)]))
            start += ref.shape[3]
    run_all(copies)


def join(backs):
    rows = backs[0].shape[2]
    return pl.pallas_call(
        join_kernel,
        out_shape=[sds((rows, 4 * sum(x.shape[3] for x in backs)), bf16)] * 3,
        in_specs=[pl.BlockSpec(memory_space=pl.ANY)] * 2,
        out_specs=[pl.BlockSpec(memory_space=pl.ANY)] * 3,
        scratch_shapes=[pltpu.SemaphoreType.DMA((24,))],
        compiler_params=params(),
        cost_estimate=NO_COST,
        name="join_heads",
    )(*backs)


def dense_body(queries, keys_in, values, out_grad, out_weight, voxel_count):
    meta = jnp.stack([lax.axis_index("shard"), voxel_count[0], lax.axis_index("core"), lax.axis_index("chips")])
    meta = meta.astype(jnp.int32)

    def send(x, k, *earlier):
        return swap(after(x, *earlier) if earlier else x, "shard", 4, k)

    across = send(out_grad, 2)
    beside = send(out_grad, 1)
    own, near1, far2a, far2b, far3a, far3b = pack(meta, queries, keys_in, values)
    piece1 = send(near1, 1)
    piece3a = send(far3a, 3, beside)
    piece2a = send(far2a, 2, across)
    piece3b = send(far3b, 3, piece3a)
    piece2b = send(far2b, 2, piece2a)
    half = across.shape[0] // 2
    corners = [send(across[:half], 1), send(after(across, piece1)[half:], 1)]
    grad_early = grad_attn(meta, (out_grad, beside, across), out_weight, 0)

    pieces = (own, piece1, piece2a, piece3a)
    *saved, heads = forward(meta, pieces, 0)
    grad_early, heads, *corners = lax.optimization_barrier((grad_early, heads, *corners))
    grads = (out_grad, beside, across, *corners)
    grad_heads = (grad_early, grad_attn(meta, grads[3:], out_weight, 3 * BLOCK))
    back_a = backward(meta, pieces, grad_heads, saved, 0)
    all_a = lax.all_to_all(back_a, "shard", split_axis=0, concat_axis=0, tiled=True)
    out_a, keep_a = weight_halves(meta, after(heads, back_a), grads)
    recv_a = swap(out_a, "core", 2, 1)
    keep_a, piece2b, piece3b = lax.optimization_barrier((keep_a, piece2b, piece3b))
    pieces = (own, piece1, piece2b, piece3b)
    *saved, heads = forward(meta, pieces, 1)
    back_b = backward(meta, pieces, grad_heads, saved, 1)
    all_b = lax.all_to_all(back_b, "shard", split_axis=0, concat_axis=0, tiled=True)
    out_b, keep_b = weight_halves(meta, after(heads, back_b), grads)
    recv_b = swap(out_b, "core", 2, 1)

    own_part, out = merge_split((keep_a, keep_b), (recv_a, recv_b))
    own_part, out = split(own_part, swap(out, DP, 8, first_flip))
    done = total_of(own_part, swap(out, DP, 8, second_flip), 1.0 / 8)
    pair = stack(done, swap(done, DP, 8, second_flip))
    pairs = [pair, swap(pair, DP, 8, first_flip)]
    grad_weight = join_weight(meta, pairs + [swap(x, "core", 2, 1) for x in pairs])
    return (*join((all_a, all_b)), grad_weight)


def attend_listed(queries, keys_in, values, block_ids, live_count):
    row_count, width_all = queries.shape
    head_count = width_all // HDIM
    block_count = row_count // BLOCK
    score_scale = 1.0 / math.sqrt(HDIM)
    query_blk = queries.reshape(block_count, BLOCK, head_count, HDIM)
    key_blk = keys_in.reshape(block_count, BLOCK, head_count, HDIM)[block_ids].reshape(
        block_count, NB * BLOCK, head_count, HDIM
    )
    value_blk = values.reshape(block_count, BLOCK, head_count, HDIM)[block_ids].reshape(
        block_count, NB * BLOCK, head_count, HDIM
    )
    query_pos = jnp.arange(row_count, dtype=jnp.int32).reshape(block_count, BLOCK)
    key_pos = (
        block_ids[:, :, None] * BLOCK + jnp.arange(BLOCK, dtype=jnp.int32)[None, None, :]
    ).reshape(block_count, NB * BLOCK)
    allowed = (key_pos[:, None, :] < live_count) | (query_pos[:, :, None] >= live_count)
    scores = (
        jnp.einsum("bqhd,bkhd->bhqk", query_blk, key_blk, preferred_element_type=jnp.float32)
        * score_scale
    )
    scores = jnp.where(allowed[:, None], scores, -jnp.inf)
    peak = jnp.max(scores, axis=-1, keepdims=True)
    weights = jnp.exp(scores - peak)
    probs = weights / jnp.sum(weights, axis=-1, keepdims=True)
    return (query_blk, key_blk, value_blk, probs)


def listed_body(queries, keys_in, values, out_grad, out_weight, block_lists, voxel_count):
    local_rows = queries.shape[0]
    live_count = voxel_count[0]
    block_ids = block_lists[0]
    positions = lax.axis_index("shard") * local_rows + jnp.arange(local_rows, dtype=jnp.int32)
    grad_live = jnp.where((positions < live_count)[:, None], out_grad, jnp.zeros_like(out_grad))
    query_head, key_head, value_head = (
        lax.all_to_all(queries, "shard", split_axis=1, concat_axis=0, tiled=True),
        lax.all_to_all(keys_in, "shard", split_axis=1, concat_axis=0, tiled=True),
        lax.all_to_all(values, "shard", split_axis=1, concat_axis=0, tiled=True),
    )
    row_count, width_all = query_head.shape
    head_count = width_all // HDIM
    block_count = row_count // BLOCK
    score_scale = 1.0 / math.sqrt(HDIM)
    query_blk, key_blk, value_blk, probs = attend_listed(
        query_head, key_head, value_head, block_ids, live_count
    )
    prob_bf = probs.astype(jnp.bfloat16)
    heads_out = (
        jnp.einsum("bhqk,bkhd->bqhd", prob_bf, value_blk, preferred_element_type=jnp.float32)
        .reshape(row_count, width_all)
        .astype(jnp.bfloat16)
    )
    row_piece = lax.all_gather(grad_live, "shard", axis=0, tiled=True)
    acc_now = jnp.einsum("rw,ro->wo", heads_out, row_piece, preferred_element_type=jnp.float32)
    product = jnp.einsum("ro,wo->rw", row_piece, out_weight, preferred_element_type=jnp.float32)
    grad_o = product.astype(jnp.bfloat16).reshape(block_count, BLOCK, head_count, HDIM)
    grad_prob = jnp.einsum("bqhd,bkhd->bhqk", grad_o, value_blk, preferred_element_type=jnp.float32)
    row_delta = jnp.sum(probs * grad_prob, axis=-1, keepdims=True)
    dscore = (probs * (grad_prob - row_delta) * score_scale).astype(jnp.bfloat16)
    grad_query = (
        jnp.einsum("bhqk,bkhd->bqhd", dscore, key_blk, preferred_element_type=jnp.float32)
        .reshape(row_count, width_all)
        .astype(jnp.bfloat16)
    )
    onehot = (
        block_ids[:, :, None] == jnp.arange(block_count, dtype=jnp.int32)[None, None, :]
    ).astype(jnp.float32)
    key_parts = jnp.einsum(
        "bhqk,bqhd->bkhd", dscore, query_blk, preferred_element_type=jnp.float32
    ).reshape(block_count, NB, BLOCK, width_all)
    value_parts = jnp.einsum(
        "bhqk,bqhd->bkhd", prob_bf, grad_o, preferred_element_type=jnp.float32
    ).reshape(block_count, NB, BLOCK, width_all)
    grad_key = (
        jnp.einsum("bjc,bjrx->crx", onehot, key_parts, precision=lax.Precision.HIGHEST)
        .reshape(row_count, width_all)
        .astype(jnp.bfloat16)
    )
    grad_value = (
        jnp.einsum("bjc,bjrx->crx", onehot, value_parts, precision=lax.Precision.HIGHEST)
        .reshape(row_count, width_all)
        .astype(jnp.bfloat16)
    )
    query_back, key_back, value_back = (
        lax.all_to_all(grad_query, "shard", split_axis=0, concat_axis=1, tiled=True),
        lax.all_to_all(grad_key, "shard", split_axis=0, concat_axis=1, tiled=True),
        lax.all_to_all(grad_value, "shard", split_axis=0, concat_axis=1, tiled=True),
    )
    scene_total = lax.axis_size(DP)
    summed = lax.psum(acc_now, DP)
    grad_weight = (summed / scene_total).astype(jnp.bfloat16)
    return (query_back, key_back, value_back, grad_weight)


def body(queries, keys_in, values, out_grad, out_weight, block_lists, voxel_count):
    dense = block_lists.shape[1] == NB and queries.shape[0] == BLOCK
    if dense and lax.axis_size("shard") == 4 and lax.axis_size("chips") == 4:
        return dense_body(queries, keys_in, values, out_grad, out_weight, voxel_count)
    return listed_body(queries, keys_in, values, out_grad, out_weight, block_lists, voxel_count)


def solution(mesh):
    chips = mesh.shape["dp"] // 2
    mesh = jax.sharding.Mesh(mesh.devices.reshape(chips, 2, -1), ("chips", "core", "shard"))
    return jax.shard_map(
        body,
        mesh=mesh,
        in_specs=(
            P((*DP, "shard"), None),
            P((*DP, "shard"), None),
            P((*DP, "shard"), None),
            P((*DP, "shard"), None),
            P("shard", None),
            P(DP, None, None),
            P(DP),
        ),
        out_specs=(
            P((*DP, "shard"), None),
            P((*DP, "shard"), None),
            P((*DP, "shard"), None),
            P("shard", None),
        ),
        check_vma=False,
    )
```

```python
import functools
import math

import jax
import jax.numpy as jnp
from jax import lax
from jax.experimental import pallas as pl
from jax.experimental.pallas import tpu as pltpu
from jax.sharding import PartitionSpec as P

HDIM = 128
BLOCK = 128
NB = 4
MIB = 1024 * 1024
DP = ("chips", "core")

Z, COUNT, CORE, CHIP = range(4)

EARLY = 3

NO_COST = pl.CostEstimate(flops=0, bytes_accessed=1024, transcendentals=0)

f32 = jnp.float32
bf16 = jnp.bfloat16


def dot(a, b, ca, cb):
    return lax.dot_general(a, b, (((ca,), (cb,)), ((), ())), preferred_element_type=f32)


def sds(shape, dtype):
    return jax.ShapeDtypeStruct(shape, dtype)


def params(mib=8):
    return pltpu.CompilerParams(vmem_limit_bytes=mib * MIB)


def swap(x, axis, size, flip):
    return lax.ppermute(x, axis, [(i, i ^ flip) for i in range(size)])


def after(x, *earlier):
    return lax.optimization_barrier((x, *earlier))[0]


def run_all(copies):
    for copy in copies:
        copy.start()
    for copy in copies:
        copy.wait()


def whole(kernel, out_shape, operands, name, scalars=0, mib=8, scratch=()):
    return pl.pallas_call(
        kernel,
        out_shape=out_shape,
        in_specs=[pl.BlockSpec(memory_space=pltpu.SMEM)] * scalars
        + [pl.BlockSpec(memory_space=pltpu.VMEM)] * (len(operands) - scalars),
        out_specs=jax.tree.map(lambda _: pl.BlockSpec(memory_space=pltpu.VMEM), out_shape),
        scratch_shapes=scratch,
        compiler_params=params(mib),
        cost_estimate=NO_COST,
        name=name,
    )(*operands)


def pack_kernel(meta, q_ref, k_ref, v_ref, *refs):
    *outs, sems = refs
    width = outs[0].shape[2]
    copies = []
    for n, out_ref in enumerate(outs):
        k, first = (n, 0) if n < 2 else (n // 2 + 1, n % 2 * EARLY * HDIM)
        start = pl.multiple_of((meta[Z] ^ k) * width + first, 128)
        for i, ref in enumerate((q_ref, k_ref, v_ref)):
            part = ref.at[:, pl.ds(start, out_ref.shape[2])]
            copies.append(pltpu.make_async_copy(part, out_ref.at[i], sems.at[3 * n + i]))
    run_all(copies)


def pack(meta, queries, keys_in, values):
    rows, width = queries.shape
    part, early = width // 4, EARLY * HDIM
    shapes = [sds((3, rows, n), bf16) for n in (part, part, early, part - early, early, part - early)]
    return pl.pallas_call(
        pack_kernel,
        out_shape=shapes,
        in_specs=[pl.BlockSpec(memory_space=pltpu.SMEM)] + [pl.BlockSpec(memory_space=pl.ANY)] * 3,
        out_specs=[pl.BlockSpec(memory_space=pltpu.VMEM)] * len(shapes),
        scratch_shapes=[pltpu.SemaphoreType.DMA((3 * len(shapes),))],
        compiler_params=params(),
        cost_estimate=NO_COST,
        name="pack_heads",
    )(meta, queries, keys_in, values)


def token_pos(shape, dim, z, start=0):
    return (lax.broadcasted_iota(jnp.int32, shape, dim) + start) ^ (z * BLOCK)


def grad_attn_kernel(start, meta, *refs):
    *grads, w_ref, out_ref = refs
    grad = jnp.concatenate([g[...] for g in grads], axis=0)
    live = token_pos((grad.shape[0], 1), 0, meta[Z], start) < meta[COUNT]
    tile = 2 * HDIM

    @pl.loop(0, w_ref.shape[0] // tile)
    def _(i):
        part = pl.ds(pl.multiple_of(i * tile, tile), tile)
        out_ref[:, part] = jnp.where(live, dot(grad, w_ref[part, :], 1, 1), 0.0).astype(bf16)


def grad_attn(meta, grads, weight, start):
    shape = (sum(g.shape[0] for g in grads), weight.shape[0])
    kernel = functools.partial(grad_attn_kernel, start)
    return whole(kernel, sds(shape, bf16), (meta, *grads, weight), "grad_attn", 1, 16)


def head_of(pieces, group, h):
    part = pieces[-1].shape[2]
    parts = []
    for p in pieces:
        start = (group * EARLY * HDIM if p.shape[2] > part else 0) + h * HDIM
        parts.append([p[i, :, start : start + HDIM] for i in range(3)])
    return (jnp.concatenate(x, axis=0) for x in zip(*parts))


def forward_kernel(group, meta, p0, p1, p2, p3, weight_ref, inverse_ref, out_ref, heads_ref, bias_ref):
    pieces = (p0, p1, p2, p3)
    rows = p0.shape[1]
    total = 4 * rows
    tile = 2 * rows
    to_power = math.log2(math.e) / math.sqrt(HDIM)
    query_live = token_pos((1, total), 1, meta[Z]) < meta[COUNT]
    key_live = token_pos((total, 1), 0, meta[Z]) < meta[COUNT]
    bias_ref[...] = jnp.where(key_live | ~query_live, 0.0, -jnp.inf)
    for h in range(p3.shape[2] // HDIM):
        cols = slice(h * HDIM, (h + 1) * HDIM)
        query, key, value = head_of(pieces, group, h)
        for t in range(2):
            part = slice(t * tile, (t + 1) * tile)
            scores = dot(key, query[part], 1, 1) + bias_ref[:, part]
            peak = jnp.max(scores, axis=0, keepdims=True)
            weights = jnp.exp2((scores - peak) * to_power).astype(bf16)
            weight_ref[h, :, part] = weights
            inverse = 1.0 / jnp.sum(weights.astype(f32), axis=0, keepdims=True)
            inverse_ref[h, :, part] = inverse
            heads = dot(value, weights, 0, 0) * inverse
            out_ref[cols, part] = heads
            heads_ref[cols, part] = jnp.where(query_live[:, part], heads, 0.0).astype(bf16)


def forward(meta, pieces, group):
    _, rows, width = pieces[-1].shape
    total = 4 * rows
    shapes = [
        sds((width // HDIM, total, total), bf16),
        sds((width // HDIM, 1, total), f32),
        sds((width, total), f32),
        sds((width, total), bf16),
    ]
    scratch = [pltpu.VMEM((total, total), f32)]
    kernel = functools.partial(forward_kernel, group)
    return whole(kernel, shapes, (meta, *pieces), "attend_forward", 1, 16, scratch)


def gradients(group, pieces, grad_refs, saved, backs):
    weight_ref, inverse_ref, out_ref = saved
    rows = pieces[0].shape[1]
    total = 4 * rows
    tile = 2 * rows
    scale = 1.0 / math.sqrt(HDIM)
    for h in range(pieces[-1].shape[2] // HDIM):
        query, key, value = head_of(pieces, group, h)
        cols = slice(h * HDIM, (h + 1) * HDIM)
        start = (group * EARLY + h) * HDIM
        grad = jnp.concatenate([ref[:, start : start + HDIM] for ref in grad_refs], axis=0)
        grad_key = grad_value = jnp.zeros((total, HDIM), f32)
        for t in range(2):
            span = slice(t * tile, (t + 1) * tile)
            weights = weight_ref[h, :, span]
            inverse = inverse_ref[h, :, span]
            turned = grad[span].astype(f32).T
            row_delta = jnp.sum(out_ref[cols, span] * turned, axis=0, keepdims=True)
            grad_prob = dot(value, grad[span], 1, 1)
            dscore = (weights.astype(f32) * ((grad_prob - row_delta) * (inverse * scale))).astype(bf16)
            grad_query = dot(key, dscore, 0, 0).T.astype(bf16)
            backs[2 * t][0, :, cols] = grad_query[:rows]
            backs[2 * t + 1][0, :, cols] = grad_query[rows:]
            grad_key += dot(dscore, query[span], 1, 0)
            grad_value += dot(weights, (turned * inverse).T.astype(bf16), 1, 0)
        for k in range(4):
            mine = slice(k * rows, (k + 1) * rows)
            backs[k][1, :, cols] = grad_key[mine].astype(bf16)
            backs[k][2, :, cols] = grad_value[mine].astype(bf16)


def backward_early_kernel(*refs):
    gradients(0, refs[:4], refs[4:6], refs[6:9], refs[9:])


def backward_early(pieces, grads, saved):
    shapes = [sds(pieces[-1].shape, bf16)] * 4
    return whole(backward_early_kernel, shapes, (*pieces, *grads, *saved), "backward_early", 0, 16)


def backward_late_kernel(meta, *refs):
    others, back_ref, own = refs[9:13], refs[13], refs[14:]
    gradients(1, refs[:4], refs[4:6], refs[6:9], own)
    first = others[0].shape[2]
    for k in range(4):
        place = meta[Z] ^ k
        back_ref[place, :, :, :first] = others[k][...]
        back_ref[place, :, :, first:] = own[k][...]


def backward_late(meta, pieces, grads, saved, others):
    _, rows, part = pieces[-1].shape
    shape = sds((4, 3, rows, others[0].shape[2] + part), bf16)
    operands = (meta, *pieces, *grads, *saved, *others)
    scratch = [pltpu.VMEM((3, rows, part), bf16)] * 4
    return whole(backward_late_kernel, shape, operands, "backward_late", 1, 16, scratch)


LINE = HDIM // 8


def line_at(meta, head, other, j):
    at = head * HDIM + ((meta[CORE] ^ other) * 4 + (meta[CHIP] ^ j)) * LINE
    return pl.ds(pl.multiple_of(at, LINE), LINE)


def weight_kernel(meta, heads_a, heads_b, *refs):
    *grads, send_ref, keep_ref = refs
    width = heads_a.shape[0] + heads_b.shape[0]
    lines = []
    for other in (1, 0):
        for j in range(4):
            for ref in (heads_a, heads_b):
                lines += [ref[line_at(meta, h, other, j), :] for h in range(ref.shape[0] // HDIM)]
    lines = jnp.concatenate(lines, axis=0)
    tile = 4 * HDIM

    @pl.loop(0, send_ref.shape[1] // tile)
    def _(i):
        part = pl.ds(pl.multiple_of(i * tile, tile), tile)
        product = dot(lines, jnp.concatenate([g[:, part] for g in grads], axis=0), 1, 0)
        send_ref[:, part] = product[: width // 2].astype(bf16)
        keep_ref[:, part] = product[width // 2 :]


def weight_halves(meta, heads, grads):
    shape = (sum(x.shape[0] for x in heads) // 2, grads[0].shape[1])
    return whole(weight_kernel, [sds(shape, bf16), sds(shape, f32)], (meta, *heads, *grads), "weight_halves", 1, 16)


def add_kernel(keep_ref, recv_ref, *outs):
    size = outs[0].shape[0]
    for j, out_ref in enumerate(outs):
        part = slice(j * size, (j + 1) * size)
        out_ref[...] = (keep_ref[part, :] + recv_ref[part, :].astype(f32)).astype(out_ref.dtype)


def add_parts(keep, recv):
    shape = (keep.shape[0] // 4, keep.shape[1])
    return whole(add_kernel, [sds(shape, f32)] + [sds(shape, bf16)] * 3, (keep, recv), "add_parts")


def total_kernel(scale, own_ref, r1, r2, r3, out_ref):
    total = own_ref[...] + r1[...].astype(f32) + r2[...].astype(f32) + r3[...].astype(f32)
    out_ref[...] = (total * scale).astype(bf16)


def total_of(own, recvs, scale):
    return whole(functools.partial(total_kernel, scale), sds(own.shape, bf16), (own, *recvs), "scene_mean")


def join_weight_kernel(meta, *refs):
    *parts, out_ref, sems = refs
    copies = []
    for n, ref in enumerate(parts):
        for h in range(ref.shape[0] // LINE):
            line = out_ref.at[line_at(meta, h, n // 4, n % 4), :]
            part = ref.at[pl.ds(h * LINE, LINE), :]
            copies.append(pltpu.make_async_copy(part, line, sems.at[len(copies)]))
    run_all(copies)


def join_weight(meta, parts):
    size, outw = parts[0].shape
    return pl.pallas_call(
        join_weight_kernel,
        out_shape=sds((8 * size, outw), bf16),
        in_specs=[pl.BlockSpec(memory_space=pltpu.SMEM)] + [pl.BlockSpec(memory_space=pltpu.VMEM)] * 8,
        out_specs=pl.BlockSpec(memory_space=pl.ANY),
        scratch_shapes=[pltpu.SemaphoreType.DMA((8 * size // LINE,))],
        compiler_params=params(),
        cost_estimate=NO_COST,
        name="join_weight",
    )(meta, *parts)


def join_kernel(back_ref, *refs):
    *outs, sems = refs
    width = back_ref.shape[3]
    copies = []
    for j in range(4):
        for i, out_ref in enumerate(outs):
            cols = out_ref.at[:, pl.ds(j * width, width)]
            copies.append(pltpu.make_async_copy(back_ref.at[j, i], cols, sems.at[len(copies)]))
    run_all(copies)


def join(back):
    _, _, rows, width = back.shape
    return pl.pallas_call(
        join_kernel,
        out_shape=[sds((rows, 4 * width), bf16)] * 3,
        in_specs=[pl.BlockSpec(memory_space=pltpu.VMEM)],
        out_specs=[pl.BlockSpec(memory_space=pl.ANY)] * 3,
        scratch_shapes=[pltpu.SemaphoreType.DMA((12,))],
        compiler_params=params(),
        cost_estimate=NO_COST,
        name="join_heads",
    )(back)


def dense_body(queries, keys_in, values, out_grad, out_weight, voxel_count):
    meta = jnp.stack([lax.axis_index("shard"), voxel_count[0], lax.axis_index("core"), lax.axis_index("chips")])
    meta = meta.astype(jnp.int32)

    def send(x, k, *earlier):
        return swap(after(x, *earlier) if earlier else x, "shard", 4, k)

    across = send(out_grad, 2)
    beside = send(out_grad, 1)
    own, near1, far2a, far2b, far3a, far3b = pack(meta, queries, keys_in, values)
    piece1 = send(near1, 1)
    piece3a = send(far3a, 3, beside)
    piece2a = send(far2a, 2, across)
    piece3b = send(far3b, 3, piece3a)
    piece2b = send(far2b, 2, piece2a)
    half = across.shape[0] // 2
    corners = [send(across[:half], 1), send(after(across, piece1)[half:], 1)]
    grad_early = grad_attn(meta, (out_grad, beside, across), out_weight, 0)

    pieces = (own, piece1, piece2a, piece3a)
    *saved, heads_a = forward(meta, pieces, 0)
    grad_early, heads_a, *corners = lax.optimization_barrier((grad_early, heads_a, *corners))
    grads = (out_grad, beside, across, *corners)
    grad_heads = (grad_early, grad_attn(meta, grads[3:], out_weight, 3 * BLOCK))
    mine = backward_early(pieces, grad_heads, saved)
    *mine, piece2b, piece3b = lax.optimization_barrier((*mine, piece2b, piece3b))
    pieces = (own, piece1, piece2b, piece3b)
    *saved, heads_b = forward(meta, pieces, 1)
    back = backward_late(meta, pieces, grad_heads, saved, mine)
    back_all = lax.all_to_all(back, "shard", split_axis=0, concat_axis=0, tiled=True)

    out, keep = weight_halves(meta, (heads_a, after(heads_b, back)), grads)
    own_part, *sends = add_parts(keep, swap(out, "core", 2, 1))
    recvs = [swap(x, "chips", 4, j + 1) for j, x in enumerate(sends)]
    done = total_of(own_part, recvs, 1.0 / 8)
    near = [done] + [swap(done, "chips", 4, j) for j in (1, 2, 3)]
    far = [swap(x, "core", 2, 1) for x in near]
    grad_weight = join_weight(meta, near + far)
    return (*join(back_all), grad_weight)


def attend_listed(queries, keys_in, values, block_ids, live_count):
    row_count, width_all = queries.shape
    head_count = width_all // HDIM
    block_count = row_count // BLOCK
    score_scale = 1.0 / math.sqrt(HDIM)
    query_blk = queries.reshape(block_count, BLOCK, head_count, HDIM)
    key_blk = keys_in.reshape(block_count, BLOCK, head_count, HDIM)[block_ids].reshape(
        block_count, NB * BLOCK, head_count, HDIM
    )
    value_blk = values.reshape(block_count, BLOCK, head_count, HDIM)[block_ids].reshape(
        block_count, NB * BLOCK, head_count, HDIM
    )
    query_pos = jnp.arange(row_count, dtype=jnp.int32).reshape(block_count, BLOCK)
    key_pos = (
        block_ids[:, :, None] * BLOCK + jnp.arange(BLOCK, dtype=jnp.int32)[None, None, :]
    ).reshape(block_count, NB * BLOCK)
    allowed = (key_pos[:, None, :] < live_count) | (query_pos[:, :, None] >= live_count)
    scores = (
        jnp.einsum("bqhd,bkhd->bhqk", query_blk, key_blk, preferred_element_type=jnp.float32)
        * score_scale
    )
    scores = jnp.where(allowed[:, None], scores, -jnp.inf)
    peak = jnp.max(scores, axis=-1, keepdims=True)
    weights = jnp.exp(scores - peak)
    probs = weights / jnp.sum(weights, axis=-1, keepdims=True)
    return (query_blk, key_blk, value_blk, probs)


def listed_body(queries, keys_in, values, out_grad, out_weight, block_lists, voxel_count):
    local_rows = queries.shape[0]
    live_count = voxel_count[0]
    block_ids = block_lists[0]
    positions = lax.axis_index("shard") * local_rows + jnp.arange(local_rows, dtype=jnp.int32)
    grad_live = jnp.where((positions < live_count)[:, None], out_grad, jnp.zeros_like(out_grad))
    query_head, key_head, value_head = (
        lax.all_to_all(queries, "shard", split_axis=1, concat_axis=0, tiled=True),
        lax.all_to_all(keys_in, "shard", split_axis=1, concat_axis=0, tiled=True),
        lax.all_to_all(values, "shard", split_axis=1, concat_axis=0, tiled=True),
    )
    row_count, width_all = query_head.shape
    head_count = width_all // HDIM
    block_count = row_count // BLOCK
    score_scale = 1.0 / math.sqrt(HDIM)
    query_blk, key_blk, value_blk, probs = attend_listed(
        query_head, key_head, value_head, block_ids, live_count
    )
    prob_bf = probs.astype(jnp.bfloat16)
    heads_out = (
        jnp.einsum("bhqk,bkhd->bqhd", prob_bf, value_blk, preferred_element_type=jnp.float32)
        .reshape(row_count, width_all)
        .astype(jnp.bfloat16)
    )
    row_piece = lax.all_gather(grad_live, "shard", axis=0, tiled=True)
    acc_now = jnp.einsum("rw,ro->wo", heads_out, row_piece, preferred_element_type=jnp.float32)
    product = jnp.einsum("ro,wo->rw", row_piece, out_weight, preferred_element_type=jnp.float32)
    grad_o = product.astype(jnp.bfloat16).reshape(block_count, BLOCK, head_count, HDIM)
    grad_prob = jnp.einsum("bqhd,bkhd->bhqk", grad_o, value_blk, preferred_element_type=jnp.float32)
    row_delta = jnp.sum(probs * grad_prob, axis=-1, keepdims=True)
    dscore = (probs * (grad_prob - row_delta) * score_scale).astype(jnp.bfloat16)
    grad_query = (
        jnp.einsum("bhqk,bkhd->bqhd", dscore, key_blk, preferred_element_type=jnp.float32)
        .reshape(row_count, width_all)
        .astype(jnp.bfloat16)
    )
    onehot = (
        block_ids[:, :, None] == jnp.arange(block_count, dtype=jnp.int32)[None, None, :]
    ).astype(jnp.float32)
    key_parts = jnp.einsum(
        "bhqk,bqhd->bkhd", dscore, query_blk, preferred_element_type=jnp.float32
    ).reshape(block_count, NB, BLOCK, width_all)
    value_parts = jnp.einsum(
        "bhqk,bqhd->bkhd", prob_bf, grad_o, preferred_element_type=jnp.float32
    ).reshape(block_count, NB, BLOCK, width_all)
    grad_key = (
        jnp.einsum("bjc,bjrx->crx", onehot, key_parts, precision=lax.Precision.HIGHEST)
        .reshape(row_count, width_all)
        .astype(jnp.bfloat16)
    )
    grad_value = (
        jnp.einsum("bjc,bjrx->crx", onehot, value_parts, precision=lax.Precision.HIGHEST)
        .reshape(row_count, width_all)
        .astype(jnp.bfloat16)
    )
    query_back, key_back, value_back = (
        lax.all_to_all(grad_query, "shard", split_axis=0, concat_axis=1, tiled=True),
        lax.all_to_all(grad_key, "shard", split_axis=0, concat_axis=1, tiled=True),
        lax.all_to_all(grad_value, "shard", split_axis=0, concat_axis=1, tiled=True),
    )
    scene_total = lax.axis_size(DP)
    summed = lax.psum(acc_now, DP)
    grad_weight = (summed / scene_total).astype(jnp.bfloat16)
    return (query_back, key_back, value_back, grad_weight)


def body(queries, keys_in, values, out_grad, out_weight, block_lists, voxel_count):
    dense = block_lists.shape[1] == NB and queries.shape[0] == BLOCK
    if dense and lax.axis_size("shard") == 4 and lax.axis_size("chips") == 4:
        return dense_body(queries, keys_in, values, out_grad, out_weight, voxel_count)
    return listed_body(queries, keys_in, values, out_grad, out_weight, block_lists, voxel_count)


def solution(mesh):
    chips = mesh.shape["dp"] // 2
    mesh = jax.sharding.Mesh(mesh.devices.reshape(chips, 2, -1), ("chips", "core", "shard"))
    return jax.shard_map(
        body,
        mesh=mesh,
        in_specs=(
            P((*DP, "shard"), None),
            P((*DP, "shard"), None),
            P((*DP, "shard"), None),
            P((*DP, "shard"), None),
            P("shard", None),
            P(DP, None, None),
            P(DP),
        ),
        out_specs=(
            P((*DP, "shard"), None),
            P((*DP, "shard"), None),
            P((*DP, "shard"), None),
            P("shard", None),
        ),
        check_vma=False,
    )
```

```python
import functools
import math

import jax
import jax.numpy as jnp
from jax import lax
from jax.experimental import pallas as pl
from jax.experimental.pallas import tpu as pltpu
from jax.sharding import PartitionSpec as P

HDIM = 128
BLOCK = 128
NB = 4
MIB = 1024 * 1024
DP = ("chips", "core")

Z, COUNT, CORE, CHIP = range(4)

EARLY = 3

NO_COST = pl.CostEstimate(flops=0, bytes_accessed=1024, transcendentals=0)

f32 = jnp.float32
bf16 = jnp.bfloat16


def dot(a, b, ca, cb):
    return lax.dot_general(a, b, (((ca,), (cb,)), ((), ())), preferred_element_type=f32)


def sds(shape, dtype):
    return jax.ShapeDtypeStruct(shape, dtype)


def params(mib=8):
    return pltpu.CompilerParams(vmem_limit_bytes=mib * MIB)


def swap(x, axis, size, flip):
    return lax.ppermute(x, axis, [(i, i ^ flip) for i in range(size)])


def after(x, *earlier):
    return lax.optimization_barrier((x, *earlier))[0]


def run_all(copies):
    for copy in copies:
        copy.start()
    for copy in copies:
        copy.wait()


def whole(kernel, out_shape, operands, name, scalars=0, mib=8, scratch=()):
    return pl.pallas_call(
        kernel,
        out_shape=out_shape,
        in_specs=[pl.BlockSpec(memory_space=pltpu.SMEM)] * scalars
        + [pl.BlockSpec(memory_space=pltpu.VMEM)] * (len(operands) - scalars),
        out_specs=jax.tree.map(lambda _: pl.BlockSpec(memory_space=pltpu.VMEM), out_shape),
        scratch_shapes=scratch,
        compiler_params=params(mib),
        cost_estimate=NO_COST,
        name=name,
    )(*operands)


def pack_kernel(meta, q_ref, k_ref, v_ref, grad_ref, mine_ref, *refs):
    *outs, sems = refs
    width = outs[0].shape[2]
    copies = [pltpu.make_async_copy(grad_ref, mine_ref, sems.at[3 * len(outs)])]
    for n, out_ref in enumerate(outs):
        k, first = (n, 0) if n < 2 else (n // 2 + 1, n % 2 * EARLY * HDIM)
        start = pl.multiple_of((meta[Z] ^ k) * width + first, 128)
        for i, ref in enumerate((q_ref, k_ref, v_ref)):
            part = ref.at[:, pl.ds(start, out_ref.shape[2])]
            copies.append(pltpu.make_async_copy(part, out_ref.at[i], sems.at[3 * n + i]))
    run_all(copies)


def pack(meta, queries, keys_in, values, grad):
    rows, width = queries.shape
    part, early = width // 4, EARLY * HDIM
    shapes = [sds((3, rows, n), bf16) for n in (part, part, early, part - early, early, part - early)]
    shapes = [sds(grad.shape, bf16)] + shapes
    return pl.pallas_call(
        pack_kernel,
        out_shape=shapes,
        in_specs=[pl.BlockSpec(memory_space=pltpu.SMEM)] + [pl.BlockSpec(memory_space=pl.ANY)] * 4,
        out_specs=[pl.BlockSpec(memory_space=pltpu.VMEM)] * len(shapes),
        scratch_shapes=[pltpu.SemaphoreType.DMA((3 * len(shapes),))],
        compiler_params=params(),
        cost_estimate=NO_COST,
        name="pack_heads",
    )(meta, queries, keys_in, values, grad)


def token_pos(shape, dim, z, start=0):
    return (lax.broadcasted_iota(jnp.int32, shape, dim) + start) ^ (z * BLOCK)


def grad_attn_kernel(start, meta, *refs):
    *grads, w_ref, out_ref = refs
    grad = jnp.concatenate([g[...] for g in grads], axis=0)
    live = token_pos((grad.shape[0], 1), 0, meta[Z], start) < meta[COUNT]
    tile = 2 * HDIM

    @pl.loop(0, w_ref.shape[0] // tile)
    def _(i):
        part = pl.ds(pl.multiple_of(i * tile, tile), tile)
        out_ref[:, part] = jnp.where(live, dot(grad, w_ref[part, :], 1, 1), 0.0).astype(bf16)


def grad_attn(meta, grads, weight, start):
    shape = (sum(g.shape[0] for g in grads), weight.shape[0])
    kernel = functools.partial(grad_attn_kernel, start)
    return whole(kernel, sds(shape, bf16), (meta, *grads, weight), "grad_attn", 1, 16)


def head_of(pieces, group, h):
    part = pieces[-1].shape[2]
    parts = []
    for p in pieces:
        start = (group * EARLY * HDIM if p.shape[2] > part else 0) + h * HDIM
        parts.append([p[i, :, start : start + HDIM] for i in range(3)])
    return (jnp.concatenate(x, axis=0) for x in zip(*parts))


def forward_kernel(group, meta, p0, p1, p2, p3, weight_ref, inverse_ref, out_ref, heads_ref, bias_ref):
    pieces = (p0, p1, p2, p3)
    rows = p0.shape[1]
    total = 4 * rows
    tile = 2 * rows
    to_power = math.log2(math.e) / math.sqrt(HDIM)
    query_live = token_pos((1, total), 1, meta[Z]) < meta[COUNT]
    key_live = token_pos((total, 1), 0, meta[Z]) < meta[COUNT]
    bias_ref[...] = jnp.where(key_live | ~query_live, 0.0, -jnp.inf)
    for h in range(p3.shape[2] // HDIM):
        cols = slice(h * HDIM, (h + 1) * HDIM)
        query, key, value = head_of(pieces, group, h)
        for t in range(2):
            part = slice(t * tile, (t + 1) * tile)
            scores = dot(key, query[part], 1, 1) + bias_ref[:, part]
            peak = jnp.max(scores, axis=0, keepdims=True)
            weights = jnp.exp2((scores - peak) * to_power).astype(bf16)
            weight_ref[h, :, part] = weights
            inverse = 1.0 / jnp.sum(weights.astype(f32), axis=0, keepdims=True)
            inverse_ref[h, :, part] = inverse
            heads = dot(value, weights, 0, 0) * inverse
            out_ref[cols, part] = heads
            heads_ref[cols, part] = jnp.where(query_live[:, part], heads, 0.0).astype(bf16)


def forward(meta, pieces, group):
    _, rows, width = pieces[-1].shape
    total = 4 * rows
    shapes = [
        sds((width // HDIM, total, total), bf16),
        sds((width // HDIM, 1, total), f32),
        sds((width, total), f32),
        sds((width, total), bf16),
    ]
    scratch = [pltpu.VMEM((total, total), f32)]
    kernel = functools.partial(forward_kernel, group)
    return whole(kernel, shapes, (meta, *pieces), "attend_forward", 1, 16, scratch)


def gradients(group, pieces, grad_refs, saved, backs):
    weight_ref, inverse_ref, out_ref = saved
    rows = pieces[0].shape[1]
    total = 4 * rows
    tile = 2 * rows
    scale = 1.0 / math.sqrt(HDIM)
    for h in range(pieces[-1].shape[2] // HDIM):
        query, key, value = head_of(pieces, group, h)
        cols = slice(h * HDIM, (h + 1) * HDIM)
        start = (group * EARLY + h) * HDIM
        grad = jnp.concatenate([ref[:, start : start + HDIM] for ref in grad_refs], axis=0)
        grad_key = grad_value = jnp.zeros((total, HDIM), f32)
        for t in range(2):
            span = slice(t * tile, (t + 1) * tile)
            weights = weight_ref[h, :, span]
            inverse = inverse_ref[h, :, span]
            turned = grad[span].astype(f32).T
            row_delta = jnp.sum(out_ref[cols, span] * turned, axis=0, keepdims=True)
            grad_prob = dot(value, grad[span], 1, 1)
            dscore = (weights.astype(f32) * ((grad_prob - row_delta) * (inverse * scale))).astype(bf16)
            grad_query = dot(key, dscore, 0, 0).T.astype(bf16)
            backs[2 * t][0, :, cols] = grad_query[:rows]
            backs[2 * t + 1][0, :, cols] = grad_query[rows:]
            grad_key += dot(dscore, query[span], 1, 0)
            grad_value += dot(weights, (turned * inverse).T.astype(bf16), 1, 0)
        for k in range(4):
            mine = slice(k * rows, (k + 1) * rows)
            backs[k][1, :, cols] = grad_key[mine].astype(bf16)
            backs[k][2, :, cols] = grad_value[mine].astype(bf16)


def backward_early_kernel(*refs):
    gradients(0, refs[:4], refs[4:6], refs[6:9], refs[9:])


def backward_early(pieces, grads, saved):
    shapes = [sds(pieces[-1].shape, bf16)] * 4
    return whole(backward_early_kernel, shapes, (*pieces, *grads, *saved), "backward_early", 0, 16)


def backward_late_kernel(meta, *refs):
    others, back_ref, own, sems = refs[9:13], refs[13], refs[14:18], refs[18]
    part = others[0].shape[2]
    copies = [
        pltpu.make_async_copy(ref, back_ref.at[meta[Z] ^ k, :, :, pl.ds(0, part)], sems.at[k])
        for k, ref in enumerate(others)
    ]
    for copy in copies:
        copy.start()
    gradients(1, refs[:4], refs[4:6], refs[6:9], own)
    for k, ref in enumerate(own):
        back_ref[meta[Z] ^ k, :, :, part:] = ref[...]
    for copy in copies:
        copy.wait()


def backward_late(meta, pieces, grads, saved, others):
    _, rows, part = pieces[-1].shape
    shape = sds((4, *pieces[0].shape), bf16)
    operands = (meta, *pieces, *grads, *saved, *others)
    scratch = [pltpu.VMEM((3, rows, part), bf16)] * 4 + [pltpu.SemaphoreType.DMA((4,))]
    return whole(backward_late_kernel, shape, operands, "backward_late", 1, 16, scratch)


LINE = HDIM // 8


def line_at(meta, head, other, j):
    at = head * HDIM + ((meta[CORE] ^ other) * 4 + (meta[CHIP] ^ j)) * LINE
    return pl.ds(pl.multiple_of(at, LINE), LINE)


def weight_kernel(meta, heads_a, heads_b, *refs):
    *grads, send_ref, keep_ref = refs
    width = heads_a.shape[0] + heads_b.shape[0]
    lines = []
    for other in (1, 0):
        for j in range(4):
            for ref in (heads_a, heads_b):
                lines += [ref[line_at(meta, h, other, j), :] for h in range(ref.shape[0] // HDIM)]
    lines = jnp.concatenate(lines, axis=0)
    tile = 4 * HDIM

    @pl.loop(0, send_ref.shape[1] // tile)
    def _(i):
        part = pl.ds(pl.multiple_of(i * tile, tile), tile)
        product = dot(lines, jnp.concatenate([g[:, part] for g in grads], axis=0), 1, 0)
        send_ref[:, part] = product[: width // 2].astype(bf16)
        keep_ref[:, part] = product[width // 2 :]


def weight_halves(meta, heads, grads):
    shape = (sum(x.shape[0] for x in heads) // 2, grads[0].shape[1])
    return whole(weight_kernel, [sds(shape, bf16), sds(shape, f32)], (meta, *heads, *grads), "weight_halves", 1, 16)


def add_kernel(keep_ref, recv_ref, *outs):
    size = outs[0].shape[0]
    for j, out_ref in enumerate(outs):
        part = slice(j * size, (j + 1) * size)
        out_ref[...] = (keep_ref[part, :] + recv_ref[part, :].astype(f32)).astype(out_ref.dtype)


def add_parts(keep, recv):
    shape = (keep.shape[0] // 4, keep.shape[1])
    return whole(add_kernel, [sds(shape, f32)] + [sds(shape, bf16)] * 3, (keep, recv), "add_parts")


def total_kernel(scale, own_ref, r1, r2, r3, out_ref):
    total = own_ref[...] + r1[...].astype(f32) + r2[...].astype(f32) + r3[...].astype(f32)
    out_ref[...] = (total * scale).astype(bf16)


def total_of(own, recvs, scale):
    return whole(functools.partial(total_kernel, scale), sds(own.shape, bf16), (own, *recvs), "scene_mean")


def join_weight_kernel(meta, *refs):
    *parts, out_ref, sems = refs
    copies = []
    for n, ref in enumerate(parts):
        for h in range(ref.shape[0] // LINE):
            line = out_ref.at[line_at(meta, h, n // 4, n % 4), :]
            part = ref.at[pl.ds(h * LINE, LINE), :]
            copies.append(pltpu.make_async_copy(part, line, sems.at[len(copies)]))
    run_all(copies)


def join_weight(meta, parts):
    size, outw = parts[0].shape
    return pl.pallas_call(
        join_weight_kernel,
        out_shape=sds((8 * size, outw), bf16),
        in_specs=[pl.BlockSpec(memory_space=pltpu.SMEM)] + [pl.BlockSpec(memory_space=pltpu.VMEM)] * 8,
        out_specs=pl.BlockSpec(memory_space=pl.ANY),
        scratch_shapes=[pltpu.SemaphoreType.DMA((8 * size // LINE,))],
        compiler_params=params(),
        cost_estimate=NO_COST,
        name="join_weight",
    )(meta, *parts)


def join_kernel(back_ref, *refs):
    *outs, sems = refs
    width = back_ref.shape[3]
    copies = []
    for j in range(4):
        for i, out_ref in enumerate(outs):
            cols = out_ref.at[:, pl.ds(j * width, width)]
            copies.append(pltpu.make_async_copy(back_ref.at[j, i], cols, sems.at[len(copies)]))
    run_all(copies)


def join(back):
    _, _, rows, width = back.shape
    return pl.pallas_call(
        join_kernel,
        out_shape=[sds((rows, 4 * width), bf16)] * 3,
        in_specs=[pl.BlockSpec(memory_space=pltpu.VMEM)],
        out_specs=[pl.BlockSpec(memory_space=pl.ANY)] * 3,
        scratch_shapes=[pltpu.SemaphoreType.DMA((12,))],
        compiler_params=params(),
        cost_estimate=NO_COST,
        name="join_heads",
    )(back)


def dense_body(queries, keys_in, values, out_grad, out_weight, voxel_count):
    meta = jnp.stack([lax.axis_index("shard"), voxel_count[0], lax.axis_index("core"), lax.axis_index("chips")])
    meta = meta.astype(jnp.int32)

    def send(x, k, *earlier):
        return swap(after(x, *earlier) if earlier else x, "shard", 4, k)

    across = send(out_grad, 2)
    beside = send(out_grad, 1)
    mine, own, near1, far2a, far2b, far3a, far3b = pack(meta, queries, keys_in, values, out_grad)
    piece1 = send(near1, 1)
    piece3a = send(far3a, 3, beside)
    piece2a = send(far2a, 2, across)
    piece3b = send(far3b, 3, piece3a)
    piece2b = send(far2b, 2, piece2a)
    half = across.shape[0] // 2
    grad_early = grad_attn(meta, (mine, beside, across), out_weight, 0)
    corners = [send(across[:half], 1), send(after(across, piece1, grad_early)[half:], 1)]

    pieces = (own, piece1, piece2a, piece3a)
    *saved, heads_a = forward(meta, pieces, 0)
    grad_early, heads_a, *corners = lax.optimization_barrier((grad_early, heads_a, *corners))
    grads = (mine, beside, across, *corners)
    grad_heads = (grad_early, grad_attn(meta, grads[3:], out_weight, 3 * BLOCK))
    others = backward_early(pieces, grad_heads, saved)
    *others, piece2b, piece3b = lax.optimization_barrier((*others, piece2b, piece3b))
    pieces = (own, piece1, piece2b, piece3b)
    *saved, heads_b = forward(meta, pieces, 1)
    back = backward_late(meta, pieces, grad_heads, saved, others)
    back_all = lax.all_to_all(back, "shard", split_axis=0, concat_axis=0, tiled=True)

    out, keep = weight_halves(meta, (heads_a, after(heads_b, back)), grads)
    own_part, *sends = add_parts(keep, swap(out, "core", 2, 1))
    recvs = [swap(x, "chips", 4, j + 1) for j, x in enumerate(sends)]
    done = total_of(own_part, recvs, 1.0 / 8)
    near = [done] + [swap(done, "chips", 4, j) for j in (1, 2, 3)]
    far = [swap(x, "core", 2, 1) for x in near]
    grads_in = join(back_all)
    far[-1] = after(far[-1], grads_in[0])
    return (*grads_in, join_weight(meta, near + far))


def attend_listed(queries, keys_in, values, block_ids, live_count):
    row_count, width_all = queries.shape
    head_count = width_all // HDIM
    block_count = row_count // BLOCK
    score_scale = 1.0 / math.sqrt(HDIM)
    query_blk = queries.reshape(block_count, BLOCK, head_count, HDIM)
    key_blk = keys_in.reshape(block_count, BLOCK, head_count, HDIM)[block_ids].reshape(
        block_count, NB * BLOCK, head_count, HDIM
    )
    value_blk = values.reshape(block_count, BLOCK, head_count, HDIM)[block_ids].reshape(
        block_count, NB * BLOCK, head_count, HDIM
    )
    query_pos = jnp.arange(row_count, dtype=jnp.int32).reshape(block_count, BLOCK)
    key_pos = (
        block_ids[:, :, None] * BLOCK + jnp.arange(BLOCK, dtype=jnp.int32)[None, None, :]
    ).reshape(block_count, NB * BLOCK)
    allowed = (key_pos[:, None, :] < live_count) | (query_pos[:, :, None] >= live_count)
    scores = (
        jnp.einsum("bqhd,bkhd->bhqk", query_blk, key_blk, preferred_element_type=jnp.float32)
        * score_scale
    )
    scores = jnp.where(allowed[:, None], scores, -jnp.inf)
    peak = jnp.max(scores, axis=-1, keepdims=True)
    weights = jnp.exp(scores - peak)
    probs = weights / jnp.sum(weights, axis=-1, keepdims=True)
    return (query_blk, key_blk, value_blk, probs)


def listed_body(queries, keys_in, values, out_grad, out_weight, block_lists, voxel_count):
    local_rows = queries.shape[0]
    live_count = voxel_count[0]
    block_ids = block_lists[0]
    positions = lax.axis_index("shard") * local_rows + jnp.arange(local_rows, dtype=jnp.int32)
    grad_live = jnp.where((positions < live_count)[:, None], out_grad, jnp.zeros_like(out_grad))
    query_head, key_head, value_head = (
        lax.all_to_all(queries, "shard", split_axis=1, concat_axis=0, tiled=True),
        lax.all_to_all(keys_in, "shard", split_axis=1, concat_axis=0, tiled=True),
        lax.all_to_all(values, "shard", split_axis=1, concat_axis=0, tiled=True),
    )
    row_count, width_all = query_head.shape
    head_count = width_all // HDIM
    block_count = row_count // BLOCK
    score_scale = 1.0 / math.sqrt(HDIM)
    query_blk, key_blk, value_blk, probs = attend_listed(
        query_head, key_head, value_head, block_ids, live_count
    )
    prob_bf = probs.astype(jnp.bfloat16)
    heads_out = (
        jnp.einsum("bhqk,bkhd->bqhd", prob_bf, value_blk, preferred_element_type=jnp.float32)
        .reshape(row_count, width_all)
        .astype(jnp.bfloat16)
    )
    row_piece = lax.all_gather(grad_live, "shard", axis=0, tiled=True)
    acc_now = jnp.einsum("rw,ro->wo", heads_out, row_piece, preferred_element_type=jnp.float32)
    product = jnp.einsum("ro,wo->rw", row_piece, out_weight, preferred_element_type=jnp.float32)
    grad_o = product.astype(jnp.bfloat16).reshape(block_count, BLOCK, head_count, HDIM)
    grad_prob = jnp.einsum("bqhd,bkhd->bhqk", grad_o, value_blk, preferred_element_type=jnp.float32)
    row_delta = jnp.sum(probs * grad_prob, axis=-1, keepdims=True)
    dscore = (probs * (grad_prob - row_delta) * score_scale).astype(jnp.bfloat16)
    grad_query = (
        jnp.einsum("bhqk,bkhd->bqhd", dscore, key_blk, preferred_element_type=jnp.float32)
        .reshape(row_count, width_all)
        .astype(jnp.bfloat16)
    )
    onehot = (
        block_ids[:, :, None] == jnp.arange(block_count, dtype=jnp.int32)[None, None, :]
    ).astype(jnp.float32)
    key_parts = jnp.einsum(
        "bhqk,bqhd->bkhd", dscore, query_blk, preferred_element_type=jnp.float32
    ).reshape(block_count, NB, BLOCK, width_all)
    value_parts = jnp.einsum(
        "bhqk,bqhd->bkhd", prob_bf, grad_o, preferred_element_type=jnp.float32
    ).reshape(block_count, NB, BLOCK, width_all)
    grad_key = (
        jnp.einsum("bjc,bjrx->crx", onehot, key_parts, precision=lax.Precision.HIGHEST)
        .reshape(row_count, width_all)
        .astype(jnp.bfloat16)
    )
    grad_value = (
        jnp.einsum("bjc,bjrx->crx", onehot, value_parts, precision=lax.Precision.HIGHEST)
        .reshape(row_count, width_all)
        .astype(jnp.bfloat16)
    )
    query_back, key_back, value_back = (
        lax.all_to_all(grad_query, "shard", split_axis=0, concat_axis=1, tiled=True),
        lax.all_to_all(grad_key, "shard", split_axis=0, concat_axis=1, tiled=True),
        lax.all_to_all(grad_value, "shard", split_axis=0, concat_axis=1, tiled=True),
    )
    scene_total = lax.axis_size(DP)
    summed = lax.psum(acc_now, DP)
    grad_weight = (summed / scene_total).astype(jnp.bfloat16)
    return (query_back, key_back, value_back, grad_weight)


def body(queries, keys_in, values, out_grad, out_weight, block_lists, voxel_count):
    dense = block_lists.shape[1] == NB and queries.shape[0] == BLOCK
    if dense and lax.axis_size("shard") == 4 and lax.axis_size("chips") == 4:
        return dense_body(queries, keys_in, values, out_grad, out_weight, voxel_count)
    return listed_body(queries, keys_in, values, out_grad, out_weight, block_lists, voxel_count)


def solution(mesh):
    chips = mesh.shape["dp"] // 2
    mesh = jax.sharding.Mesh(mesh.devices.reshape(chips, 2, -1), ("chips", "core", "shard"))
    return jax.shard_map(
        body,
        mesh=mesh,
        in_specs=(
            P((*DP, "shard"), None),
            P((*DP, "shard"), None),
            P((*DP, "shard"), None),
            P((*DP, "shard"), None),
            P("shard", None),
            P(DP, None, None),
            P(DP),
        ),
        out_specs=(
            P((*DP, "shard"), None),
            P((*DP, "shard"), None),
            P((*DP, "shard"), None),
            P("shard", None),
        ),
        check_vma=False,
    )
```

```python
import functools
import math

import jax
import jax.numpy as jnp
from jax import lax
from jax.experimental import pallas as pl
from jax.experimental.pallas import tpu as pltpu
from jax.sharding import PartitionSpec as P

HDIM = 128
BLOCK = 128
NB = 4
MIB = 1024 * 1024
DP = ("chips", "core")

Z, COUNT, CORE, CHIP = range(4)

EARLY = 3

NO_COST = pl.CostEstimate(flops=0, bytes_accessed=1024, transcendentals=0)

f32 = jnp.float32
bf16 = jnp.bfloat16


def dot(a, b, ca, cb):
    return lax.dot_general(a, b, (((ca,), (cb,)), ((), ())), preferred_element_type=f32)


def sds(shape, dtype):
    return jax.ShapeDtypeStruct(shape, dtype)


def params(mib=2):
    return pltpu.CompilerParams(vmem_limit_bytes=mib * MIB)


def swap(x, axis, size, flip):
    return lax.ppermute(x, axis, [(i, i ^ flip) for i in range(size)])


def after(x, *earlier):
    return lax.optimization_barrier((x, *earlier))[0]


def run_all(copies):
    for copy in copies:
        copy.start()
    for copy in copies:
        copy.wait()


def whole(kernel, out_shape, operands, name, scalars=0, mib=2, scratch=()):
    return pl.pallas_call(
        kernel,
        out_shape=out_shape,
        in_specs=[pl.BlockSpec(memory_space=pltpu.SMEM)] * scalars
        + [pl.BlockSpec(memory_space=pltpu.VMEM)] * (len(operands) - scalars),
        out_specs=jax.tree.map(lambda _: pl.BlockSpec(memory_space=pltpu.VMEM), out_shape),
        scratch_shapes=scratch,
        compiler_params=params(mib),
        cost_estimate=NO_COST,
        name=name,
    )(*operands)


def pack_kernel(meta, q_ref, k_ref, v_ref, grad_ref, mine_ref, *refs):
    *outs, sems = refs
    width = outs[0].shape[2]
    copies = [pltpu.make_async_copy(grad_ref, mine_ref, sems.at[3 * len(outs)])]
    for n, out_ref in enumerate(outs):
        k, first = (n, 0) if n < 2 else (n // 2 + 1, n % 2 * EARLY * HDIM)
        start = pl.multiple_of((meta[Z] ^ k) * width + first, 128)
        for i, ref in enumerate((q_ref, k_ref, v_ref)):
            part = ref.at[:, pl.ds(start, out_ref.shape[2])]
            copies.append(pltpu.make_async_copy(part, out_ref.at[i], sems.at[3 * n + i]))
    run_all(copies)


def pack(meta, queries, keys_in, values, grad):
    rows, width = queries.shape
    part, early = width // 4, EARLY * HDIM
    shapes = [sds((3, rows, n), bf16) for n in (part, part, early, part - early, early, part - early)]
    shapes = [sds(grad.shape, bf16)] + shapes
    return pl.pallas_call(
        pack_kernel,
        out_shape=shapes,
        in_specs=[pl.BlockSpec(memory_space=pltpu.SMEM)] + [pl.BlockSpec(memory_space=pl.ANY)] * 4,
        out_specs=[pl.BlockSpec(memory_space=pltpu.VMEM)] * len(shapes),
        scratch_shapes=[pltpu.SemaphoreType.DMA((3 * len(shapes),))],
        compiler_params=params(),
        cost_estimate=NO_COST,
        name="pack_heads",
    )(meta, queries, keys_in, values, grad)


def token_pos(shape, dim, z, start=0):
    return (lax.broadcasted_iota(jnp.int32, shape, dim) + start) ^ (z * BLOCK)


def grad_attn_kernel(start, meta, *refs):
    *grads, w_ref, out_ref = refs
    grad = jnp.concatenate([g[...] for g in grads], axis=0)
    live = token_pos((grad.shape[0], 1), 0, meta[Z], start) < meta[COUNT]
    tile = 2 * HDIM

    @pl.loop(0, w_ref.shape[0] // tile)
    def _(i):
        part = pl.ds(pl.multiple_of(i * tile, tile), tile)
        out_ref[:, part] = jnp.where(live, dot(grad, w_ref[part, :], 1, 1), 0.0).astype(bf16)


def grad_attn(meta, grads, weight, start):
    shape = (sum(g.shape[0] for g in grads), weight.shape[0])
    kernel = functools.partial(grad_attn_kernel, start)
    return whole(kernel, sds(shape, bf16), (meta, *grads, weight), "grad_attn", 1, 6)


def head_of(pieces, group, h):
    part = pieces[-1].shape[2]
    parts = []
    for p in pieces:
        start = (group * EARLY * HDIM if p.shape[2] > part else 0) + h * HDIM
        parts.append([p[i, :, start : start + HDIM] for i in range(3)])
    return (jnp.concatenate(x, axis=0) for x in zip(*parts))


def forward_kernel(group, meta, p0, p1, p2, p3, weight_ref, inverse_ref, out_ref, heads_ref, bias_ref):
    pieces = (p0, p1, p2, p3)
    rows = p0.shape[1]
    total = 4 * rows
    tile = 2 * rows
    to_power = math.log2(math.e) / math.sqrt(HDIM)
    query_live = token_pos((1, total), 1, meta[Z]) < meta[COUNT]
    key_live = token_pos((total, 1), 0, meta[Z]) < meta[COUNT]
    bias_ref[...] = jnp.where(key_live | ~query_live, 0.0, -jnp.inf)
    for h in range(p3.shape[2] // HDIM):
        cols = slice(h * HDIM, (h + 1) * HDIM)
        query, key, value = head_of(pieces, group, h)
        for t in range(2):
            part = slice(t * tile, (t + 1) * tile)
            scores = dot(key, query[part], 1, 1) + bias_ref[:, part]
            peak = jnp.max(scores, axis=0, keepdims=True)
            weights = jnp.exp2((scores - peak) * to_power).astype(bf16)
            weight_ref[h, :, part] = weights
            inverse = 1.0 / jnp.sum(weights.astype(f32), axis=0, keepdims=True)
            inverse_ref[h, :, part] = inverse
            heads = dot(value, weights, 0, 0) * inverse
            out_ref[cols, part] = heads
            heads_ref[cols, part] = jnp.where(query_live[:, part], heads, 0.0).astype(bf16)


def forward(meta, pieces, group):
    _, rows, width = pieces[-1].shape
    total = 4 * rows
    shapes = [
        sds((width // HDIM, total, total), bf16),
        sds((width // HDIM, 1, total), f32),
        sds((width, total), f32),
        sds((width, total), bf16),
    ]
    scratch = [pltpu.VMEM((total, total), f32)]
    kernel = functools.partial(forward_kernel, group)
    return whole(kernel, shapes, (meta, *pieces), "attend_forward", 1, 8, scratch)


def backward_kernel(meta, own, near, far2a, far3a, far2b, far3b, early_ref, late_ref, *refs):
    saved, back_ref, backs = (refs[:3], refs[3:6]), refs[6], refs[7:]
    rows = own.shape[1]
    total = 4 * rows
    tile = 2 * rows
    scale = 1.0 / math.sqrt(HDIM)
    for n in range(own.shape[2] // HDIM):
        group, h = divmod(n, EARLY)
        query, key, value = head_of(((own, near, far2a, far3a), (own, near, far2b, far3b))[group], group, h)
        weight_ref, inverse_ref, out_ref = saved[group]
        here = slice(h * HDIM, (h + 1) * HDIM)
        cols = slice(n * HDIM, (n + 1) * HDIM)
        grad = jnp.concatenate([early_ref[:, cols], late_ref[:, cols]], axis=0)
        grad_key = grad_value = jnp.zeros((total, HDIM), f32)
        for t in range(2):
            span = slice(t * tile, (t + 1) * tile)
            weights = weight_ref[h, :, span]
            inverse = inverse_ref[h, :, span]
            turned = grad[span].astype(f32).T
            row_delta = jnp.sum(out_ref[here, span] * turned, axis=0, keepdims=True)
            grad_prob = dot(value, grad[span], 1, 1)
            dscore = (weights.astype(f32) * ((grad_prob - row_delta) * (inverse * scale))).astype(bf16)
            grad_query = dot(key, dscore, 0, 0).T.astype(bf16)
            backs[2 * t][0, :, cols] = grad_query[:rows]
            backs[2 * t + 1][0, :, cols] = grad_query[rows:]
            grad_key += dot(dscore, query[span], 1, 0)
            grad_value += dot(weights, (turned * inverse).T.astype(bf16), 1, 0)
        for k in range(4):
            mine = slice(k * rows, (k + 1) * rows)
            backs[k][1, :, cols] = grad_key[mine].astype(bf16)
            backs[k][2, :, cols] = grad_value[mine].astype(bf16)
    for k, ref in enumerate(backs):
        back_ref[meta[Z] ^ k] = ref[...]


def backward(meta, pieces, grads, saved):
    shape = sds((4, *pieces[0].shape), bf16)
    scratch = [pltpu.VMEM(pieces[0].shape, bf16)] * 4
    return whole(backward_kernel, shape, (meta, *pieces, *grads, *saved), "attend_backward", 1, 8, scratch)


LINE = HDIM // 8


def line_at(meta, head, other, j):
    at = head * HDIM + ((meta[CORE] ^ other) * 4 + (meta[CHIP] ^ j)) * LINE
    return pl.ds(pl.multiple_of(at, LINE), LINE)


def weight_kernel(meta, heads_a, heads_b, *refs):
    *grads, send_ref, keep_ref = refs
    width = heads_a.shape[0] + heads_b.shape[0]
    lines = []
    for other in (1, 0):
        for j in range(4):
            for ref in (heads_a, heads_b):
                lines += [ref[line_at(meta, h, other, j), :] for h in range(ref.shape[0] // HDIM)]
    lines = jnp.concatenate(lines, axis=0)
    tile = 4 * HDIM

    @pl.loop(0, send_ref.shape[1] // tile)
    def _(i):
        part = pl.ds(pl.multiple_of(i * tile, tile), tile)
        product = dot(lines, jnp.concatenate([g[:, part] for g in grads], axis=0), 1, 0)
        send_ref[:, part] = product[: width // 2].astype(bf16)
        keep_ref[:, part] = product[width // 2 :]


def weight_halves(meta, heads, grads):
    shape = (sum(x.shape[0] for x in heads) // 2, grads[0].shape[1])
    return whole(weight_kernel, [sds(shape, bf16), sds(shape, f32)], (meta, *heads, *grads), "weight_halves", 1, 6)


def add_kernel(keep_ref, recv_ref, *outs):
    size = outs[0].shape[0]
    for j, out_ref in enumerate(outs):
        part = slice(j * size, (j + 1) * size)
        out_ref[...] = (keep_ref[part, :] + recv_ref[part, :].astype(f32)).astype(out_ref.dtype)


def add_parts(keep, recv):
    shape = (keep.shape[0] // 4, keep.shape[1])
    return whole(add_kernel, [sds(shape, f32)] + [sds(shape, bf16)] * 3, (keep, recv), "add_parts")


def total_kernel(scale, own_ref, r1, r2, r3, out_ref):
    total = own_ref[...] + r1[...].astype(f32) + r2[...].astype(f32) + r3[...].astype(f32)
    out_ref[...] = (total * scale).astype(bf16)


def total_of(own, recvs, scale):
    return whole(functools.partial(total_kernel, scale), sds(own.shape, bf16), (own, *recvs), "scene_mean")


def join_weight_kernel(meta, *refs):
    *parts, out_ref, sems = refs
    copies = []
    for n, ref in enumerate(parts):
        for h in range(ref.shape[0] // LINE):
            line = out_ref.at[line_at(meta, h, n // 4, n % 4), :]
            part = ref.at[pl.ds(h * LINE, LINE), :]
            copies.append(pltpu.make_async_copy(part, line, sems.at[len(copies)]))
    run_all(copies)


def join_weight(meta, parts):
    size, outw = parts[0].shape
    return pl.pallas_call(
        join_weight_kernel,
        out_shape=sds((8 * size, outw), bf16),
        in_specs=[pl.BlockSpec(memory_space=pltpu.SMEM)] + [pl.BlockSpec(memory_space=pltpu.VMEM)] * 8,
        out_specs=pl.BlockSpec(memory_space=pl.ANY),
        scratch_shapes=[pltpu.SemaphoreType.DMA((8 * size // LINE,))],
        compiler_params=params(),
        cost_estimate=NO_COST,
        name="join_weight",
    )(meta, *parts)


def join_kernel(back_ref, *refs):
    *outs, sems = refs
    width = back_ref.shape[3]
    copies = []
    for j in range(4):
        for i, out_ref in enumerate(outs):
            cols = out_ref.at[:, pl.ds(j * width, width)]
            copies.append(pltpu.make_async_copy(back_ref.at[j, i], cols, sems.at[len(copies)]))
    run_all(copies)


def join(back):
    _, _, rows, width = back.shape
    return pl.pallas_call(
        join_kernel,
        out_shape=[sds((rows, 4 * width), bf16)] * 3,
        in_specs=[pl.BlockSpec(memory_space=pltpu.VMEM)],
        out_specs=[pl.BlockSpec(memory_space=pl.ANY)] * 3,
        scratch_shapes=[pltpu.SemaphoreType.DMA((12,))],
        compiler_params=params(),
        cost_estimate=NO_COST,
        name="join_heads",
    )(back)


def dense_body(queries, keys_in, values, out_grad, out_weight, voxel_count):
    meta = jnp.stack([lax.axis_index("shard"), voxel_count[0], lax.axis_index("core"), lax.axis_index("chips")])
    meta = meta.astype(jnp.int32)

    def send(x, k, *earlier):
        return swap(after(x, *earlier) if earlier else x, "shard", 4, k)

    across = send(out_grad, 2)
    beside = send(out_grad, 1)
    mine, own, near1, far2a, far2b, far3a, far3b = pack(meta, queries, keys_in, values, out_grad)
    piece1 = send(near1, 1)
    piece3a = send(far3a, 3, beside)
    piece2a = send(far2a, 2, across)
    piece3b = send(far3b, 3, piece3a)
    piece2b = send(far2b, 2, piece2a)
    half = across.shape[0] // 2
    grad_early = grad_attn(meta, (mine, beside, across), out_weight, 0)
    corners = [send(across[:half], 1), send(after(across, piece1, grad_early)[half:], 1)]

    *saved_a, heads_a = forward(meta, (own, piece1, piece2a, piece3a), 0)
    heads_a, piece2b, piece3b = lax.optimization_barrier((heads_a, piece2b, piece3b))
    *saved_b, heads_b = forward(meta, (own, piece1, piece2b, piece3b), 1)
    grad_early, heads_b, *corners = lax.optimization_barrier((grad_early, heads_b, *corners))
    grads = (mine, beside, across, *corners)

    out, keep = weight_halves(meta, (heads_a, heads_b), grads)
    recv = swap(out, "core", 2, 1)
    grad_late = grad_attn(meta, after(grads[3:], out), out_weight, 3 * BLOCK)
    pieces = (own, piece1, piece2a, piece3a, piece2b, piece3b)
    back = backward(meta, pieces, (grad_early, grad_late), (*saved_a, *saved_b))
    back_all = lax.all_to_all(after(back, recv), "shard", split_axis=0, concat_axis=0, tiled=True)

    own_part, *sends = add_parts(after(keep, back), recv)
    recvs = [swap(x, "chips", 4, j + 1) for j, x in enumerate(sends)]
    done = total_of(own_part, recvs, 1.0 / 8)
    near = [done] + [swap(done, "chips", 4, j) for j in (1, 2, 3)]
    far = [swap(x, "core", 2, 1) for x in near]
    grads_in = join(back_all)
    far[-1] = after(far[-1], grads_in[0])
    return (*grads_in, join_weight(meta, near + far))


def attend_listed(queries, keys_in, values, block_ids, live_count):
    row_count, width_all = queries.shape
    head_count = width_all // HDIM
    block_count = row_count // BLOCK
    score_scale = 1.0 / math.sqrt(HDIM)
    query_blk = queries.reshape(block_count, BLOCK, head_count, HDIM)
    key_blk = keys_in.reshape(block_count, BLOCK, head_count, HDIM)[block_ids].reshape(
        block_count, NB * BLOCK, head_count, HDIM
    )
    value_blk = values.reshape(block_count, BLOCK, head_count, HDIM)[block_ids].reshape(
        block_count, NB * BLOCK, head_count, HDIM
    )
    query_pos = jnp.arange(row_count, dtype=jnp.int32).reshape(block_count, BLOCK)
    key_pos = (
        block_ids[:, :, None] * BLOCK + jnp.arange(BLOCK, dtype=jnp.int32)[None, None, :]
    ).reshape(block_count, NB * BLOCK)
    allowed = (key_pos[:, None, :] < live_count) | (query_pos[:, :, None] >= live_count)
    scores = (
        jnp.einsum("bqhd,bkhd->bhqk", query_blk, key_blk, preferred_element_type=jnp.float32)
        * score_scale
    )
    scores = jnp.where(allowed[:, None], scores, -jnp.inf)
    peak = jnp.max(scores, axis=-1, keepdims=True)
    weights = jnp.exp(scores - peak)
    probs = weights / jnp.sum(weights, axis=-1, keepdims=True)
    return (query_blk, key_blk, value_blk, probs)


def listed_body(queries, keys_in, values, out_grad, out_weight, block_lists, voxel_count):
    local_rows = queries.shape[0]
    live_count = voxel_count[0]
    block_ids = block_lists[0]
    positions = lax.axis_index("shard") * local_rows + jnp.arange(local_rows, dtype=jnp.int32)
    grad_live = jnp.where((positions < live_count)[:, None], out_grad, jnp.zeros_like(out_grad))
    query_head, key_head, value_head = (
        lax.all_to_all(queries, "shard", split_axis=1, concat_axis=0, tiled=True),
        lax.all_to_all(keys_in, "shard", split_axis=1, concat_axis=0, tiled=True),
        lax.all_to_all(values, "shard", split_axis=1, concat_axis=0, tiled=True),
    )
    row_count, width_all = query_head.shape
    head_count = width_all // HDIM
    block_count = row_count // BLOCK
    score_scale = 1.0 / math.sqrt(HDIM)
    query_blk, key_blk, value_blk, probs = attend_listed(
        query_head, key_head, value_head, block_ids, live_count
    )
    prob_bf = probs.astype(jnp.bfloat16)
    heads_out = (
        jnp.einsum("bhqk,bkhd->bqhd", prob_bf, value_blk, preferred_element_type=jnp.float32)
        .reshape(row_count, width_all)
        .astype(jnp.bfloat16)
    )
    row_piece = lax.all_gather(grad_live, "shard", axis=0, tiled=True)
    acc_now = jnp.einsum("rw,ro->wo", heads_out, row_piece, preferred_element_type=jnp.float32)
    product = jnp.einsum("ro,wo->rw", row_piece, out_weight, preferred_element_type=jnp.float32)
    grad_o = product.astype(jnp.bfloat16).reshape(block_count, BLOCK, head_count, HDIM)
    grad_prob = jnp.einsum("bqhd,bkhd->bhqk", grad_o, value_blk, preferred_element_type=jnp.float32)
    row_delta = jnp.sum(probs * grad_prob, axis=-1, keepdims=True)
    dscore = (probs * (grad_prob - row_delta) * score_scale).astype(jnp.bfloat16)
    grad_query = (
        jnp.einsum("bhqk,bkhd->bqhd", dscore, key_blk, preferred_element_type=jnp.float32)
        .reshape(row_count, width_all)
        .astype(jnp.bfloat16)
    )
    onehot = (
        block_ids[:, :, None] == jnp.arange(block_count, dtype=jnp.int32)[None, None, :]
    ).astype(jnp.float32)
    key_parts = jnp.einsum(
        "bhqk,bqhd->bkhd", dscore, query_blk, preferred_element_type=jnp.float32
    ).reshape(block_count, NB, BLOCK, width_all)
    value_parts = jnp.einsum(
        "bhqk,bqhd->bkhd", prob_bf, grad_o, preferred_element_type=jnp.float32
    ).reshape(block_count, NB, BLOCK, width_all)
    grad_key = (
        jnp.einsum("bjc,bjrx->crx", onehot, key_parts, precision=lax.Precision.HIGHEST)
        .reshape(row_count, width_all)
        .astype(jnp.bfloat16)
    )
    grad_value = (
        jnp.einsum("bjc,bjrx->crx", onehot, value_parts, precision=lax.Precision.HIGHEST)
        .reshape(row_count, width_all)
        .astype(jnp.bfloat16)
    )
    query_back, key_back, value_back = (
        lax.all_to_all(grad_query, "shard", split_axis=0, concat_axis=1, tiled=True),
        lax.all_to_all(grad_key, "shard", split_axis=0, concat_axis=1, tiled=True),
        lax.all_to_all(grad_value, "shard", split_axis=0, concat_axis=1, tiled=True),
    )
    scene_total = lax.axis_size(DP)
    summed = lax.psum(acc_now, DP)
    grad_weight = (summed / scene_total).astype(jnp.bfloat16)
    return (query_back, key_back, value_back, grad_weight)


def body(queries, keys_in, values, out_grad, out_weight, block_lists, voxel_count):
    dense = block_lists.shape[1] == NB and queries.shape[0] == BLOCK
    if dense and lax.axis_size("shard") == 4 and lax.axis_size("chips") == 4:
        return dense_body(queries, keys_in, values, out_grad, out_weight, voxel_count)
    return listed_body(queries, keys_in, values, out_grad, out_weight, block_lists, voxel_count)


def solution(mesh):
    chips = mesh.shape["dp"] // 2
    mesh = jax.sharding.Mesh(mesh.devices.reshape(chips, 2, -1), ("chips", "core", "shard"))
    return jax.shard_map(
        body,
        mesh=mesh,
        in_specs=(
            P((*DP, "shard"), None),
            P((*DP, "shard"), None),
            P((*DP, "shard"), None),
            P((*DP, "shard"), None),
            P("shard", None),
            P(DP, None, None),
            P(DP),
        ),
        out_specs=(
            P((*DP, "shard"), None),
            P((*DP, "shard"), None),
            P((*DP, "shard"), None),
            P("shard", None),
        ),
        check_vma=False,
    )
```

```python
import functools
import math

import jax
import jax.numpy as jnp
from jax import lax
from jax.experimental import pallas as pl
from jax.experimental.pallas import tpu as pltpu
from jax.sharding import PartitionSpec as P

HDIM = 128
BLOCK = 128
NB = 4
MIB = 1024 * 1024
DP = ("chips", "core")

Z, COUNT, CORE, CHIP = range(4)

EARLY = 3

NO_COST = pl.CostEstimate(flops=0, bytes_accessed=1024, transcendentals=0)

f32 = jnp.float32
bf16 = jnp.bfloat16


def dot(a, b, ca, cb):
    return lax.dot_general(a, b, (((ca,), (cb,)), ((), ())), preferred_element_type=f32)


def sds(shape, dtype):
    return jax.ShapeDtypeStruct(shape, dtype)


def params(mib=2):
    return pltpu.CompilerParams(vmem_limit_bytes=mib * MIB)


def swap(x, axis, size, flip):
    return lax.ppermute(x, axis, [(i, i ^ flip) for i in range(size)])


def after(x, *earlier):
    return lax.optimization_barrier((x, *earlier))[0]


def run_all(copies):
    for copy in copies:
        copy.start()
    for copy in copies:
        copy.wait()


def whole(kernel, out_shape, operands, name, scalars=0, mib=2, scratch=()):
    return pl.pallas_call(
        kernel,
        out_shape=out_shape,
        in_specs=[pl.BlockSpec(memory_space=pltpu.SMEM)] * scalars
        + [pl.BlockSpec(memory_space=pltpu.VMEM)] * (len(operands) - scalars),
        out_specs=jax.tree.map(lambda _: pl.BlockSpec(memory_space=pltpu.VMEM), out_shape),
        scratch_shapes=scratch,
        compiler_params=params(mib),
        cost_estimate=NO_COST,
        name=name,
    )(*operands)


def pack_kernel(meta, q_ref, k_ref, v_ref, grad_ref, mine_ref, *refs):
    *outs, sems = refs
    width = outs[0].shape[2]
    copies = [pltpu.make_async_copy(grad_ref, mine_ref, sems.at[3 * len(outs)])]
    for n, out_ref in enumerate(outs):
        k, first = (n, 0) if n < 2 else (n // 2 + 1, n % 2 * EARLY * HDIM)
        start = pl.multiple_of((meta[Z] ^ k) * width + first, 128)
        for i, ref in enumerate((q_ref, k_ref, v_ref)):
            part = ref.at[:, pl.ds(start, out_ref.shape[2])]
            copies.append(pltpu.make_async_copy(part, out_ref.at[i], sems.at[3 * n + i]))
    run_all(copies)


def pack(meta, queries, keys_in, values, grad):
    rows, width = queries.shape
    part, early = width // 4, EARLY * HDIM
    shapes = [sds((3, rows, n), bf16) for n in (part, part, early, part - early, early, part - early)]
    shapes = [sds(grad.shape, bf16)] + shapes
    return pl.pallas_call(
        pack_kernel,
        out_shape=shapes,
        in_specs=[pl.BlockSpec(memory_space=pltpu.SMEM)] + [pl.BlockSpec(memory_space=pl.ANY)] * 4,
        out_specs=[pl.BlockSpec(memory_space=pltpu.VMEM)] * len(shapes),
        scratch_shapes=[pltpu.SemaphoreType.DMA((3 * len(shapes),))],
        compiler_params=params(),
        cost_estimate=NO_COST,
        name="pack_heads",
    )(meta, queries, keys_in, values, grad)


def token_pos(shape, dim, z, start=0):
    return (lax.broadcasted_iota(jnp.int32, shape, dim) + start) ^ (z * BLOCK)


def grad_attn_kernel(start, meta, *refs):
    *grads, w_ref, out_ref = refs
    grad = jnp.concatenate([g[...] for g in grads], axis=0)
    live = token_pos((grad.shape[0], 1), 0, meta[Z], start) < meta[COUNT]
    tile = 2 * HDIM

    @pl.loop(0, w_ref.shape[0] // tile)
    def _(i):
        part = pl.ds(pl.multiple_of(i * tile, tile), tile)
        out_ref[:, part] = jnp.where(live, dot(grad, w_ref[part, :], 1, 1), 0.0).astype(bf16)


def grad_attn(meta, grads, weight, start):
    shape = (sum(g.shape[0] for g in grads), weight.shape[0])
    kernel = functools.partial(grad_attn_kernel, start)
    return whole(kernel, sds(shape, bf16), (meta, *grads, weight), "grad_attn", 1, 6)


def head_of(pieces, group, h):
    part = pieces[-1].shape[2]
    parts = []
    for p in pieces:
        start = (group * EARLY * HDIM if p.shape[2] > part else 0) + h * HDIM
        parts.append([p[i, :, start : start + HDIM] for i in range(3)])
    return (jnp.concatenate(x, axis=0) for x in zip(*parts))


def forward_kernel(group, meta, p0, p1, p2, p3, weight_ref, inverse_ref, out_ref, heads_ref, bias_ref):
    pieces = (p0, p1, p2, p3)
    rows = p0.shape[1]
    total = 4 * rows
    tile = 2 * rows
    to_power = math.log2(math.e) / math.sqrt(HDIM)
    query_live = token_pos((1, total), 1, meta[Z]) < meta[COUNT]
    key_live = token_pos((total, 1), 0, meta[Z]) < meta[COUNT]
    bias_ref[...] = jnp.where(key_live | ~query_live, 0.0, -jnp.inf)
    for h in range(p3.shape[2] // HDIM):
        cols = slice(h * HDIM, (h + 1) * HDIM)
        query, key, value = head_of(pieces, group, h)
        for t in range(2):
            part = slice(t * tile, (t + 1) * tile)
            scores = dot(key, query[part], 1, 1) + bias_ref[:, part]
            peak = jnp.max(scores, axis=0, keepdims=True)
            weights = jnp.exp2((scores - peak) * to_power).astype(bf16)
            weight_ref[h, :, part] = weights
            inverse = 1.0 / jnp.sum(weights.astype(f32), axis=0, keepdims=True)
            inverse_ref[h, :, part] = inverse
            heads = dot(value, weights, 0, 0) * inverse
            out_ref[cols, part] = heads
            heads_ref[cols, part] = jnp.where(query_live[:, part], heads, 0.0).astype(bf16)


def forward(meta, pieces, group):
    _, rows, width = pieces[-1].shape
    total = 4 * rows
    shapes = [
        sds((width // HDIM, total, total), bf16),
        sds((width // HDIM, 1, total), f32),
        sds((width, total), f32),
        sds((width, total), bf16),
    ]
    scratch = [pltpu.VMEM((total, total), f32)]
    kernel = functools.partial(forward_kernel, group)
    return whole(kernel, shapes, (meta, *pieces), "attend_forward", 1, 8, scratch)


def backward_kernel(own, near, far2a, far3a, far2b, far3b, early_ref, late_ref, *refs):
    saved, backs = (refs[:3], refs[3:6]), refs[6:]
    rows = own.shape[1]
    total = 4 * rows
    tile = 2 * rows
    scale = 1.0 / math.sqrt(HDIM)
    for n in range(own.shape[2] // HDIM):
        group, h = divmod(n, EARLY)
        query, key, value = head_of(((own, near, far2a, far3a), (own, near, far2b, far3b))[group], group, h)
        weight_ref, inverse_ref, out_ref = saved[group]
        here = slice(h * HDIM, (h + 1) * HDIM)
        cols = slice(n * HDIM, (n + 1) * HDIM)
        grad = jnp.concatenate([early_ref[:, cols], late_ref[:, cols]], axis=0)
        grad_key = grad_value = jnp.zeros((total, HDIM), f32)
        for t in range(2):
            span = slice(t * tile, (t + 1) * tile)
            weights = weight_ref[h, :, span]
            inverse = inverse_ref[h, :, span]
            turned = grad[span].astype(f32).T
            row_delta = jnp.sum(out_ref[here, span] * turned, axis=0, keepdims=True)
            grad_prob = dot(value, grad[span], 1, 1)
            dscore = (weights.astype(f32) * ((grad_prob - row_delta) * (inverse * scale))).astype(bf16)
            grad_query = dot(key, dscore, 0, 0).T.astype(bf16)
            backs[2 * t][0, :, cols] = grad_query[:rows]
            backs[2 * t + 1][0, :, cols] = grad_query[rows:]
            grad_key += dot(dscore, query[span], 1, 0)
            grad_value += dot(weights, (turned * inverse).T.astype(bf16), 1, 0)
        for k in range(4):
            mine = slice(k * rows, (k + 1) * rows)
            backs[k][1, :, cols] = grad_key[mine].astype(bf16)
            backs[k][2, :, cols] = grad_value[mine].astype(bf16)


def backward(pieces, grads, saved):
    shapes = [sds(pieces[0].shape, bf16)] * 4
    return whole(backward_kernel, shapes, (*pieces, *grads, *saved), "attend_backward", 0, 8)


LINE = HDIM // 8


def line_at(meta, head, other, j):
    at = head * HDIM + ((meta[CORE] ^ other) * 4 + (meta[CHIP] ^ j)) * LINE
    return pl.ds(pl.multiple_of(at, LINE), LINE)


def weight_kernel(meta, heads_a, heads_b, *refs):
    *grads, send_ref, keep_ref = refs
    width = heads_a.shape[0] + heads_b.shape[0]
    lines = []
    for other in (1, 0):
        for j in range(4):
            for ref in (heads_a, heads_b):
                lines += [ref[line_at(meta, h, other, j), :] for h in range(ref.shape[0] // HDIM)]
    lines = jnp.concatenate(lines, axis=0)
    tile = 4 * HDIM

    @pl.loop(0, send_ref.shape[1] // tile)
    def _(i):
        part = pl.ds(pl.multiple_of(i * tile, tile), tile)
        product = dot(lines, jnp.concatenate([g[:, part] for g in grads], axis=0), 1, 0)
        send_ref[:, part] = product[: width // 2].astype(bf16)
        keep_ref[:, part] = product[width // 2 :]


def weight_halves(meta, heads, grads):
    shape = (sum(x.shape[0] for x in heads) // 2, grads[0].shape[1])
    return whole(weight_kernel, [sds(shape, bf16), sds(shape, f32)], (meta, *heads, *grads), "weight_halves", 1, 6)


def add_kernel(keep_ref, recv_ref, *outs):
    size = outs[0].shape[0]
    for j, out_ref in enumerate(outs):
        part = slice(j * size, (j + 1) * size)
        out_ref[...] = (keep_ref[part, :] + recv_ref[part, :].astype(f32)).astype(out_ref.dtype)


def add_parts(keep, recv):
    shape = (keep.shape[0] // 4, keep.shape[1])
    return whole(add_kernel, [sds(shape, f32)] + [sds(shape, bf16)] * 3, (keep, recv), "add_parts")


def total_kernel(scale, own_ref, r1, r2, r3, out_ref):
    total = own_ref[...] + r1[...].astype(f32) + r2[...].astype(f32) + r3[...].astype(f32)
    out_ref[...] = (total * scale).astype(bf16)


def total_of(own, recvs, scale):
    return whole(functools.partial(total_kernel, scale), sds(own.shape, bf16), (own, *recvs), "scene_mean")


def join_weight_kernel(first, count, meta, *refs):
    parts, out_ref, sems = refs[:count], refs[-2], refs[-1]
    copies = []
    for p, ref in enumerate(parts, first):
        for h in range(ref.shape[0] // LINE):
            line = out_ref.at[line_at(meta, h, p // 4, p % 4), :]
            part = ref.at[pl.ds(h * LINE, LINE), :]
            copies.append(pltpu.make_async_copy(part, line, sems.at[len(copies)]))
    run_all(copies)


def join_weight(meta, parts, first=0, out=None):
    size, outw = parts[0].shape
    more = () if out is None else (out,)
    return pl.pallas_call(
        functools.partial(join_weight_kernel, first, len(parts)),
        out_shape=sds((8 * size, outw), bf16),
        in_specs=[pl.BlockSpec(memory_space=pltpu.SMEM)]
        + [pl.BlockSpec(memory_space=pltpu.VMEM)] * len(parts)
        + [pl.BlockSpec(memory_space=pl.ANY)] * len(more),
        out_specs=pl.BlockSpec(memory_space=pl.ANY),
        scratch_shapes=[pltpu.SemaphoreType.DMA((len(parts) * size // LINE,))],
        input_output_aliases={1 + len(parts): 0} if more else {},
        compiler_params=params(),
        cost_estimate=NO_COST,
        name="join_weight",
    )(meta, *parts, *more)


def join_kernel(meta, *refs):
    *pieces, sems = refs
    pieces, outs = pieces[:4], pieces[4:]
    width = pieces[0].shape[2]
    copies = []
    for k, ref in enumerate(pieces):
        start = pl.multiple_of((meta[Z] ^ k) * width, 128)
        for i, out_ref in enumerate(outs):
            copies.append(pltpu.make_async_copy(ref.at[i], out_ref.at[:, pl.ds(start, width)], sems.at[3 * k + i]))
    run_all(copies)


def join(meta, pieces):
    _, rows, width = pieces[0].shape
    return pl.pallas_call(
        join_kernel,
        out_shape=[sds((rows, 4 * width), bf16)] * 3,
        in_specs=[pl.BlockSpec(memory_space=pltpu.SMEM)] + [pl.BlockSpec(memory_space=pltpu.VMEM)] * 4,
        out_specs=[pl.BlockSpec(memory_space=pl.ANY)] * 3,
        scratch_shapes=[pltpu.SemaphoreType.DMA((12,))],
        compiler_params=params(),
        cost_estimate=NO_COST,
        name="join_heads",
    )(meta, *pieces)


def dense_body(queries, keys_in, values, out_grad, out_weight, voxel_count):
    meta = jnp.stack([lax.axis_index("shard"), voxel_count[0], lax.axis_index("core"), lax.axis_index("chips")])
    meta = meta.astype(jnp.int32)

    def send(x, k, *earlier):
        return swap(after(x, *earlier) if earlier else x, "shard", 4, k)

    across = send(out_grad, 2)
    beside = send(out_grad, 1)
    mine, own, near1, far2a, far2b, far3a, far3b = pack(meta, queries, keys_in, values, out_grad)
    piece1 = send(near1, 1)
    piece3a = send(far3a, 3, beside)
    piece2a = send(far2a, 2, across)
    piece3b = send(far3b, 3, piece3a)
    piece2b = send(far2b, 2, piece2a)
    half = across.shape[0] // 2
    grad_early = grad_attn(meta, (mine, beside, across), out_weight, 0)
    corners = [send(across[:half], 1), send(after(across, piece1, grad_early)[half:], 1)]

    *saved_a, heads_a = forward(meta, (own, piece1, piece2a, piece3a), 0)
    heads_a, piece2b, piece3b = lax.optimization_barrier((heads_a, piece2b, piece3b))
    *saved_b, heads_b = forward(meta, (own, piece1, piece2b, piece3b), 1)
    grad_early, heads_b, *corners = lax.optimization_barrier((grad_early, heads_b, *corners))
    grads = (mine, beside, across, *corners)

    out, keep = weight_halves(meta, (heads_a, heads_b), grads)
    recv = swap(out, "core", 2, 1)
    grad_late = grad_attn(meta, after(grads[3:], out), out_weight, 3 * BLOCK)
    pieces = (own, piece1, piece2a, piece3a, piece2b, piece3b)
    own0, *backs = backward(pieces, (grad_early, grad_late), (*saved_a, *saved_b))
    own_part, *sends = add_parts(after(keep, own0), recv)
    recvs = [swap(x, "chips", 4, j + 1) for j, x in enumerate(sends)]
    back1 = send(backs[0], 1)
    back2, back3 = send(backs[1], 2), send(backs[2], 3, recvs[0])
    done = total_of(after(own_part, back1), recvs, 1.0 / 8)
    near = [done] + [swap(done, "chips", 4, j) for j in (1, 2, 3)]
    weight = join_weight(meta, near)
    weight, *near, back2, back3 = lax.optimization_barrier((weight, *near, back2, back3))
    far = [swap(x, "core", 2, 1) for x in near]
    return (*join(meta, (own0, back1, back2, back3)), join_weight(meta, far, 4, weight))


def attend_listed(queries, keys_in, values, block_ids, live_count):
    row_count, width_all = queries.shape
    head_count = width_all // HDIM
    block_count = row_count // BLOCK
    score_scale = 1.0 / math.sqrt(HDIM)
    query_blk = queries.reshape(block_count, BLOCK, head_count, HDIM)
    key_blk = keys_in.reshape(block_count, BLOCK, head_count, HDIM)[block_ids].reshape(
        block_count, NB * BLOCK, head_count, HDIM
    )
    value_blk = values.reshape(block_count, BLOCK, head_count, HDIM)[block_ids].reshape(
        block_count, NB * BLOCK, head_count, HDIM
    )
    query_pos = jnp.arange(row_count, dtype=jnp.int32).reshape(block_count, BLOCK)
    key_pos = (
        block_ids[:, :, None] * BLOCK + jnp.arange(BLOCK, dtype=jnp.int32)[None, None, :]
    ).reshape(block_count, NB * BLOCK)
    allowed = (key_pos[:, None, :] < live_count) | (query_pos[:, :, None] >= live_count)
    scores = (
        jnp.einsum("bqhd,bkhd->bhqk", query_blk, key_blk, preferred_element_type=jnp.float32)
        * score_scale
    )
    scores = jnp.where(allowed[:, None], scores, -jnp.inf)
    peak = jnp.max(scores, axis=-1, keepdims=True)
    weights = jnp.exp(scores - peak)
    probs = weights / jnp.sum(weights, axis=-1, keepdims=True)
    return (query_blk, key_blk, value_blk, probs)


def listed_body(queries, keys_in, values, out_grad, out_weight, block_lists, voxel_count):
    local_rows = queries.shape[0]
    live_count = voxel_count[0]
    block_ids = block_lists[0]
    positions = lax.axis_index("shard") * local_rows + jnp.arange(local_rows, dtype=jnp.int32)
    grad_live = jnp.where((positions < live_count)[:, None], out_grad, jnp.zeros_like(out_grad))
    query_head, key_head, value_head = (
        lax.all_to_all(queries, "shard", split_axis=1, concat_axis=0, tiled=True),
        lax.all_to_all(keys_in, "shard", split_axis=1, concat_axis=0, tiled=True),
        lax.all_to_all(values, "shard", split_axis=1, concat_axis=0, tiled=True),
    )
    row_count, width_all = query_head.shape
    head_count = width_all // HDIM
    block_count = row_count // BLOCK
    score_scale = 1.0 / math.sqrt(HDIM)
    query_blk, key_blk, value_blk, probs = attend_listed(
        query_head, key_head, value_head, block_ids, live_count
    )
    prob_bf = probs.astype(jnp.bfloat16)
    heads_out = (
        jnp.einsum("bhqk,bkhd->bqhd", prob_bf, value_blk, preferred_element_type=jnp.float32)
        .reshape(row_count, width_all)
        .astype(jnp.bfloat16)
    )
    row_piece = lax.all_gather(grad_live, "shard", axis=0, tiled=True)
    acc_now = jnp.einsum("rw,ro->wo", heads_out, row_piece, preferred_element_type=jnp.float32)
    product = jnp.einsum("ro,wo->rw", row_piece, out_weight, preferred_element_type=jnp.float32)
    grad_o = product.astype(jnp.bfloat16).reshape(block_count, BLOCK, head_count, HDIM)
    grad_prob = jnp.einsum("bqhd,bkhd->bhqk", grad_o, value_blk, preferred_element_type=jnp.float32)
    row_delta = jnp.sum(probs * grad_prob, axis=-1, keepdims=True)
    dscore = (probs * (grad_prob - row_delta) * score_scale).astype(jnp.bfloat16)
    grad_query = (
        jnp.einsum("bhqk,bkhd->bqhd", dscore, key_blk, preferred_element_type=jnp.float32)
        .reshape(row_count, width_all)
        .astype(jnp.bfloat16)
    )
    onehot = (
        block_ids[:, :, None] == jnp.arange(block_count, dtype=jnp.int32)[None, None, :]
    ).astype(jnp.float32)
    key_parts = jnp.einsum(
        "bhqk,bqhd->bkhd", dscore, query_blk, preferred_element_type=jnp.float32
    ).reshape(block_count, NB, BLOCK, width_all)
    value_parts = jnp.einsum(
        "bhqk,bqhd->bkhd", prob_bf, grad_o, preferred_element_type=jnp.float32
    ).reshape(block_count, NB, BLOCK, width_all)
    grad_key = (
        jnp.einsum("bjc,bjrx->crx", onehot, key_parts, precision=lax.Precision.HIGHEST)
        .reshape(row_count, width_all)
        .astype(jnp.bfloat16)
    )
    grad_value = (
        jnp.einsum("bjc,bjrx->crx", onehot, value_parts, precision=lax.Precision.HIGHEST)
        .reshape(row_count, width_all)
        .astype(jnp.bfloat16)
    )
    query_back, key_back, value_back = (
        lax.all_to_all(grad_query, "shard", split_axis=0, concat_axis=1, tiled=True),
        lax.all_to_all(grad_key, "shard", split_axis=0, concat_axis=1, tiled=True),
        lax.all_to_all(grad_value, "shard", split_axis=0, concat_axis=1, tiled=True),
    )
    scene_total = lax.axis_size(DP)
    summed = lax.psum(acc_now, DP)
    grad_weight = (summed / scene_total).astype(jnp.bfloat16)
    return (query_back, key_back, value_back, grad_weight)


def body(queries, keys_in, values, out_grad, out_weight, block_lists, voxel_count):
    dense = block_lists.shape[1] == NB and queries.shape[0] == BLOCK
    if dense and lax.axis_size("shard") == 4 and lax.axis_size("chips") == 4:
        return dense_body(queries, keys_in, values, out_grad, out_weight, voxel_count)
    return listed_body(queries, keys_in, values, out_grad, out_weight, block_lists, voxel_count)


def solution(mesh):
    chips = mesh.shape["dp"] // 2
    mesh = jax.sharding.Mesh(mesh.devices.reshape(chips, 2, -1), ("chips", "core", "shard"))
    return jax.shard_map(
        body,
        mesh=mesh,
        in_specs=(
            P((*DP, "shard"), None),
            P((*DP, "shard"), None),
            P((*DP, "shard"), None),
            P((*DP, "shard"), None),
            P("shard", None),
            P(DP, None, None),
            P(DP),
        ),
        out_specs=(
            P((*DP, "shard"), None),
            P((*DP, "shard"), None),
            P((*DP, "shard"), None),
            P("shard", None),
        ),
        check_vma=False,
    )
```

```python
import functools
import math

import jax
import jax.numpy as jnp
from jax import lax
from jax.experimental import pallas as pl
from jax.experimental.pallas import tpu as pltpu
from jax.sharding import PartitionSpec as P

HDIM = 128
BLOCK = 128
NB = 4
MIB = 1024 * 1024
DP = ("chips", "core")

Z, COUNT, CORE, CHIP = range(4)

EARLY = 3

NO_COST = pl.CostEstimate(flops=0, bytes_accessed=1024, transcendentals=0)

f32 = jnp.float32
bf16 = jnp.bfloat16


def dot(a, b, ca, cb):
    return lax.dot_general(a, b, (((ca,), (cb,)), ((), ())), preferred_element_type=f32)


def sds(shape, dtype):
    return jax.ShapeDtypeStruct(shape, dtype)


def params(mib=2):
    return pltpu.CompilerParams(vmem_limit_bytes=mib * MIB)


def swap(x, axis, size, flip):
    return lax.ppermute(x, axis, [(i, i ^ flip) for i in range(size)])


def after(x, *earlier):
    return lax.optimization_barrier((x, *earlier))[0]


def run_all(copies):
    for copy in copies:
        copy.start()
    for copy in copies:
        copy.wait()


def whole(kernel, out_shape, operands, name, scalars=0, mib=2, scratch=()):
    return pl.pallas_call(
        kernel,
        out_shape=out_shape,
        in_specs=[pl.BlockSpec(memory_space=pltpu.SMEM)] * scalars
        + [pl.BlockSpec(memory_space=pltpu.VMEM)] * (len(operands) - scalars),
        out_specs=jax.tree.map(lambda _: pl.BlockSpec(memory_space=pltpu.VMEM), out_shape),
        scratch_shapes=scratch,
        compiler_params=params(mib),
        cost_estimate=NO_COST,
        name=name,
    )(*operands)


def pack_kernel(meta, q_ref, k_ref, v_ref, grad_ref, mine_ref, *refs):
    *outs, sems = refs
    width = outs[0].shape[2]
    copies = [pltpu.make_async_copy(grad_ref, mine_ref, sems.at[3 * len(outs)])]
    for n, out_ref in enumerate(outs):
        k, first = (n, 0) if n < 2 else (n // 2 + 1, n % 2 * EARLY * HDIM)
        start = pl.multiple_of((meta[Z] ^ k) * width + first, 128)
        for i, ref in enumerate((q_ref, k_ref, v_ref)):
            part = ref.at[:, pl.ds(start, out_ref.shape[2])]
            copies.append(pltpu.make_async_copy(part, out_ref.at[i], sems.at[3 * n + i]))
    run_all(copies)


def pack(meta, queries, keys_in, values, grad):
    rows, width = queries.shape
    part, early = width // 4, EARLY * HDIM
    shapes = [sds((3, rows, n), bf16) for n in (part, part, early, part - early, early, part - early)]
    shapes = [sds(grad.shape, bf16)] + shapes
    return pl.pallas_call(
        pack_kernel,
        out_shape=shapes,
        in_specs=[pl.BlockSpec(memory_space=pltpu.SMEM)] + [pl.BlockSpec(memory_space=pl.ANY)] * 4,
        out_specs=[pl.BlockSpec(memory_space=pltpu.VMEM)] * len(shapes),
        scratch_shapes=[pltpu.SemaphoreType.DMA((3 * len(shapes),))],
        compiler_params=params(),
        cost_estimate=NO_COST,
        name="pack_heads",
    )(meta, queries, keys_in, values, grad)


def token_pos(shape, dim, z, start=0):
    return (lax.broadcasted_iota(jnp.int32, shape, dim) + start) ^ (z * BLOCK)


def grad_attn_kernel(start, meta, *refs):
    *grads, w_ref, out_ref = refs
    grad = jnp.concatenate([g[...] for g in grads], axis=0)
    live = token_pos((grad.shape[0], 1), 0, meta[Z], start) < meta[COUNT]
    tile = 2 * HDIM

    @pl.loop(0, w_ref.shape[0] // tile)
    def _(i):
        part = pl.ds(pl.multiple_of(i * tile, tile), tile)
        out_ref[:, part] = jnp.where(live, dot(grad, w_ref[part, :], 1, 1), 0.0).astype(bf16)


def grad_attn(meta, grads, weight, start):
    shape = (sum(g.shape[0] for g in grads), weight.shape[0])
    kernel = functools.partial(grad_attn_kernel, start)
    return whole(kernel, sds(shape, bf16), (meta, *grads, weight), "grad_attn", 1, 6)


def head_of(pieces, group, h):
    part = pieces[-1].shape[2]
    parts = []
    for p in pieces:
        start = (group * EARLY * HDIM if p.shape[2] > part else 0) + h * HDIM
        parts.append([p[i, :, start : start + HDIM] for i in range(3)])
    return (jnp.concatenate(x, axis=0) for x in zip(*parts))


def forward_kernel(group, meta, p0, p1, p2, p3, weight_ref, inverse_ref, out_ref, heads_ref, bias_ref):
    pieces = (p0, p1, p2, p3)
    rows = p0.shape[1]
    total = 4 * rows
    tile = 2 * rows
    to_power = math.log2(math.e) / math.sqrt(HDIM)
    query_live = token_pos((1, total), 1, meta[Z]) < meta[COUNT]
    key_live = token_pos((total, 1), 0, meta[Z]) < meta[COUNT]
    bias_ref[...] = jnp.where(key_live | ~query_live, 0.0, -jnp.inf)
    for h in range(p3.shape[2] // HDIM):
        cols = slice(h * HDIM, (h + 1) * HDIM)
        query, key, value = head_of(pieces, group, h)
        for t in range(2):
            part = slice(t * tile, (t + 1) * tile)
            scores = dot(key, query[part], 1, 1) + bias_ref[:, part]
            peak = jnp.max(scores, axis=0, keepdims=True)
            weights = jnp.exp2((scores - peak) * to_power).astype(bf16)
            weight_ref[h, :, part] = weights
            inverse = 1.0 / jnp.sum(weights.astype(f32), axis=0, keepdims=True)
            inverse_ref[h, :, part] = inverse
            heads = dot(value, weights, 0, 0) * inverse
            out_ref[cols, part] = heads
            heads_ref[cols, part] = jnp.where(query_live[:, part], heads, 0.0).astype(bf16)


def forward(meta, pieces, group):
    _, rows, width = pieces[-1].shape
    total = 4 * rows
    shapes = [
        sds((width // HDIM, total, total), bf16),
        sds((width // HDIM, 1, total), f32),
        sds((width, total), f32),
        sds((width, total), bf16),
    ]
    scratch = [pltpu.VMEM((total, total), f32)]
    kernel = functools.partial(forward_kernel, group)
    return whole(kernel, shapes, (meta, *pieces), "attend_forward", 1, 8, scratch)


def backward_kernel(own, near, far2a, far3a, far2b, far3b, early_ref, late_ref, *refs):
    saved, backs = (refs[:3], refs[3:6]), refs[6:]
    rows = own.shape[1]
    total = 4 * rows
    tile = 2 * rows
    scale = 1.0 / math.sqrt(HDIM)
    for n in range(own.shape[2] // HDIM):
        group, h = divmod(n, EARLY)
        query, key, value = head_of(((own, near, far2a, far3a), (own, near, far2b, far3b))[group], group, h)
        weight_ref, inverse_ref, out_ref = saved[group]
        here = slice(h * HDIM, (h + 1) * HDIM)
        cols = slice(n * HDIM, (n + 1) * HDIM)
        grad = jnp.concatenate([early_ref[:, cols], late_ref[:, cols]], axis=0)
        grad_key = grad_value = jnp.zeros((total, HDIM), f32)
        for t in range(2):
            span = slice(t * tile, (t + 1) * tile)
            weights = weight_ref[h, :, span]
            inverse = inverse_ref[h, :, span]
            turned = grad[span].astype(f32).T
            row_delta = jnp.sum(out_ref[here, span] * turned, axis=0, keepdims=True)
            grad_prob = dot(value, grad[span], 1, 1)
            dscore = (weights.astype(f32) * ((grad_prob - row_delta) * (inverse * scale))).astype(bf16)
            grad_query = dot(key, dscore, 0, 0).T.astype(bf16)
            backs[2 * t][0, :, cols] = grad_query[:rows]
            backs[2 * t + 1][0, :, cols] = grad_query[rows:]
            grad_key += dot(dscore, query[span], 1, 0)
            grad_value += dot(weights, (turned * inverse).T.astype(bf16), 1, 0)
        for k in range(4):
            mine = slice(k * rows, (k + 1) * rows)
            backs[k][1, :, cols] = grad_key[mine].astype(bf16)
            backs[k][2, :, cols] = grad_value[mine].astype(bf16)


def backward(pieces, grads, saved):
    shapes = [sds(pieces[0].shape, bf16)] * 4
    return whole(backward_kernel, shapes, (*pieces, *grads, *saved), "attend_backward", 0, 8)


LINE = HDIM // 8


def line_at(meta, head, other, j):
    at = head * HDIM + ((meta[CORE] ^ other) * 4 + (meta[CHIP] ^ j)) * LINE
    return pl.ds(pl.multiple_of(at, LINE), LINE)


def weight_kernel(meta, heads_a, heads_b, *refs):
    *grads, send_ref, keep_ref = refs
    width = heads_a.shape[0] + heads_b.shape[0]
    lines = []
    for other in (1, 0):
        for j in range(4):
            for ref in (heads_a, heads_b):
                lines += [ref[line_at(meta, h, other, j), :] for h in range(ref.shape[0] // HDIM)]
    lines = jnp.concatenate(lines, axis=0)
    tile = 4 * HDIM

    @pl.loop(0, send_ref.shape[1] // tile)
    def _(i):
        part = pl.ds(pl.multiple_of(i * tile, tile), tile)
        product = dot(lines, jnp.concatenate([g[:, part] for g in grads], axis=0), 1, 0)
        send_ref[:, part] = product[: width // 2].astype(bf16)
        keep_ref[:, part] = product[width // 2 :]


def weight_halves(meta, heads, grads):
    shape = (sum(x.shape[0] for x in heads) // 2, grads[0].shape[1])
    return whole(weight_kernel, [sds(shape, bf16), sds(shape, f32)], (meta, *heads, *grads), "weight_halves", 1, 6)


def add_kernel(keep_ref, recv_ref, *outs):
    size = outs[0].shape[0]
    for j, out_ref in enumerate(outs):
        part = slice(j * size, (j + 1) * size)
        out_ref[...] = (keep_ref[part, :] + recv_ref[part, :].astype(f32)).astype(out_ref.dtype)


def add_parts(keep, recv):
    shape = (keep.shape[0] // 4, keep.shape[1])
    return whole(add_kernel, [sds(shape, f32)] + [sds(shape, bf16)] * 3, (keep, recv), "add_parts")


def total_kernel(scale, own_ref, r1, r2, r3, out_ref):
    total = own_ref[...] + r1[...].astype(f32) + r2[...].astype(f32) + r3[...].astype(f32)
    out_ref[...] = (total * scale).astype(bf16)


def total_of(own, recvs, scale):
    return whole(functools.partial(total_kernel, scale), sds(own.shape, bf16), (own, *recvs), "scene_mean")


def join_weight_kernel(first, count, meta, *refs):
    parts, out_ref, sems = refs[:count], refs[-2], refs[-1]
    copies = []
    for p, ref in enumerate(parts, first):
        for h in range(ref.shape[0] // LINE):
            line = out_ref.at[line_at(meta, h, p // 4, p % 4), :]
            part = ref.at[pl.ds(h * LINE, LINE), :]
            copies.append(pltpu.make_async_copy(part, line, sems.at[len(copies)]))
    run_all(copies)


def join_weight(meta, parts, first=0, out=None):
    size, outw = parts[0].shape
    more = () if out is None else (out,)
    return pl.pallas_call(
        functools.partial(join_weight_kernel, first, len(parts)),
        out_shape=sds((8 * size, outw), bf16),
        in_specs=[pl.BlockSpec(memory_space=pltpu.SMEM)]
        + [pl.BlockSpec(memory_space=pltpu.VMEM)] * len(parts)
        + [pl.BlockSpec(memory_space=pl.ANY)] * len(more),
        out_specs=pl.BlockSpec(memory_space=pl.ANY),
        scratch_shapes=[pltpu.SemaphoreType.DMA((len(parts) * size // LINE,))],
        input_output_aliases={1 + len(parts): 0} if more else {},
        compiler_params=params(),
        cost_estimate=NO_COST,
        name="join_weight",
    )(meta, *parts, *more)


def join_kernel(meta, *refs):
    *pieces, sems = refs
    pieces, outs = pieces[:4], pieces[4:]
    width = pieces[0].shape[2]
    copies = []
    for k, ref in enumerate(pieces):
        start = pl.multiple_of((meta[Z] ^ k) * width, 128)
        for i, out_ref in enumerate(outs):
            copies.append(pltpu.make_async_copy(ref.at[i], out_ref.at[:, pl.ds(start, width)], sems.at[3 * k + i]))
    run_all(copies)


def join(meta, pieces):
    _, rows, width = pieces[0].shape
    return pl.pallas_call(
        join_kernel,
        out_shape=[sds((rows, 4 * width), bf16)] * 3,
        in_specs=[pl.BlockSpec(memory_space=pltpu.SMEM)] + [pl.BlockSpec(memory_space=pltpu.VMEM)] * 4,
        out_specs=[pl.BlockSpec(memory_space=pl.ANY)] * 3,
        scratch_shapes=[pltpu.SemaphoreType.DMA((12,))],
        compiler_params=params(),
        cost_estimate=NO_COST,
        name="join_heads",
    )(meta, *pieces)


def dense_body(queries, keys_in, values, out_grad, out_weight, voxel_count):
    meta = jnp.stack([lax.axis_index("shard"), voxel_count[0], lax.axis_index("core"), lax.axis_index("chips")])
    meta = meta.astype(jnp.int32)

    def send(x, k, *earlier):
        return swap(after(x, *earlier) if earlier else x, "shard", 4, k)

    across = send(out_grad, 2)
    beside = send(out_grad, 1)
    mine, own, near1, far2a, far2b, far3a, far3b = pack(meta, queries, keys_in, values, out_grad)
    piece1 = send(near1, 1)
    piece3a = send(far3a, 3, beside)
    piece2a = send(far2a, 2, across)
    piece3b = send(far3b, 3, piece3a)
    piece2b = send(far2b, 2, piece2a)
    half = across.shape[0] // 2
    grad_early = grad_attn(meta, (mine, beside, across), out_weight, 0)
    corners = [send(across[:half], 1), send(after(across, piece1, grad_early)[half:], 1)]

    *saved_a, heads_a = forward(meta, (own, piece1, piece2a, piece3a), 0)
    heads_a, piece2b, piece3b = lax.optimization_barrier((heads_a, piece2b, piece3b))
    *saved_b, heads_b = forward(meta, (own, piece1, piece2b, piece3b), 1)
    grad_early, heads_b, *corners = lax.optimization_barrier((grad_early, heads_b, *corners))
    grads = (mine, beside, across, *corners)

    out, keep = weight_halves(meta, (heads_a, heads_b), grads)
    recv = swap(out, "core", 2, 1)
    grad_late = grad_attn(meta, after(grads[3:], out), out_weight, 3 * BLOCK)
    pieces = (own, piece1, piece2a, piece3a, piece2b, piece3b)
    own0, *backs = backward(pieces, (grad_early, grad_late), (*saved_a, *saved_b))
    own_part, *sends = add_parts(after(keep, own0), recv)
    recvs = [swap(x, "chips", 4, j + 1) for j, x in enumerate(sends)]
    back3, back2 = send(backs[2], 3), send(backs[1], 2)
    done = total_of(own_part, recvs, 1.0 / 8)
    near = [done] + [swap(done, "chips", 4, j) for j in (1, 2, 3)]
    back1 = send(backs[0], 1, near[1])
    weight = join_weight(meta, near)
    weight, *near, back2, back3 = lax.optimization_barrier((weight, *near, back2, back3))
    far = [swap(x, "core", 2, 1) for x in near]
    return (*join(meta, (own0, back1, back2, back3)), join_weight(meta, far, 4, weight))


def attend_listed(queries, keys_in, values, block_ids, live_count):
    row_count, width_all = queries.shape
    head_count = width_all // HDIM
    block_count = row_count // BLOCK
    score_scale = 1.0 / math.sqrt(HDIM)
    query_blk = queries.reshape(block_count, BLOCK, head_count, HDIM)
    key_blk = keys_in.reshape(block_count, BLOCK, head_count, HDIM)[block_ids].reshape(
        block_count, NB * BLOCK, head_count, HDIM
    )
    value_blk = values.reshape(block_count, BLOCK, head_count, HDIM)[block_ids].reshape(
        block_count, NB * BLOCK, head_count, HDIM
    )
    query_pos = jnp.arange(row_count, dtype=jnp.int32).reshape(block_count, BLOCK)
    key_pos = (
        block_ids[:, :, None] * BLOCK + jnp.arange(BLOCK, dtype=jnp.int32)[None, None, :]
    ).reshape(block_count, NB * BLOCK)
    allowed = (key_pos[:, None, :] < live_count) | (query_pos[:, :, None] >= live_count)
    scores = (
        jnp.einsum("bqhd,bkhd->bhqk", query_blk, key_blk, preferred_element_type=jnp.float32)
        * score_scale
    )
    scores = jnp.where(allowed[:, None], scores, -jnp.inf)
    peak = jnp.max(scores, axis=-1, keepdims=True)
    weights = jnp.exp(scores - peak)
    probs = weights / jnp.sum(weights, axis=-1, keepdims=True)
    return (query_blk, key_blk, value_blk, probs)


def listed_body(queries, keys_in, values, out_grad, out_weight, block_lists, voxel_count):
    local_rows = queries.shape[0]
    live_count = voxel_count[0]
    block_ids = block_lists[0]
    positions = lax.axis_index("shard") * local_rows + jnp.arange(local_rows, dtype=jnp.int32)
    grad_live = jnp.where((positions < live_count)[:, None], out_grad, jnp.zeros_like(out_grad))
    query_head, key_head, value_head = (
        lax.all_to_all(queries, "shard", split_axis=1, concat_axis=0, tiled=True),
        lax.all_to_all(keys_in, "shard", split_axis=1, concat_axis=0, tiled=True),
        lax.all_to_all(values, "shard", split_axis=1, concat_axis=0, tiled=True),
    )
    row_count, width_all = query_head.shape
    head_count = width_all // HDIM
    block_count = row_count // BLOCK
    score_scale = 1.0 / math.sqrt(HDIM)
    query_blk, key_blk, value_blk, probs = attend_listed(
        query_head, key_head, value_head, block_ids, live_count
    )
    prob_bf = probs.astype(jnp.bfloat16)
    heads_out = (
        jnp.einsum("bhqk,bkhd->bqhd", prob_bf, value_blk, preferred_element_type=jnp.float32)
        .reshape(row_count, width_all)
        .astype(jnp.bfloat16)
    )
    row_piece = lax.all_gather(grad_live, "shard", axis=0, tiled=True)
    acc_now = jnp.einsum("rw,ro->wo", heads_out, row_piece, preferred_element_type=jnp.float32)
    product = jnp.einsum("ro,wo->rw", row_piece, out_weight, preferred_element_type=jnp.float32)
    grad_o = product.astype(jnp.bfloat16).reshape(block_count, BLOCK, head_count, HDIM)
    grad_prob = jnp.einsum("bqhd,bkhd->bhqk", grad_o, value_blk, preferred_element_type=jnp.float32)
    row_delta = jnp.sum(probs * grad_prob, axis=-1, keepdims=True)
    dscore = (probs * (grad_prob - row_delta) * score_scale).astype(jnp.bfloat16)
    grad_query = (
        jnp.einsum("bhqk,bkhd->bqhd", dscore, key_blk, preferred_element_type=jnp.float32)
        .reshape(row_count, width_all)
        .astype(jnp.bfloat16)
    )
    onehot = (
        block_ids[:, :, None] == jnp.arange(block_count, dtype=jnp.int32)[None, None, :]
    ).astype(jnp.float32)
    key_parts = jnp.einsum(
        "bhqk,bqhd->bkhd", dscore, query_blk, preferred_element_type=jnp.float32
    ).reshape(block_count, NB, BLOCK, width_all)
    value_parts = jnp.einsum(
        "bhqk,bqhd->bkhd", prob_bf, grad_o, preferred_element_type=jnp.float32
    ).reshape(block_count, NB, BLOCK, width_all)
    grad_key = (
        jnp.einsum("bjc,bjrx->crx", onehot, key_parts, precision=lax.Precision.HIGHEST)
        .reshape(row_count, width_all)
        .astype(jnp.bfloat16)
    )
    grad_value = (
        jnp.einsum("bjc,bjrx->crx", onehot, value_parts, precision=lax.Precision.HIGHEST)
        .reshape(row_count, width_all)
        .astype(jnp.bfloat16)
    )
    query_back, key_back, value_back = (
        lax.all_to_all(grad_query, "shard", split_axis=0, concat_axis=1, tiled=True),
        lax.all_to_all(grad_key, "shard", split_axis=0, concat_axis=1, tiled=True),
        lax.all_to_all(grad_value, "shard", split_axis=0, concat_axis=1, tiled=True),
    )
    scene_total = lax.axis_size(DP)
    summed = lax.psum(acc_now, DP)
    grad_weight = (summed / scene_total).astype(jnp.bfloat16)
    return (query_back, key_back, value_back, grad_weight)


def body(queries, keys_in, values, out_grad, out_weight, block_lists, voxel_count):
    dense = block_lists.shape[1] == NB and queries.shape[0] == BLOCK
    if dense and lax.axis_size("shard") == 4 and lax.axis_size("chips") == 4:
        return dense_body(queries, keys_in, values, out_grad, out_weight, voxel_count)
    return listed_body(queries, keys_in, values, out_grad, out_weight, block_lists, voxel_count)


def solution(mesh):
    chips = mesh.shape["dp"] // 2
    mesh = jax.sharding.Mesh(mesh.devices.reshape(chips, 2, -1), ("chips", "core", "shard"))
    return jax.shard_map(
        body,
        mesh=mesh,
        in_specs=(
            P((*DP, "shard"), None),
            P((*DP, "shard"), None),
            P((*DP, "shard"), None),
            P((*DP, "shard"), None),
            P("shard", None),
            P(DP, None, None),
            P(DP),
        ),
        out_specs=(
            P((*DP, "shard"), None),
            P((*DP, "shard"), None),
            P((*DP, "shard"), None),
            P("shard", None),
        ),
        check_vma=False,
    )
```

```python
import functools
import math

import jax
import jax.numpy as jnp
from jax import lax
from jax.experimental import pallas as pl
from jax.experimental.pallas import tpu as pltpu
from jax.sharding import PartitionSpec as P

HDIM = 128
BLOCK = 128
NB = 4
MIB = 1024 * 1024
DP = ("chips", "core")

Z, COUNT, CORE, CHIP = range(4)

EARLY = 3

NO_COST = pl.CostEstimate(flops=0, bytes_accessed=1024, transcendentals=0)

f32 = jnp.float32
bf16 = jnp.bfloat16


def dot(a, b, ca, cb):
    return lax.dot_general(a, b, (((ca,), (cb,)), ((), ())), preferred_element_type=f32)


def sds(shape, dtype):
    return jax.ShapeDtypeStruct(shape, dtype)


def params(mib=2):
    return pltpu.CompilerParams(vmem_limit_bytes=mib * MIB)


def swap(x, axis, size, flip):
    return lax.ppermute(x, axis, [(i, i ^ flip) for i in range(size)])


def after(x, *earlier):
    return lax.optimization_barrier((x, *earlier))[0]


def run_all(copies):
    for copy in copies:
        copy.start()
    for copy in copies:
        copy.wait()


def whole(kernel, out_shape, operands, name, scalars=0, mib=2, scratch=()):
    return pl.pallas_call(
        kernel,
        out_shape=out_shape,
        in_specs=[pl.BlockSpec(memory_space=pltpu.SMEM)] * scalars
        + [pl.BlockSpec(memory_space=pltpu.VMEM)] * (len(operands) - scalars),
        out_specs=jax.tree.map(lambda _: pl.BlockSpec(memory_space=pltpu.VMEM), out_shape),
        scratch_shapes=scratch,
        compiler_params=params(mib),
        cost_estimate=NO_COST,
        name=name,
    )(*operands)


def pack_kernel(meta, q_ref, k_ref, v_ref, grad_ref, mine_ref, *refs):
    *outs, sems = refs
    width = outs[0].shape[2]
    copies = [pltpu.make_async_copy(grad_ref, mine_ref, sems.at[3 * len(outs)])]
    for n, out_ref in enumerate(outs):
        k, first = (n, 0) if n < 2 else (n // 2 + 1, n % 2 * EARLY * HDIM)
        start = pl.multiple_of((meta[Z] ^ k) * width + first, 128)
        for i, ref in enumerate((q_ref, k_ref, v_ref)):
            part = ref.at[:, pl.ds(start, out_ref.shape[2])]
            copies.append(pltpu.make_async_copy(part, out_ref.at[i], sems.at[3 * n + i]))
    run_all(copies)


def pack(meta, queries, keys_in, values, grad):
    rows, width = queries.shape
    part, early = width // 4, EARLY * HDIM
    shapes = [sds((3, rows, n), bf16) for n in (part, part, early, part - early, early, part - early)]
    shapes = [sds(grad.shape, bf16)] + shapes
    return pl.pallas_call(
        pack_kernel,
        out_shape=shapes,
        in_specs=[pl.BlockSpec(memory_space=pltpu.SMEM)] + [pl.BlockSpec(memory_space=pl.ANY)] * 4,
        out_specs=[pl.BlockSpec(memory_space=pltpu.VMEM)] * len(shapes),
        scratch_shapes=[pltpu.SemaphoreType.DMA((3 * len(shapes),))],
        compiler_params=params(),
        cost_estimate=NO_COST,
        name="pack_heads",
    )(meta, queries, keys_in, values, grad)


def token_pos(shape, dim, z, start=0):
    return (lax.broadcasted_iota(jnp.int32, shape, dim) + start) ^ (z * BLOCK)


def grad_attn_kernel(start, meta, *refs):
    *grads, w_ref, out_ref = refs
    grad = jnp.concatenate([g[...] for g in grads], axis=0)
    live = token_pos((grad.shape[0], 1), 0, meta[Z], start) < meta[COUNT]
    tile = 2 * HDIM

    @pl.loop(0, w_ref.shape[0] // tile)
    def _(i):
        part = pl.ds(pl.multiple_of(i * tile, tile), tile)
        out_ref[:, part] = jnp.where(live, dot(grad, w_ref[part, :], 1, 1), 0.0).astype(bf16)


def grad_attn(meta, grads, weight, start):
    shape = (sum(g.shape[0] for g in grads), weight.shape[0])
    kernel = functools.partial(grad_attn_kernel, start)
    return whole(kernel, sds(shape, bf16), (meta, *grads, weight), "grad_attn", 1, 6)


def head_of(pieces, group, h):
    part = pieces[-1].shape[2]
    parts = []
    for p in pieces:
        start = (group * EARLY * HDIM if p.shape[2] > part else 0) + h * HDIM
        parts.append([p[i, :, start : start + HDIM] for i in range(3)])
    return (jnp.concatenate(x, axis=0) for x in zip(*parts))


def forward_kernel(group, meta, p0, p1, p2, p3, weight_ref, inverse_ref, out_ref, heads_ref, bias_ref):
    pieces = (p0, p1, p2, p3)
    rows = p0.shape[1]
    total = 4 * rows
    tile = 2 * rows
    to_power = math.log2(math.e) / math.sqrt(HDIM)
    query_live = token_pos((1, total), 1, meta[Z]) < meta[COUNT]
    key_live = token_pos((total, 1), 0, meta[Z]) < meta[COUNT]
    bias_ref[...] = jnp.where(key_live | ~query_live, 0.0, -jnp.inf)
    for h in range(p3.shape[2] // HDIM):
        cols = slice(h * HDIM, (h + 1) * HDIM)
        query, key, value = head_of(pieces, group, h)
        for t in range(2):
            part = slice(t * tile, (t + 1) * tile)
            scores = dot(key, query[part], 1, 1) + bias_ref[:, part]
            peak = jnp.max(scores, axis=0, keepdims=True)
            weights = jnp.exp2((scores - peak) * to_power).astype(bf16)
            weight_ref[h, :, part] = weights
            inverse = 1.0 / jnp.sum(weights.astype(f32), axis=0, keepdims=True)
            inverse_ref[h, :, part] = inverse
            heads = dot(value, weights, 0, 0) * inverse
            out_ref[cols, part] = heads
            heads_ref[cols, part] = jnp.where(query_live[:, part], heads, 0.0).astype(bf16)


def forward(meta, pieces, group):
    _, rows, width = pieces[-1].shape
    total = 4 * rows
    shapes = [
        sds((width // HDIM, total, total), bf16),
        sds((width // HDIM, 1, total), f32),
        sds((width, total), f32),
        sds((width, total), bf16),
    ]
    scratch = [pltpu.VMEM((total, total), f32)]
    kernel = functools.partial(forward_kernel, group)
    return whole(kernel, shapes, (meta, *pieces), "attend_forward", 1, 8, scratch)


def span_gradients(query, key, value, grad, weights, inverse, outs):
    turned = grad.astype(f32).T
    row_delta = jnp.sum(outs * turned, axis=0, keepdims=True)
    grad_prob = dot(value, grad, 1, 1)
    factor = inverse * (1.0 / math.sqrt(HDIM))
    dscore = (weights.astype(f32) * ((grad_prob - row_delta) * factor)).astype(bf16)
    grad_query = dot(key, dscore, 0, 0).T.astype(bf16)
    grad_value = dot(weights, (turned * inverse).T.astype(bf16), 1, 0)
    return grad_query, dot(dscore, query, 1, 0), grad_value


def backward_early_kernel(*refs):
    pieces, (grad_ref, weight_ref, inverse_ref, out_ref, query_out, key_out, value_out) = refs[:4], refs[4:]
    early = grad_ref.shape[0]
    for h in range(pieces[-1].shape[2] // HDIM):
        cols = slice(h * HDIM, (h + 1) * HDIM)
        query, key, value = head_of(pieces, 0, h)
        grad_key = grad_value = 0.0
        for span in (slice(0, 2 * BLOCK), slice(2 * BLOCK, early)):
            grad_query, add_key, add_value = span_gradients(
                query[span], key, value, grad_ref[span, cols],
                weight_ref[h, :, span], inverse_ref[h, :, span], out_ref[cols, span],
            )
            query_out[span, cols] = grad_query
            grad_key += add_key
            grad_value += add_value
        key_out[:, cols] = grad_key
        value_out[:, cols] = grad_value


def backward_early(pieces, grad, saved):
    _, rows, part = pieces[-1].shape
    shapes = [sds((grad.shape[0], part), bf16), sds((4 * rows, part), f32), sds((4 * rows, part), f32)]
    return whole(backward_early_kernel, shapes, (*pieces, grad, *saved), "backward_early", 0, 8)


def backward_kernel(own, near, far2a, far3a, far2b, far3b, early_ref, late_ref, *refs):
    saved, done, backs = (refs[:3], refs[3:6]), refs[6:9], refs[9:]
    rows = own.shape[1]
    early, total = early_ref.shape[0], 4 * rows
    for n in range(own.shape[2] // HDIM):
        group, h = divmod(n, EARLY)
        query, key, value = head_of(((own, near, far2a, far3a), (own, near, far2b, far3b))[group], group, h)
        weight_ref, inverse_ref, out_ref = saved[group]
        here = slice(h * HDIM, (h + 1) * HDIM)
        cols = slice(n * HDIM, (n + 1) * HDIM)
        if group == 0:
            spans = ((slice(early, total), late_ref[:, cols]),)
            grad_key, grad_value = done[1][:, here], done[2][:, here]
            for k in range(early // rows):
                backs[k][0, :, cols] = done[0][k * rows : (k + 1) * rows, here]
        else:
            grad = jnp.concatenate([early_ref[:, cols], late_ref[:, cols]], axis=0)
            spans = [(slice(t, t + 2 * rows), grad[t : t + 2 * rows]) for t in (0, 2 * rows)]
            grad_key = grad_value = 0.0
        for span, grad in spans:
            grad_query, add_key, add_value = span_gradients(
                query[span], key, value, grad, weight_ref[h, :, span], inverse_ref[h, :, span], out_ref[here, span]
            )
            for k in range(span.start // rows, span.stop // rows):
                at = k * rows - span.start
                backs[k][0, :, cols] = grad_query[at : at + rows]
            grad_key += add_key
            grad_value += add_value
        for k in range(4):
            mine = slice(k * rows, (k + 1) * rows)
            backs[k][1, :, cols] = grad_key[mine].astype(bf16)
            backs[k][2, :, cols] = grad_value[mine].astype(bf16)


def backward(pieces, grads, saved, done):
    shapes = [sds(pieces[0].shape, bf16)] * 4
    return whole(backward_kernel, shapes, (*pieces, *grads, *saved, *done), "attend_backward", 0, 8)


LINE = HDIM // 8


def line_at(meta, head, other, j):
    at = head * HDIM + ((meta[CORE] ^ other) * 4 + (meta[CHIP] ^ j)) * LINE
    return pl.ds(pl.multiple_of(at, LINE), LINE)


def weight_kernel(meta, heads_a, heads_b, *refs):
    *grads, send_ref, keep_ref = refs
    width = heads_a.shape[0] + heads_b.shape[0]
    lines = []
    for other in (1, 0):
        for j in range(4):
            for ref in (heads_a, heads_b):
                lines += [ref[line_at(meta, h, other, j), :] for h in range(ref.shape[0] // HDIM)]
    lines = jnp.concatenate(lines, axis=0)
    tile = 4 * HDIM

    @pl.loop(0, send_ref.shape[1] // tile)
    def _(i):
        part = pl.ds(pl.multiple_of(i * tile, tile), tile)
        product = dot(lines, jnp.concatenate([g[:, part] for g in grads], axis=0), 1, 0)
        send_ref[:, part] = product[: width // 2].astype(bf16)
        keep_ref[:, part] = product[width // 2 :]


def weight_halves(meta, heads, grads):
    shape = (sum(x.shape[0] for x in heads) // 2, grads[0].shape[1])
    return whole(weight_kernel, [sds(shape, bf16), sds(shape, f32)], (meta, *heads, *grads), "weight_halves", 1, 6)


def add_kernel(keep_ref, recv_ref, *outs):
    size = outs[0].shape[0]
    for j, out_ref in enumerate(outs):
        part = slice(j * size, (j + 1) * size)
        out_ref[...] = (keep_ref[part, :] + recv_ref[part, :].astype(f32)).astype(out_ref.dtype)


def add_parts(keep, recv):
    shape = (keep.shape[0] // 4, keep.shape[1])
    return whole(add_kernel, [sds(shape, f32)] + [sds(shape, bf16)] * 3, (keep, recv), "add_parts")


def total_kernel(scale, own_ref, r1, r2, r3, out_ref):
    total = own_ref[...] + r1[...].astype(f32) + r2[...].astype(f32) + r3[...].astype(f32)
    out_ref[...] = (total * scale).astype(bf16)


def total_of(own, recvs, scale):
    return whole(functools.partial(total_kernel, scale), sds(own.shape, bf16), (own, *recvs), "scene_mean")


def weight_copies(meta, parts, first, out_ref, sems):
    copies = []
    for p, ref in enumerate(parts, first):
        for h in range(ref.shape[0] // LINE):
            line = out_ref.at[line_at(meta, h, p // 4, p % 4), :]
            copies.append(pltpu.make_async_copy(ref.at[pl.ds(h * LINE, LINE), :], line, sems.at[len(copies)]))
    return copies


def head_copies(meta, pieces, outs, sems):
    copies = []
    for k, ref in pieces.items():
        width = ref.shape[2]
        start = pl.multiple_of((meta[Z] ^ k) * width, 128)
        for i, out_ref in enumerate(outs):
            part = out_ref.at[:, pl.ds(start, width)]
            copies.append(pltpu.make_async_copy(ref.at[i], part, sems.at[len(copies)]))
    return copies


def join(kernel, meta, parts, shapes, copies, name, outs=()):
    return pl.pallas_call(
        kernel,
        out_shape=shapes,
        in_specs=[pl.BlockSpec(memory_space=pltpu.SMEM)]
        + [pl.BlockSpec(memory_space=pltpu.VMEM)] * len(parts)
        + [pl.BlockSpec(memory_space=pl.ANY)] * len(outs),
        out_specs=[pl.BlockSpec(memory_space=pl.ANY)] * len(shapes),
        scratch_shapes=[pltpu.SemaphoreType.DMA((n,)) for n in copies],
        input_output_aliases={1 + len(parts) + i: i for i in range(len(outs))},
        compiler_params=params(),
        cost_estimate=NO_COST,
        name=name,
    )(meta, *parts, *outs)


def join_weight_kernel(meta, *refs):
    run_all(weight_copies(meta, refs[:4], 0, refs[4], refs[5]))


def join_weight(meta, near):
    size, outw = near[0].shape
    return join(join_weight_kernel, meta, near, [sds((8 * size, outw), bf16)], [4 * size // LINE], "join_weight")[0]


def join_heads_kernel(meta, own, back2, back3, *refs):
    run_all(head_copies(meta, {0: own, 2: back2, 3: back3}, refs[:3], refs[3]))


def join_heads(meta, own, back2, back3):
    _, rows, width = own.shape
    shapes = [sds((rows, 4 * width), bf16)] * 3
    return join(join_heads_kernel, meta, (own, back2, back3), shapes, [9], "join_heads")


def join_last_kernel(meta, *refs):
    far, back1, outs, sems = refs[:4], refs[4], refs[9:13], refs[13:]
    run_all(weight_copies(meta, far, 4, outs[3], sems[0]) + head_copies(meta, {1: back1}, outs[:3], sems[1]))


def join_last(meta, far, back1, outs):
    shapes = [sds(x.shape, x.dtype) for x in outs]
    return join(join_last_kernel, meta, (*far, back1), shapes, [4 * far[0].shape[0] // LINE, 3], "join_last", outs)


def dense_body(queries, keys_in, values, out_grad, out_weight, voxel_count):
    meta = jnp.stack([lax.axis_index("shard"), voxel_count[0], lax.axis_index("core"), lax.axis_index("chips")])
    meta = meta.astype(jnp.int32)

    def send(x, k, *earlier):
        return swap(after(x, *earlier) if earlier else x, "shard", 4, k)

    across = send(out_grad, 2)
    beside = send(out_grad, 1)
    mine, own, near1, far2a, far2b, far3a, far3b = pack(meta, queries, keys_in, values, out_grad)
    piece1 = send(near1, 1)
    piece3a = send(far3a, 3, beside)
    piece2a = send(far2a, 2, across)
    piece3b = send(far3b, 3, piece3a)
    piece2b = send(far2b, 2, piece2a)
    half = across.shape[0] // 2
    grad_early = grad_attn(meta, (mine, beside, across), out_weight, 0)
    corners = [send(across[:half], 1), send(after(across, piece1, grad_early)[half:], 1)]

    *saved_a, heads_a = forward(meta, (own, piece1, piece2a, piece3a), 0)
    early = backward_early((own, piece1, piece2a, piece3a), grad_early, saved_a)
    heads_a, *early, piece2b, piece3b = lax.optimization_barrier((heads_a, *early, piece2b, piece3b))
    *saved_b, heads_b = forward(meta, (own, piece1, piece2b, piece3b), 1)
    grad_early, heads_b, *corners = lax.optimization_barrier((grad_early, heads_b, *corners))
    grads = (mine, beside, across, *corners)

    out, keep = weight_halves(meta, (heads_a, heads_b), grads)
    recv = swap(out, "core", 2, 1)
    grad_late = grad_attn(meta, after(grads[3:], out), out_weight, 3 * BLOCK)
    pieces = (own, piece1, piece2a, piece3a, piece2b, piece3b)
    own0, *backs = backward(pieces, (grad_early, grad_late), (*saved_a, *saved_b), early)
    own_part, *sends = add_parts(after(keep, own0), recv)
    recvs = [swap(x, "chips", 4, j + 1) for j, x in enumerate(sends)]
    back3, back2 = send(backs[2], 3), send(backs[1], 2)
    done = total_of(own_part, recvs, 1.0 / 8)
    near = [done] + [swap(done, "chips", 4, j) for j in (1, 2, 3)]
    back1 = send(backs[0], 1, near[1])
    weight = join_weight(meta, near)
    weight, *near, back2, back3 = lax.optimization_barrier((weight, *near, back2, back3))
    far = [swap(x, "core", 2, 1) for x in near]
    heads = join_heads(meta, own0, back2, back3)
    return tuple(join_last(meta, far, back1, (*heads, weight)))


def attend_listed(queries, keys_in, values, block_ids, live_count):
    row_count, width_all = queries.shape
    head_count = width_all // HDIM
    block_count = row_count // BLOCK
    score_scale = 1.0 / math.sqrt(HDIM)
    query_blk = queries.reshape(block_count, BLOCK, head_count, HDIM)
    key_blk = keys_in.reshape(block_count, BLOCK, head_count, HDIM)[block_ids].reshape(
        block_count, NB * BLOCK, head_count, HDIM
    )
    value_blk = values.reshape(block_count, BLOCK, head_count, HDIM)[block_ids].reshape(
        block_count, NB * BLOCK, head_count, HDIM
    )
    query_pos = jnp.arange(row_count, dtype=jnp.int32).reshape(block_count, BLOCK)
    key_pos = (
        block_ids[:, :, None] * BLOCK + jnp.arange(BLOCK, dtype=jnp.int32)[None, None, :]
    ).reshape(block_count, NB * BLOCK)
    allowed = (key_pos[:, None, :] < live_count) | (query_pos[:, :, None] >= live_count)
    scores = (
        jnp.einsum("bqhd,bkhd->bhqk", query_blk, key_blk, preferred_element_type=jnp.float32)
        * score_scale
    )
    scores = jnp.where(allowed[:, None], scores, -jnp.inf)
    peak = jnp.max(scores, axis=-1, keepdims=True)
    weights = jnp.exp(scores - peak)
    probs = weights / jnp.sum(weights, axis=-1, keepdims=True)
    return (query_blk, key_blk, value_blk, probs)


def listed_body(queries, keys_in, values, out_grad, out_weight, block_lists, voxel_count):
    local_rows = queries.shape[0]
    live_count = voxel_count[0]
    block_ids = block_lists[0]
    positions = lax.axis_index("shard") * local_rows + jnp.arange(local_rows, dtype=jnp.int32)
    grad_live = jnp.where((positions < live_count)[:, None], out_grad, jnp.zeros_like(out_grad))
    query_head, key_head, value_head = (
        lax.all_to_all(queries, "shard", split_axis=1, concat_axis=0, tiled=True),
        lax.all_to_all(keys_in, "shard", split_axis=1, concat_axis=0, tiled=True),
        lax.all_to_all(values, "shard", split_axis=1, concat_axis=0, tiled=True),
    )
    row_count, width_all = query_head.shape
    head_count = width_all // HDIM
    block_count = row_count // BLOCK
    score_scale = 1.0 / math.sqrt(HDIM)
    query_blk, key_blk, value_blk, probs = attend_listed(
        query_head, key_head, value_head, block_ids, live_count
    )
    prob_bf = probs.astype(jnp.bfloat16)
    heads_out = (
        jnp.einsum("bhqk,bkhd->bqhd", prob_bf, value_blk, preferred_element_type=jnp.float32)
        .reshape(row_count, width_all)
        .astype(jnp.bfloat16)
    )
    row_piece = lax.all_gather(grad_live, "shard", axis=0, tiled=True)
    acc_now = jnp.einsum("rw,ro->wo", heads_out, row_piece, preferred_element_type=jnp.float32)
    product = jnp.einsum("ro,wo->rw", row_piece, out_weight, preferred_element_type=jnp.float32)
    grad_o = product.astype(jnp.bfloat16).reshape(block_count, BLOCK, head_count, HDIM)
    grad_prob = jnp.einsum("bqhd,bkhd->bhqk", grad_o, value_blk, preferred_element_type=jnp.float32)
    row_delta = jnp.sum(probs * grad_prob, axis=-1, keepdims=True)
    dscore = (probs * (grad_prob - row_delta) * score_scale).astype(jnp.bfloat16)
    grad_query = (
        jnp.einsum("bhqk,bkhd->bqhd", dscore, key_blk, preferred_element_type=jnp.float32)
        .reshape(row_count, width_all)
        .astype(jnp.bfloat16)
    )
    onehot = (
        block_ids[:, :, None] == jnp.arange(block_count, dtype=jnp.int32)[None, None, :]
    ).astype(jnp.float32)
    key_parts = jnp.einsum(
        "bhqk,bqhd->bkhd", dscore, query_blk, preferred_element_type=jnp.float32
    ).reshape(block_count, NB, BLOCK, width_all)
    value_parts = jnp.einsum(
        "bhqk,bqhd->bkhd", prob_bf, grad_o, preferred_element_type=jnp.float32
    ).reshape(block_count, NB, BLOCK, width_all)
    grad_key = (
        jnp.einsum("bjc,bjrx->crx", onehot, key_parts, precision=lax.Precision.HIGHEST)
        .reshape(row_count, width_all)
        .astype(jnp.bfloat16)
    )
    grad_value = (
        jnp.einsum("bjc,bjrx->crx", onehot, value_parts, precision=lax.Precision.HIGHEST)
        .reshape(row_count, width_all)
        .astype(jnp.bfloat16)
    )
    query_back, key_back, value_back = (
        lax.all_to_all(grad_query, "shard", split_axis=0, concat_axis=1, tiled=True),
        lax.all_to_all(grad_key, "shard", split_axis=0, concat_axis=1, tiled=True),
        lax.all_to_all(grad_value, "shard", split_axis=0, concat_axis=1, tiled=True),
    )
    scene_total = lax.axis_size(DP)
    summed = lax.psum(acc_now, DP)
    grad_weight = (summed / scene_total).astype(jnp.bfloat16)
    return (query_back, key_back, value_back, grad_weight)


def body(queries, keys_in, values, out_grad, out_weight, block_lists, voxel_count):
    dense = block_lists.shape[1] == NB and queries.shape[0] == BLOCK
    if dense and lax.axis_size("shard") == 4 and lax.axis_size("chips") == 4:
        return dense_body(queries, keys_in, values, out_grad, out_weight, voxel_count)
    return listed_body(queries, keys_in, values, out_grad, out_weight, block_lists, voxel_count)


def solution(mesh):
    chips = mesh.shape["dp"] // 2
    mesh = jax.sharding.Mesh(mesh.devices.reshape(chips, 2, -1), ("chips", "core", "shard"))
    return jax.shard_map(
        body,
        mesh=mesh,
        in_specs=(
            P((*DP, "shard"), None),
            P((*DP, "shard"), None),
            P((*DP, "shard"), None),
            P((*DP, "shard"), None),
            P("shard", None),
            P(DP, None, None),
            P(DP),
        ),
        out_specs=(
            P((*DP, "shard"), None),
            P((*DP, "shard"), None),
            P((*DP, "shard"), None),
            P("shard", None),
        ),
        check_vma=False,
    )
```

```python
import functools
import math

import jax
import jax.numpy as jnp
from jax import lax
from jax.experimental import pallas as pl
from jax.experimental.pallas import tpu as pltpu
from jax.sharding import PartitionSpec as P

HDIM = 128
BLOCK = 128
NB = 4
MIB = 1024 * 1024
DP = ("chips", "core")

Z, COUNT, CORE, CHIP = range(4)

EARLY = 3

NO_COST = pl.CostEstimate(flops=0, bytes_accessed=1024, transcendentals=0)

f32 = jnp.float32
bf16 = jnp.bfloat16


def dot(a, b, ca, cb):
    return lax.dot_general(a, b, (((ca,), (cb,)), ((), ())), preferred_element_type=f32)


def sds(shape, dtype):
    return jax.ShapeDtypeStruct(shape, dtype)


def params(mib=2):
    return pltpu.CompilerParams(vmem_limit_bytes=mib * MIB)


def swap(x, axis, size, flip):
    return lax.ppermute(x, axis, [(i, i ^ flip) for i in range(size)])


def after(x, *earlier):
    return lax.optimization_barrier((x, *earlier))[0]


def run_all(copies):
    for copy in copies:
        copy.start()
    for copy in copies:
        copy.wait()


def whole(kernel, out_shape, operands, name, scalars=0, mib=2, scratch=()):
    return pl.pallas_call(
        kernel,
        out_shape=out_shape,
        in_specs=[pl.BlockSpec(memory_space=pltpu.SMEM)] * scalars
        + [pl.BlockSpec(memory_space=pltpu.VMEM)] * (len(operands) - scalars),
        out_specs=jax.tree.map(lambda _: pl.BlockSpec(memory_space=pltpu.VMEM), out_shape),
        scratch_shapes=scratch,
        compiler_params=params(mib),
        cost_estimate=NO_COST,
        name=name,
    )(*operands)


def pack_kernel(meta, q_ref, k_ref, v_ref, grad_ref, mine_ref, *refs):
    *outs, sems = refs
    width = outs[0].shape[2]
    copies = [pltpu.make_async_copy(grad_ref, mine_ref, sems.at[3 * len(outs)])]
    for n, out_ref in enumerate(outs):
        k, first = (n, 0) if n < 2 else (n // 2 + 1, n % 2 * EARLY * HDIM)
        start = pl.multiple_of((meta[Z] ^ k) * width + first, 128)
        for i, ref in enumerate((q_ref, k_ref, v_ref)):
            part = ref.at[:, pl.ds(start, out_ref.shape[2])]
            copies.append(pltpu.make_async_copy(part, out_ref.at[i], sems.at[3 * n + i]))
    run_all(copies)


def pack(meta, queries, keys_in, values, grad):
    rows, width = queries.shape
    part, early = width // 4, EARLY * HDIM
    shapes = [sds((3, rows, n), bf16) for n in (part, part, early, part - early, early, part - early)]
    shapes = [sds(grad.shape, bf16)] + shapes
    return pl.pallas_call(
        pack_kernel,
        out_shape=shapes,
        in_specs=[pl.BlockSpec(memory_space=pltpu.SMEM)] + [pl.BlockSpec(memory_space=pl.ANY)] * 4,
        out_specs=[pl.BlockSpec(memory_space=pltpu.VMEM)] * len(shapes),
        scratch_shapes=[pltpu.SemaphoreType.DMA((3 * len(shapes),))],
        compiler_params=params(),
        cost_estimate=NO_COST,
        name="pack_heads",
    )(meta, queries, keys_in, values, grad)


def token_pos(shape, dim, z, start=0):
    return (lax.broadcasted_iota(jnp.int32, shape, dim) + start) ^ (z * BLOCK)


def grad_attn_kernel(start, meta, *refs):
    *grads, w_ref, out_ref = refs
    grad = jnp.concatenate([g[...] for g in grads], axis=0)
    live = token_pos((grad.shape[0], 1), 0, meta[Z], start) < meta[COUNT]
    tile = 2 * HDIM

    @pl.loop(0, w_ref.shape[0] // tile)
    def _(i):
        part = pl.ds(pl.multiple_of(i * tile, tile), tile)
        out_ref[:, part] = jnp.where(live, dot(grad, w_ref[part, :], 1, 1), 0.0).astype(bf16)


def grad_attn(meta, grads, weight, start):
    shape = (sum(g.shape[0] for g in grads), weight.shape[0])
    kernel = functools.partial(grad_attn_kernel, start)
    return whole(kernel, sds(shape, bf16), (meta, *grads, weight), "grad_attn", 1, 6)


def head_of(pieces, group, h):
    part = pieces[-1].shape[2]
    parts = []
    for p in pieces:
        start = (group * EARLY * HDIM if p.shape[2] > part else 0) + h * HDIM
        parts.append([p[i, :, start : start + HDIM] for i in range(3)])
    return (jnp.concatenate(x, axis=0) for x in zip(*parts))


def forward_kernel(group, meta, p0, p1, p2, p3, weight_ref, inverse_ref, out_ref, heads_ref, bias_ref):
    pieces = (p0, p1, p2, p3)
    rows = p0.shape[1]
    total = 4 * rows
    tile = 2 * rows
    to_power = math.log2(math.e) / math.sqrt(HDIM)
    query_live = token_pos((1, total), 1, meta[Z]) < meta[COUNT]
    key_live = token_pos((total, 1), 0, meta[Z]) < meta[COUNT]
    bias_ref[...] = jnp.where(key_live | ~query_live, 0.0, -jnp.inf)
    for h in range(p3.shape[2] // HDIM):
        cols = slice(h * HDIM, (h + 1) * HDIM)
        query, key, value = head_of(pieces, group, h)
        for t in range(2):
            part = slice(t * tile, (t + 1) * tile)
            scores = dot(key, query[part], 1, 1) + bias_ref[:, part]
            peak = jnp.max(scores, axis=0, keepdims=True)
            weights = jnp.exp2((scores - peak) * to_power).astype(bf16)
            weight_ref[h, :, part] = weights
            inverse = 1.0 / jnp.sum(weights.astype(f32), axis=0, keepdims=True)
            inverse_ref[h, :, part] = inverse
            heads = dot(value, weights, 0, 0) * inverse
            out_ref[cols, part] = heads
            heads_ref[cols, part] = jnp.where(query_live[:, part], heads, 0.0).astype(bf16)


def forward(meta, pieces, group):
    _, rows, width = pieces[-1].shape
    total = 4 * rows
    shapes = [
        sds((width // HDIM, total, total), bf16),
        sds((width // HDIM, 1, total), f32),
        sds((width, total), f32),
        sds((width, total), bf16),
    ]
    scratch = [pltpu.VMEM((total, total), f32)]
    kernel = functools.partial(forward_kernel, group)
    return whole(kernel, shapes, (meta, *pieces), "attend_forward", 1, 8, scratch)


def span_gradients(query, key, value, grad, weights, inverse, outs):
    turned = grad.astype(f32).T
    row_delta = jnp.sum(outs * turned, axis=0, keepdims=True)
    grad_prob = dot(value, grad, 1, 1)
    factor = inverse * (1.0 / math.sqrt(HDIM))
    dscore = (weights.astype(f32) * ((grad_prob - row_delta) * factor)).astype(bf16)
    grad_query = dot(key, dscore, 0, 0).T.astype(bf16)
    grad_value = dot(weights, (turned * inverse).T.astype(bf16), 1, 0)
    return grad_query, dot(dscore, query, 1, 0), grad_value


def backward_early_kernel(*refs):
    pieces, (grad_ref, weight_ref, inverse_ref, out_ref, query_out, key_out, value_out) = refs[:4], refs[4:]
    early = grad_ref.shape[0]
    for h in range(pieces[-1].shape[2] // HDIM):
        cols = slice(h * HDIM, (h + 1) * HDIM)
        query, key, value = head_of(pieces, 0, h)
        grad_key = grad_value = 0.0
        for span in (slice(0, 2 * BLOCK), slice(2 * BLOCK, early)):
            grad_query, add_key, add_value = span_gradients(
                query[span], key, value, grad_ref[span, cols],
                weight_ref[h, :, span], inverse_ref[h, :, span], out_ref[cols, span],
            )
            query_out[span, cols] = grad_query
            grad_key += add_key
            grad_value += add_value
        key_out[:, cols] = grad_key
        value_out[:, cols] = grad_value


def backward_early(pieces, grad, saved):
    _, rows, part = pieces[-1].shape
    shapes = [sds((grad.shape[0], part), bf16), sds((4 * rows, part), f32), sds((4 * rows, part), f32)]
    return whole(backward_early_kernel, shapes, (*pieces, grad, *saved), "backward_early", 0, 8)


def backward_kernel(own, near, far2a, far3a, far2b, far3b, early_ref, late_ref, *refs):
    saved, done, backs = (refs[:3], refs[3:6]), refs[6:9], refs[9:]
    rows = own.shape[1]
    early, total = early_ref.shape[0], 4 * rows
    for n in range(own.shape[2] // HDIM):
        group, h = divmod(n, EARLY)
        query, key, value = head_of(((own, near, far2a, far3a), (own, near, far2b, far3b))[group], group, h)
        weight_ref, inverse_ref, out_ref = saved[group]
        here = slice(h * HDIM, (h + 1) * HDIM)
        cols = slice(n * HDIM, (n + 1) * HDIM)
        if group == 0:
            spans = ((slice(early, total), late_ref[:, cols]),)
            grad_key, grad_value = done[1][:, here], done[2][:, here]
            for k in range(early // rows):
                backs[k][0, :, cols] = done[0][k * rows : (k + 1) * rows, here]
        else:
            grad = jnp.concatenate([early_ref[:, cols], late_ref[:, cols]], axis=0)
            spans = [(slice(t, t + 2 * rows), grad[t : t + 2 * rows]) for t in (0, 2 * rows)]
            grad_key = grad_value = 0.0
        for span, grad in spans:
            grad_query, add_key, add_value = span_gradients(
                query[span], key, value, grad, weight_ref[h, :, span], inverse_ref[h, :, span], out_ref[here, span]
            )
            for k in range(span.start // rows, span.stop // rows):
                at = k * rows - span.start
                backs[k][0, :, cols] = grad_query[at : at + rows]
            grad_key += add_key
            grad_value += add_value
        for k in range(4):
            mine = slice(k * rows, (k + 1) * rows)
            backs[k][1, :, cols] = grad_key[mine].astype(bf16)
            backs[k][2, :, cols] = grad_value[mine].astype(bf16)


def backward(pieces, grads, saved, done):
    shapes = [sds(pieces[0].shape, bf16)] * 4
    return whole(backward_kernel, shapes, (*pieces, *grads, *saved, *done), "attend_backward", 0, 8)


LINE = HDIM // 8


def line_at(meta, head, other, j):
    at = head * HDIM + ((meta[CORE] ^ other) * 4 + (meta[CHIP] ^ j)) * LINE
    return pl.ds(pl.multiple_of(at, LINE), LINE)


def weight_kernel(meta, heads_a, heads_b, *refs):
    *grads, send_ref, keep_ref = refs
    width = heads_a.shape[0] + heads_b.shape[0]
    lines = []
    for other in (1, 0):
        for j in range(4):
            for ref in (heads_a, heads_b):
                lines += [ref[line_at(meta, h, other, j), :] for h in range(ref.shape[0] // HDIM)]
    lines = jnp.concatenate(lines, axis=0)
    tile = 4 * HDIM

    @pl.loop(0, send_ref.shape[1] // tile)
    def _(i):
        part = pl.ds(pl.multiple_of(i * tile, tile), tile)
        product = dot(lines, jnp.concatenate([g[:, part] for g in grads], axis=0), 1, 0)
        send_ref[:, part] = product[: width // 2].astype(bf16)
        keep_ref[:, part] = product[width // 2 :]


def weight_halves(meta, heads, grads):
    shape = (sum(x.shape[0] for x in heads) // 2, grads[0].shape[1])
    return whole(weight_kernel, [sds(shape, bf16), sds(shape, f32)], (meta, *heads, *grads), "weight_halves", 1, 6)


def add_kernel(keep_ref, recv_ref, *outs):
    size = outs[0].shape[0]
    for j, out_ref in enumerate(outs):
        part = slice(j * size, (j + 1) * size)
        out_ref[...] = (keep_ref[part, :] + recv_ref[part, :].astype(f32)).astype(out_ref.dtype)


def add_parts(keep, recv):
    shape = (keep.shape[0] // 4, keep.shape[1])
    return whole(add_kernel, [sds(shape, f32)] + [sds(shape, bf16)] * 3, (keep, recv), "add_parts")


def total_kernel(scale, own_ref, r1, r2, r3, out_ref):
    total = own_ref[...] + r1[...].astype(f32) + r2[...].astype(f32) + r3[...].astype(f32)
    out_ref[...] = (total * scale).astype(bf16)


def total_of(own, recvs, scale):
    return whole(functools.partial(total_kernel, scale), sds(own.shape, bf16), (own, *recvs), "scene_mean")


def weight_copies(meta, parts, first, out_ref, sems):
    copies = []
    for p, ref in enumerate(parts, first):
        for h in range(ref.shape[0] // LINE):
            line = out_ref.at[line_at(meta, h, p // 4, p % 4), :]
            copies.append(pltpu.make_async_copy(ref.at[pl.ds(h * LINE, LINE), :], line, sems.at[len(copies)]))
    return copies


def head_copies(meta, pieces, outs, sems):
    copies = []
    for k, ref in pieces.items():
        width = ref.shape[2]
        start = pl.multiple_of((meta[Z] ^ k) * width, 128)
        for i, out_ref in enumerate(outs):
            part = out_ref.at[:, pl.ds(start, width)]
            copies.append(pltpu.make_async_copy(ref.at[i], part, sems.at[len(copies)]))
    return copies


def join(kernel, meta, parts, shapes, copies, name, outs=()):
    return pl.pallas_call(
        kernel,
        out_shape=shapes,
        in_specs=[pl.BlockSpec(memory_space=pltpu.SMEM)]
        + [pl.BlockSpec(memory_space=pltpu.VMEM)] * len(parts)
        + [pl.BlockSpec(memory_space=pl.ANY)] * len(outs),
        out_specs=[pl.BlockSpec(memory_space=pl.ANY)] * len(shapes),
        scratch_shapes=[pltpu.SemaphoreType.DMA((n,)) for n in copies],
        input_output_aliases={1 + len(parts) + i: i for i in range(len(outs))},
        compiler_params=params(),
        cost_estimate=NO_COST,
        name=name,
    )(meta, *parts, *outs)


def join_weight_kernel(meta, *refs):
    run_all(weight_copies(meta, refs[:4], 0, refs[4], refs[5]))


def join_weight(meta, near):
    size, outw = near[0].shape
    return join(join_weight_kernel, meta, near, [sds((8 * size, outw), bf16)], [4 * size // LINE], "join_weight")[0]


def join_heads_kernel(meta, own, back2, back3, *refs):
    run_all(head_copies(meta, {0: own, 2: back2, 3: back3}, refs[:3], refs[3]))


def join_heads(meta, own, back2, back3):
    _, rows, width = own.shape
    shapes = [sds((rows, 4 * width), bf16)] * 3
    return join(join_heads_kernel, meta, (own, back2, back3), shapes, [9], "join_heads")


def join_last_kernel(meta, *refs):
    far, back1, outs, sems = refs[:4], refs[4], refs[9:13], refs[13:]
    run_all(weight_copies(meta, far, 4, outs[3], sems[0]) + head_copies(meta, {1: back1}, outs[:3], sems[1]))


def join_last(meta, far, back1, outs):
    shapes = [sds(x.shape, x.dtype) for x in outs]
    return join(join_last_kernel, meta, (*far, back1), shapes, [4 * far[0].shape[0] // LINE, 3], "join_last", outs)


def dense_body(queries, keys_in, values, out_grad, out_weight, voxel_count):
    meta = jnp.stack([lax.axis_index("shard"), voxel_count[0], lax.axis_index("core"), lax.axis_index("chips")])
    meta = meta.astype(jnp.int32)

    def send(x, k, *earlier):
        return swap(after(x, *earlier) if earlier else x, "shard", 4, k)

    across = send(out_grad, 2)
    beside = send(out_grad, 1)
    mine, own, near1, far2a, far2b, far3a, far3b = pack(meta, queries, keys_in, values, out_grad)
    piece1 = send(near1, 1)
    piece3a = send(far3a, 3, beside)
    piece2a = send(far2a, 2, across)
    piece3b = send(far3b, 3, piece3a)
    piece2b = send(far2b, 2, piece2a)
    half = across.shape[0] // 2
    grad_early = grad_attn(meta, (mine, beside, across), out_weight, 0)
    corners = [send(across[:half], 1), send(after(across, piece1, grad_early)[half:], 1)]

    *saved_a, heads_a = forward(meta, (own, piece1, piece2a, piece3a), 0)
    early = backward_early((own, piece1, piece2a, piece3a), grad_early, saved_a)
    heads_a, *early, piece2b, piece3b = lax.optimization_barrier((heads_a, *early, piece2b, piece3b))
    *saved_b, heads_b = forward(meta, (own, piece1, piece2b, piece3b), 1)
    grad_early, heads_b, *corners = lax.optimization_barrier((grad_early, heads_b, *corners))
    grads = (mine, beside, across, *corners)

    out, keep = weight_halves(meta, (heads_a, heads_b), grads)
    recv = swap(out, "core", 2, 1)
    grad_late = grad_attn(meta, after(grads[3:], out), out_weight, 3 * BLOCK)
    pieces = (own, piece1, piece2a, piece3a, piece2b, piece3b)
    own0, *backs = backward(pieces, (grad_early, grad_late), (*saved_a, *saved_b), early)
    own_part, *sends = add_parts(after(keep, own0), recv)
    recvs = [swap(x, "chips", 4, j + 1) for j, x in enumerate(sends)]
    back2, back1 = send(backs[1], 2), send(backs[0], 1)
    back3 = send(backs[2], 3, recvs[1])
    done = total_of(after(own_part, back2), recvs, 1.0 / 8)
    near = [done] + [swap(done, "chips", 4, j) for j in (1, 2, 3)]
    weight = join_weight(meta, near)
    weight, *near, back3 = lax.optimization_barrier((weight, *near, back3))
    far = [swap(x, "core", 2, 1) for x in near]
    heads = join_heads(meta, own0, back2, back3)
    return tuple(join_last(meta, far, back1, (*heads, weight)))


def attend_listed(queries, keys_in, values, block_ids, live_count):
    row_count, width_all = queries.shape
    head_count = width_all // HDIM
    block_count = row_count // BLOCK
    score_scale = 1.0 / math.sqrt(HDIM)
    query_blk = queries.reshape(block_count, BLOCK, head_count, HDIM)
    key_blk = keys_in.reshape(block_count, BLOCK, head_count, HDIM)[block_ids].reshape(
        block_count, NB * BLOCK, head_count, HDIM
    )
    value_blk = values.reshape(block_count, BLOCK, head_count, HDIM)[block_ids].reshape(
        block_count, NB * BLOCK, head_count, HDIM
    )
    query_pos = jnp.arange(row_count, dtype=jnp.int32).reshape(block_count, BLOCK)
    key_pos = (
        block_ids[:, :, None] * BLOCK + jnp.arange(BLOCK, dtype=jnp.int32)[None, None, :]
    ).reshape(block_count, NB * BLOCK)
    allowed = (key_pos[:, None, :] < live_count) | (query_pos[:, :, None] >= live_count)
    scores = (
        jnp.einsum("bqhd,bkhd->bhqk", query_blk, key_blk, preferred_element_type=jnp.float32)
        * score_scale
    )
    scores = jnp.where(allowed[:, None], scores, -jnp.inf)
    peak = jnp.max(scores, axis=-1, keepdims=True)
    weights = jnp.exp(scores - peak)
    probs = weights / jnp.sum(weights, axis=-1, keepdims=True)
    return (query_blk, key_blk, value_blk, probs)


def listed_body(queries, keys_in, values, out_grad, out_weight, block_lists, voxel_count):
    local_rows = queries.shape[0]
    live_count = voxel_count[0]
    block_ids = block_lists[0]
    positions = lax.axis_index("shard") * local_rows + jnp.arange(local_rows, dtype=jnp.int32)
    grad_live = jnp.where((positions < live_count)[:, None], out_grad, jnp.zeros_like(out_grad))
    query_head, key_head, value_head = (
        lax.all_to_all(queries, "shard", split_axis=1, concat_axis=0, tiled=True),
        lax.all_to_all(keys_in, "shard", split_axis=1, concat_axis=0, tiled=True),
        lax.all_to_all(values, "shard", split_axis=1, concat_axis=0, tiled=True),
    )
    row_count, width_all = query_head.shape
    head_count = width_all // HDIM
    block_count = row_count // BLOCK
    score_scale = 1.0 / math.sqrt(HDIM)
    query_blk, key_blk, value_blk, probs = attend_listed(
        query_head, key_head, value_head, block_ids, live_count
    )
    prob_bf = probs.astype(jnp.bfloat16)
    heads_out = (
        jnp.einsum("bhqk,bkhd->bqhd", prob_bf, value_blk, preferred_element_type=jnp.float32)
        .reshape(row_count, width_all)
        .astype(jnp.bfloat16)
    )
    row_piece = lax.all_gather(grad_live, "shard", axis=0, tiled=True)
    acc_now = jnp.einsum("rw,ro->wo", heads_out, row_piece, preferred_element_type=jnp.float32)
    product = jnp.einsum("ro,wo->rw", row_piece, out_weight, preferred_element_type=jnp.float32)
    grad_o = product.astype(jnp.bfloat16).reshape(block_count, BLOCK, head_count, HDIM)
    grad_prob = jnp.einsum("bqhd,bkhd->bhqk", grad_o, value_blk, preferred_element_type=jnp.float32)
    row_delta = jnp.sum(probs * grad_prob, axis=-1, keepdims=True)
    dscore = (probs * (grad_prob - row_delta) * score_scale).astype(jnp.bfloat16)
    grad_query = (
        jnp.einsum("bhqk,bkhd->bqhd", dscore, key_blk, preferred_element_type=jnp.float32)
        .reshape(row_count, width_all)
        .astype(jnp.bfloat16)
    )
    onehot = (
        block_ids[:, :, None] == jnp.arange(block_count, dtype=jnp.int32)[None, None, :]
    ).astype(jnp.float32)
    key_parts = jnp.einsum(
        "bhqk,bqhd->bkhd", dscore, query_blk, preferred_element_type=jnp.float32
    ).reshape(block_count, NB, BLOCK, width_all)
    value_parts = jnp.einsum(
        "bhqk,bqhd->bkhd", prob_bf, grad_o, preferred_element_type=jnp.float32
    ).reshape(block_count, NB, BLOCK, width_all)
    grad_key = (
        jnp.einsum("bjc,bjrx->crx", onehot, key_parts, precision=lax.Precision.HIGHEST)
        .reshape(row_count, width_all)
        .astype(jnp.bfloat16)
    )
    grad_value = (
        jnp.einsum("bjc,bjrx->crx", onehot, value_parts, precision=lax.Precision.HIGHEST)
        .reshape(row_count, width_all)
        .astype(jnp.bfloat16)
    )
    query_back, key_back, value_back = (
        lax.all_to_all(grad_query, "shard", split_axis=0, concat_axis=1, tiled=True),
        lax.all_to_all(grad_key, "shard", split_axis=0, concat_axis=1, tiled=True),
        lax.all_to_all(grad_value, "shard", split_axis=0, concat_axis=1, tiled=True),
    )
    scene_total = lax.axis_size(DP)
    summed = lax.psum(acc_now, DP)
    grad_weight = (summed / scene_total).astype(jnp.bfloat16)
    return (query_back, key_back, value_back, grad_weight)


def body(queries, keys_in, values, out_grad, out_weight, block_lists, voxel_count):
    dense = block_lists.shape[1] == NB and queries.shape[0] == BLOCK
    if dense and lax.axis_size("shard") == 4 and lax.axis_size("chips") == 4:
        return dense_body(queries, keys_in, values, out_grad, out_weight, voxel_count)
    return listed_body(queries, keys_in, values, out_grad, out_weight, block_lists, voxel_count)


def solution(mesh):
    chips = mesh.shape["dp"] // 2
    mesh = jax.sharding.Mesh(mesh.devices.reshape(chips, 2, -1), ("chips", "core", "shard"))
    return jax.shard_map(
        body,
        mesh=mesh,
        in_specs=(
            P((*DP, "shard"), None),
            P((*DP, "shard"), None),
            P((*DP, "shard"), None),
            P((*DP, "shard"), None),
            P("shard", None),
            P(DP, None, None),
            P(DP),
        ),
        out_specs=(
            P((*DP, "shard"), None),
            P((*DP, "shard"), None),
            P((*DP, "shard"), None),
            P("shard", None),
        ),
        check_vma=False,
    )
```

```python
import functools
import math

import jax
import jax.numpy as jnp
from jax import lax
from jax.experimental import pallas as pl
from jax.experimental.pallas import tpu as pltpu
from jax.sharding import PartitionSpec as P

HDIM = 128
BLOCK = 128
NB = 4
MIB = 1024 * 1024
DP = ("chips", "core")

Z, COUNT, CORE, CHIP = range(4)

EARLY = 3

NO_COST = pl.CostEstimate(flops=0, bytes_accessed=1024, transcendentals=0)

f32 = jnp.float32
bf16 = jnp.bfloat16


def dot(a, b, ca, cb):
    return lax.dot_general(a, b, (((ca,), (cb,)), ((), ())), preferred_element_type=f32)


def sds(shape, dtype):
    return jax.ShapeDtypeStruct(shape, dtype)


def params(mib=2):
    return pltpu.CompilerParams(vmem_limit_bytes=mib * MIB)


def swap(x, axis, size, flip):
    return lax.ppermute(x, axis, [(i, i ^ flip) for i in range(size)])


def after(x, *earlier):
    return lax.optimization_barrier((x, *earlier))[0]


def run_all(copies):
    for copy in copies:
        copy.start()
    for copy in copies:
        copy.wait()


def whole(kernel, out_shape, operands, name, scalars=0, mib=2, scratch=()):
    return pl.pallas_call(
        kernel,
        out_shape=out_shape,
        in_specs=[pl.BlockSpec(memory_space=pltpu.SMEM)] * scalars
        + [pl.BlockSpec(memory_space=pltpu.VMEM)] * (len(operands) - scalars),
        out_specs=jax.tree.map(lambda _: pl.BlockSpec(memory_space=pltpu.VMEM), out_shape),
        scratch_shapes=scratch,
        compiler_params=params(mib),
        cost_estimate=NO_COST,
        name=name,
    )(*operands)


def pack_kernel(meta, q_ref, k_ref, v_ref, grad_ref, mine_ref, *refs):
    *outs, sems = refs
    width = outs[0].shape[2]
    copies = [pltpu.make_async_copy(grad_ref, mine_ref, sems.at[3 * len(outs)])]
    for n, out_ref in enumerate(outs):
        k, first = (n, 0) if n < 2 else (n // 2 + 1, n % 2 * EARLY * HDIM)
        start = pl.multiple_of((meta[Z] ^ k) * width + first, 128)
        for i, ref in enumerate((q_ref, k_ref, v_ref)):
            part = ref.at[:, pl.ds(start, out_ref.shape[2])]
            copies.append(pltpu.make_async_copy(part, out_ref.at[i], sems.at[3 * n + i]))
    run_all(copies)


def pack(meta, queries, keys_in, values, grad):
    rows, width = queries.shape
    part, early = width // 4, EARLY * HDIM
    shapes = [sds((3, rows, n), bf16) for n in (part, part, early, part - early, early, part - early)]
    shapes = [sds(grad.shape, bf16)] + shapes
    return pl.pallas_call(
        pack_kernel,
        out_shape=shapes,
        in_specs=[pl.BlockSpec(memory_space=pltpu.SMEM)] + [pl.BlockSpec(memory_space=pl.ANY)] * 4,
        out_specs=[pl.BlockSpec(memory_space=pltpu.VMEM)] * len(shapes),
        scratch_shapes=[pltpu.SemaphoreType.DMA((3 * len(shapes),))],
        compiler_params=params(),
        cost_estimate=NO_COST,
        name="pack_heads",
    )(meta, queries, keys_in, values, grad)


def token_pos(shape, dim, z, start=0):
    return (lax.broadcasted_iota(jnp.int32, shape, dim) + start) ^ (z * BLOCK)


def grad_attn_kernel(start, meta, *refs):
    *grads, w_ref, out_ref = refs
    grad = jnp.concatenate([g[...] for g in grads], axis=0)
    live = token_pos((grad.shape[0], 1), 0, meta[Z], start) < meta[COUNT]
    tile = 2 * HDIM

    @pl.loop(0, w_ref.shape[0] // tile)
    def _(i):
        part = pl.ds(pl.multiple_of(i * tile, tile), tile)
        out_ref[:, part] = jnp.where(live, dot(grad, w_ref[part, :], 1, 1), 0.0).astype(bf16)


def grad_attn(meta, grads, weight, start):
    shape = (sum(g.shape[0] for g in grads), weight.shape[0])
    kernel = functools.partial(grad_attn_kernel, start)
    return whole(kernel, sds(shape, bf16), (meta, *grads, weight), "grad_attn", 1, 6)


def head_of(pieces, group, h):
    part = pieces[-1].shape[2]
    parts = []
    for p in pieces:
        start = (group * EARLY * HDIM if p.shape[2] > part else 0) + h * HDIM
        parts.append([p[i, :, start : start + HDIM] for i in range(3)])
    return (jnp.concatenate(x, axis=0) for x in zip(*parts))


def forward_kernel(group, meta, p0, p1, p2, p3, weight_ref, inverse_ref, out_ref, heads_ref, bias_ref):
    pieces = (p0, p1, p2, p3)
    rows = p0.shape[1]
    total = 4 * rows
    tile = 2 * rows
    to_power = math.log2(math.e) / math.sqrt(HDIM)
    query_live = token_pos((1, total), 1, meta[Z]) < meta[COUNT]
    key_live = token_pos((total, 1), 0, meta[Z]) < meta[COUNT]
    bias_ref[...] = jnp.where(key_live | ~query_live, 0.0, -jnp.inf)
    for h in range(p3.shape[2] // HDIM):
        cols = slice(h * HDIM, (h + 1) * HDIM)
        query, key, value = head_of(pieces, group, h)
        for t in range(2):
            part = slice(t * tile, (t + 1) * tile)
            scores = dot(key, query[part], 1, 1) + bias_ref[:, part]
            peak = jnp.max(scores, axis=0, keepdims=True)
            weights = jnp.exp2((scores - peak) * to_power).astype(bf16)
            weight_ref[h, :, part] = weights
            inverse = 1.0 / jnp.sum(weights.astype(f32), axis=0, keepdims=True)
            inverse_ref[h, :, part] = inverse
            heads = dot(value, weights, 0, 0) * inverse
            out_ref[cols, part] = heads
            heads_ref[cols, part] = jnp.where(query_live[:, part], heads, 0.0).astype(bf16)


def forward(meta, pieces, group):
    _, rows, width = pieces[-1].shape
    total = 4 * rows
    shapes = [
        sds((width // HDIM, total, total), bf16),
        sds((width // HDIM, 1, total), f32),
        sds((width, total), f32),
        sds((width, total), bf16),
    ]
    scratch = [pltpu.VMEM((total, total), f32)]
    kernel = functools.partial(forward_kernel, group)
    return whole(kernel, shapes, (meta, *pieces), "attend_forward", 1, 8, scratch)


def span_gradients(query, key, value, grad, weights, inverse, outs):
    turned = grad.astype(f32).T
    row_delta = jnp.sum(outs * turned, axis=0, keepdims=True)
    grad_prob = dot(value, grad, 1, 1)
    factor = inverse * (1.0 / math.sqrt(HDIM))
    dscore = (weights.astype(f32) * ((grad_prob - row_delta) * factor)).astype(bf16)
    grad_query = dot(key, dscore, 0, 0).T.astype(bf16)
    grad_value = dot(weights, (turned * inverse).T.astype(bf16), 1, 0)
    return grad_query, dot(dscore, query, 1, 0), grad_value


def backward_early_kernel(*refs):
    pieces, (grad_ref, weight_ref, inverse_ref, out_ref, query_out, key_out, value_out) = refs[:4], refs[4:]
    early = grad_ref.shape[0]
    for h in range(pieces[-1].shape[2] // HDIM):
        cols = slice(h * HDIM, (h + 1) * HDIM)
        query, key, value = head_of(pieces, 0, h)
        grad_key = grad_value = 0.0
        for span in (slice(0, 2 * BLOCK), slice(2 * BLOCK, early)):
            grad_query, add_key, add_value = span_gradients(
                query[span], key, value, grad_ref[span, cols],
                weight_ref[h, :, span], inverse_ref[h, :, span], out_ref[cols, span],
            )
            query_out[span, cols] = grad_query
            grad_key += add_key
            grad_value += add_value
        key_out[:, cols] = grad_key
        value_out[:, cols] = grad_value


def backward_early(pieces, grad, saved):
    _, rows, part = pieces[-1].shape
    shapes = [sds((grad.shape[0], part), bf16), sds((4 * rows, part), f32), sds((4 * rows, part), f32)]
    return whole(backward_early_kernel, shapes, (*pieces, grad, *saved), "backward_early", 0, 8)


def backward_kernel(own, near, far2a, far3a, far2b, far3b, early_ref, late_ref, *refs):
    saved, done, backs = (refs[:3], refs[3:6]), refs[6:9], refs[9:]
    rows = own.shape[1]
    early, total = early_ref.shape[0], 4 * rows
    for n in range(own.shape[2] // HDIM):
        group, h = divmod(n, EARLY)
        query, key, value = head_of(((own, near, far2a, far3a), (own, near, far2b, far3b))[group], group, h)
        weight_ref, inverse_ref, out_ref = saved[group]
        here = slice(h * HDIM, (h + 1) * HDIM)
        cols = slice(n * HDIM, (n + 1) * HDIM)
        if group == 0:
            spans = ((slice(early, total), late_ref[:, cols]),)
            grad_key, grad_value = done[1][:, here], done[2][:, here]
            for k in range(early // rows):
                backs[k][0, :, cols] = done[0][k * rows : (k + 1) * rows, here]
        else:
            grad = jnp.concatenate([early_ref[:, cols], late_ref[:, cols]], axis=0)
            spans = [(slice(t, t + 2 * rows), grad[t : t + 2 * rows]) for t in (0, 2 * rows)]
            grad_key = grad_value = 0.0
        for span, grad in spans:
            grad_query, add_key, add_value = span_gradients(
                query[span], key, value, grad, weight_ref[h, :, span], inverse_ref[h, :, span], out_ref[here, span]
            )
            for k in range(span.start // rows, span.stop // rows):
                at = k * rows - span.start
                backs[k][0, :, cols] = grad_query[at : at + rows]
            grad_key += add_key
            grad_value += add_value
        for k in range(4):
            mine = slice(k * rows, (k + 1) * rows)
            backs[k][1, :, cols] = grad_key[mine].astype(bf16)
            backs[k][2, :, cols] = grad_value[mine].astype(bf16)


def backward(pieces, grads, saved, done):
    shapes = [sds(pieces[0].shape, bf16)] * 4
    return whole(backward_kernel, shapes, (*pieces, *grads, *saved, *done), "attend_backward", 0, 8)


LINE = HDIM // 8


def line_at(meta, head, other, j):
    at = head * HDIM + ((meta[CORE] ^ other) * 4 + (meta[CHIP] ^ j)) * LINE
    return pl.ds(pl.multiple_of(at, LINE), LINE)


def weight_kernel(meta, heads_a, heads_b, *refs):
    *grads, send_ref, keep_ref = refs
    width = heads_a.shape[0] + heads_b.shape[0]
    lines = []
    for other in (1, 0):
        for j in range(4):
            for ref in (heads_a, heads_b):
                lines += [ref[line_at(meta, h, other, j), :] for h in range(ref.shape[0] // HDIM)]
    lines = jnp.concatenate(lines, axis=0)
    tile = 4 * HDIM

    @pl.loop(0, send_ref.shape[1] // tile)
    def _(i):
        part = pl.ds(pl.multiple_of(i * tile, tile), tile)
        product = dot(lines, jnp.concatenate([g[:, part] for g in grads], axis=0), 1, 0)
        send_ref[:, part] = product[: width // 2].astype(bf16)
        keep_ref[:, part] = product[width // 2 :]


def weight_halves(meta, heads, grads):
    shape = (sum(x.shape[0] for x in heads) // 2, grads[0].shape[1])
    return whole(weight_kernel, [sds(shape, bf16), sds(shape, f32)], (meta, *heads, *grads), "weight_halves", 1, 6)


def add_kernel(keep_ref, recv_ref, *outs):
    size = outs[0].shape[0]
    for j, out_ref in enumerate(outs):
        part = slice(j * size, (j + 1) * size)
        out_ref[...] = (keep_ref[part, :] + recv_ref[part, :].astype(f32)).astype(out_ref.dtype)


def add_parts(keep, recv):
    shape = (keep.shape[0] // 4, keep.shape[1])
    return whole(add_kernel, [sds(shape, f32)] + [sds(shape, bf16)] * 3, (keep, recv), "add_parts")


def total_kernel(scale, own_ref, r1, r2, r3, out_ref):
    total = own_ref[...] + r1[...].astype(f32) + r2[...].astype(f32) + r3[...].astype(f32)
    out_ref[...] = (total * scale).astype(bf16)


def total_of(own, recvs, scale):
    return whole(functools.partial(total_kernel, scale), sds(own.shape, bf16), (own, *recvs), "scene_mean")


def weight_copies(meta, parts, first, out_ref, sems):
    copies = []
    for p, ref in enumerate(parts, first):
        for h in range(ref.shape[0] // LINE):
            line = out_ref.at[line_at(meta, h, p // 4, p % 4), :]
            copies.append(pltpu.make_async_copy(ref.at[pl.ds(h * LINE, LINE), :], line, sems.at[len(copies)]))
    return copies


def head_copies(meta, pieces, outs, sems):
    copies = []
    for k, ref in pieces.items():
        width = ref.shape[2]
        start = pl.multiple_of((meta[Z] ^ k) * width, 128)
        for i, out_ref in enumerate(outs):
            part = out_ref.at[:, pl.ds(start, width)]
            copies.append(pltpu.make_async_copy(ref.at[i], part, sems.at[len(copies)]))
    return copies


def join(kernel, meta, parts, shapes, copies, name, outs=()):
    return pl.pallas_call(
        kernel,
        out_shape=shapes,
        in_specs=[pl.BlockSpec(memory_space=pltpu.SMEM)]
        + [pl.BlockSpec(memory_space=pltpu.VMEM)] * len(parts)
        + [pl.BlockSpec(memory_space=pl.ANY)] * len(outs),
        out_specs=[pl.BlockSpec(memory_space=pl.ANY)] * len(shapes),
        scratch_shapes=[pltpu.SemaphoreType.DMA((n,)) for n in copies],
        input_output_aliases={1 + len(parts) + i: i for i in range(len(outs))},
        compiler_params=params(),
        cost_estimate=NO_COST,
        name=name,
    )(meta, *parts, *outs)


def join_weight_kernel(meta, *refs):
    run_all(weight_copies(meta, refs[:4], 0, refs[4], refs[5]))


def join_weight(meta, near):
    size, outw = near[0].shape
    return join(join_weight_kernel, meta, near, [sds((8 * size, outw), bf16)], [4 * size // LINE], "join_weight")[0]


def join_heads_kernel(meta, own, back2, *refs):
    run_all(head_copies(meta, {0: own, 2: back2}, refs[:3], refs[3]))


def join_heads(meta, own, back2):
    _, rows, width = own.shape
    shapes = [sds((rows, 4 * width), bf16)] * 3
    return join(join_heads_kernel, meta, (own, back2), shapes, [6], "join_heads")


def join_last_kernel(meta, *refs):
    far, back1, back3, outs, sems = refs[:4], refs[4], refs[5], refs[10:14], refs[14:]
    heads = head_copies(meta, {1: back1, 3: back3}, outs[:3], sems[1])
    run_all(weight_copies(meta, far, 4, outs[3], sems[0]) + heads)


def join_last(meta, far, back1, back3, outs):
    shapes = [sds(x.shape, x.dtype) for x in outs]
    parts = (*far, back1, back3)
    return join(join_last_kernel, meta, parts, shapes, [4 * far[0].shape[0] // LINE, 6], "join_last", outs)


def dense_body(queries, keys_in, values, out_grad, out_weight, voxel_count):
    meta = jnp.stack([lax.axis_index("shard"), voxel_count[0], lax.axis_index("core"), lax.axis_index("chips")])
    meta = meta.astype(jnp.int32)

    def send(x, k, *earlier):
        return swap(after(x, *earlier) if earlier else x, "shard", 4, k)

    across = send(out_grad, 2)
    beside = send(out_grad, 1)
    mine, own, near1, far2a, far2b, far3a, far3b = pack(meta, queries, keys_in, values, out_grad)
    piece1 = send(near1, 1)
    piece3a = send(far3a, 3, across)
    piece2a = send(far2a, 2, across)
    piece3b = send(far3b, 3, piece3a)
    piece2b = send(far2b, 2, piece2a)
    half = across.shape[0] // 2
    grad_early = grad_attn(meta, (mine, beside, across), out_weight, 0)
    corners = [send(across[:half], 1), send(after(across, piece1, grad_early)[half:], 1)]

    *saved_a, heads_a = forward(meta, (own, piece1, piece2a, piece3a), 0)
    early = backward_early((own, piece1, piece2a, piece3a), grad_early, saved_a)
    heads_a, *early, piece2b, piece3b = lax.optimization_barrier((heads_a, *early, piece2b, piece3b))
    *saved_b, heads_b = forward(meta, (own, piece1, piece2b, piece3b), 1)
    grad_early, heads_b, *corners = lax.optimization_barrier((grad_early, heads_b, *corners))
    grads = (mine, beside, across, *corners)

    out, keep = weight_halves(meta, (heads_a, heads_b), grads)
    recv = swap(out, "core", 2, 1)
    grad_late = grad_attn(meta, after(grads[3:], out), out_weight, 3 * BLOCK)
    pieces = (own, piece1, piece2a, piece3a, piece2b, piece3b)
    own0, *backs = backward(pieces, (grad_early, grad_late), (*saved_a, *saved_b), early)
    own_part, *sends = add_parts(after(keep, own0), recv)
    recvs = [swap(x, "chips", 4, j + 1) for j, x in enumerate(sends)]
    back3, back2 = send(backs[2], 3), send(backs[1], 2)
    done = total_of(own_part, recvs, 1.0 / 8)
    near = [done] + [swap(done, "chips", 4, j) for j in (1, 2, 3)]
    back1 = send(backs[0], 1, near[1])
    outs = (*join_heads(meta, own0, back2), join_weight(meta, near))
    *outs, near1, back2, back3 = lax.optimization_barrier((*outs, near[1], back2, back3))
    far = [swap(x, "core", 2, 1) for x in (near[0], near1, *near[2:])]
    return tuple(join_last(meta, far, back1, back3, outs))


def attend_listed(queries, keys_in, values, block_ids, live_count):
    row_count, width_all = queries.shape
    head_count = width_all // HDIM
    block_count = row_count // BLOCK
    score_scale = 1.0 / math.sqrt(HDIM)
    query_blk = queries.reshape(block_count, BLOCK, head_count, HDIM)
    key_blk = keys_in.reshape(block_count, BLOCK, head_count, HDIM)[block_ids].reshape(
        block_count, NB * BLOCK, head_count, HDIM
    )
    value_blk = values.reshape(block_count, BLOCK, head_count, HDIM)[block_ids].reshape(
        block_count, NB * BLOCK, head_count, HDIM
    )
    query_pos = jnp.arange(row_count, dtype=jnp.int32).reshape(block_count, BLOCK)
    key_pos = (
        block_ids[:, :, None] * BLOCK + jnp.arange(BLOCK, dtype=jnp.int32)[None, None, :]
    ).reshape(block_count, NB * BLOCK)
    allowed = (key_pos[:, None, :] < live_count) | (query_pos[:, :, None] >= live_count)
    scores = (
        jnp.einsum("bqhd,bkhd->bhqk", query_blk, key_blk, preferred_element_type=jnp.float32)
        * score_scale
    )
    scores = jnp.where(allowed[:, None], scores, -jnp.inf)
    peak = jnp.max(scores, axis=-1, keepdims=True)
    weights = jnp.exp(scores - peak)
    probs = weights / jnp.sum(weights, axis=-1, keepdims=True)
    return (query_blk, key_blk, value_blk, probs)


def listed_body(queries, keys_in, values, out_grad, out_weight, block_lists, voxel_count):
    local_rows = queries.shape[0]
    live_count = voxel_count[0]
    block_ids = block_lists[0]
    positions = lax.axis_index("shard") * local_rows + jnp.arange(local_rows, dtype=jnp.int32)
    grad_live = jnp.where((positions < live_count)[:, None], out_grad, jnp.zeros_like(out_grad))
    query_head, key_head, value_head = (
        lax.all_to_all(queries, "shard", split_axis=1, concat_axis=0, tiled=True),
        lax.all_to_all(keys_in, "shard", split_axis=1, concat_axis=0, tiled=True),
        lax.all_to_all(values, "shard", split_axis=1, concat_axis=0, tiled=True),
    )
    row_count, width_all = query_head.shape
    head_count = width_all // HDIM
    block_count = row_count // BLOCK
    score_scale = 1.0 / math.sqrt(HDIM)
    query_blk, key_blk, value_blk, probs = attend_listed(
        query_head, key_head, value_head, block_ids, live_count
    )
    prob_bf = probs.astype(jnp.bfloat16)
    heads_out = (
        jnp.einsum("bhqk,bkhd->bqhd", prob_bf, value_blk, preferred_element_type=jnp.float32)
        .reshape(row_count, width_all)
        .astype(jnp.bfloat16)
    )
    row_piece = lax.all_gather(grad_live, "shard", axis=0, tiled=True)
    acc_now = jnp.einsum("rw,ro->wo", heads_out, row_piece, preferred_element_type=jnp.float32)
    product = jnp.einsum("ro,wo->rw", row_piece, out_weight, preferred_element_type=jnp.float32)
    grad_o = product.astype(jnp.bfloat16).reshape(block_count, BLOCK, head_count, HDIM)
    grad_prob = jnp.einsum("bqhd,bkhd->bhqk", grad_o, value_blk, preferred_element_type=jnp.float32)
    row_delta = jnp.sum(probs * grad_prob, axis=-1, keepdims=True)
    dscore = (probs * (grad_prob - row_delta) * score_scale).astype(jnp.bfloat16)
    grad_query = (
        jnp.einsum("bhqk,bkhd->bqhd", dscore, key_blk, preferred_element_type=jnp.float32)
        .reshape(row_count, width_all)
        .astype(jnp.bfloat16)
    )
    onehot = (
        block_ids[:, :, None] == jnp.arange(block_count, dtype=jnp.int32)[None, None, :]
    ).astype(jnp.float32)
    key_parts = jnp.einsum(
        "bhqk,bqhd->bkhd", dscore, query_blk, preferred_element_type=jnp.float32
    ).reshape(block_count, NB, BLOCK, width_all)
    value_parts = jnp.einsum(
        "bhqk,bqhd->bkhd", prob_bf, grad_o, preferred_element_type=jnp.float32
    ).reshape(block_count, NB, BLOCK, width_all)
    grad_key = (
        jnp.einsum("bjc,bjrx->crx", onehot, key_parts, precision=lax.Precision.HIGHEST)
        .reshape(row_count, width_all)
        .astype(jnp.bfloat16)
    )
    grad_value = (
        jnp.einsum("bjc,bjrx->crx", onehot, value_parts, precision=lax.Precision.HIGHEST)
        .reshape(row_count, width_all)
        .astype(jnp.bfloat16)
    )
    query_back, key_back, value_back = (
        lax.all_to_all(grad_query, "shard", split_axis=0, concat_axis=1, tiled=True),
        lax.all_to_all(grad_key, "shard", split_axis=0, concat_axis=1, tiled=True),
        lax.all_to_all(grad_value, "shard", split_axis=0, concat_axis=1, tiled=True),
    )
    scene_total = lax.axis_size(DP)
    summed = lax.psum(acc_now, DP)
    grad_weight = (summed / scene_total).astype(jnp.bfloat16)
    return (query_back, key_back, value_back, grad_weight)


def body(queries, keys_in, values, out_grad, out_weight, block_lists, voxel_count):
    dense = block_lists.shape[1] == NB and queries.shape[0] == BLOCK
    if dense and lax.axis_size("shard") == 4 and lax.axis_size("chips") == 4:
        return dense_body(queries, keys_in, values, out_grad, out_weight, voxel_count)
    return listed_body(queries, keys_in, values, out_grad, out_weight, block_lists, voxel_count)


def solution(mesh):
    chips = mesh.shape["dp"] // 2
    mesh = jax.sharding.Mesh(mesh.devices.reshape(chips, 2, -1), ("chips", "core", "shard"))
    return jax.shard_map(
        body,
        mesh=mesh,
        in_specs=(
            P((*DP, "shard"), None),
            P((*DP, "shard"), None),
            P((*DP, "shard"), None),
            P((*DP, "shard"), None),
            P("shard", None),
            P(DP, None, None),
            P(DP),
        ),
        out_specs=(
            P((*DP, "shard"), None),
            P((*DP, "shard"), None),
            P((*DP, "shard"), None),
            P("shard", None),
        ),
        check_vma=False,
    )
```

```python
import functools
import math

import jax
import jax.numpy as jnp
from jax import lax
from jax.experimental import pallas as pl
from jax.experimental.pallas import tpu as pltpu
from jax.sharding import PartitionSpec as P

HDIM = 128
BLOCK = 128
NB = 4
MIB = 1024 * 1024
DP = ("chips", "core")

Z, COUNT, CORE, CHIP = range(4)

EARLY = 3

NO_COST = pl.CostEstimate(flops=0, bytes_accessed=1024, transcendentals=0)

f32 = jnp.float32
bf16 = jnp.bfloat16


def dot(a, b, ca, cb):
    return lax.dot_general(a, b, (((ca,), (cb,)), ((), ())), preferred_element_type=f32)


def sds(shape, dtype):
    return jax.ShapeDtypeStruct(shape, dtype)


def params(mib=2):
    return pltpu.CompilerParams(vmem_limit_bytes=mib * MIB)


def swap(x, axis, size, flip):
    return lax.ppermute(x, axis, [(i, i ^ flip) for i in range(size)])


def after(x, *earlier):
    return lax.optimization_barrier((x, *earlier))[0]


def run_all(copies):
    for copy in copies:
        copy.start()
    for copy in copies:
        copy.wait()


def whole(kernel, out_shape, operands, name, scalars=0, mib=2, scratch=()):
    return pl.pallas_call(
        kernel,
        out_shape=out_shape,
        in_specs=[pl.BlockSpec(memory_space=pltpu.SMEM)] * scalars
        + [pl.BlockSpec(memory_space=pltpu.VMEM)] * (len(operands) - scalars),
        out_specs=jax.tree.map(lambda _: pl.BlockSpec(memory_space=pltpu.VMEM), out_shape),
        scratch_shapes=scratch,
        compiler_params=params(mib),
        cost_estimate=NO_COST,
        name=name,
    )(*operands)


def pack_kernel(meta, q_ref, k_ref, v_ref, grad_ref, mine_ref, *refs):
    *outs, sems = refs
    width = outs[0].shape[2]
    copies = [pltpu.make_async_copy(grad_ref, mine_ref, sems.at[3 * len(outs)])]
    for n, out_ref in enumerate(outs):
        k, first = (n, 0) if n < 2 else (n // 2 + 1, n % 2 * EARLY * HDIM)
        start = pl.multiple_of((meta[Z] ^ k) * width + first, 128)
        for i, ref in enumerate((q_ref, k_ref, v_ref)):
            part = ref.at[:, pl.ds(start, out_ref.shape[2])]
            copies.append(pltpu.make_async_copy(part, out_ref.at[i], sems.at[3 * n + i]))
    run_all(copies)


def pack(meta, queries, keys_in, values, grad):
    rows, width = queries.shape
    part, early = width // 4, EARLY * HDIM
    shapes = [sds((3, rows, n), bf16) for n in (part, part, early, part - early, early, part - early)]
    shapes = [sds(grad.shape, bf16)] + shapes
    return pl.pallas_call(
        pack_kernel,
        out_shape=shapes,
        in_specs=[pl.BlockSpec(memory_space=pltpu.SMEM)] + [pl.BlockSpec(memory_space=pl.ANY)] * 4,
        out_specs=[pl.BlockSpec(memory_space=pltpu.VMEM)] * len(shapes),
        scratch_shapes=[pltpu.SemaphoreType.DMA((3 * len(shapes),))],
        compiler_params=params(),
        cost_estimate=NO_COST,
        name="pack_heads",
    )(meta, queries, keys_in, values, grad)


def token_pos(shape, dim, z, start=0):
    return (lax.broadcasted_iota(jnp.int32, shape, dim) + start) ^ (z * BLOCK)


def grad_attn_kernel(start, meta, *refs):
    *grads, w_ref, out_ref = refs
    grad = jnp.concatenate([g[...] for g in grads], axis=0)
    live = token_pos((grad.shape[0], 1), 0, meta[Z], start) < meta[COUNT]
    tile = 2 * HDIM

    for i in range(w_ref.shape[0] // tile):
        part = slice(i * tile, (i + 1) * tile)
        out_ref[:, part] = jnp.where(live, dot(grad, w_ref[part, :], 1, 1), 0.0).astype(bf16)


def grad_attn(meta, grads, weight, start):
    shape = (sum(g.shape[0] for g in grads), weight.shape[0])
    kernel = functools.partial(grad_attn_kernel, start)
    return whole(kernel, sds(shape, bf16), (meta, *grads, weight), "grad_attn", 1, 6)


def head_of(pieces, group, h):
    part = pieces[-1].shape[2]
    parts = []
    for p in pieces:
        start = (group * EARLY * HDIM if p.shape[2] > part else 0) + h * HDIM
        parts.append([p[i, :, start : start + HDIM] for i in range(3)])
    return (jnp.concatenate(x, axis=0) for x in zip(*parts))


def forward_kernel(group, meta, *refs):
    pieces, (weight_ref, inverse_ref, out_ref, heads_ref) = refs[:4], refs[-4:] if group else refs[4:8]
    bias_ref = refs[4] if group else refs[8]
    rows = pieces[0].shape[1]
    total = 4 * rows
    tile = 2 * rows
    to_power = math.log2(math.e) / math.sqrt(HDIM)
    query_live = token_pos((1, total), 1, meta[Z]) < meta[COUNT]
    if group == 0:
        key_live = token_pos((total, 1), 0, meta[Z]) < meta[COUNT]
        bias_ref[...] = jnp.where(key_live | ~query_live, 0.0, -jnp.inf)
    for h in range(pieces[-1].shape[2] // HDIM):
        cols = slice(h * HDIM, (h + 1) * HDIM)
        query, key, value = head_of(pieces, group, h)
        for t in range(2):
            part = slice(t * tile, (t + 1) * tile)
            scores = dot(key, query[part], 1, 1) + bias_ref[:, part]
            peak = jnp.max(scores, axis=0, keepdims=True)
            weights = jnp.exp2((scores - peak) * to_power).astype(bf16)
            weight_ref[h, :, part] = weights
            inverse = 1.0 / jnp.sum(weights.astype(f32), axis=0, keepdims=True)
            inverse_ref[h, :, part] = inverse
            heads = dot(value, weights, 0, 0) * inverse
            out_ref[cols, part] = heads
            heads_ref[cols, part] = jnp.where(query_live[:, part], heads, 0.0).astype(bf16)


def forward(meta, pieces, group, *bias):
    _, rows, width = pieces[-1].shape
    total = 4 * rows
    shapes = [
        sds((width // HDIM, total, total), bf16),
        sds((width // HDIM, 1, total), f32),
        sds((width, total), f32),
        sds((width, total), bf16),
    ] + ([] if bias else [sds((total, total), f32)])
    kernel = functools.partial(forward_kernel, group)
    return whole(kernel, shapes, (meta, *pieces, *bias), "attend_forward", 1, 8)


def span_gradients(query, key, value, grad, weights, inverse, outs):
    turned = grad.astype(f32).T
    row_delta = jnp.sum(outs * turned, axis=0, keepdims=True)
    grad_prob = dot(value, grad, 1, 1)
    factor = inverse * (1.0 / math.sqrt(HDIM))
    dscore = (weights.astype(f32) * ((grad_prob - row_delta) * factor)).astype(bf16)
    grad_query = dot(key, dscore, 0, 0).T.astype(bf16)
    grad_value = dot(weights, (turned * inverse).T.astype(bf16), 1, 0)
    return grad_query, dot(dscore, query, 1, 0), grad_value


def backward_early_kernel(*refs):
    pieces, (grad_ref, weight_ref, inverse_ref, out_ref, query_out, key_out, value_out) = refs[:4], refs[4:]
    early = grad_ref.shape[0]
    for h in range(pieces[-1].shape[2] // HDIM):
        cols = slice(h * HDIM, (h + 1) * HDIM)
        query, key, value = head_of(pieces, 0, h)
        grad_key = grad_value = 0.0
        for span in (slice(0, 2 * BLOCK), slice(2 * BLOCK, early)):
            grad_query, add_key, add_value = span_gradients(
                query[span], key, value, grad_ref[span, cols],
                weight_ref[h, :, span], inverse_ref[h, :, span], out_ref[cols, span],
            )
            query_out[span, cols] = grad_query
            grad_key += add_key
            grad_value += add_value
        key_out[:, cols] = grad_key
        value_out[:, cols] = grad_value


def backward_early(pieces, grad, saved):
    _, rows, part = pieces[-1].shape
    shapes = [sds((grad.shape[0], part), bf16), sds((4 * rows, part), f32), sds((4 * rows, part), f32)]
    return whole(backward_early_kernel, shapes, (*pieces, grad, *saved), "backward_early", 0, 8)


def backward_kernel(own, near, far2a, far3a, far2b, far3b, early_ref, late_ref, *refs):
    saved, done, backs = (refs[:3], refs[3:6]), refs[6:9], refs[9:]
    rows = own.shape[1]
    early, total = early_ref.shape[0], 4 * rows
    for n in range(own.shape[2] // HDIM):
        group, h = divmod(n, EARLY)
        query, key, value = head_of(((own, near, far2a, far3a), (own, near, far2b, far3b))[group], group, h)
        weight_ref, inverse_ref, out_ref = saved[group]
        here = slice(h * HDIM, (h + 1) * HDIM)
        cols = slice(n * HDIM, (n + 1) * HDIM)
        if group == 0:
            spans = ((slice(early, total), late_ref[:, cols]),)
            grad_key, grad_value = done[1][:, here], done[2][:, here]
            for k in range(early // rows):
                backs[k][0, :, cols] = done[0][k * rows : (k + 1) * rows, here]
        else:
            grad = jnp.concatenate([early_ref[:, cols], late_ref[:, cols]], axis=0)
            spans = [(slice(t, t + 2 * rows), grad[t : t + 2 * rows]) for t in (0, 2 * rows)]
            grad_key = grad_value = 0.0
        for span, grad in spans:
            grad_query, add_key, add_value = span_gradients(
                query[span], key, value, grad, weight_ref[h, :, span], inverse_ref[h, :, span], out_ref[here, span]
            )
            for k in range(span.start // rows, span.stop // rows):
                at = k * rows - span.start
                backs[k][0, :, cols] = grad_query[at : at + rows]
            grad_key += add_key
            grad_value += add_value
        for k in range(4):
            mine = slice(k * rows, (k + 1) * rows)
            backs[k][1, :, cols] = grad_key[mine].astype(bf16)
            backs[k][2, :, cols] = grad_value[mine].astype(bf16)


def backward(pieces, grads, saved, done):
    shapes = [sds(pieces[0].shape, bf16)] * 4
    return whole(backward_kernel, shapes, (*pieces, *grads, *saved, *done), "attend_backward", 0, 8)


LINE = HDIM // 8


def line_at(meta, head, other, j):
    at = head * HDIM + ((meta[CORE] ^ other) * 4 + (meta[CHIP] ^ j)) * LINE
    return pl.ds(pl.multiple_of(at, LINE), LINE)


def weight_kernel(meta, heads_a, heads_b, *refs):
    *grads, send_ref, keep_ref = refs
    width = heads_a.shape[0] + heads_b.shape[0]
    lines = []
    for other in (1, 0):
        for j in range(4):
            for ref in (heads_a, heads_b):
                lines += [ref[line_at(meta, h, other, j), :] for h in range(ref.shape[0] // HDIM)]
    lines = jnp.concatenate(lines, axis=0)
    tile = 4 * HDIM

    for i in range(send_ref.shape[1] // tile):
        part = slice(i * tile, (i + 1) * tile)
        product = dot(lines, jnp.concatenate([g[:, part] for g in grads], axis=0), 1, 0)
        send_ref[:, part] = product[: width // 2].astype(bf16)
        keep_ref[:, part] = product[width // 2 :]


def weight_halves(meta, heads, grads):
    shape = (sum(x.shape[0] for x in heads) // 2, grads[0].shape[1])
    return whole(weight_kernel, [sds(shape, bf16), sds(shape, f32)], (meta, *heads, *grads), "weight_halves", 1, 6)


def add_kernel(keep_ref, recv_ref, *outs):
    size = outs[0].shape[0]
    for j, out_ref in enumerate(outs):
        part = slice(j * size, (j + 1) * size)
        out_ref[...] = (keep_ref[part, :] + recv_ref[part, :].astype(f32)).astype(out_ref.dtype)


def add_parts(keep, recv):
    shape = (keep.shape[0] // 4, keep.shape[1])
    return whole(add_kernel, [sds(shape, f32)] + [sds(shape, bf16)] * 3, (keep, recv), "add_parts")


def total_kernel(scale, own_ref, r1, r2, r3, out_ref):
    total = own_ref[...] + r1[...].astype(f32) + r2[...].astype(f32) + r3[...].astype(f32)
    out_ref[...] = (total * scale).astype(bf16)


def total_of(own, recvs, scale):
    return whole(functools.partial(total_kernel, scale), sds(own.shape, bf16), (own, *recvs), "scene_mean")


def weight_copies(meta, parts, first, out_ref, sems):
    copies = []
    for p, ref in enumerate(parts, first):
        for h in range(ref.shape[0] // LINE):
            line = out_ref.at[line_at(meta, h, p // 4, p % 4), :]
            copies.append(pltpu.make_async_copy(ref.at[pl.ds(h * LINE, LINE), :], line, sems.at[len(copies)]))
    return copies


def head_copies(meta, pieces, outs, sems):
    copies = []
    for k, ref in pieces.items():
        width = ref.shape[2]
        start = pl.multiple_of((meta[Z] ^ k) * width, 128)
        for i, out_ref in enumerate(outs):
            part = out_ref.at[:, pl.ds(start, width)]
            copies.append(pltpu.make_async_copy(ref.at[i], part, sems.at[len(copies)]))
    return copies


def join(kernel, meta, parts, shapes, copies, name, outs=()):
    return pl.pallas_call(
        kernel,
        out_shape=shapes,
        in_specs=[pl.BlockSpec(memory_space=pltpu.SMEM)]
        + [pl.BlockSpec(memory_space=pltpu.VMEM)] * len(parts)
        + [pl.BlockSpec(memory_space=pl.ANY)] * len(outs),
        out_specs=[pl.BlockSpec(memory_space=pl.ANY)] * len(shapes),
        scratch_shapes=[pltpu.SemaphoreType.DMA((n,)) for n in copies],
        input_output_aliases={1 + len(parts) + i: i for i in range(len(outs))},
        compiler_params=params(),
        cost_estimate=NO_COST,
        name=name,
    )(meta, *parts, *outs)


def join_weight_kernel(meta, *refs):
    run_all(weight_copies(meta, refs[:4], 0, refs[4], refs[5]))


def join_weight(meta, near):
    size, outw = near[0].shape
    return join(join_weight_kernel, meta, near, [sds((8 * size, outw), bf16)], [4 * size // LINE], "join_weight")[0]


def join_heads_kernel(meta, own, back2, back3, *refs):
    run_all(head_copies(meta, {0: own, 2: back2, 3: back3}, refs[:3], refs[3]))


def join_heads(meta, own, back2, back3):
    _, rows, width = own.shape
    shapes = [sds((rows, 4 * width), bf16)] * 3
    return join(join_heads_kernel, meta, (own, back2, back3), shapes, [9], "join_heads")


def join_last_kernel(meta, *refs):
    far, back1, outs, sems = refs[:4], refs[4], refs[9:13], refs[13:]
    run_all(weight_copies(meta, far, 4, outs[3], sems[0]) + head_copies(meta, {1: back1}, outs[:3], sems[1]))


def join_last(meta, far, back1, outs):
    shapes = [sds(x.shape, x.dtype) for x in outs]
    return join(join_last_kernel, meta, (*far, back1), shapes, [4 * far[0].shape[0] // LINE, 3], "join_last", outs)


def dense_body(queries, keys_in, values, out_grad, out_weight, voxel_count):
    meta = jnp.stack([lax.axis_index("shard"), voxel_count[0], lax.axis_index("core"), lax.axis_index("chips")])
    meta = meta.astype(jnp.int32)

    def send(x, k, *earlier):
        return swap(after(x, *earlier) if earlier else x, "shard", 4, k)

    across = send(out_grad, 2)
    beside = send(out_grad, 1)
    mine, own, near1, far2a, far2b, far3a, far3b = pack(meta, queries, keys_in, values, out_grad)
    piece1 = send(near1, 1)
    piece3a = send(far3a, 3, beside)
    piece2a = send(far2a, 2, across)
    piece3b = send(far3b, 3, piece3a)
    piece2b = send(far2b, 2, piece2a)
    half = across.shape[0] // 2
    grad_early = grad_attn(meta, (mine, beside, across), out_weight, 0)
    corners = [send(across[:half], 1), send(after(across, piece1, grad_early)[half:], 1)]

    *saved_a, heads_a, bias = forward(meta, (own, piece1, piece2a, piece3a), 0)
    early = backward_early((own, piece1, piece2a, piece3a), grad_early, saved_a)
    heads_a, *early, piece2b, piece3b = lax.optimization_barrier((heads_a, *early, piece2b, piece3b))
    *saved_b, heads_b = forward(meta, (own, piece1, piece2b, piece3b), 1, bias)
    grad_early, heads_b, *corners = lax.optimization_barrier((grad_early, heads_b, *corners))
    grads = (mine, beside, across, *corners)

    out, keep = weight_halves(meta, (heads_a, heads_b), grads)
    recv = swap(out, "core", 2, 1)
    grad_late = grad_attn(meta, after(grads[3:], out), out_weight, 3 * BLOCK)
    pieces = (own, piece1, piece2a, piece3a, piece2b, piece3b)
    own0, *backs = backward(pieces, (grad_early, grad_late), (*saved_a, *saved_b), early)
    own_part, *sends = add_parts(after(keep, own0), recv)
    recvs = [swap(x, "chips", 4, j + 1) for j, x in enumerate(sends)]
    back3, back2 = send(backs[2], 3), send(backs[1], 2)
    done = total_of(own_part, recvs, 1.0 / 8)
    near = [done] + [swap(done, "chips", 4, j) for j in (1, 2, 3)]
    back1 = send(backs[0], 1, near[1])
    weight = join_weight(meta, near)
    weight, *near, back2, back3 = lax.optimization_barrier((weight, *near, back2, back3))
    far = [swap(x, "core", 2, 1) for x in near]
    heads = join_heads(meta, own0, back2, back3)
    return tuple(join_last(meta, far, back1, (*heads, weight)))


def attend_listed(queries, keys_in, values, block_ids, live_count):
    row_count, width_all = queries.shape
    head_count = width_all // HDIM
    block_count = row_count // BLOCK
    score_scale = 1.0 / math.sqrt(HDIM)
    query_blk = queries.reshape(block_count, BLOCK, head_count, HDIM)
    key_blk = keys_in.reshape(block_count, BLOCK, head_count, HDIM)[block_ids].reshape(
        block_count, NB * BLOCK, head_count, HDIM
    )
    value_blk = values.reshape(block_count, BLOCK, head_count, HDIM)[block_ids].reshape(
        block_count, NB * BLOCK, head_count, HDIM
    )
    query_pos = jnp.arange(row_count, dtype=jnp.int32).reshape(block_count, BLOCK)
    key_pos = (
        block_ids[:, :, None] * BLOCK + jnp.arange(BLOCK, dtype=jnp.int32)[None, None, :]
    ).reshape(block_count, NB * BLOCK)
    allowed = (key_pos[:, None, :] < live_count) | (query_pos[:, :, None] >= live_count)
    scores = (
        jnp.einsum("bqhd,bkhd->bhqk", query_blk, key_blk, preferred_element_type=jnp.float32)
        * score_scale
    )
    scores = jnp.where(allowed[:, None], scores, -jnp.inf)
    peak = jnp.max(scores, axis=-1, keepdims=True)
    weights = jnp.exp(scores - peak)
    probs = weights / jnp.sum(weights, axis=-1, keepdims=True)
    return (query_blk, key_blk, value_blk, probs)


def listed_body(queries, keys_in, values, out_grad, out_weight, block_lists, voxel_count):
    local_rows = queries.shape[0]
    live_count = voxel_count[0]
    block_ids = block_lists[0]
    positions = lax.axis_index("shard") * local_rows + jnp.arange(local_rows, dtype=jnp.int32)
    grad_live = jnp.where((positions < live_count)[:, None], out_grad, jnp.zeros_like(out_grad))
    query_head, key_head, value_head = (
        lax.all_to_all(queries, "shard", split_axis=1, concat_axis=0, tiled=True),
        lax.all_to_all(keys_in, "shard", split_axis=1, concat_axis=0, tiled=True),
        lax.all_to_all(values, "shard", split_axis=1, concat_axis=0, tiled=True),
    )
    row_count, width_all = query_head.shape
    head_count = width_all // HDIM
    block_count = row_count // BLOCK
    score_scale = 1.0 / math.sqrt(HDIM)
    query_blk, key_blk, value_blk, probs = attend_listed(
        query_head, key_head, value_head, block_ids, live_count
    )
    prob_bf = probs.astype(jnp.bfloat16)
    heads_out = (
        jnp.einsum("bhqk,bkhd->bqhd", prob_bf, value_blk, preferred_element_type=jnp.float32)
        .reshape(row_count, width_all)
        .astype(jnp.bfloat16)
    )
    row_piece = lax.all_gather(grad_live, "shard", axis=0, tiled=True)
    acc_now = jnp.einsum("rw,ro->wo", heads_out, row_piece, preferred_element_type=jnp.float32)
    product = jnp.einsum("ro,wo->rw", row_piece, out_weight, preferred_element_type=jnp.float32)
    grad_o = product.astype(jnp.bfloat16).reshape(block_count, BLOCK, head_count, HDIM)
    grad_prob = jnp.einsum("bqhd,bkhd->bhqk", grad_o, value_blk, preferred_element_type=jnp.float32)
    row_delta = jnp.sum(probs * grad_prob, axis=-1, keepdims=True)
    dscore = (probs * (grad_prob - row_delta) * score_scale).astype(jnp.bfloat16)
    grad_query = (
        jnp.einsum("bhqk,bkhd->bqhd", dscore, key_blk, preferred_element_type=jnp.float32)
        .reshape(row_count, width_all)
        .astype(jnp.bfloat16)
    )
    onehot = (
        block_ids[:, :, None] == jnp.arange(block_count, dtype=jnp.int32)[None, None, :]
    ).astype(jnp.float32)
    key_parts = jnp.einsum(
        "bhqk,bqhd->bkhd", dscore, query_blk, preferred_element_type=jnp.float32
    ).reshape(block_count, NB, BLOCK, width_all)
    value_parts = jnp.einsum(
        "bhqk,bqhd->bkhd", prob_bf, grad_o, preferred_element_type=jnp.float32
    ).reshape(block_count, NB, BLOCK, width_all)
    grad_key = (
        jnp.einsum("bjc,bjrx->crx", onehot, key_parts, precision=lax.Precision.HIGHEST)
        .reshape(row_count, width_all)
        .astype(jnp.bfloat16)
    )
    grad_value = (
        jnp.einsum("bjc,bjrx->crx", onehot, value_parts, precision=lax.Precision.HIGHEST)
        .reshape(row_count, width_all)
        .astype(jnp.bfloat16)
    )
    query_back, key_back, value_back = (
        lax.all_to_all(grad_query, "shard", split_axis=0, concat_axis=1, tiled=True),
        lax.all_to_all(grad_key, "shard", split_axis=0, concat_axis=1, tiled=True),
        lax.all_to_all(grad_value, "shard", split_axis=0, concat_axis=1, tiled=True),
    )
    scene_total = lax.axis_size(DP)
    summed = lax.psum(acc_now, DP)
    grad_weight = (summed / scene_total).astype(jnp.bfloat16)
    return (query_back, key_back, value_back, grad_weight)


def body(queries, keys_in, values, out_grad, out_weight, block_lists, voxel_count):
    dense = block_lists.shape[1] == NB and queries.shape[0] == BLOCK
    if dense and lax.axis_size("shard") == 4 and lax.axis_size("chips") == 4:
        return dense_body(queries, keys_in, values, out_grad, out_weight, voxel_count)
    return listed_body(queries, keys_in, values, out_grad, out_weight, block_lists, voxel_count)


def solution(mesh):
    chips = mesh.shape["dp"] // 2
    mesh = jax.sharding.Mesh(mesh.devices.reshape(chips, 2, -1), ("chips", "core", "shard"))
    return jax.shard_map(
        body,
        mesh=mesh,
        in_specs=(
            P((*DP, "shard"), None),
            P((*DP, "shard"), None),
            P((*DP, "shard"), None),
            P((*DP, "shard"), None),
            P("shard", None),
            P(DP, None, None),
            P(DP),
        ),
        out_specs=(
            P((*DP, "shard"), None),
            P((*DP, "shard"), None),
            P((*DP, "shard"), None),
            P("shard", None),
        ),
        check_vma=False,
    )
```

```python
import functools
import math

import jax
import jax.numpy as jnp
from jax import lax
from jax.experimental import pallas as pl
from jax.experimental.pallas import tpu as pltpu
from jax.sharding import PartitionSpec as P

HDIM = 128
BLOCK = 128
NB = 4
MIB = 1024 * 1024
DP = ("chips", "core")

Z, COUNT, CORE, CHIP = range(4)

EARLY = 3

NO_COST = pl.CostEstimate(flops=0, bytes_accessed=1024, transcendentals=0)

f32 = jnp.float32
bf16 = jnp.bfloat16


def dot(a, b, ca, cb):
    return lax.dot_general(a, b, (((ca,), (cb,)), ((), ())), preferred_element_type=f32)


def sds(shape, dtype):
    return jax.ShapeDtypeStruct(shape, dtype)


def params(mib=2):
    return pltpu.CompilerParams(vmem_limit_bytes=mib * MIB)


def swap(x, axis, size, flip):
    return lax.ppermute(x, axis, [(i, i ^ flip) for i in range(size)])


def after(x, *earlier):
    return lax.optimization_barrier((x, *earlier))[0]


def run_all(copies):
    for copy in copies:
        copy.start()
    for copy in copies:
        copy.wait()


def whole(kernel, out_shape, operands, name, scalars=0, mib=2, scratch=()):
    return pl.pallas_call(
        kernel,
        out_shape=out_shape,
        in_specs=[pl.BlockSpec(memory_space=pltpu.SMEM)] * scalars
        + [pl.BlockSpec(memory_space=pltpu.VMEM)] * (len(operands) - scalars),
        out_specs=jax.tree.map(lambda _: pl.BlockSpec(memory_space=pltpu.VMEM), out_shape),
        scratch_shapes=scratch,
        compiler_params=params(mib),
        cost_estimate=NO_COST,
        name=name,
    )(*operands)


def pack_kernel(meta, q_ref, k_ref, v_ref, grad_ref, mine_ref, *refs):
    *outs, sems = refs
    width = outs[0].shape[2]
    copies = [pltpu.make_async_copy(grad_ref, mine_ref, sems.at[3 * len(outs)])]
    for n, out_ref in enumerate(outs):
        k, first = (n, 0) if n < 2 else (n // 2 + 1, n % 2 * EARLY * HDIM)
        start = pl.multiple_of((meta[Z] ^ k) * width + first, 128)
        for i, ref in enumerate((q_ref, k_ref, v_ref)):
            part = ref.at[:, pl.ds(start, out_ref.shape[2])]
            copies.append(pltpu.make_async_copy(part, out_ref.at[i], sems.at[3 * n + i]))
    run_all(copies)


def pack(meta, queries, keys_in, values, grad):
    rows, width = queries.shape
    part, early = width // 4, EARLY * HDIM
    shapes = [sds((3, rows, n), bf16) for n in (part, part, early, part - early, early, part - early)]
    shapes = [sds(grad.shape, bf16)] + shapes
    return pl.pallas_call(
        pack_kernel,
        out_shape=shapes,
        in_specs=[pl.BlockSpec(memory_space=pltpu.SMEM)] + [pl.BlockSpec(memory_space=pl.ANY)] * 4,
        out_specs=[pl.BlockSpec(memory_space=pltpu.VMEM)] * len(shapes),
        scratch_shapes=[pltpu.SemaphoreType.DMA((3 * len(shapes),))],
        compiler_params=params(),
        cost_estimate=NO_COST,
        name="pack_heads",
    )(meta, queries, keys_in, values, grad)


def token_pos(shape, dim, z, start=0):
    return (lax.broadcasted_iota(jnp.int32, shape, dim) + start) ^ (z * BLOCK)


def grad_attn_kernel(start, meta, *refs):
    *grads, w_ref, out_ref = refs
    grad = jnp.concatenate([g[...] for g in grads], axis=0)
    live = token_pos((grad.shape[0], 1), 0, meta[Z], start) < meta[COUNT]
    tile = 2 * HDIM

    for i in range(w_ref.shape[0] // tile):
        part = slice(i * tile, (i + 1) * tile)
        out_ref[:, part] = jnp.where(live, dot(grad, w_ref[part, :], 1, 1), 0.0).astype(bf16)


def grad_attn(meta, grads, weight, start):
    shape = (sum(g.shape[0] for g in grads), weight.shape[0])
    kernel = functools.partial(grad_attn_kernel, start)
    return whole(kernel, sds(shape, bf16), (meta, *grads, weight), "grad_attn", 1, 6)


def head_of(pieces, group, h):
    part = pieces[-1].shape[2]
    parts = []
    for p in pieces:
        start = (group * EARLY * HDIM if p.shape[2] > part else 0) + h * HDIM
        parts.append([p[i, :, start : start + HDIM] for i in range(3)])
    return (jnp.concatenate(x, axis=0) for x in zip(*parts))


def forward_kernel(group, meta, *refs):
    pieces, (weight_ref, inverse_ref, out_ref, heads_ref) = refs[:4], refs[-4:] if group else refs[4:8]
    bias_ref = refs[4] if group else refs[8]
    rows = pieces[0].shape[1]
    total = 4 * rows
    tile = 2 * rows
    to_power = math.log2(math.e) / math.sqrt(HDIM)
    query_live = token_pos((1, total), 1, meta[Z]) < meta[COUNT]
    if group == 0:
        key_live = token_pos((total, 1), 0, meta[Z]) < meta[COUNT]
        bias_ref[...] = jnp.where(key_live | ~query_live, 0.0, -jnp.inf)
    for h in range(pieces[-1].shape[2] // HDIM):
        cols = slice(h * HDIM, (h + 1) * HDIM)
        query, key, value = head_of(pieces, group, h)
        for t in range(2):
            part = slice(t * tile, (t + 1) * tile)
            scores = dot(key, query[part], 1, 1) + bias_ref[:, part]
            peak = jnp.max(scores, axis=0, keepdims=True)
            weights = jnp.exp2((scores - peak) * to_power).astype(bf16)
            weight_ref[h, :, part] = weights
            inverse = 1.0 / jnp.sum(weights.astype(f32), axis=0, keepdims=True)
            inverse_ref[h, :, part] = inverse
            heads = dot(value, weights, 0, 0) * inverse
            out_ref[cols, part] = heads
            heads_ref[cols, part] = jnp.where(query_live[:, part], heads, 0.0).astype(bf16)


def forward(meta, pieces, group, *bias):
    _, rows, width = pieces[-1].shape
    total = 4 * rows
    shapes = [
        sds((width // HDIM, total, total), bf16),
        sds((width // HDIM, 1, total), f32),
        sds((width, total), f32),
        sds((width, total), bf16),
    ] + ([] if bias else [sds((total, total), f32)])
    kernel = functools.partial(forward_kernel, group)
    return whole(kernel, shapes, (meta, *pieces, *bias), "attend_forward", 1, 8)


def span_gradients(query, key, value, grad, weights, inverse, outs):
    turned = grad.astype(f32).T
    row_delta = jnp.sum(outs * turned, axis=0, keepdims=True)
    grad_prob = dot(value, grad, 1, 1)
    factor = inverse * (1.0 / math.sqrt(HDIM))
    dscore = (weights.astype(f32) * ((grad_prob - row_delta) * factor)).astype(bf16)
    grad_query = dot(key, dscore, 0, 0).T.astype(bf16)
    grad_value = dot(weights, (turned * inverse).T.astype(bf16), 1, 0)
    return grad_query, dot(dscore, query, 1, 0), grad_value


def backward_early_kernel(*refs):
    pieces, (grad_ref, weight_ref, inverse_ref, out_ref, query_out, key_out, value_out) = refs[:4], refs[4:]
    early = grad_ref.shape[0]
    for h in range(pieces[-1].shape[2] // HDIM):
        cols = slice(h * HDIM, (h + 1) * HDIM)
        query, key, value = head_of(pieces, 0, h)
        grad_key = grad_value = 0.0
        for span in (slice(0, 2 * BLOCK), slice(2 * BLOCK, early)):
            grad_query, add_key, add_value = span_gradients(
                query[span], key, value, grad_ref[span, cols],
                weight_ref[h, :, span], inverse_ref[h, :, span], out_ref[cols, span],
            )
            query_out[span, cols] = grad_query
            grad_key += add_key
            grad_value += add_value
        key_out[:, cols] = grad_key
        value_out[:, cols] = grad_value


def backward_early(pieces, grad, saved):
    _, rows, part = pieces[-1].shape
    shapes = [sds((grad.shape[0], part), bf16), sds((4 * rows, part), f32), sds((4 * rows, part), f32)]
    return whole(backward_early_kernel, shapes, (*pieces, grad, *saved), "backward_early", 0, 8)


def backward_kernel(own, near, far2a, far3a, far2b, far3b, early_ref, late_ref, *refs):
    saved, done, backs = (refs[:3], refs[3:6]), refs[6:9], refs[9:]
    rows = own.shape[1]
    early, total = early_ref.shape[0], 4 * rows
    for n in range(own.shape[2] // HDIM):
        group, h = divmod(n, EARLY)
        query, key, value = head_of(((own, near, far2a, far3a), (own, near, far2b, far3b))[group], group, h)
        weight_ref, inverse_ref, out_ref = saved[group]
        here = slice(h * HDIM, (h + 1) * HDIM)
        cols = slice(n * HDIM, (n + 1) * HDIM)
        if group == 0:
            spans = ((slice(early, total), late_ref[:, cols]),)
            grad_key, grad_value = done[1][:, here], done[2][:, here]
            for k in range(early // rows):
                backs[k][0, :, cols] = done[0][k * rows : (k + 1) * rows, here]
        else:
            grad = jnp.concatenate([early_ref[:, cols], late_ref[:, cols]], axis=0)
            spans = [(slice(t, t + 2 * rows), grad[t : t + 2 * rows]) for t in (0, 2 * rows)]
            grad_key = grad_value = 0.0
        for span, grad in spans:
            grad_query, add_key, add_value = span_gradients(
                query[span], key, value, grad, weight_ref[h, :, span], inverse_ref[h, :, span], out_ref[here, span]
            )
            for k in range(span.start // rows, span.stop // rows):
                at = k * rows - span.start
                backs[k][0, :, cols] = grad_query[at : at + rows]
            grad_key += add_key
            grad_value += add_value
        for k in range(4):
            mine = slice(k * rows, (k + 1) * rows)
            backs[k][1, :, cols] = grad_key[mine].astype(bf16)
            backs[k][2, :, cols] = grad_value[mine].astype(bf16)


def backward(pieces, grads, saved, done):
    shapes = [sds(pieces[0].shape, bf16)] * 4
    return whole(backward_kernel, shapes, (*pieces, *grads, *saved, *done), "attend_backward", 0, 8)


LINE = HDIM // 8
WIDE = 14 * HDIM


def line_at(meta, head, other, j):
    at = head * HDIM + ((meta[CORE] ^ other) * 4 + (meta[CHIP] ^ j)) * LINE
    return pl.ds(pl.multiple_of(at, LINE), LINE)


def weight_kernel(meta, heads_a, heads_b, *refs):
    *grads, send_ref, keep_ref = refs
    width = heads_a.shape[0] + heads_b.shape[0]
    lines = []
    for other in (1, 0):
        for j in range(4):
            for ref in (heads_a, heads_b):
                lines += [ref[line_at(meta, h, other, j), :] for h in range(ref.shape[0] // HDIM)]
    lines = jnp.concatenate(lines, axis=0)
    tile = 4 * HDIM

    for i in range(send_ref.shape[1] // tile):
        part = slice(i * tile, (i + 1) * tile)
        product = dot(lines, jnp.concatenate([g[:, part] for g in grads], axis=0), 1, 0)
        send_ref[:, part] = product[: width // 2].astype(bf16)
        keep_ref[:, part] = product[width // 2 :]


def weight_halves(meta, heads, grads):
    shape = (sum(x.shape[0] for x in heads) // 2, grads[0].shape[1])
    return whole(weight_kernel, [sds(shape, bf16), sds(shape, f32)], (meta, *heads, *grads), "weight_halves", 1, 6)


def add_kernel(keep_ref, recv_ref, *outs):
    size = outs[0].shape[0]
    for j, out_ref in enumerate(outs):
        part = slice(j * size, (j + 1) * size)
        out_ref[...] = (keep_ref[part, :] + recv_ref[part, :].astype(f32)).astype(out_ref.dtype)


def add_parts(keep, recv):
    shape = (keep.shape[0] // 4, keep.shape[1])
    return whole(add_kernel, [sds(shape, f32)] + [sds(shape, bf16)] * 3, (keep, recv), "add_parts")


def total_kernel(scale, own_ref, r1, r2, r3, out_ref, wide_ref, rest_ref):
    total = own_ref[...] + r1[...].astype(f32) + r2[...].astype(f32) + r3[...].astype(f32)
    total = (total * scale).astype(bf16)
    out_ref[...] = total
    wide_ref[...] = total[:, :WIDE].astype(f32)
    rest_ref[...] = total[:, WIDE:]


def total_of(own, recvs, scale):
    rows, outw = own.shape
    shapes = [sds(own.shape, bf16), sds((rows, WIDE), f32), sds((rows, outw - WIDE), bf16)]
    return whole(functools.partial(total_kernel, scale), shapes, (own, *recvs), "scene_mean")


def weight_copies(meta, parts, first, out_ref, sems, start=0):
    copies = []
    for p, ref in enumerate(parts, first):
        for h in range(ref.shape[0] // LINE):
            line = out_ref.at[line_at(meta, h, p // 4, p % 4), pl.ds(start, ref.shape[1])]
            copies.append(pltpu.make_async_copy(ref.at[pl.ds(h * LINE, LINE), :], line, sems.at[len(copies)]))
    return copies


def head_copies(meta, pieces, outs, sems):
    copies = []
    for k, ref in pieces.items():
        width = ref.shape[2]
        start = pl.multiple_of((meta[Z] ^ k) * width, 128)
        for i, out_ref in enumerate(outs):
            part = out_ref.at[:, pl.ds(start, width)]
            copies.append(pltpu.make_async_copy(ref.at[i], part, sems.at[len(copies)]))
    return copies


def join_kernel(meta, *refs):
    near, (wide, rest), far, pieces = refs[:4], refs[4:6], refs[6:9], refs[9:13]
    outs, weight, narrow, sems = refs[13:16], refs[16], refs[17], refs[18:]
    copies = weight_copies(meta, near, 0, weight, sems[0]) + weight_copies(meta, far, 5, weight, sems[1])
    copies += weight_copies(meta, (rest,), 4, weight, sems[2], WIDE)
    copies += head_copies(meta, dict(enumerate(pieces)), outs, sems[3])
    for copy in copies:
        copy.start()
    narrow[...] = wide[...].astype(bf16)
    run_all(weight_copies(meta, (narrow,), 4, weight, sems[4]))
    for copy in copies:
        copy.wait()


def join(meta, near, far, pieces):
    size, outw = near[0].shape
    _, rows, width = pieces[0].shape
    parts = (*near, *far, *pieces)
    lines = size // LINE
    return pl.pallas_call(
        join_kernel,
        out_shape=[sds((rows, 4 * width), bf16)] * 3 + [sds((8 * size, outw), bf16)],
        in_specs=[pl.BlockSpec(memory_space=pltpu.SMEM)] + [pl.BlockSpec(memory_space=pltpu.VMEM)] * len(parts),
        out_specs=[pl.BlockSpec(memory_space=pl.ANY)] * 4,
        scratch_shapes=[pltpu.VMEM(far[0].shape, bf16)]
        + [pltpu.SemaphoreType.DMA((n,)) for n in (4 * lines, 3 * lines, lines, 12, lines)],
        compiler_params=params(),
        cost_estimate=NO_COST,
        name="join",
    )(meta, *parts)


def dense_body(queries, keys_in, values, out_grad, out_weight, voxel_count):
    meta = jnp.stack([lax.axis_index("shard"), voxel_count[0], lax.axis_index("core"), lax.axis_index("chips")])
    meta = meta.astype(jnp.int32)

    def send(x, k, *earlier):
        return swap(after(x, *earlier) if earlier else x, "shard", 4, k)

    across = send(out_grad, 2)
    beside = send(out_grad, 1)
    mine, own, near1, far2a, far2b, far3a, far3b = pack(meta, queries, keys_in, values, out_grad)
    piece1 = send(near1, 1)
    piece3a = send(far3a, 3, beside)
    piece2a = send(far2a, 2, across)
    piece3b = send(far3b, 3, piece3a)
    piece2b = send(far2b, 2, piece2a)
    half = across.shape[0] // 2
    grad_early = grad_attn(meta, (mine, beside, across), out_weight, 0)
    corners = [send(across[:half], 1), send(after(across, piece1, grad_early)[half:], 1)]

    *saved_a, heads_a, bias = forward(meta, (own, piece1, piece2a, piece3a), 0)
    early = backward_early((own, piece1, piece2a, piece3a), grad_early, saved_a)
    heads_a, *early, piece2b, piece3b = lax.optimization_barrier((heads_a, *early, piece2b, piece3b))
    *saved_b, heads_b = forward(meta, (own, piece1, piece2b, piece3b), 1, bias)
    grad_early, heads_b, *corners = lax.optimization_barrier((grad_early, heads_b, *corners))
    grads = (mine, beside, across, *corners)

    out, keep = weight_halves(meta, (heads_a, heads_b), grads)
    recv = swap(out, "core", 2, 1)
    grad_late = grad_attn(meta, after(grads[3:], out), out_weight, 3 * BLOCK)
    pieces = (own, piece1, piece2a, piece3a, piece2b, piece3b)
    own0, *backs = backward(pieces, (grad_early, grad_late), (*saved_a, *saved_b), early)
    own_part, *sends = add_parts(after(keep, own0), recv)
    recvs = [swap(x, "chips", 4, j + 1) for j, x in enumerate(sends)]
    back3, back2, back1 = (send(backs[k - 1], k) for k in (3, 2, 1))
    done, wide, rest = total_of(own_part, recvs, 1.0 / 8)
    after_near = after(done, back1)
    near = [swap(after_near if j == 3 else done, "chips", 4, j) for j in (1, 2, 3)]

    wide, back2, back3 = lax.optimization_barrier((wide, back2, back3))
    far = [swap(x, "core", 2, 1) for x in (wide, rest, *near)]
    return tuple(join(meta, (done, *near), far, (own0, back1, back2, back3)))


def attend_listed(queries, keys_in, values, block_ids, live_count):
    row_count, width_all = queries.shape
    head_count = width_all // HDIM
    block_count = row_count // BLOCK
    score_scale = 1.0 / math.sqrt(HDIM)
    query_blk = queries.reshape(block_count, BLOCK, head_count, HDIM)
    key_blk = keys_in.reshape(block_count, BLOCK, head_count, HDIM)[block_ids].reshape(
        block_count, NB * BLOCK, head_count, HDIM
    )
    value_blk = values.reshape(block_count, BLOCK, head_count, HDIM)[block_ids].reshape(
        block_count, NB * BLOCK, head_count, HDIM
    )
    query_pos = jnp.arange(row_count, dtype=jnp.int32).reshape(block_count, BLOCK)
    key_pos = (
        block_ids[:, :, None] * BLOCK + jnp.arange(BLOCK, dtype=jnp.int32)[None, None, :]
    ).reshape(block_count, NB * BLOCK)
    allowed = (key_pos[:, None, :] < live_count) | (query_pos[:, :, None] >= live_count)
    scores = (
        jnp.einsum("bqhd,bkhd->bhqk", query_blk, key_blk, preferred_element_type=jnp.float32)
        * score_scale
    )
    scores = jnp.where(allowed[:, None], scores, -jnp.inf)
    peak = jnp.max(scores, axis=-1, keepdims=True)
    weights = jnp.exp(scores - peak)
    probs = weights / jnp.sum(weights, axis=-1, keepdims=True)
    return (query_blk, key_blk, value_blk, probs)


def listed_body(queries, keys_in, values, out_grad, out_weight, block_lists, voxel_count):
    local_rows = queries.shape[0]
    live_count = voxel_count[0]
    block_ids = block_lists[0]
    positions = lax.axis_index("shard") * local_rows + jnp.arange(local_rows, dtype=jnp.int32)
    grad_live = jnp.where((positions < live_count)[:, None], out_grad, jnp.zeros_like(out_grad))
    query_head, key_head, value_head = (
        lax.all_to_all(queries, "shard", split_axis=1, concat_axis=0, tiled=True),
        lax.all_to_all(keys_in, "shard", split_axis=1, concat_axis=0, tiled=True),
        lax.all_to_all(values, "shard", split_axis=1, concat_axis=0, tiled=True),
    )
    row_count, width_all = query_head.shape
    head_count = width_all // HDIM
    block_count = row_count // BLOCK
    score_scale = 1.0 / math.sqrt(HDIM)
    query_blk, key_blk, value_blk, probs = attend_listed(
        query_head, key_head, value_head, block_ids, live_count
    )
    prob_bf = probs.astype(jnp.bfloat16)
    heads_out = (
        jnp.einsum("bhqk,bkhd->bqhd", prob_bf, value_blk, preferred_element_type=jnp.float32)
        .reshape(row_count, width_all)
        .astype(jnp.bfloat16)
    )
    row_piece = lax.all_gather(grad_live, "shard", axis=0, tiled=True)
    acc_now = jnp.einsum("rw,ro->wo", heads_out, row_piece, preferred_element_type=jnp.float32)
    product = jnp.einsum("ro,wo->rw", row_piece, out_weight, preferred_element_type=jnp.float32)
    grad_o = product.astype(jnp.bfloat16).reshape(block_count, BLOCK, head_count, HDIM)
    grad_prob = jnp.einsum("bqhd,bkhd->bhqk", grad_o, value_blk, preferred_element_type=jnp.float32)
    row_delta = jnp.sum(probs * grad_prob, axis=-1, keepdims=True)
    dscore = (probs * (grad_prob - row_delta) * score_scale).astype(jnp.bfloat16)
    grad_query = (
        jnp.einsum("bhqk,bkhd->bqhd", dscore, key_blk, preferred_element_type=jnp.float32)
        .reshape(row_count, width_all)
        .astype(jnp.bfloat16)
    )
    onehot = (
        block_ids[:, :, None] == jnp.arange(block_count, dtype=jnp.int32)[None, None, :]
    ).astype(jnp.float32)
    key_parts = jnp.einsum(
        "bhqk,bqhd->bkhd", dscore, query_blk, preferred_element_type=jnp.float32
    ).reshape(block_count, NB, BLOCK, width_all)
    value_parts = jnp.einsum(
        "bhqk,bqhd->bkhd", prob_bf, grad_o, preferred_element_type=jnp.float32
    ).reshape(block_count, NB, BLOCK, width_all)
    grad_key = (
        jnp.einsum("bjc,bjrx->crx", onehot, key_parts, precision=lax.Precision.HIGHEST)
        .reshape(row_count, width_all)
        .astype(jnp.bfloat16)
    )
    grad_value = (
        jnp.einsum("bjc,bjrx->crx", onehot, value_parts, precision=lax.Precision.HIGHEST)
        .reshape(row_count, width_all)
        .astype(jnp.bfloat16)
    )
    query_back, key_back, value_back = (
        lax.all_to_all(grad_query, "shard", split_axis=0, concat_axis=1, tiled=True),
        lax.all_to_all(grad_key, "shard", split_axis=0, concat_axis=1, tiled=True),
        lax.all_to_all(grad_value, "shard", split_axis=0, concat_axis=1, tiled=True),
    )
    scene_total = lax.axis_size(DP)
    summed = lax.psum(acc_now, DP)
    grad_weight = (summed / scene_total).astype(jnp.bfloat16)
    return (query_back, key_back, value_back, grad_weight)


def body(queries, keys_in, values, out_grad, out_weight, block_lists, voxel_count):
    dense = block_lists.shape[1] == NB and queries.shape[0] == BLOCK
    if dense and lax.axis_size("shard") == 4 and lax.axis_size("chips") == 4:
        return dense_body(queries, keys_in, values, out_grad, out_weight, voxel_count)
    return listed_body(queries, keys_in, values, out_grad, out_weight, block_lists, voxel_count)


def solution(mesh):
    chips = mesh.shape["dp"] // 2
    mesh = jax.sharding.Mesh(mesh.devices.reshape(chips, 2, -1), ("chips", "core", "shard"))
    return jax.shard_map(
        body,
        mesh=mesh,
        in_specs=(
            P((*DP, "shard"), None),
            P((*DP, "shard"), None),
            P((*DP, "shard"), None),
            P((*DP, "shard"), None),
            P("shard", None),
            P(DP, None, None),
            P(DP),
        ),
        out_specs=(
            P((*DP, "shard"), None),
            P((*DP, "shard"), None),
            P((*DP, "shard"), None),
            P("shard", None),
        ),
        check_vma=False,
    )
```

```python
import functools
import math

import jax
import jax.numpy as jnp
from jax import lax
from jax.experimental import pallas as pl
from jax.experimental.pallas import tpu as pltpu
from jax.sharding import PartitionSpec as P

HDIM = 128
BLOCK = 128
NB = 4
MIB = 1024 * 1024
DP = ("chips", "core")

Z, COUNT, CORE, CHIP = range(4)

EARLY = 3

NO_COST = pl.CostEstimate(flops=0, bytes_accessed=1024, transcendentals=0)

f32 = jnp.float32
bf16 = jnp.bfloat16


def dot(a, b, ca, cb):
    return lax.dot_general(a, b, (((ca,), (cb,)), ((), ())), preferred_element_type=f32)


def sds(shape, dtype):
    return jax.ShapeDtypeStruct(shape, dtype)


def params(mib=2):
    return pltpu.CompilerParams(vmem_limit_bytes=mib * MIB)


def swap(x, axis, size, flip):
    return lax.ppermute(x, axis, [(i, i ^ flip) for i in range(size)])


def after(x, *earlier):
    return lax.optimization_barrier((x, *earlier))[0]


def run_all(copies):
    for copy in copies:
        copy.start()
    for copy in copies:
        copy.wait()


def whole(kernel, out_shape, operands, name, scalars=0, mib=2, scratch=()):
    return pl.pallas_call(
        kernel,
        out_shape=out_shape,
        in_specs=[pl.BlockSpec(memory_space=pltpu.SMEM)] * scalars
        + [pl.BlockSpec(memory_space=pltpu.VMEM)] * (len(operands) - scalars),
        out_specs=jax.tree.map(lambda _: pl.BlockSpec(memory_space=pltpu.VMEM), out_shape),
        scratch_shapes=scratch,
        compiler_params=params(mib),
        cost_estimate=NO_COST,
        name=name,
    )(*operands)


def pack_kernel(meta, q_ref, k_ref, v_ref, grad_ref, mine_ref, *refs):
    *outs, sems = refs
    width = outs[0].shape[2]
    copies = [pltpu.make_async_copy(grad_ref, mine_ref, sems.at[3 * len(outs)])]
    for n, out_ref in enumerate(outs):
        k, first = (n, 0) if n < 2 else (n // 2 + 1, n % 2 * EARLY * HDIM)
        start = pl.multiple_of((meta[Z] ^ k) * width + first, 128)
        for i, ref in enumerate((q_ref, k_ref, v_ref)):
            part = ref.at[:, pl.ds(start, out_ref.shape[2])]
            copies.append(pltpu.make_async_copy(part, out_ref.at[i], sems.at[3 * n + i]))
    run_all(copies)


def pack(meta, queries, keys_in, values, grad):
    rows, width = queries.shape
    part, early = width // 4, EARLY * HDIM
    shapes = [sds((3, rows, n), bf16) for n in (part, part, early, part - early, early, part - early)]
    shapes = [sds(grad.shape, bf16)] + shapes
    return pl.pallas_call(
        pack_kernel,
        out_shape=shapes,
        in_specs=[pl.BlockSpec(memory_space=pltpu.SMEM)] + [pl.BlockSpec(memory_space=pl.ANY)] * 4,
        out_specs=[pl.BlockSpec(memory_space=pltpu.VMEM)] * len(shapes),
        scratch_shapes=[pltpu.SemaphoreType.DMA((3 * len(shapes),))],
        compiler_params=params(),
        cost_estimate=NO_COST,
        name="pack_heads",
    )(meta, queries, keys_in, values, grad)


def token_pos(shape, dim, z, start=0):
    return (lax.broadcasted_iota(jnp.int32, shape, dim) + start) ^ (z * BLOCK)


def grad_attn_kernel(start, meta, *refs):
    *grads, w_ref, out_ref = refs
    grad = jnp.concatenate([g[...] for g in grads], axis=0)
    live = token_pos((grad.shape[0], 1), 0, meta[Z], start) < meta[COUNT]
    tile = 2 * HDIM

    for i in range(w_ref.shape[0] // tile):
        part = slice(i * tile, (i + 1) * tile)
        out_ref[:, part] = jnp.where(live, dot(grad, w_ref[part, :], 1, 1), 0.0).astype(bf16)


def grad_attn(meta, grads, weight, start):
    shape = (sum(g.shape[0] for g in grads), weight.shape[0])
    kernel = functools.partial(grad_attn_kernel, start)
    return whole(kernel, sds(shape, bf16), (meta, *grads, weight), "grad_attn", 1, 6)


def head_of(pieces, group, h):
    part = pieces[-1].shape[2]
    parts = []
    for p in pieces:
        start = (group * EARLY * HDIM if p.shape[2] > part else 0) + h * HDIM
        parts.append([p[i, :, start : start + HDIM] for i in range(3)])
    return (jnp.concatenate(x, axis=0) for x in zip(*parts))


def span_forward(query, key, value, bias, live, weight_ref, inverse_ref, out_ref, heads_ref, h, span):
    cols = slice(h * HDIM, (h + 1) * HDIM)
    scores = dot(key, query[span], 1, 1) + bias
    peak = jnp.max(scores, axis=0, keepdims=True)
    weights = jnp.exp2((scores - peak) * (math.log2(math.e) / math.sqrt(HDIM))).astype(bf16)
    weight_ref[h, :, span] = weights
    inverse = 1.0 / jnp.sum(weights.astype(f32), axis=0, keepdims=True)
    inverse_ref[h, :, span] = inverse
    heads = dot(value, weights, 0, 0) * inverse
    out_ref[cols, span] = heads
    heads_ref[cols, span] = jnp.where(live, heads, 0.0).astype(bf16)


def forward_shapes(pieces):
    _, rows, width = pieces[-1].shape
    total = 4 * rows
    return [
        sds((width // HDIM, total, total), bf16),
        sds((width // HDIM, 1, total), f32),
        sds((width, total), f32),
        sds((width, total), bf16),
    ]


def forward_kernel(meta, p0, p1, p2, p3, weight_ref, inverse_ref, out_ref, heads_ref, bias_ref):
    pieces = (p0, p1, p2, p3)
    rows = p0.shape[1]
    total = 4 * rows
    query_live = token_pos((1, total), 1, meta[Z]) < meta[COUNT]
    key_live = token_pos((total, 1), 0, meta[Z]) < meta[COUNT]
    bias_ref[...] = jnp.where(key_live | ~query_live, 0.0, -jnp.inf)
    for h in range(p3.shape[2] // HDIM):
        query, key, value = head_of(pieces, 0, h)
        for t in range(2):
            span = slice(2 * rows * t, 2 * rows * (t + 1))
            outs = (weight_ref, inverse_ref, out_ref, heads_ref, h, span)
            span_forward(query, key, value, bias_ref[:, span], query_live[:, span], *outs)


def forward(meta, pieces):
    total = 4 * pieces[-1].shape[1]
    shapes = forward_shapes(pieces) + [sds((total, total), f32)]
    return whole(forward_kernel, shapes, (meta, *pieces), "attend_forward", 1, 8)


def span_gradients(query, key, value, grad, weights, inverse, outs):
    turned = grad.astype(f32).T
    row_delta = jnp.sum(outs * turned, axis=0, keepdims=True)
    grad_prob = dot(value, grad, 1, 1)
    factor = inverse * (1.0 / math.sqrt(HDIM))
    dscore = (weights.astype(f32) * ((grad_prob - row_delta) * factor)).astype(bf16)
    grad_query = dot(key, dscore, 0, 0).T.astype(bf16)
    grad_value = dot(weights, (turned * inverse).T.astype(bf16), 1, 0)
    return grad_query, dot(dscore, query, 1, 0), grad_value


def backward_early_kernel(*refs):
    pieces, (grad_ref, weight_ref, inverse_ref, out_ref, query_out, key_out, value_out) = refs[:4], refs[4:]
    early = grad_ref.shape[0]
    for h in range(pieces[-1].shape[2] // HDIM):
        cols = slice(h * HDIM, (h + 1) * HDIM)
        query, key, value = head_of(pieces, 0, h)
        grad_key = grad_value = 0.0
        for span in (slice(0, 2 * BLOCK), slice(2 * BLOCK, early)):
            grad_query, add_key, add_value = span_gradients(
                query[span], key, value, grad_ref[span, cols],
                weight_ref[h, :, span], inverse_ref[h, :, span], out_ref[cols, span],
            )
            query_out[span, cols] = grad_query
            grad_key += add_key
            grad_value += add_value
        key_out[:, cols] = grad_key
        value_out[:, cols] = grad_value


def backward_early(pieces, grad, saved):
    _, rows, part = pieces[-1].shape
    shapes = [sds((grad.shape[0], part), bf16), sds((4 * rows, part), f32), sds((4 * rows, part), f32)]
    return whole(backward_early_kernel, shapes, (*pieces, grad, *saved), "backward_early", 0, 8)


def backward_kernel(own, near, far2a, far3a, far2b, far3b, early_ref, late_ref, *refs):
    saved, done, backs = (refs[:3], refs[3:6]), refs[6:9], refs[9:]
    rows = own.shape[1]
    early, total = early_ref.shape[0], 4 * rows
    for n in range(own.shape[2] // HDIM):
        group, h = divmod(n, EARLY)
        query, key, value = head_of(((own, near, far2a, far3a), (own, near, far2b, far3b))[group], group, h)
        weight_ref, inverse_ref, out_ref = saved[group]
        here = slice(h * HDIM, (h + 1) * HDIM)
        cols = slice(n * HDIM, (n + 1) * HDIM)
        if group == 0:
            spans = ((slice(early, total), late_ref[:, cols]),)
            grad_key, grad_value = done[1][:, here], done[2][:, here]
            for k in range(early // rows):
                backs[k][0, :, cols] = done[0][k * rows : (k + 1) * rows, here]
        else:
            grad = jnp.concatenate([early_ref[:, cols], late_ref[:, cols]], axis=0)
            spans = [(slice(t, t + 2 * rows), grad[t : t + 2 * rows]) for t in (0, 2 * rows)]
            grad_key = grad_value = 0.0
        for span, grad in spans:
            grad_query, add_key, add_value = span_gradients(
                query[span], key, value, grad, weight_ref[h, :, span], inverse_ref[h, :, span], out_ref[here, span]
            )
            for k in range(span.start // rows, span.stop // rows):
                at = k * rows - span.start
                backs[k][0, :, cols] = grad_query[at : at + rows]
            grad_key += add_key
            grad_value += add_value
        for k in range(4):
            mine = slice(k * rows, (k + 1) * rows)
            backs[k][1, :, cols] = grad_key[mine].astype(bf16)
            backs[k][2, :, cols] = grad_value[mine].astype(bf16)


def backward(pieces, grads, saved, done):
    shapes = [sds(pieces[0].shape, bf16)] * 4
    return whole(backward_kernel, shapes, (*pieces, *grads, *saved, *done), "attend_backward", 0, 8)


LINE = HDIM // 8


def line_at(meta, head, other, j):
    at = head * HDIM + ((meta[CORE] ^ other) * 4 + (meta[CHIP] ^ j)) * LINE
    return pl.ds(pl.multiple_of(at, LINE), LINE)


def lines_of(meta, heads_ref):
    lines = []
    for other in (1, 0):
        for j in range(4):
            lines += [heads_ref[line_at(meta, h, other, j), :] for h in range(heads_ref.shape[0] // HDIM)]
    return jnp.concatenate(lines, axis=0)


def weight_kernel(meta, p0, p1, p2, p3, bias_ref, heads_a, *refs):
    pieces, grads = (p0, p1, p2, p3), refs[:-6]
    weight_ref, inverse_ref, out_ref, send_ref, keep_ref, heads_b = refs[-6:]
    rows = p0.shape[1]
    query_live = token_pos((1, 4 * rows), 1, meta[Z]) < meta[COUNT]
    tile = 4 * HDIM
    tiles = send_ref.shape[1] // tile
    whole_size = send_ref.shape[0] // 4

    def product(lines, first, i):
        cols = slice(i * tile, (i + 1) * tile)
        result = dot(lines, jnp.concatenate([g[:, cols] for g in grads], axis=0), 1, 0)
        size = lines.shape[0] // 8
        for j in range(4):
            at = slice(j * whole_size + first, j * whole_size + first + size)
            send_ref[at, cols] = result[j * size : (j + 1) * size].astype(bf16)
            keep_ref[at, cols] = result[(4 + j) * size : (5 + j) * size]

    lines = lines_of(meta, heads_a)
    count = p3.shape[2] // HDIM
    for n in range(max(tiles, 2 * count)):
        if n < 2 * count:
            h, t = divmod(n, 2)
            query, key, value = head_of(pieces, 1, h)
            span = slice(2 * rows * t, 2 * rows * (t + 1))
            outs = (weight_ref, inverse_ref, out_ref, heads_b, h, span)
            span_forward(query, key, value, bias_ref[:, span], query_live[:, span], *outs)
        if n < tiles:
            product(lines, 0, n)
    lines_b = lines_of(meta, heads_b)
    for i in range(tiles):
        product(lines_b, lines.shape[0] // 8, i)


def weight_halves(meta, pieces, bias, heads, grads):
    forward_out = forward_shapes(pieces)
    width = heads.shape[0] + pieces[-1].shape[2]
    shape = (width // 2, grads[0].shape[1])
    shapes = forward_out[:3] + [sds(shape, bf16), sds(shape, f32)]
    scratch = [pltpu.VMEM(forward_out[3].shape, bf16)]
    return whole(weight_kernel, shapes, (meta, *pieces, bias, heads, *grads), "weight_halves", 1, 10, scratch)


def add_kernel(keep_ref, recv_ref, *outs):
    size = outs[0].shape[0]
    for j, out_ref in enumerate(outs):
        part = slice(j * size, (j + 1) * size)
        out_ref[...] = (keep_ref[part, :] + recv_ref[part, :].astype(f32)).astype(out_ref.dtype)


def add_parts(keep, recv):
    shape = (keep.shape[0] // 4, keep.shape[1])
    return whole(add_kernel, [sds(shape, f32)] + [sds(shape, bf16)] * 3, (keep, recv), "add_parts")


def total_kernel(scale, own_ref, r1, r2, r3, out_ref):
    total = own_ref[...] + r1[...].astype(f32) + r2[...].astype(f32) + r3[...].astype(f32)
    out_ref[...] = (total * scale).astype(bf16)


def total_of(own, recvs, scale):
    return whole(functools.partial(total_kernel, scale), sds(own.shape, bf16), (own, *recvs), "scene_mean")


def weight_copies(meta, parts, first, out_ref, sems):
    copies = []
    for p, ref in enumerate(parts, first):
        for h in range(ref.shape[0] // LINE):
            line = out_ref.at[line_at(meta, h, p // 4, p % 4), :]
            copies.append(pltpu.make_async_copy(ref.at[pl.ds(h * LINE, LINE), :], line, sems.at[len(copies)]))
    return copies


def head_copies(meta, pieces, outs, sems):
    copies = []
    for k, ref in pieces.items():
        width = ref.shape[2]
        start = pl.multiple_of((meta[Z] ^ k) * width, 128)
        for i, out_ref in enumerate(outs):
            part = out_ref.at[:, pl.ds(start, width)]
            copies.append(pltpu.make_async_copy(ref.at[i], part, sems.at[len(copies)]))
    return copies


def join(kernel, meta, parts, shapes, copies, name, outs=()):
    return pl.pallas_call(
        kernel,
        out_shape=shapes,
        in_specs=[pl.BlockSpec(memory_space=pltpu.SMEM)]
        + [pl.BlockSpec(memory_space=pltpu.VMEM)] * len(parts)
        + [pl.BlockSpec(memory_space=pl.ANY)] * len(outs),
        out_specs=[pl.BlockSpec(memory_space=pl.ANY)] * len(shapes),
        scratch_shapes=[pltpu.SemaphoreType.DMA((n,)) for n in copies],
        input_output_aliases={1 + len(parts) + i: i for i in range(len(outs))},
        compiler_params=params(),
        cost_estimate=NO_COST,
        name=name,
    )(meta, *parts, *outs)


def join_weight_kernel(meta, *refs):
    run_all(weight_copies(meta, refs[:4], 0, refs[4], refs[5]))


def join_weight(meta, near):
    size, outw = near[0].shape
    return join(join_weight_kernel, meta, near, [sds((8 * size, outw), bf16)], [4 * size // LINE], "join_weight")[0]


def join_heads_kernel(meta, own, back2, back3, *refs):
    run_all(head_copies(meta, {0: own, 2: back2, 3: back3}, refs[:3], refs[3]))


def join_heads(meta, own, back2, back3):
    _, rows, width = own.shape
    shapes = [sds((rows, 4 * width), bf16)] * 3
    return join(join_heads_kernel, meta, (own, back2, back3), shapes, [9], "join_heads")


def join_last_kernel(meta, *refs):
    far, back1, outs, sems = refs[:4], refs[4], refs[9:13], refs[13:]
    run_all(weight_copies(meta, far, 4, outs[3], sems[0]) + head_copies(meta, {1: back1}, outs[:3], sems[1]))


def join_last(meta, far, back1, outs):
    shapes = [sds(x.shape, x.dtype) for x in outs]
    return join(join_last_kernel, meta, (*far, back1), shapes, [4 * far[0].shape[0] // LINE, 3], "join_last", outs)


def dense_body(queries, keys_in, values, out_grad, out_weight, voxel_count):
    meta = jnp.stack([lax.axis_index("shard"), voxel_count[0], lax.axis_index("core"), lax.axis_index("chips")])
    meta = meta.astype(jnp.int32)

    def send(x, k, *earlier):
        return swap(after(x, *earlier) if earlier else x, "shard", 4, k)

    across = send(out_grad, 2)
    beside = send(out_grad, 1)
    mine, own, near1, far2a, far2b, far3a, far3b = pack(meta, queries, keys_in, values, out_grad)
    piece1 = send(near1, 1)
    piece3a = send(far3a, 3, beside)
    piece2a = send(far2a, 2, across)
    piece3b = send(far3b, 3, piece3a)
    piece2b = send(far2b, 2, piece2a)
    half = across.shape[0] // 2
    grad_early = grad_attn(meta, (mine, beside, across), out_weight, 0)
    corners = [send(across[:half], 1), send(after(across, piece1, grad_early)[half:], 1)]

    *saved_a, heads_a, bias = forward(meta, (own, piece1, piece2a, piece3a))
    early = backward_early((own, piece1, piece2a, piece3a), grad_early, saved_a)
    heads_a, *early, piece2b, piece3b = lax.optimization_barrier((heads_a, *early, piece2b, piece3b))
    grad_early, piece2b, *corners = lax.optimization_barrier((grad_early, piece2b, *corners))
    grads = (mine, beside, across, *corners)

    *saved_b, out, keep = weight_halves(meta, (own, piece1, piece2b, piece3b), bias, heads_a, grads)
    recv = swap(out, "core", 2, 1)
    grad_late = grad_attn(meta, after(grads[3:], out), out_weight, 3 * BLOCK)
    pieces = (own, piece1, piece2a, piece3a, piece2b, piece3b)
    own0, *backs = backward(pieces, (grad_early, grad_late), (*saved_a, *saved_b), early)
    own_part, *sends = add_parts(after(keep, own0), recv)
    recvs = [swap(x, "chips", 4, j + 1) for j, x in enumerate(sends)]
    back3, back2 = send(backs[2], 3), send(backs[1], 2)
    done = total_of(own_part, recvs, 1.0 / 8)
    near = [done] + [swap(done, "chips", 4, j) for j in (1, 2, 3)]
    back1 = send(backs[0], 1, near[1])
    weight = join_weight(meta, near)
    weight, *near, back2, back3 = lax.optimization_barrier((weight, *near, back2, back3))
    far = [swap(x, "core", 2, 1) for x in near]
    heads = join_heads(meta, own0, back2, back3)
    return tuple(join_last(meta, far, back1, (*heads, weight)))


def attend_listed(queries, keys_in, values, block_ids, live_count):
    row_count, width_all = queries.shape
    head_count = width_all // HDIM
    block_count = row_count // BLOCK
    score_scale = 1.0 / math.sqrt(HDIM)
    query_blk = queries.reshape(block_count, BLOCK, head_count, HDIM)
    key_blk = keys_in.reshape(block_count, BLOCK, head_count, HDIM)[block_ids].reshape(
        block_count, NB * BLOCK, head_count, HDIM
    )
    value_blk = values.reshape(block_count, BLOCK, head_count, HDIM)[block_ids].reshape(
        block_count, NB * BLOCK, head_count, HDIM
    )
    query_pos = jnp.arange(row_count, dtype=jnp.int32).reshape(block_count, BLOCK)
    key_pos = (
        block_ids[:, :, None] * BLOCK + jnp.arange(BLOCK, dtype=jnp.int32)[None, None, :]
    ).reshape(block_count, NB * BLOCK)
    allowed = (key_pos[:, None, :] < live_count) | (query_pos[:, :, None] >= live_count)
    scores = (
        jnp.einsum("bqhd,bkhd->bhqk", query_blk, key_blk, preferred_element_type=jnp.float32)
        * score_scale
    )
    scores = jnp.where(allowed[:, None], scores, -jnp.inf)
    peak = jnp.max(scores, axis=-1, keepdims=True)
    weights = jnp.exp(scores - peak)
    probs = weights / jnp.sum(weights, axis=-1, keepdims=True)
    return (query_blk, key_blk, value_blk, probs)


def listed_body(queries, keys_in, values, out_grad, out_weight, block_lists, voxel_count):
    local_rows = queries.shape[0]
    live_count = voxel_count[0]
    block_ids = block_lists[0]
    positions = lax.axis_index("shard") * local_rows + jnp.arange(local_rows, dtype=jnp.int32)
    grad_live = jnp.where((positions < live_count)[:, None], out_grad, jnp.zeros_like(out_grad))
    query_head, key_head, value_head = (
        lax.all_to_all(queries, "shard", split_axis=1, concat_axis=0, tiled=True),
        lax.all_to_all(keys_in, "shard", split_axis=1, concat_axis=0, tiled=True),
        lax.all_to_all(values, "shard", split_axis=1, concat_axis=0, tiled=True),
    )
    row_count, width_all = query_head.shape
    head_count = width_all // HDIM
    block_count = row_count // BLOCK
    score_scale = 1.0 / math.sqrt(HDIM)
    query_blk, key_blk, value_blk, probs = attend_listed(
        query_head, key_head, value_head, block_ids, live_count
    )
    prob_bf = probs.astype(jnp.bfloat16)
    heads_out = (
        jnp.einsum("bhqk,bkhd->bqhd", prob_bf, value_blk, preferred_element_type=jnp.float32)
        .reshape(row_count, width_all)
        .astype(jnp.bfloat16)
    )
    row_piece = lax.all_gather(grad_live, "shard", axis=0, tiled=True)
    acc_now = jnp.einsum("rw,ro->wo", heads_out, row_piece, preferred_element_type=jnp.float32)
    product = jnp.einsum("ro,wo->rw", row_piece, out_weight, preferred_element_type=jnp.float32)
    grad_o = product.astype(jnp.bfloat16).reshape(block_count, BLOCK, head_count, HDIM)
    grad_prob = jnp.einsum("bqhd,bkhd->bhqk", grad_o, value_blk, preferred_element_type=jnp.float32)
    row_delta = jnp.sum(probs * grad_prob, axis=-1, keepdims=True)
    dscore = (probs * (grad_prob - row_delta) * score_scale).astype(jnp.bfloat16)
    grad_query = (
        jnp.einsum("bhqk,bkhd->bqhd", dscore, key_blk, preferred_element_type=jnp.float32)
        .reshape(row_count, width_all)
        .astype(jnp.bfloat16)
    )
    onehot = (
        block_ids[:, :, None] == jnp.arange(block_count, dtype=jnp.int32)[None, None, :]
    ).astype(jnp.float32)
    key_parts = jnp.einsum(
        "bhqk,bqhd->bkhd", dscore, query_blk, preferred_element_type=jnp.float32
    ).reshape(block_count, NB, BLOCK, width_all)
    value_parts = jnp.einsum(
        "bhqk,bqhd->bkhd", prob_bf, grad_o, preferred_element_type=jnp.float32
    ).reshape(block_count, NB, BLOCK, width_all)
    grad_key = (
        jnp.einsum("bjc,bjrx->crx", onehot, key_parts, precision=lax.Precision.HIGHEST)
        .reshape(row_count, width_all)
        .astype(jnp.bfloat16)
    )
    grad_value = (
        jnp.einsum("bjc,bjrx->crx", onehot, value_parts, precision=lax.Precision.HIGHEST)
        .reshape(row_count, width_all)
        .astype(jnp.bfloat16)
    )
    query_back, key_back, value_back = (
        lax.all_to_all(grad_query, "shard", split_axis=0, concat_axis=1, tiled=True),
        lax.all_to_all(grad_key, "shard", split_axis=0, concat_axis=1, tiled=True),
        lax.all_to_all(grad_value, "shard", split_axis=0, concat_axis=1, tiled=True),
    )
    scene_total = lax.axis_size(DP)
    summed = lax.psum(acc_now, DP)
    grad_weight = (summed / scene_total).astype(jnp.bfloat16)
    return (query_back, key_back, value_back, grad_weight)


def body(queries, keys_in, values, out_grad, out_weight, block_lists, voxel_count):
    dense = block_lists.shape[1] == NB and queries.shape[0] == BLOCK
    if dense and lax.axis_size("shard") == 4 and lax.axis_size("chips") == 4:
        return dense_body(queries, keys_in, values, out_grad, out_weight, voxel_count)
    return listed_body(queries, keys_in, values, out_grad, out_weight, block_lists, voxel_count)


def solution(mesh):
    chips = mesh.shape["dp"] // 2
    mesh = jax.sharding.Mesh(mesh.devices.reshape(chips, 2, -1), ("chips", "core", "shard"))
    return jax.shard_map(
        body,
        mesh=mesh,
        in_specs=(
            P((*DP, "shard"), None),
            P((*DP, "shard"), None),
            P((*DP, "shard"), None),
            P((*DP, "shard"), None),
            P("shard", None),
            P(DP, None, None),
            P(DP),
        ),
        out_specs=(
            P((*DP, "shard"), None),
            P((*DP, "shard"), None),
            P((*DP, "shard"), None),
            P("shard", None),
        ),
        check_vma=False,
    )
```

```python
import functools
import math

import jax
import jax.numpy as jnp
from jax import lax
from jax.experimental import pallas as pl
from jax.experimental.pallas import tpu as pltpu
from jax.sharding import PartitionSpec as P

HDIM = 128
BLOCK = 128
NB = 4
MIB = 1024 * 1024
DP = ("chips", "core")

Z, COUNT, CORE, CHIP = range(4)

EARLY = 3

NO_COST = pl.CostEstimate(flops=0, bytes_accessed=1024, transcendentals=0)

f32 = jnp.float32
bf16 = jnp.bfloat16


def dot(a, b, ca, cb):
    return lax.dot_general(a, b, (((ca,), (cb,)), ((), ())), preferred_element_type=f32)


def sds(shape, dtype):
    return jax.ShapeDtypeStruct(shape, dtype)


def params(mib=2):
    return pltpu.CompilerParams(vmem_limit_bytes=mib * MIB)


def swap(x, axis, size, flip):
    return lax.ppermute(x, axis, [(i, i ^ flip) for i in range(size)])


def after(x, *earlier):
    return lax.optimization_barrier((x, *earlier))[0]


def run_all(copies):
    for copy in copies:
        copy.start()
    for copy in copies:
        copy.wait()


def whole(kernel, out_shape, operands, name, scalars=0, mib=2, scratch=()):
    return pl.pallas_call(
        kernel,
        out_shape=out_shape,
        in_specs=[pl.BlockSpec(memory_space=pltpu.SMEM)] * scalars
        + [pl.BlockSpec(memory_space=pltpu.VMEM)] * (len(operands) - scalars),
        out_specs=jax.tree.map(lambda _: pl.BlockSpec(memory_space=pltpu.VMEM), out_shape),
        scratch_shapes=scratch,
        compiler_params=params(mib),
        cost_estimate=NO_COST,
        name=name,
    )(*operands)


def pack_kernel(meta, q_ref, k_ref, v_ref, grad_ref, mine_ref, *refs):
    *outs, sems = refs
    width = outs[0].shape[2]
    copies = [pltpu.make_async_copy(grad_ref, mine_ref, sems.at[3 * len(outs)])]
    for n, out_ref in enumerate(outs):
        k, first = (n, 0) if n < 2 else (n // 2 + 1, n % 2 * EARLY * HDIM)
        start = pl.multiple_of((meta[Z] ^ k) * width + first, 128)
        for i, ref in enumerate((q_ref, k_ref, v_ref)):
            part = ref.at[:, pl.ds(start, out_ref.shape[2])]
            copies.append(pltpu.make_async_copy(part, out_ref.at[i], sems.at[3 * n + i]))
    run_all(copies)


def pack(meta, queries, keys_in, values, grad):
    rows, width = queries.shape
    part, early = width // 4, EARLY * HDIM
    shapes = [sds((3, rows, n), bf16) for n in (part, part, early, part - early, early, part - early)]
    shapes = [sds(grad.shape, bf16)] + shapes
    return pl.pallas_call(
        pack_kernel,
        out_shape=shapes,
        in_specs=[pl.BlockSpec(memory_space=pltpu.SMEM)] + [pl.BlockSpec(memory_space=pl.ANY)] * 4,
        out_specs=[pl.BlockSpec(memory_space=pltpu.VMEM)] * len(shapes),
        scratch_shapes=[pltpu.SemaphoreType.DMA((3 * len(shapes),))],
        compiler_params=params(),
        cost_estimate=NO_COST,
        name="pack_heads",
    )(meta, queries, keys_in, values, grad)


def token_pos(shape, dim, z, start=0):
    return (lax.broadcasted_iota(jnp.int32, shape, dim) + start) ^ (z * BLOCK)


def grad_attn_kernel(start, meta, *refs):
    *grads, w_ref, out_ref = refs
    grad = jnp.concatenate([g[...] for g in grads], axis=0)
    live = token_pos((grad.shape[0], 1), 0, meta[Z], start) < meta[COUNT]
    tile = 2 * HDIM

    for i in range(w_ref.shape[0] // tile):
        part = slice(i * tile, (i + 1) * tile)
        out_ref[:, part] = jnp.where(live, dot(grad, w_ref[part, :], 1, 1), 0.0).astype(bf16)


def grad_attn(meta, grads, weight, start):
    shape = (sum(g.shape[0] for g in grads), weight.shape[0])
    kernel = functools.partial(grad_attn_kernel, start)
    return whole(kernel, sds(shape, bf16), (meta, *grads, weight), "grad_attn", 1, 6)


def head_of(pieces, group, h):
    part = pieces[-1].shape[2]
    parts = []
    for p in pieces:
        start = (group * EARLY * HDIM if p.shape[2] > part else 0) + h * HDIM
        parts.append([p[i, :, start : start + HDIM] for i in range(3)])
    return (jnp.concatenate(x, axis=0) for x in zip(*parts))


def span_forward(query, key, value, bias, live, weight_ref, inverse_ref, out_ref, heads_ref, h, span):
    cols = slice(h * HDIM, (h + 1) * HDIM)
    scores = dot(key, query[span], 1, 1) + bias
    peak = jnp.max(scores, axis=0, keepdims=True)
    weights = jnp.exp2((scores - peak) * (math.log2(math.e) / math.sqrt(HDIM))).astype(bf16)
    weight_ref[h, :, span] = weights
    inverse = 1.0 / jnp.sum(weights.astype(f32), axis=0, keepdims=True)
    inverse_ref[h, :, span] = inverse
    heads = dot(value, weights, 0, 0) * inverse
    out_ref[cols, span] = heads
    heads_ref[cols, span] = jnp.where(live, heads, 0.0).astype(bf16)


def forward_shapes(pieces):
    _, rows, width = pieces[-1].shape
    total = 4 * rows
    return [
        sds((width // HDIM, total, total), bf16),
        sds((width // HDIM, 1, total), f32),
        sds((width, total), f32),
        sds((width, total), bf16),
    ]


def forward_kernel(meta, p0, p1, p2, p3, weight_ref, inverse_ref, out_ref, heads_ref, bias_ref):
    pieces = (p0, p1, p2, p3)
    rows = p0.shape[1]
    total = 4 * rows
    query_live = token_pos((1, total), 1, meta[Z]) < meta[COUNT]
    key_live = token_pos((total, 1), 0, meta[Z]) < meta[COUNT]
    bias_ref[...] = jnp.where(key_live | ~query_live, 0.0, -jnp.inf)
    for h in range(p3.shape[2] // HDIM):
        query, key, value = head_of(pieces, 0, h)
        for t in range(2):
            span = slice(2 * rows * t, 2 * rows * (t + 1))
            outs = (weight_ref, inverse_ref, out_ref, heads_ref, h, span)
            span_forward(query, key, value, bias_ref[:, span], query_live[:, span], *outs)


def forward(meta, pieces):
    total = 4 * pieces[-1].shape[1]
    shapes = forward_shapes(pieces) + [sds((total, total), f32)]
    return whole(forward_kernel, shapes, (meta, *pieces), "attend_forward", 1, 8)


def span_gradients(query, key, value, grad, weights, inverse, outs):
    turned = grad.astype(f32).T
    row_delta = jnp.sum(outs * turned, axis=0, keepdims=True)
    grad_prob = dot(value, grad, 1, 1)
    factor = inverse * (1.0 / math.sqrt(HDIM))
    dscore = (weights.astype(f32) * ((grad_prob - row_delta) * factor)).astype(bf16)
    grad_query = dot(key, dscore, 0, 0).T.astype(bf16)
    grad_value = dot(weights, (turned * inverse).T.astype(bf16), 1, 0)
    return grad_query, dot(dscore, query, 1, 0), grad_value


def backward_early_kernel(*refs):
    pieces, (grad_ref, weight_ref, inverse_ref, out_ref, query_out, key_out, value_out) = refs[:4], refs[4:]
    early = grad_ref.shape[0]
    for h in range(pieces[-1].shape[2] // HDIM):
        cols = slice(h * HDIM, (h + 1) * HDIM)
        query, key, value = head_of(pieces, 0, h)
        grad_key = grad_value = 0.0
        for span in (slice(0, 2 * BLOCK), slice(2 * BLOCK, early)):
            grad_query, add_key, add_value = span_gradients(
                query[span], key, value, grad_ref[span, cols],
                weight_ref[h, :, span], inverse_ref[h, :, span], out_ref[cols, span],
            )
            query_out[span, cols] = grad_query
            grad_key += add_key
            grad_value += add_value
        key_out[:, cols] = grad_key
        value_out[:, cols] = grad_value


def backward_early(pieces, grad, saved):
    _, rows, part = pieces[-1].shape
    shapes = [sds((grad.shape[0], part), bf16), sds((4 * rows, part), f32), sds((4 * rows, part), f32)]
    return whole(backward_early_kernel, shapes, (*pieces, grad, *saved), "backward_early", 0, 8)


def backward_kernel(meta, own, near, far2a, far3a, far2b, far3b, early_ref, corner0, corner1, w_ref, *refs):
    saved, done, backs, late_ref = (refs[:3], refs[3:6]), refs[6:9], refs[9:13], refs[13]
    rows = own.shape[1]
    early, total = early_ref.shape[0], 4 * rows
    heads = own.shape[2] // HDIM
    sums = {}

    def head_span(n, span, grad):
        group, h = divmod(n, EARLY)
        query, key, value = head_of(((own, near, far2a, far3a), (own, near, far2b, far3b))[group], group, h)
        weight_ref, inverse_ref, out_ref = saved[group]
        here = slice(h * HDIM, (h + 1) * HDIM)
        cols = slice(n * HDIM, (n + 1) * HDIM)
        grad_query, add_key, add_value = span_gradients(
            query[span], key, value, grad, weight_ref[h, :, span], inverse_ref[h, :, span], out_ref[here, span]
        )
        for k in range(span.start // rows, span.stop // rows):
            at = k * rows - span.start
            backs[k][0, :, cols] = grad_query[at : at + rows]
        grad_key, grad_value = sums.get(n, (0.0, 0.0))
        sums[n] = (grad_key + add_key, grad_value + add_value)

    for n in range(EARLY, heads):
        head_span(n, slice(0, 2 * rows), early_ref[: 2 * rows, n * HDIM : (n + 1) * HDIM])
    corner = jnp.concatenate([corner0[...], corner1[...]], axis=0)
    live = token_pos((rows, 1), 0, meta[Z], early) < meta[COUNT]
    tile = 2 * HDIM
    for i in range(w_ref.shape[0] // tile):
        part = slice(i * tile, (i + 1) * tile)
        late_ref[:, part] = jnp.where(live, dot(corner, w_ref[part, :], 1, 1), 0.0).astype(bf16)
    for n in range(heads):
        cols = slice(n * HDIM, (n + 1) * HDIM)
        if n < EARLY:
            sums[n] = (done[1][:, cols], done[2][:, cols])
            for k in range(early // rows):
                backs[k][0, :, cols] = done[0][k * rows : (k + 1) * rows, cols]
            head_span(n, slice(early, total), late_ref[:, cols])
        else:
            grad = jnp.concatenate([early_ref[2 * rows :, cols], late_ref[:, cols]], axis=0)
            head_span(n, slice(2 * rows, total), grad)
        for k in range(4):
            mine = slice(k * rows, (k + 1) * rows)
            backs[k][1, :, cols] = sums[n][0][mine].astype(bf16)
            backs[k][2, :, cols] = sums[n][1][mine].astype(bf16)


def backward(meta, pieces, grad, corners, weight, saved, done):
    shapes = [sds(pieces[0].shape, bf16)] * 4
    operands = (meta, *pieces, grad, *corners, weight, *saved, *done)
    scratch = [pltpu.VMEM((pieces[0].shape[1], weight.shape[0]), bf16)]
    return whole(backward_kernel, shapes, operands, "attend_backward", 1, 10, scratch)


LINE = HDIM // 8


def line_at(meta, head, other, j):
    at = head * HDIM + ((meta[CORE] ^ other) * 4 + (meta[CHIP] ^ j)) * LINE
    return pl.ds(pl.multiple_of(at, LINE), LINE)


def lines_of(meta, heads_ref):
    lines = []
    for other in (1, 0):
        for j in range(4):
            lines += [heads_ref[line_at(meta, h, other, j), :] for h in range(heads_ref.shape[0] // HDIM)]
    return jnp.concatenate(lines, axis=0)


def weight_kernel(meta, p0, p1, p2, p3, bias_ref, heads_a, *refs):
    pieces, grads = (p0, p1, p2, p3), refs[:-6]
    weight_ref, inverse_ref, out_ref, send_ref, keep_ref, heads_b = refs[-6:]
    rows = p0.shape[1]
    query_live = token_pos((1, 4 * rows), 1, meta[Z]) < meta[COUNT]
    tile = 4 * HDIM
    tiles = send_ref.shape[1] // tile
    whole_size = send_ref.shape[0] // 4

    def product(lines, first, i):
        cols = slice(i * tile, (i + 1) * tile)
        result = dot(lines, jnp.concatenate([g[:, cols] for g in grads], axis=0), 1, 0)
        size = lines.shape[0] // 8
        for j in range(4):
            at = slice(j * whole_size + first, j * whole_size + first + size)
            send_ref[at, cols] = result[j * size : (j + 1) * size].astype(bf16)
            keep_ref[at, cols] = result[(4 + j) * size : (5 + j) * size]

    lines = lines_of(meta, heads_a)
    count = p3.shape[2] // HDIM
    for n in range(max(tiles, 2 * count)):
        if n < 2 * count:
            h, t = divmod(n, 2)
            query, key, value = head_of(pieces, 1, h)
            span = slice(2 * rows * t, 2 * rows * (t + 1))
            outs = (weight_ref, inverse_ref, out_ref, heads_b, h, span)
            span_forward(query, key, value, bias_ref[:, span], query_live[:, span], *outs)
        if n < tiles:
            product(lines, 0, n)
    lines_b = lines_of(meta, heads_b)
    for i in range(tiles):
        product(lines_b, lines.shape[0] // 8, i)


def weight_halves(meta, pieces, bias, heads, grads):
    forward_out = forward_shapes(pieces)
    width = heads.shape[0] + pieces[-1].shape[2]
    shape = (width // 2, grads[0].shape[1])
    shapes = forward_out[:3] + [sds(shape, bf16), sds(shape, f32)]
    scratch = [pltpu.VMEM(forward_out[3].shape, bf16)]
    return whole(weight_kernel, shapes, (meta, *pieces, bias, heads, *grads), "weight_halves", 1, 10, scratch)


def add_kernel(keep_ref, recv_ref, *outs):
    size = outs[0].shape[0]
    for j, out_ref in enumerate(outs):
        part = slice(j * size, (j + 1) * size)
        out_ref[...] = (keep_ref[part, :] + recv_ref[part, :].astype(f32)).astype(out_ref.dtype)


def add_parts(keep, recv):
    shape = (keep.shape[0] // 4, keep.shape[1])
    return whole(add_kernel, [sds(shape, f32)] + [sds(shape, bf16)] * 3, (keep, recv), "add_parts")


def total_kernel(scale, own_ref, r1, r2, r3, out_ref):
    total = own_ref[...] + r1[...].astype(f32) + r2[...].astype(f32) + r3[...].astype(f32)
    out_ref[...] = (total * scale).astype(bf16)


def total_of(own, recvs, scale):
    return whole(functools.partial(total_kernel, scale), sds(own.shape, bf16), (own, *recvs), "scene_mean")


def weight_copies(meta, parts, first, out_ref, sems):
    copies = []
    for p, ref in enumerate(parts, first):
        for h in range(ref.shape[0] // LINE):
            line = out_ref.at[line_at(meta, h, p // 4, p % 4), :]
            copies.append(pltpu.make_async_copy(ref.at[pl.ds(h * LINE, LINE), :], line, sems.at[len(copies)]))
    return copies


def head_copies(meta, pieces, outs, sems):
    copies = []
    for k, ref in pieces.items():
        width = ref.shape[2]
        start = pl.multiple_of((meta[Z] ^ k) * width, 128)
        for i, out_ref in enumerate(outs):
            part = out_ref.at[:, pl.ds(start, width)]
            copies.append(pltpu.make_async_copy(ref.at[i], part, sems.at[len(copies)]))
    return copies


def join(kernel, meta, parts, shapes, copies, name, outs=()):
    return pl.pallas_call(
        kernel,
        out_shape=shapes,
        in_specs=[pl.BlockSpec(memory_space=pltpu.SMEM)]
        + [pl.BlockSpec(memory_space=pltpu.VMEM)] * len(parts)
        + [pl.BlockSpec(memory_space=pl.ANY)] * len(outs),
        out_specs=[pl.BlockSpec(memory_space=pl.ANY)] * len(shapes),
        scratch_shapes=[pltpu.SemaphoreType.DMA((n,)) for n in copies],
        input_output_aliases={1 + len(parts) + i: i for i in range(len(outs))},
        compiler_params=params(),
        cost_estimate=NO_COST,
        name=name,
    )(meta, *parts, *outs)


def join_weight_kernel(meta, *refs):
    run_all(weight_copies(meta, refs[:4], 0, refs[4], refs[5]))


def join_weight(meta, near):
    size, outw = near[0].shape
    return join(join_weight_kernel, meta, near, [sds((8 * size, outw), bf16)], [4 * size // LINE], "join_weight")[0]


def join_heads_kernel(meta, own, back2, back3, *refs):
    run_all(head_copies(meta, {0: own, 2: back2, 3: back3}, refs[:3], refs[3]))


def join_heads(meta, own, back2, back3):
    _, rows, width = own.shape
    shapes = [sds((rows, 4 * width), bf16)] * 3
    return join(join_heads_kernel, meta, (own, back2, back3), shapes, [9], "join_heads")


def join_last_kernel(meta, *refs):
    far, back1, outs, sems = refs[:4], refs[4], refs[9:13], refs[13:]
    run_all(weight_copies(meta, far, 4, outs[3], sems[0]) + head_copies(meta, {1: back1}, outs[:3], sems[1]))


def join_last(meta, far, back1, outs):
    shapes = [sds(x.shape, x.dtype) for x in outs]
    return join(join_last_kernel, meta, (*far, back1), shapes, [4 * far[0].shape[0] // LINE, 3], "join_last", outs)


def dense_body(queries, keys_in, values, out_grad, out_weight, voxel_count):
    meta = jnp.stack([lax.axis_index("shard"), voxel_count[0], lax.axis_index("core"), lax.axis_index("chips")])
    meta = meta.astype(jnp.int32)

    def send(x, k, *earlier):
        return swap(after(x, *earlier) if earlier else x, "shard", 4, k)

    across = send(out_grad, 2)
    beside = send(out_grad, 1)
    mine, own, near1, far2a, far2b, far3a, far3b = pack(meta, queries, keys_in, values, out_grad)
    piece1 = send(near1, 1)
    piece3a = send(far3a, 3, beside)
    piece2a = send(far2a, 2, across)
    piece3b = send(far3b, 3, piece3a)
    piece2b = send(far2b, 2, piece2a)
    half = across.shape[0] // 2
    grad_early = grad_attn(meta, (mine, beside, across), out_weight, 0)
    corners = [send(across[:half], 1), send(after(across, piece1, grad_early)[half:], 1)]

    *saved_a, heads_a, bias = forward(meta, (own, piece1, piece2a, piece3a))
    early = backward_early((own, piece1, piece2a, piece3a), grad_early, saved_a)
    heads_a, *early, piece2b, piece3b = lax.optimization_barrier((heads_a, *early, piece2b, piece3b))
    grad_early, piece2b, *corners = lax.optimization_barrier((grad_early, piece2b, *corners))
    grads = (mine, beside, across, *corners)

    *saved_b, out, keep = weight_halves(meta, (own, piece1, piece2b, piece3b), bias, heads_a, grads)
    recv = swap(out, "core", 2, 1)
    corners = after(grads[3:], out)
    pieces = (own, piece1, piece2a, piece3a, piece2b, piece3b)
    own0, *backs = backward(meta, pieces, grad_early, corners, out_weight, (*saved_a, *saved_b), early)
    own_part, *sends = add_parts(after(keep, own0), recv)
    recvs = [swap(x, "chips", 4, j + 1) for j, x in enumerate(sends)]
    back3, back2 = send(backs[2], 3), send(backs[1], 2)
    done = total_of(own_part, recvs, 1.0 / 8)
    near = [done] + [swap(done, "chips", 4, j) for j in (1, 2, 3)]
    back1 = send(backs[0], 1, near[1])
    weight = join_weight(meta, near)
    weight, *near, back2, back3 = lax.optimization_barrier((weight, *near, back2, back3))
    far = [swap(x, "core", 2, 1) for x in near]
    heads = join_heads(meta, own0, back2, back3)
    return tuple(join_last(meta, far, back1, (*heads, weight)))


def attend_listed(queries, keys_in, values, block_ids, live_count):
    row_count, width_all = queries.shape
    head_count = width_all // HDIM
    block_count = row_count // BLOCK
    score_scale = 1.0 / math.sqrt(HDIM)
    query_blk = queries.reshape(block_count, BLOCK, head_count, HDIM)
    key_blk = keys_in.reshape(block_count, BLOCK, head_count, HDIM)[block_ids].reshape(
        block_count, NB * BLOCK, head_count, HDIM
    )
    value_blk = values.reshape(block_count, BLOCK, head_count, HDIM)[block_ids].reshape(
        block_count, NB * BLOCK, head_count, HDIM
    )
    query_pos = jnp.arange(row_count, dtype=jnp.int32).reshape(block_count, BLOCK)
    key_pos = (
        block_ids[:, :, None] * BLOCK + jnp.arange(BLOCK, dtype=jnp.int32)[None, None, :]
    ).reshape(block_count, NB * BLOCK)
    allowed = (key_pos[:, None, :] < live_count) | (query_pos[:, :, None] >= live_count)
    scores = (
        jnp.einsum("bqhd,bkhd->bhqk", query_blk, key_blk, preferred_element_type=jnp.float32)
        * score_scale
    )
    scores = jnp.where(allowed[:, None], scores, -jnp.inf)
    peak = jnp.max(scores, axis=-1, keepdims=True)
    weights = jnp.exp(scores - peak)
    probs = weights / jnp.sum(weights, axis=-1, keepdims=True)
    return (query_blk, key_blk, value_blk, probs)


def listed_body(queries, keys_in, values, out_grad, out_weight, block_lists, voxel_count):
    local_rows = queries.shape[0]
    live_count = voxel_count[0]
    block_ids = block_lists[0]
    positions = lax.axis_index("shard") * local_rows + jnp.arange(local_rows, dtype=jnp.int32)
    grad_live = jnp.where((positions < live_count)[:, None], out_grad, jnp.zeros_like(out_grad))
    query_head, key_head, value_head = (
        lax.all_to_all(queries, "shard", split_axis=1, concat_axis=0, tiled=True),
        lax.all_to_all(keys_in, "shard", split_axis=1, concat_axis=0, tiled=True),
        lax.all_to_all(values, "shard", split_axis=1, concat_axis=0, tiled=True),
    )
    row_count, width_all = query_head.shape
    head_count = width_all // HDIM
    block_count = row_count // BLOCK
    score_scale = 1.0 / math.sqrt(HDIM)
    query_blk, key_blk, value_blk, probs = attend_listed(
        query_head, key_head, value_head, block_ids, live_count
    )
    prob_bf = probs.astype(jnp.bfloat16)
    heads_out = (
        jnp.einsum("bhqk,bkhd->bqhd", prob_bf, value_blk, preferred_element_type=jnp.float32)
        .reshape(row_count, width_all)
        .astype(jnp.bfloat16)
    )
    row_piece = lax.all_gather(grad_live, "shard", axis=0, tiled=True)
    acc_now = jnp.einsum("rw,ro->wo", heads_out, row_piece, preferred_element_type=jnp.float32)
    product = jnp.einsum("ro,wo->rw", row_piece, out_weight, preferred_element_type=jnp.float32)
    grad_o = product.astype(jnp.bfloat16).reshape(block_count, BLOCK, head_count, HDIM)
    grad_prob = jnp.einsum("bqhd,bkhd->bhqk", grad_o, value_blk, preferred_element_type=jnp.float32)
    row_delta = jnp.sum(probs * grad_prob, axis=-1, keepdims=True)
    dscore = (probs * (grad_prob - row_delta) * score_scale).astype(jnp.bfloat16)
    grad_query = (
        jnp.einsum("bhqk,bkhd->bqhd", dscore, key_blk, preferred_element_type=jnp.float32)
        .reshape(row_count, width_all)
        .astype(jnp.bfloat16)
    )
    onehot = (
        block_ids[:, :, None] == jnp.arange(block_count, dtype=jnp.int32)[None, None, :]
    ).astype(jnp.float32)
    key_parts = jnp.einsum(
        "bhqk,bqhd->bkhd", dscore, query_blk, preferred_element_type=jnp.float32
    ).reshape(block_count, NB, BLOCK, width_all)
    value_parts = jnp.einsum(
        "bhqk,bqhd->bkhd", prob_bf, grad_o, preferred_element_type=jnp.float32
    ).reshape(block_count, NB, BLOCK, width_all)
    grad_key = (
        jnp.einsum("bjc,bjrx->crx", onehot, key_parts, precision=lax.Precision.HIGHEST)
        .reshape(row_count, width_all)
        .astype(jnp.bfloat16)
    )
    grad_value = (
        jnp.einsum("bjc,bjrx->crx", onehot, value_parts, precision=lax.Precision.HIGHEST)
        .reshape(row_count, width_all)
        .astype(jnp.bfloat16)
    )
    query_back, key_back, value_back = (
        lax.all_to_all(grad_query, "shard", split_axis=0, concat_axis=1, tiled=True),
        lax.all_to_all(grad_key, "shard", split_axis=0, concat_axis=1, tiled=True),
        lax.all_to_all(grad_value, "shard", split_axis=0, concat_axis=1, tiled=True),
    )
    scene_total = lax.axis_size(DP)
    summed = lax.psum(acc_now, DP)
    grad_weight = (summed / scene_total).astype(jnp.bfloat16)
    return (query_back, key_back, value_back, grad_weight)


def body(queries, keys_in, values, out_grad, out_weight, block_lists, voxel_count):
    dense = block_lists.shape[1] == NB and queries.shape[0] == BLOCK
    if dense and lax.axis_size("shard") == 4 and lax.axis_size("chips") == 4:
        return dense_body(queries, keys_in, values, out_grad, out_weight, voxel_count)
    return listed_body(queries, keys_in, values, out_grad, out_weight, block_lists, voxel_count)


def solution(mesh):
    chips = mesh.shape["dp"] // 2
    mesh = jax.sharding.Mesh(mesh.devices.reshape(chips, 2, -1), ("chips", "core", "shard"))
    return jax.shard_map(
        body,
        mesh=mesh,
        in_specs=(
            P((*DP, "shard"), None),
            P((*DP, "shard"), None),
            P((*DP, "shard"), None),
            P((*DP, "shard"), None),
            P("shard", None),
            P(DP, None, None),
            P(DP),
        ),
        out_specs=(
            P((*DP, "shard"), None),
            P((*DP, "shard"), None),
            P((*DP, "shard"), None),
            P("shard", None),
        ),
        check_vma=False,
    )
```

```python
import functools
import math

import jax
import jax.numpy as jnp
from jax import lax
from jax.experimental import pallas as pl
from jax.experimental.pallas import tpu as pltpu
from jax.sharding import PartitionSpec as P

HDIM = 128
BLOCK = 128
NB = 4
MIB = 1024 * 1024
DP = ("chips", "core")

Z, COUNT, CORE, CHIP = range(4)

EARLY = 3

NO_COST = pl.CostEstimate(flops=0, bytes_accessed=1024, transcendentals=0)

f32 = jnp.float32
bf16 = jnp.bfloat16


def dot(a, b, ca, cb):
    return lax.dot_general(a, b, (((ca,), (cb,)), ((), ())), preferred_element_type=f32)


def sds(shape, dtype):
    return jax.ShapeDtypeStruct(shape, dtype)


def params(mib=2):
    return pltpu.CompilerParams(vmem_limit_bytes=mib * MIB)


def swap(x, axis, size, flip):
    return lax.ppermute(x, axis, [(i, i ^ flip) for i in range(size)])


def after(x, *earlier):
    return lax.optimization_barrier((x, *earlier))[0]


def run_all(copies):
    for copy in copies:
        copy.start()
    for copy in copies:
        copy.wait()


def whole(kernel, out_shape, operands, name, scalars=0, mib=2, scratch=()):
    return pl.pallas_call(
        kernel,
        out_shape=out_shape,
        in_specs=[pl.BlockSpec(memory_space=pltpu.SMEM)] * scalars
        + [pl.BlockSpec(memory_space=pltpu.VMEM)] * (len(operands) - scalars),
        out_specs=jax.tree.map(lambda _: pl.BlockSpec(memory_space=pltpu.VMEM), out_shape),
        scratch_shapes=scratch,
        compiler_params=params(mib),
        cost_estimate=NO_COST,
        name=name,
    )(*operands)


def pack_kernel(meta, q_ref, k_ref, v_ref, *refs):
    *outs, sems = refs
    width = outs[0].shape[2]
    copies = []
    for n, out_ref in enumerate(outs):
        k, first = (n, 0) if n < 2 else (n // 2 + 1, n % 2 * EARLY * HDIM)
        start = pl.multiple_of((meta[Z] ^ k) * width + first, 128)
        for i, ref in enumerate((q_ref, k_ref, v_ref)):
            part = ref.at[:, pl.ds(start, out_ref.shape[2])]
            copies.append(pltpu.make_async_copy(part, out_ref.at[i], sems.at[3 * n + i]))
    run_all(copies)


def pack(meta, queries, keys_in, values):
    rows, width = queries.shape
    part, early = width // 4, EARLY * HDIM
    shapes = [sds((3, rows, n), bf16) for n in (part, part, early, part - early, early, part - early)]
    return pl.pallas_call(
        pack_kernel,
        out_shape=shapes,
        in_specs=[pl.BlockSpec(memory_space=pltpu.SMEM)] + [pl.BlockSpec(memory_space=pl.ANY)] * 3,
        out_specs=[pl.BlockSpec(memory_space=pltpu.VMEM)] * len(shapes),
        scratch_shapes=[pltpu.SemaphoreType.DMA((3 * len(shapes),))],
        compiler_params=params(),
        cost_estimate=NO_COST,
        name="pack_heads",
    )(meta, queries, keys_in, values)


def hold_kernel(in_ref, out_ref):
    out_ref[...] = in_ref[...]


def hold(x):
    return whole(hold_kernel, sds(x.shape, x.dtype), (x,), "hold")


def token_pos(shape, dim, z, start=0):
    return (lax.broadcasted_iota(jnp.int32, shape, dim) + start) ^ (z * BLOCK)


def grad_attn_kernel(start, meta, *refs):
    *grads, w_ref, out_ref = refs
    grad = jnp.concatenate([g[...] for g in grads], axis=0)
    live = token_pos((grad.shape[0], 1), 0, meta[Z], start) < meta[COUNT]
    tile = 2 * HDIM

    for i in range(w_ref.shape[0] // tile):
        part = slice(i * tile, (i + 1) * tile)
        out_ref[:, part] = jnp.where(live, dot(grad, w_ref[part, :], 1, 1), 0.0).astype(bf16)


def grad_attn(meta, grads, weight, start):
    shape = (sum(g.shape[0] for g in grads), weight.shape[0])
    kernel = functools.partial(grad_attn_kernel, start)
    return whole(kernel, sds(shape, bf16), (meta, *grads, weight), "grad_attn", 1, 6)


def head_of(pieces, group, h):
    part = pieces[-1].shape[2]
    parts = []
    for p in pieces:
        start = (group * EARLY * HDIM if p.shape[2] > part else 0) + h * HDIM
        parts.append([p[i, :, start : start + HDIM] for i in range(3)])
    return (jnp.concatenate(x, axis=0) for x in zip(*parts))


def span_forward(query, key, value, bias, live, weight_ref, inverse_ref, out_ref, heads_ref, h, span):
    cols = slice(h * HDIM, (h + 1) * HDIM)
    scores = dot(key, query[span], 1, 1) + bias
    peak = jnp.max(scores, axis=0, keepdims=True)
    weights = jnp.exp2((scores - peak) * (math.log2(math.e) / math.sqrt(HDIM))).astype(bf16)
    weight_ref[h, :, span] = weights
    inverse = 1.0 / jnp.sum(weights.astype(f32), axis=0, keepdims=True)
    inverse_ref[h, :, span] = inverse
    heads = dot(value, weights, 0, 0) * inverse
    out_ref[cols, span] = heads
    heads_ref[cols, span] = jnp.where(live, heads, 0.0).astype(bf16)


def forward_shapes(pieces):
    _, rows, width = pieces[-1].shape
    total = 4 * rows
    return [
        sds((width // HDIM, total, total), bf16),
        sds((width // HDIM, 1, total), f32),
        sds((width, total), f32),
        sds((width, total), bf16),
    ]


def forward_kernel(meta, p0, p1, p2, p3, weight_ref, inverse_ref, out_ref, heads_ref, bias_ref):
    pieces = (p0, p1, p2, p3)
    rows = p0.shape[1]
    total = 4 * rows
    query_live = token_pos((1, total), 1, meta[Z]) < meta[COUNT]
    key_live = token_pos((total, 1), 0, meta[Z]) < meta[COUNT]
    bias_ref[...] = jnp.where(key_live | ~query_live, 0.0, -jnp.inf)
    for h in range(p3.shape[2] // HDIM):
        query, key, value = head_of(pieces, 0, h)
        for t in range(2):
            span = slice(2 * rows * t, 2 * rows * (t + 1))
            outs = (weight_ref, inverse_ref, out_ref, heads_ref, h, span)
            span_forward(query, key, value, bias_ref[:, span], query_live[:, span], *outs)


def forward(meta, pieces):
    total = 4 * pieces[-1].shape[1]
    shapes = forward_shapes(pieces) + [sds((total, total), f32)]
    return whole(forward_kernel, shapes, (meta, *pieces), "attend_forward", 1, 8)


def span_gradients(query, key, value, grad, weights, inverse, outs):
    turned = grad.astype(f32).T
    row_delta = jnp.sum(outs * turned, axis=0, keepdims=True)
    grad_prob = dot(value, grad, 1, 1)
    factor = inverse * (1.0 / math.sqrt(HDIM))
    dscore = (weights.astype(f32) * ((grad_prob - row_delta) * factor)).astype(bf16)
    grad_query = dot(key, dscore, 0, 0).T.astype(bf16)
    grad_value = dot(weights, (turned * inverse).T.astype(bf16), 1, 0)
    return grad_query, dot(dscore, query, 1, 0), grad_value


def backward_early_kernel(*refs):
    pieces, (grad_ref, weight_ref, inverse_ref, out_ref, query_out, key_out, value_out) = refs[:4], refs[4:]
    early = grad_ref.shape[0]
    for h in range(pieces[-1].shape[2] // HDIM):
        cols = slice(h * HDIM, (h + 1) * HDIM)
        query, key, value = head_of(pieces, 0, h)
        grad_key = grad_value = 0.0
        for span in (slice(0, 2 * BLOCK), slice(2 * BLOCK, early)):
            grad_query, add_key, add_value = span_gradients(
                query[span], key, value, grad_ref[span, cols],
                weight_ref[h, :, span], inverse_ref[h, :, span], out_ref[cols, span],
            )
            query_out[span, cols] = grad_query
            grad_key += add_key
            grad_value += add_value
        key_out[:, cols] = grad_key
        value_out[:, cols] = grad_value


def backward_early(pieces, grad, saved):
    _, rows, part = pieces[-1].shape
    shapes = [sds((grad.shape[0], part), bf16), sds((4 * rows, part), f32), sds((4 * rows, part), f32)]
    return whole(backward_early_kernel, shapes, (*pieces, grad, *saved), "backward_early", 0, 8)


def backward_kernel(meta, own, near, far2a, far3a, far2b, far3b, early_ref, corner0, corner1, w_ref, *refs):
    saved, done, backs, late_ref = (refs[:3], refs[3:6]), refs[6:9], refs[9:13], refs[13]
    rows = own.shape[1]
    early, total = early_ref.shape[0], 4 * rows
    heads = own.shape[2] // HDIM
    sums = {}

    def head_span(n, span, grad):
        group, h = divmod(n, EARLY)
        query, key, value = head_of(((own, near, far2a, far3a), (own, near, far2b, far3b))[group], group, h)
        weight_ref, inverse_ref, out_ref = saved[group]
        here = slice(h * HDIM, (h + 1) * HDIM)
        cols = slice(n * HDIM, (n + 1) * HDIM)
        grad_query, add_key, add_value = span_gradients(
            query[span], key, value, grad, weight_ref[h, :, span], inverse_ref[h, :, span], out_ref[here, span]
        )
        for k in range(span.start // rows, span.stop // rows):
            at = k * rows - span.start
            backs[k][0, :, cols] = grad_query[at : at + rows]
        grad_key, grad_value = sums.get(n, (0.0, 0.0))
        sums[n] = (grad_key + add_key, grad_value + add_value)

    for n in range(EARLY, heads):
        head_span(n, slice(0, 2 * rows), early_ref[: 2 * rows, n * HDIM : (n + 1) * HDIM])
    corner = jnp.concatenate([corner0[...], corner1[...]], axis=0)
    live = token_pos((rows, 1), 0, meta[Z], early) < meta[COUNT]
    tile = 2 * HDIM
    for i in range(w_ref.shape[0] // tile):
        part = slice(i * tile, (i + 1) * tile)
        late_ref[:, part] = jnp.where(live, dot(corner, w_ref[part, :], 1, 1), 0.0).astype(bf16)
    for n in range(heads):
        cols = slice(n * HDIM, (n + 1) * HDIM)
        if n < EARLY:
            sums[n] = (done[1][:, cols], done[2][:, cols])
            for k in range(early // rows):
                backs[k][0, :, cols] = done[0][k * rows : (k + 1) * rows, cols]
            head_span(n, slice(early, total), late_ref[:, cols])
        else:
            grad = jnp.concatenate([early_ref[2 * rows :, cols], late_ref[:, cols]], axis=0)
            head_span(n, slice(2 * rows, total), grad)
        for k in range(4):
            mine = slice(k * rows, (k + 1) * rows)
            backs[k][1, :, cols] = sums[n][0][mine].astype(bf16)
            backs[k][2, :, cols] = sums[n][1][mine].astype(bf16)


def backward(meta, pieces, grad, corners, weight, saved, done):
    shapes = [sds(pieces[0].shape, bf16)] * 4
    operands = (meta, *pieces, grad, *corners, weight, *saved, *done)
    scratch = [pltpu.VMEM((pieces[0].shape[1], weight.shape[0]), bf16)]
    return whole(backward_kernel, shapes, operands, "attend_backward", 1, 10, scratch)


LINE = HDIM // 8


def line_at(meta, head, other, j):
    at = head * HDIM + ((meta[CORE] ^ other) * 4 + (meta[CHIP] ^ j)) * LINE
    return pl.ds(pl.multiple_of(at, LINE), LINE)


def lines_of(meta, heads_ref):
    lines = []
    for other in (1, 0):
        for j in range(4):
            lines += [heads_ref[line_at(meta, h, other, j), :] for h in range(heads_ref.shape[0] // HDIM)]
    return jnp.concatenate(lines, axis=0)


def weight_kernel(meta, p0, p1, p2, p3, bias_ref, heads_a, *refs):
    pieces, grads = (p0, p1, p2, p3), refs[:-6]
    weight_ref, inverse_ref, out_ref, send_ref, keep_ref, heads_b = refs[-6:]
    rows = p0.shape[1]
    query_live = token_pos((1, 4 * rows), 1, meta[Z]) < meta[COUNT]
    tile = 4 * HDIM
    tiles = send_ref.shape[1] // tile
    whole_size = send_ref.shape[0] // 4

    def product(lines, first, i):
        cols = slice(i * tile, (i + 1) * tile)
        result = dot(lines, jnp.concatenate([g[:, cols] for g in grads], axis=0), 1, 0)
        size = lines.shape[0] // 8
        for j in range(4):
            at = slice(j * whole_size + first, j * whole_size + first + size)
            send_ref[at, cols] = result[j * size : (j + 1) * size].astype(bf16)
            keep_ref[at, cols] = result[(4 + j) * size : (5 + j) * size]

    lines = lines_of(meta, heads_a)
    count = p3.shape[2] // HDIM
    for n in range(max(tiles, 2 * count)):
        if n < 2 * count:
            h, t = divmod(n, 2)
            query, key, value = head_of(pieces, 1, h)
            span = slice(2 * rows * t, 2 * rows * (t + 1))
            outs = (weight_ref, inverse_ref, out_ref, heads_b, h, span)
            span_forward(query, key, value, bias_ref[:, span], query_live[:, span], *outs)
        if n < tiles:
            product(lines, 0, n)
    lines_b = lines_of(meta, heads_b)
    for i in range(tiles):
        product(lines_b, lines.shape[0] // 8, i)


def weight_halves(meta, pieces, bias, heads, grads):
    forward_out = forward_shapes(pieces)
    width = heads.shape[0] + pieces[-1].shape[2]
    shape = (width // 2, grads[0].shape[1])
    shapes = forward_out[:3] + [sds(shape, bf16), sds(shape, f32)]
    scratch = [pltpu.VMEM(forward_out[3].shape, bf16)]
    return whole(weight_kernel, shapes, (meta, *pieces, bias, heads, *grads), "weight_halves", 1, 10, scratch)


def add_kernel(keep_ref, recv_ref, *outs):
    size = outs[0].shape[0]
    for j, out_ref in enumerate(outs):
        part = slice(j * size, (j + 1) * size)
        out_ref[...] = (keep_ref[part, :] + recv_ref[part, :].astype(f32)).astype(out_ref.dtype)


def add_parts(keep, recv):
    shape = (keep.shape[0] // 4, keep.shape[1])
    return whole(add_kernel, [sds(shape, f32)] + [sds(shape, bf16)] * 3, (keep, recv), "add_parts")


def total_kernel(scale, own_ref, r1, r2, r3, out_ref):
    total = own_ref[...] + r1[...].astype(f32) + r2[...].astype(f32) + r3[...].astype(f32)
    out_ref[...] = (total * scale).astype(bf16)


def total_of(own, recvs, scale):
    return whole(functools.partial(total_kernel, scale), sds(own.shape, bf16), (own, *recvs), "scene_mean")


def weight_copies(meta, parts, first, out_ref, sems):
    copies = []
    for p, ref in enumerate(parts, first):
        for h in range(ref.shape[0] // LINE):
            line = out_ref.at[line_at(meta, h, p // 4, p % 4), :]
            copies.append(pltpu.make_async_copy(ref.at[pl.ds(h * LINE, LINE), :], line, sems.at[len(copies)]))
    return copies


def head_copies(meta, pieces, outs, sems):
    copies = []
    for k, ref in pieces.items():
        width = ref.shape[2]
        start = pl.multiple_of((meta[Z] ^ k) * width, 128)
        for i, out_ref in enumerate(outs):
            part = out_ref.at[:, pl.ds(start, width)]
            copies.append(pltpu.make_async_copy(ref.at[i], part, sems.at[len(copies)]))
    return copies


def join(kernel, meta, parts, shapes, copies, name, outs=()):
    return pl.pallas_call(
        kernel,
        out_shape=shapes,
        in_specs=[pl.BlockSpec(memory_space=pltpu.SMEM)]
        + [pl.BlockSpec(memory_space=pltpu.VMEM)] * len(parts)
        + [pl.BlockSpec(memory_space=pl.ANY)] * len(outs),
        out_specs=[pl.BlockSpec(memory_space=pl.ANY)] * len(shapes),
        scratch_shapes=[pltpu.SemaphoreType.DMA((n,)) for n in copies],
        input_output_aliases={1 + len(parts) + i: i for i in range(len(outs))},
        compiler_params=params(),
        cost_estimate=NO_COST,
        name=name,
    )(meta, *parts, *outs)


def join_weight_kernel(meta, *refs):
    run_all(weight_copies(meta, refs[:4], 0, refs[4], refs[5]))


def join_weight(meta, near):
    size, outw = near[0].shape
    return join(join_weight_kernel, meta, near, [sds((8 * size, outw), bf16)], [4 * size // LINE], "join_weight")[0]


def join_heads_kernel(meta, own, back2, back3, *refs):
    run_all(head_copies(meta, {0: own, 2: back2, 3: back3}, refs[:3], refs[3]))


def join_heads(meta, own, back2, back3):
    _, rows, width = own.shape
    shapes = [sds((rows, 4 * width), bf16)] * 3
    return join(join_heads_kernel, meta, (own, back2, back3), shapes, [9], "join_heads")


def join_last_kernel(meta, *refs):
    far, back1, outs, sems = refs[:4], refs[4], refs[9:13], refs[13:]
    run_all(weight_copies(meta, far, 4, outs[3], sems[0]) + head_copies(meta, {1: back1}, outs[:3], sems[1]))


def join_last(meta, far, back1, outs):
    shapes = [sds(x.shape, x.dtype) for x in outs]
    return join(join_last_kernel, meta, (*far, back1), shapes, [4 * far[0].shape[0] // LINE, 3], "join_last", outs)


def dense_body(queries, keys_in, values, out_grad, out_weight, voxel_count):
    meta = jnp.stack([lax.axis_index("shard"), voxel_count[0], lax.axis_index("core"), lax.axis_index("chips")])
    meta = meta.astype(jnp.int32)

    def send(x, k, *earlier):
        return swap(after(x, *earlier) if earlier else x, "shard", 4, k)

    across = send(out_grad, 2)
    beside = send(out_grad, 1)
    own, near1, far2a, far2b, far3a, far3b = pack(meta, queries, keys_in, values)
    piece1 = send(near1, 1)
    piece3a = send(far3a, 3, beside)
    piece2a = send(far2a, 2, across)
    piece3b = send(far3b, 3, piece3a)
    piece2b = send(far2b, 2, piece2a)
    half = across.shape[0] // 2
    mine = hold(after(out_grad, across))
    grad_early = grad_attn(meta, (mine, beside, across), out_weight, 0)
    corners = [send(across[:half], 1), send(after(across, piece1, grad_early)[half:], 1)]

    *saved_a, heads_a, bias = forward(meta, (own, piece1, piece2a, piece3a))
    early = backward_early((own, piece1, piece2a, piece3a), grad_early, saved_a)
    heads_a, *early, piece2b, piece3b = lax.optimization_barrier((heads_a, *early, piece2b, piece3b))
    grad_early, piece2b, *corners = lax.optimization_barrier((grad_early, piece2b, *corners))
    grads = (mine, beside, across, *corners)

    *saved_b, out, keep = weight_halves(meta, (own, piece1, piece2b, piece3b), bias, heads_a, grads)
    recv = swap(out, "core", 2, 1)
    corners = after(grads[3:], out)
    pieces = (own, piece1, piece2a, piece3a, piece2b, piece3b)
    own0, *backs = backward(meta, pieces, grad_early, corners, out_weight, (*saved_a, *saved_b), early)
    own_part, *sends = add_parts(after(keep, own0), recv)
    recvs = [swap(x, "chips", 4, j + 1) for j, x in enumerate(sends)]
    back3, back2 = send(backs[2], 3), send(backs[1], 2)
    done = total_of(own_part, recvs, 1.0 / 8)
    near = [done] + [swap(done, "chips", 4, j) for j in (1, 2, 3)]
    back1 = send(backs[0], 1, near[1])
    weight = join_weight(meta, near)
    weight, *near, back2, back3 = lax.optimization_barrier((weight, *near, back2, back3))
    far = [swap(x, "core", 2, 1) for x in near]
    heads = join_heads(meta, own0, back2, back3)
    return tuple(join_last(meta, far, back1, (*heads, weight)))


def attend_listed(queries, keys_in, values, block_ids, live_count):
    row_count, width_all = queries.shape
    head_count = width_all // HDIM
    block_count = row_count // BLOCK
    score_scale = 1.0 / math.sqrt(HDIM)
    query_blk = queries.reshape(block_count, BLOCK, head_count, HDIM)
    key_blk = keys_in.reshape(block_count, BLOCK, head_count, HDIM)[block_ids].reshape(
        block_count, NB * BLOCK, head_count, HDIM
    )
    value_blk = values.reshape(block_count, BLOCK, head_count, HDIM)[block_ids].reshape(
        block_count, NB * BLOCK, head_count, HDIM
    )
    query_pos = jnp.arange(row_count, dtype=jnp.int32).reshape(block_count, BLOCK)
    key_pos = (
        block_ids[:, :, None] * BLOCK + jnp.arange(BLOCK, dtype=jnp.int32)[None, None, :]
    ).reshape(block_count, NB * BLOCK)
    allowed = (key_pos[:, None, :] < live_count) | (query_pos[:, :, None] >= live_count)
    scores = (
        jnp.einsum("bqhd,bkhd->bhqk", query_blk, key_blk, preferred_element_type=jnp.float32)
        * score_scale
    )
    scores = jnp.where(allowed[:, None], scores, -jnp.inf)
    peak = jnp.max(scores, axis=-1, keepdims=True)
    weights = jnp.exp(scores - peak)
    probs = weights / jnp.sum(weights, axis=-1, keepdims=True)
    return (query_blk, key_blk, value_blk, probs)


def listed_body(queries, keys_in, values, out_grad, out_weight, block_lists, voxel_count):
    local_rows = queries.shape[0]
    live_count = voxel_count[0]
    block_ids = block_lists[0]
    positions = lax.axis_index("shard") * local_rows + jnp.arange(local_rows, dtype=jnp.int32)
    grad_live = jnp.where((positions < live_count)[:, None], out_grad, jnp.zeros_like(out_grad))
    query_head, key_head, value_head = (
        lax.all_to_all(queries, "shard", split_axis=1, concat_axis=0, tiled=True),
        lax.all_to_all(keys_in, "shard", split_axis=1, concat_axis=0, tiled=True),
        lax.all_to_all(values, "shard", split_axis=1, concat_axis=0, tiled=True),
    )
    row_count, width_all = query_head.shape
    head_count = width_all // HDIM
    block_count = row_count // BLOCK
    score_scale = 1.0 / math.sqrt(HDIM)
    query_blk, key_blk, value_blk, probs = attend_listed(
        query_head, key_head, value_head, block_ids, live_count
    )
    prob_bf = probs.astype(jnp.bfloat16)
    heads_out = (
        jnp.einsum("bhqk,bkhd->bqhd", prob_bf, value_blk, preferred_element_type=jnp.float32)
        .reshape(row_count, width_all)
        .astype(jnp.bfloat16)
    )
    row_piece = lax.all_gather(grad_live, "shard", axis=0, tiled=True)
    acc_now = jnp.einsum("rw,ro->wo", heads_out, row_piece, preferred_element_type=jnp.float32)
    product = jnp.einsum("ro,wo->rw", row_piece, out_weight, preferred_element_type=jnp.float32)
    grad_o = product.astype(jnp.bfloat16).reshape(block_count, BLOCK, head_count, HDIM)
    grad_prob = jnp.einsum("bqhd,bkhd->bhqk", grad_o, value_blk, preferred_element_type=jnp.float32)
    row_delta = jnp.sum(probs * grad_prob, axis=-1, keepdims=True)
    dscore = (probs * (grad_prob - row_delta) * score_scale).astype(jnp.bfloat16)
    grad_query = (
        jnp.einsum("bhqk,bkhd->bqhd", dscore, key_blk, preferred_element_type=jnp.float32)
        .reshape(row_count, width_all)
        .astype(jnp.bfloat16)
    )
    onehot = (
        block_ids[:, :, None] == jnp.arange(block_count, dtype=jnp.int32)[None, None, :]
    ).astype(jnp.float32)
    key_parts = jnp.einsum(
        "bhqk,bqhd->bkhd", dscore, query_blk, preferred_element_type=jnp.float32
    ).reshape(block_count, NB, BLOCK, width_all)
    value_parts = jnp.einsum(
        "bhqk,bqhd->bkhd", prob_bf, grad_o, preferred_element_type=jnp.float32
    ).reshape(block_count, NB, BLOCK, width_all)
    grad_key = (
        jnp.einsum("bjc,bjrx->crx", onehot, key_parts, precision=lax.Precision.HIGHEST)
        .reshape(row_count, width_all)
        .astype(jnp.bfloat16)
    )
    grad_value = (
        jnp.einsum("bjc,bjrx->crx", onehot, value_parts, precision=lax.Precision.HIGHEST)
        .reshape(row_count, width_all)
        .astype(jnp.bfloat16)
    )
    query_back, key_back, value_back = (
        lax.all_to_all(grad_query, "shard", split_axis=0, concat_axis=1, tiled=True),
        lax.all_to_all(grad_key, "shard", split_axis=0, concat_axis=1, tiled=True),
        lax.all_to_all(grad_value, "shard", split_axis=0, concat_axis=1, tiled=True),
    )
    scene_total = lax.axis_size(DP)
    summed = lax.psum(acc_now, DP)
    grad_weight = (summed / scene_total).astype(jnp.bfloat16)
    return (query_back, key_back, value_back, grad_weight)


def body(queries, keys_in, values, out_grad, out_weight, block_lists, voxel_count):
    dense = block_lists.shape[1] == NB and queries.shape[0] == BLOCK
    if dense and lax.axis_size("shard") == 4 and lax.axis_size("chips") == 4:
        return dense_body(queries, keys_in, values, out_grad, out_weight, voxel_count)
    return listed_body(queries, keys_in, values, out_grad, out_weight, block_lists, voxel_count)


def solution(mesh):
    chips = mesh.shape["dp"] // 2
    mesh = jax.sharding.Mesh(mesh.devices.reshape(chips, 2, -1), ("chips", "core", "shard"))
    return jax.shard_map(
        body,
        mesh=mesh,
        in_specs=(
            P((*DP, "shard"), None),
            P((*DP, "shard"), None),
            P((*DP, "shard"), None),
            P((*DP, "shard"), None),
            P("shard", None),
            P(DP, None, None),
            P(DP),
        ),
        out_specs=(
            P((*DP, "shard"), None),
            P((*DP, "shard"), None),
            P((*DP, "shard"), None),
            P("shard", None),
        ),
        check_vma=False,
    )
```

```python
import functools
import math

import jax
import jax.numpy as jnp
from jax import lax
from jax.experimental import pallas as pl
from jax.experimental.pallas import tpu as pltpu
from jax.sharding import PartitionSpec as P

HDIM = 128
BLOCK = 128
NB = 4
MIB = 1024 * 1024
DP = ("chips", "core")

Z, COUNT, CORE, CHIP = range(4)

EARLY = 3

NO_COST = pl.CostEstimate(flops=0, bytes_accessed=1024, transcendentals=0)

f32 = jnp.float32
bf16 = jnp.bfloat16


def dot(a, b, ca, cb):
    return lax.dot_general(a, b, (((ca,), (cb,)), ((), ())), preferred_element_type=f32)


def sds(shape, dtype):
    return jax.ShapeDtypeStruct(shape, dtype)


def params(mib=2):
    return pltpu.CompilerParams(vmem_limit_bytes=mib * MIB)


def swap(x, axis, size, flip):
    return lax.ppermute(x, axis, [(i, i ^ flip) for i in range(size)])


def after(x, *earlier):
    return lax.optimization_barrier((x, *earlier))[0]


def run_all(copies):
    for copy in copies:
        copy.start()
    for copy in copies:
        copy.wait()


def whole(kernel, out_shape, operands, name, scalars=0, mib=2, scratch=()):
    return pl.pallas_call(
        kernel,
        out_shape=out_shape,
        in_specs=[pl.BlockSpec(memory_space=pltpu.SMEM)] * scalars
        + [pl.BlockSpec(memory_space=pltpu.VMEM)] * (len(operands) - scalars),
        out_specs=jax.tree.map(lambda _: pl.BlockSpec(memory_space=pltpu.VMEM), out_shape),
        scratch_shapes=scratch,
        compiler_params=params(mib),
        cost_estimate=NO_COST,
        name=name,
    )(*operands)


def pack_kernel(meta, q_ref, k_ref, v_ref, *refs):
    *outs, sems = refs
    width = outs[0].shape[2]
    copies = []
    for n, out_ref in enumerate(outs):
        k, first = (n, 0) if n < 2 else (n // 2 + 1, n % 2 * EARLY * HDIM)
        start = pl.multiple_of((meta[Z] ^ k) * width + first, 128)
        for i, ref in enumerate((q_ref, k_ref, v_ref)):
            part = ref.at[:, pl.ds(start, out_ref.shape[2])]
            copies.append(pltpu.make_async_copy(part, out_ref.at[i], sems.at[3 * n + i]))
    run_all(copies)


def pack(meta, queries, keys_in, values):
    rows, width = queries.shape
    part, early = width // 4, EARLY * HDIM
    shapes = [sds((3, rows, n), bf16) for n in (part, part, early, part - early, early, part - early)]
    return pl.pallas_call(
        pack_kernel,
        out_shape=shapes,
        in_specs=[pl.BlockSpec(memory_space=pltpu.SMEM)] + [pl.BlockSpec(memory_space=pl.ANY)] * 3,
        out_specs=[pl.BlockSpec(memory_space=pltpu.VMEM)] * len(shapes),
        scratch_shapes=[pltpu.SemaphoreType.DMA((3 * len(shapes),))],
        compiler_params=params(),
        cost_estimate=NO_COST,
        name="pack_heads",
    )(meta, queries, keys_in, values)


def hold_kernel(in_ref, out_ref):
    out_ref[...] = in_ref[...]


def hold(x):
    return whole(hold_kernel, sds(x.shape, x.dtype), (x,), "hold")


def token_pos(shape, dim, z, start=0):
    return (lax.broadcasted_iota(jnp.int32, shape, dim) + start) ^ (z * BLOCK)


def grad_attn_kernel(start, meta, *refs):
    *grads, w_ref, out_ref = refs
    grad = jnp.concatenate([g[...] for g in grads], axis=0)
    live = token_pos((grad.shape[0], 1), 0, meta[Z], start) < meta[COUNT]
    tile = 2 * HDIM

    for i in range(w_ref.shape[0] // tile):
        part = slice(i * tile, (i + 1) * tile)
        out_ref[:, part] = jnp.where(live, dot(grad, w_ref[part, :], 1, 1), 0.0).astype(bf16)


def grad_attn(meta, grads, weight, start):
    shape = (sum(g.shape[0] for g in grads), weight.shape[0])
    kernel = functools.partial(grad_attn_kernel, start)
    return whole(kernel, sds(shape, bf16), (meta, *grads, weight), "grad_attn", 1, 6)


def head_of(pieces, group, h):
    part = pieces[-1].shape[2]
    parts = []
    for p in pieces:
        start = (group * EARLY * HDIM if p.shape[2] > part else 0) + h * HDIM
        parts.append([p[i, :, start : start + HDIM] for i in range(3)])
    return (jnp.concatenate(x, axis=0) for x in zip(*parts))


def span_forward(query, key, value, bias, live, weight_ref, inverse_ref, out_ref, heads_ref, h, span):
    cols = slice(h * HDIM, (h + 1) * HDIM)
    scores = dot(key, query[span], 1, 1) + bias
    peak = jnp.max(scores, axis=0, keepdims=True)
    weights = jnp.exp2((scores - peak) * (math.log2(math.e) / math.sqrt(HDIM))).astype(bf16)
    weight_ref[h, :, span] = weights
    inverse = 1.0 / jnp.sum(weights.astype(f32), axis=0, keepdims=True)
    inverse_ref[h, :, span] = inverse
    heads = dot(value, weights, 0, 0) * inverse
    out_ref[cols, span] = heads
    heads_ref[cols, span] = jnp.where(live, heads, 0.0).astype(bf16)


def forward_shapes(pieces):
    _, rows, width = pieces[-1].shape
    total = 4 * rows
    return [
        sds((width // HDIM, total, total), bf16),
        sds((width // HDIM, 1, total), f32),
        sds((width, total), f32),
        sds((width, total), bf16),
    ]


def forward_kernel(meta, p0, p1, p2, p3, weight_ref, inverse_ref, out_ref, heads_ref, bias_ref):
    pieces = (p0, p1, p2, p3)
    rows = p0.shape[1]
    total = 4 * rows
    query_live = token_pos((1, total), 1, meta[Z]) < meta[COUNT]
    key_live = token_pos((total, 1), 0, meta[Z]) < meta[COUNT]
    bias_ref[...] = jnp.where(key_live | ~query_live, 0.0, -jnp.inf)
    for h in range(p3.shape[2] // HDIM):
        query, key, value = head_of(pieces, 0, h)
        for t in range(2):
            span = slice(2 * rows * t, 2 * rows * (t + 1))
            outs = (weight_ref, inverse_ref, out_ref, heads_ref, h, span)
            span_forward(query, key, value, bias_ref[:, span], query_live[:, span], *outs)


def forward(meta, pieces):
    total = 4 * pieces[-1].shape[1]
    shapes = forward_shapes(pieces) + [sds((total, total), f32)]
    return whole(forward_kernel, shapes, (meta, *pieces), "attend_forward", 1, 8)


def span_gradients(query, key, value, grad, weights, inverse, outs):
    turned = grad.astype(f32).T
    row_delta = jnp.sum(outs * turned, axis=0, keepdims=True)
    grad_prob = dot(value, grad, 1, 1)
    factor = inverse * (1.0 / math.sqrt(HDIM))
    dscore = (weights.astype(f32) * ((grad_prob - row_delta) * factor)).astype(bf16)
    grad_query = dot(key, dscore, 0, 0).T.astype(bf16)
    grad_value = dot(weights, (turned * inverse).T.astype(bf16), 1, 0)
    return grad_query, dot(dscore, query, 1, 0), grad_value


def backward_early_kernel(*refs):
    pieces, (grad_ref, weight_ref, inverse_ref, out_ref, query_out, key_out, value_out) = refs[:4], refs[4:]
    early = grad_ref.shape[0]
    for h in range(pieces[-1].shape[2] // HDIM):
        cols = slice(h * HDIM, (h + 1) * HDIM)
        query, key, value = head_of(pieces, 0, h)
        grad_key = grad_value = 0.0
        for span in (slice(0, 2 * BLOCK), slice(2 * BLOCK, early)):
            grad_query, add_key, add_value = span_gradients(
                query[span], key, value, grad_ref[span, cols],
                weight_ref[h, :, span], inverse_ref[h, :, span], out_ref[cols, span],
            )
            query_out[span, cols] = grad_query
            grad_key += add_key
            grad_value += add_value
        key_out[:, cols] = grad_key
        value_out[:, cols] = grad_value


def backward_early(pieces, grad, saved):
    _, rows, part = pieces[-1].shape
    shapes = [sds((grad.shape[0], part), bf16), sds((4 * rows, part), f32), sds((4 * rows, part), f32)]
    return whole(backward_early_kernel, shapes, (*pieces, grad, *saved), "backward_early", 0, 8)


def backward_kernel(meta, own, near, far2a, far3a, far2b, far3b, early_ref, corner0, corner1, w_ref, *refs):
    saved, done, backs, late_ref = (refs[:3], refs[3:6]), refs[6:9], refs[9:13], refs[13]
    rows = own.shape[1]
    early, total = early_ref.shape[0], 4 * rows
    heads = own.shape[2] // HDIM
    sums = {}

    def head_span(n, span, grad):
        group, h = divmod(n, EARLY)
        query, key, value = head_of(((own, near, far2a, far3a), (own, near, far2b, far3b))[group], group, h)
        weight_ref, inverse_ref, out_ref = saved[group]
        here = slice(h * HDIM, (h + 1) * HDIM)
        cols = slice(n * HDIM, (n + 1) * HDIM)
        grad_query, add_key, add_value = span_gradients(
            query[span], key, value, grad, weight_ref[h, :, span], inverse_ref[h, :, span], out_ref[here, span]
        )
        for k in range(span.start // rows, span.stop // rows):
            at = k * rows - span.start
            backs[k][0, :, cols] = grad_query[at : at + rows]
        grad_key, grad_value = sums.get(n, (0.0, 0.0))
        sums[n] = (grad_key + add_key, grad_value + add_value)

    for n in range(EARLY, heads):
        head_span(n, slice(0, 2 * rows), early_ref[: 2 * rows, n * HDIM : (n + 1) * HDIM])
    corner = jnp.concatenate([corner0[...], corner1[...]], axis=0)
    live = token_pos((rows, 1), 0, meta[Z], early) < meta[COUNT]
    tile = 2 * HDIM
    for i in range(w_ref.shape[0] // tile):
        part = slice(i * tile, (i + 1) * tile)
        late_ref[:, part] = jnp.where(live, dot(corner, w_ref[part, :], 1, 1), 0.0).astype(bf16)
    for n in range(heads):
        cols = slice(n * HDIM, (n + 1) * HDIM)
        if n < EARLY:
            sums[n] = (done[1][:, cols], done[2][:, cols])
            for k in range(early // rows):
                backs[k][0, :, cols] = done[0][k * rows : (k + 1) * rows, cols]
            head_span(n, slice(early, total), late_ref[:, cols])
        else:
            grad = jnp.concatenate([early_ref[2 * rows :, cols], late_ref[:, cols]], axis=0)
            head_span(n, slice(2 * rows, total), grad)
        for k in range(4):
            mine = slice(k * rows, (k + 1) * rows)
            backs[k][1, :, cols] = sums[n][0][mine].astype(bf16)
            backs[k][2, :, cols] = sums[n][1][mine].astype(bf16)


def backward(meta, pieces, grad, corners, weight, saved, done):
    shapes = [sds(pieces[0].shape, bf16)] * 4
    operands = (meta, *pieces, grad, *corners, weight, *saved, *done)
    scratch = [pltpu.VMEM((pieces[0].shape[1], weight.shape[0]), bf16)]
    return whole(backward_kernel, shapes, operands, "attend_backward", 1, 10, scratch)


LINE = HDIM // 8


def line_at(meta, head, other, j):
    at = head * HDIM + ((meta[CORE] ^ other) * 4 + (meta[CHIP] ^ j)) * LINE
    return pl.ds(pl.multiple_of(at, LINE), LINE)


def lines_of(meta, heads_ref):
    lines = []
    for other in (1, 0):
        for j in range(4):
            lines += [heads_ref[line_at(meta, h, other, j), :] for h in range(heads_ref.shape[0] // HDIM)]
    return jnp.concatenate(lines, axis=0)


def weight_kernel(meta, p0, p1, p2, p3, bias_ref, heads_a, *refs):
    pieces, grads = (p0, p1, p2, p3), refs[:-6]
    weight_ref, inverse_ref, out_ref, send_ref, keep_ref, heads_b = refs[-6:]
    rows = p0.shape[1]
    query_live = token_pos((1, 4 * rows), 1, meta[Z]) < meta[COUNT]
    tile = 4 * HDIM
    tiles = send_ref.shape[1] // tile
    whole_size = send_ref.shape[0] // 4

    def product(lines, first, i):
        cols = slice(i * tile, (i + 1) * tile)
        result = dot(lines, jnp.concatenate([g[:, cols] for g in grads], axis=0), 1, 0)
        size = lines.shape[0] // 8
        for j in range(4):
            at = slice(j * whole_size + first, j * whole_size + first + size)
            send_ref[at, cols] = result[j * size : (j + 1) * size].astype(bf16)
            keep_ref[at, cols] = result[(4 + j) * size : (5 + j) * size]

    lines = lines_of(meta, heads_a)
    count = p3.shape[2] // HDIM
    for n in range(max(tiles, 2 * count)):
        if n < 2 * count:
            h, t = divmod(n, 2)
            query, key, value = head_of(pieces, 1, h)
            span = slice(2 * rows * t, 2 * rows * (t + 1))
            outs = (weight_ref, inverse_ref, out_ref, heads_b, h, span)
            span_forward(query, key, value, bias_ref[:, span], query_live[:, span], *outs)
        if n < tiles:
            product(lines, 0, n)
    lines_b = lines_of(meta, heads_b)
    for i in range(tiles):
        product(lines_b, lines.shape[0] // 8, i)


def weight_halves(meta, pieces, bias, heads, grads):
    forward_out = forward_shapes(pieces)
    width = heads.shape[0] + pieces[-1].shape[2]
    shape = (width // 2, grads[0].shape[1])
    shapes = forward_out[:3] + [sds(shape, bf16), sds(shape, f32)]
    scratch = [pltpu.VMEM(forward_out[3].shape, bf16)]
    return whole(weight_kernel, shapes, (meta, *pieces, bias, heads, *grads), "weight_halves", 1, 10, scratch)


def add_kernel(keep_ref, recv_ref, *outs):
    size = outs[0].shape[0]
    for j, out_ref in enumerate(outs):
        part = slice(j * size, (j + 1) * size)
        out_ref[...] = (keep_ref[part, :] + recv_ref[part, :].astype(f32)).astype(out_ref.dtype)


def add_parts(keep, recv):
    shape = (keep.shape[0] // 4, keep.shape[1])
    return whole(add_kernel, [sds(shape, f32)] + [sds(shape, bf16)] * 3, (keep, recv), "add_parts")


def total_kernel(scale, own_ref, r1, r2, r3, out_ref):
    total = own_ref[...] + r1[...].astype(f32) + r2[...].astype(f32) + r3[...].astype(f32)
    out_ref[...] = (total * scale).astype(bf16)


def total_of(own, recvs, scale):
    return whole(functools.partial(total_kernel, scale), sds(own.shape, bf16), (own, *recvs), "scene_mean")


def weight_copies(meta, parts, first, out_ref, sems):
    copies = []
    for p, ref in enumerate(parts, first):
        for h in range(ref.shape[0] // LINE):
            line = out_ref.at[line_at(meta, h, p // 4, p % 4), :]
            copies.append(pltpu.make_async_copy(ref.at[pl.ds(h * LINE, LINE), :], line, sems.at[len(copies)]))
    return copies


def head_copies(meta, pieces, outs, sems):
    copies = []
    for k, ref in pieces.items():
        width = ref.shape[2]
        start = pl.multiple_of((meta[Z] ^ k) * width, 128)
        for i, out_ref in enumerate(outs):
            part = out_ref.at[:, pl.ds(start, width)]
            copies.append(pltpu.make_async_copy(ref.at[i], part, sems.at[len(copies)]))
    return copies


def join(kernel, meta, parts, shapes, copies, name, outs=()):
    return pl.pallas_call(
        kernel,
        out_shape=shapes,
        in_specs=[pl.BlockSpec(memory_space=pltpu.SMEM)]
        + [pl.BlockSpec(memory_space=pltpu.VMEM)] * len(parts)
        + [pl.BlockSpec(memory_space=pl.ANY)] * len(outs),
        out_specs=[pl.BlockSpec(memory_space=pl.ANY)] * len(shapes),
        scratch_shapes=[pltpu.SemaphoreType.DMA((n,)) for n in copies],
        input_output_aliases={1 + len(parts) + i: i for i in range(len(outs))},
        compiler_params=params(),
        cost_estimate=NO_COST,
        name=name,
    )(meta, *parts, *outs)


def join_weight_kernel(meta, *refs):
    run_all(weight_copies(meta, refs[:4], 0, refs[4], refs[5]))


def join_weight(meta, near):
    size, outw = near[0].shape
    return join(join_weight_kernel, meta, near, [sds((8 * size, outw), bf16)], [4 * size // LINE], "join_weight")[0]


def join_heads_kernel(meta, own, back2, back3, *refs):
    run_all(head_copies(meta, {0: own, 2: back2, 3: back3}, refs[:3], refs[3]))


def join_heads(meta, own, back2, back3):
    _, rows, width = own.shape
    shapes = [sds((rows, 4 * width), bf16)] * 3
    return join(join_heads_kernel, meta, (own, back2, back3), shapes, [9], "join_heads")


def join_last_kernel(meta, *refs):
    far, back1, outs, sems = refs[:4], refs[4], refs[9:13], refs[13:]
    run_all(weight_copies(meta, far, 4, outs[3], sems[0]) + head_copies(meta, {1: back1}, outs[:3], sems[1]))


def join_last(meta, far, back1, outs):
    shapes = [sds(x.shape, x.dtype) for x in outs]
    return join(join_last_kernel, meta, (*far, back1), shapes, [4 * far[0].shape[0] // LINE, 3], "join_last", outs)


def dense_body(queries, keys_in, values, out_grad, out_weight, voxel_count):
    meta = jnp.stack([lax.axis_index("shard"), voxel_count[0], lax.axis_index("core"), lax.axis_index("chips")])
    meta = meta.astype(jnp.int32)

    def send(x, k, *earlier):
        return swap(after(x, *earlier) if earlier else x, "shard", 4, k)

    across = send(out_grad, 2)
    beside = send(out_grad, 1)
    own, near1, far2a, far2b, far3a, far3b = pack(meta, queries, keys_in, values)
    piece1 = send(near1, 1)
    piece3a = send(far3a, 3, beside)
    piece2a = send(far2a, 2, across)
    piece3b = send(far3b, 3, piece3a)
    piece2b = send(far2b, 2, piece2a)
    half = across.shape[0] // 2
    mine = hold(after(out_grad, across))
    grad_early = grad_attn(meta, (mine, beside, across), out_weight, 0)
    corners = [send(across[:half], 1), send(after(across, piece1, grad_early)[half:], 1)]

    *saved_a, heads_a, bias = forward(meta, (own, piece1, piece2a, piece3a))
    early = backward_early((own, piece1, piece2a, piece3a), grad_early, saved_a)
    heads_a, *early, piece2b, piece3b = lax.optimization_barrier((heads_a, *early, piece2b, piece3b))
    grad_early, piece2b, *corners = lax.optimization_barrier((grad_early, piece2b, *corners))
    grads = (mine, beside, across, *corners)

    *saved_b, out, keep = weight_halves(meta, (own, piece1, piece2b, piece3b), bias, heads_a, grads)
    recv = swap(out, "core", 2, 1)
    corners = after(grads[3:], out)
    pieces = (own, piece1, piece2a, piece3a, piece2b, piece3b)
    own0, *backs = backward(meta, pieces, grad_early, corners, out_weight, (*saved_a, *saved_b), early)
    own_part, *sends = add_parts(after(keep, own0), recv)
    recvs = [swap(x, "chips", 4, j + 1) for j, x in enumerate(sends)]
    back2, back3 = send(backs[1], 2), send(backs[2], 3)
    done = total_of(own_part, recvs, 1.0 / 8)
    near = [done] + [swap(done, "chips", 4, j) for j in (1, 2, 3)]
    back1 = send(backs[0], 1, near[1])
    weight = join_weight(meta, near)
    weight, *near, back3, back2 = lax.optimization_barrier((weight, *near, back3, back2))
    far = [swap(x, "core", 2, 1) for x in near]
    heads = join_heads(meta, own0, back2, back3)
    return tuple(join_last(meta, far, back1, (*heads, weight)))


def attend_listed(queries, keys_in, values, block_ids, live_count):
    row_count, width_all = queries.shape
    head_count = width_all // HDIM
    block_count = row_count // BLOCK
    score_scale = 1.0 / math.sqrt(HDIM)
    query_blk = queries.reshape(block_count, BLOCK, head_count, HDIM)
    key_blk = keys_in.reshape(block_count, BLOCK, head_count, HDIM)[block_ids].reshape(
        block_count, NB * BLOCK, head_count, HDIM
    )
    value_blk = values.reshape(block_count, BLOCK, head_count, HDIM)[block_ids].reshape(
        block_count, NB * BLOCK, head_count, HDIM
    )
    query_pos = jnp.arange(row_count, dtype=jnp.int32).reshape(block_count, BLOCK)
    key_pos = (
        block_ids[:, :, None] * BLOCK + jnp.arange(BLOCK, dtype=jnp.int32)[None, None, :]
    ).reshape(block_count, NB * BLOCK)
    allowed = (key_pos[:, None, :] < live_count) | (query_pos[:, :, None] >= live_count)
    scores = (
        jnp.einsum("bqhd,bkhd->bhqk", query_blk, key_blk, preferred_element_type=jnp.float32)
        * score_scale
    )
    scores = jnp.where(allowed[:, None], scores, -jnp.inf)
    peak = jnp.max(scores, axis=-1, keepdims=True)
    weights = jnp.exp(scores - peak)
    probs = weights / jnp.sum(weights, axis=-1, keepdims=True)
    return (query_blk, key_blk, value_blk, probs)


def listed_body(queries, keys_in, values, out_grad, out_weight, block_lists, voxel_count):
    local_rows = queries.shape[0]
    live_count = voxel_count[0]
    block_ids = block_lists[0]
    positions = lax.axis_index("shard") * local_rows + jnp.arange(local_rows, dtype=jnp.int32)
    grad_live = jnp.where((positions < live_count)[:, None], out_grad, jnp.zeros_like(out_grad))
    query_head, key_head, value_head = (
        lax.all_to_all(queries, "shard", split_axis=1, concat_axis=0, tiled=True),
        lax.all_to_all(keys_in, "shard", split_axis=1, concat_axis=0, tiled=True),
        lax.all_to_all(values, "shard", split_axis=1, concat_axis=0, tiled=True),
    )
    row_count, width_all = query_head.shape
    head_count = width_all // HDIM
    block_count = row_count // BLOCK
    score_scale = 1.0 / math.sqrt(HDIM)
    query_blk, key_blk, value_blk, probs = attend_listed(
        query_head, key_head, value_head, block_ids, live_count
    )
    prob_bf = probs.astype(jnp.bfloat16)
    heads_out = (
        jnp.einsum("bhqk,bkhd->bqhd", prob_bf, value_blk, preferred_element_type=jnp.float32)
        .reshape(row_count, width_all)
        .astype(jnp.bfloat16)
    )
    row_piece = lax.all_gather(grad_live, "shard", axis=0, tiled=True)
    acc_now = jnp.einsum("rw,ro->wo", heads_out, row_piece, preferred_element_type=jnp.float32)
    product = jnp.einsum("ro,wo->rw", row_piece, out_weight, preferred_element_type=jnp.float32)
    grad_o = product.astype(jnp.bfloat16).reshape(block_count, BLOCK, head_count, HDIM)
    grad_prob = jnp.einsum("bqhd,bkhd->bhqk", grad_o, value_blk, preferred_element_type=jnp.float32)
    row_delta = jnp.sum(probs * grad_prob, axis=-1, keepdims=True)
    dscore = (probs * (grad_prob - row_delta) * score_scale).astype(jnp.bfloat16)
    grad_query = (
        jnp.einsum("bhqk,bkhd->bqhd", dscore, key_blk, preferred_element_type=jnp.float32)
        .reshape(row_count, width_all)
        .astype(jnp.bfloat16)
    )
    onehot = (
        block_ids[:, :, None] == jnp.arange(block_count, dtype=jnp.int32)[None, None, :]
    ).astype(jnp.float32)
    key_parts = jnp.einsum(
        "bhqk,bqhd->bkhd", dscore, query_blk, preferred_element_type=jnp.float32
    ).reshape(block_count, NB, BLOCK, width_all)
    value_parts = jnp.einsum(
        "bhqk,bqhd->bkhd", prob_bf, grad_o, preferred_element_type=jnp.float32
    ).reshape(block_count, NB, BLOCK, width_all)
    grad_key = (
        jnp.einsum("bjc,bjrx->crx", onehot, key_parts, precision=lax.Precision.HIGHEST)
        .reshape(row_count, width_all)
        .astype(jnp.bfloat16)
    )
    grad_value = (
        jnp.einsum("bjc,bjrx->crx", onehot, value_parts, precision=lax.Precision.HIGHEST)
        .reshape(row_count, width_all)
        .astype(jnp.bfloat16)
    )
    query_back, key_back, value_back = (
        lax.all_to_all(grad_query, "shard", split_axis=0, concat_axis=1, tiled=True),
        lax.all_to_all(grad_key, "shard", split_axis=0, concat_axis=1, tiled=True),
        lax.all_to_all(grad_value, "shard", split_axis=0, concat_axis=1, tiled=True),
    )
    scene_total = lax.axis_size(DP)
    summed = lax.psum(acc_now, DP)
    grad_weight = (summed / scene_total).astype(jnp.bfloat16)
    return (query_back, key_back, value_back, grad_weight)


def body(queries, keys_in, values, out_grad, out_weight, block_lists, voxel_count):
    dense = block_lists.shape[1] == NB and queries.shape[0] == BLOCK
    if dense and lax.axis_size("shard") == 4 and lax.axis_size("chips") == 4:
        return dense_body(queries, keys_in, values, out_grad, out_weight, voxel_count)
    return listed_body(queries, keys_in, values, out_grad, out_weight, block_lists, voxel_count)


def solution(mesh):
    chips = mesh.shape["dp"] // 2
    mesh = jax.sharding.Mesh(mesh.devices.reshape(chips, 2, -1), ("chips", "core", "shard"))
    return jax.shard_map(
        body,
        mesh=mesh,
        in_specs=(
            P((*DP, "shard"), None),
            P((*DP, "shard"), None),
            P((*DP, "shard"), None),
            P((*DP, "shard"), None),
            P("shard", None),
            P(DP, None, None),
            P(DP),
        ),
        out_specs=(
            P((*DP, "shard"), None),
            P((*DP, "shard"), None),
            P((*DP, "shard"), None),
            P("shard", None),
        ),
        check_vma=False,
    )
```

```python
import functools
import math

import jax
import jax.numpy as jnp
from jax import lax
from jax.experimental import pallas as pl
from jax.experimental.pallas import tpu as pltpu
from jax.sharding import PartitionSpec as P

HDIM = 128
BLOCK = 128
NB = 4
MIB = 1024 * 1024
DP = ("chips", "core")

Z, COUNT, CORE, CHIP = range(4)

EARLY = 3

NO_COST = pl.CostEstimate(flops=0, bytes_accessed=1024, transcendentals=0)

f32 = jnp.float32
bf16 = jnp.bfloat16


def dot(a, b, ca, cb):
    return lax.dot_general(a, b, (((ca,), (cb,)), ((), ())), preferred_element_type=f32)


def sds(shape, dtype):
    return jax.ShapeDtypeStruct(shape, dtype)


def params(mib=2):
    return pltpu.CompilerParams(vmem_limit_bytes=mib * MIB)


def swap(x, axis, size, flip):
    return lax.ppermute(x, axis, [(i, i ^ flip) for i in range(size)])


def after(x, *earlier):
    return lax.optimization_barrier((x, *earlier))[0]


def run_all(copies):
    for copy in copies:
        copy.start()
    for copy in copies:
        copy.wait()


def whole(kernel, out_shape, operands, name, scalars=0, mib=2, scratch=()):
    return pl.pallas_call(
        kernel,
        out_shape=out_shape,
        in_specs=[pl.BlockSpec(memory_space=pltpu.SMEM)] * scalars
        + [pl.BlockSpec(memory_space=pltpu.VMEM)] * (len(operands) - scalars),
        out_specs=jax.tree.map(lambda _: pl.BlockSpec(memory_space=pltpu.VMEM), out_shape),
        scratch_shapes=scratch,
        compiler_params=params(mib),
        cost_estimate=NO_COST,
        name=name,
    )(*operands)


def pack_kernel(meta, q_ref, k_ref, v_ref, *refs):
    *outs, sems = refs
    width = outs[0].shape[2]
    copies = []
    for n, out_ref in enumerate(outs):
        k, first = (n, 0) if n < 2 else (n // 2 + 1, n % 2 * EARLY * HDIM)
        start = pl.multiple_of((meta[Z] ^ k) * width + first, 128)
        for i, ref in enumerate((q_ref, k_ref, v_ref)):
            part = ref.at[:, pl.ds(start, out_ref.shape[2])]
            copies.append(pltpu.make_async_copy(part, out_ref.at[i], sems.at[3 * n + i]))
    run_all(copies)


def pack(meta, queries, keys_in, values):
    rows, width = queries.shape
    part, early = width // 4, EARLY * HDIM
    shapes = [sds((3, rows, n), bf16) for n in (part, part, early, part - early, early, part - early)]
    return pl.pallas_call(
        pack_kernel,
        out_shape=shapes,
        in_specs=[pl.BlockSpec(memory_space=pltpu.SMEM)] + [pl.BlockSpec(memory_space=pl.ANY)] * 3,
        out_specs=[pl.BlockSpec(memory_space=pltpu.VMEM)] * len(shapes),
        scratch_shapes=[pltpu.SemaphoreType.DMA((3 * len(shapes),))],
        compiler_params=params(),
        cost_estimate=NO_COST,
        name="pack_heads",
    )(meta, queries, keys_in, values)


def hold_kernel(in_ref, out_ref):
    out_ref[...] = in_ref[...]


def hold(x):
    return whole(hold_kernel, sds(x.shape, x.dtype), (x,), "hold")


def token_pos(shape, dim, z, start=0):
    return (lax.broadcasted_iota(jnp.int32, shape, dim) + start) ^ (z * BLOCK)


def grad_attn_kernel(start, meta, *refs):
    *grads, w_ref, out_ref = refs
    grad = jnp.concatenate([g[...] for g in grads], axis=0)
    live = token_pos((grad.shape[0], 1), 0, meta[Z], start) < meta[COUNT]
    tile = 2 * HDIM

    for i in range(w_ref.shape[0] // tile):
        part = slice(i * tile, (i + 1) * tile)
        out_ref[:, part] = jnp.where(live, dot(grad, w_ref[part, :], 1, 1), 0.0).astype(bf16)


def grad_attn(meta, grads, weight, start):
    shape = (sum(g.shape[0] for g in grads), weight.shape[0])
    kernel = functools.partial(grad_attn_kernel, start)
    return whole(kernel, sds(shape, bf16), (meta, *grads, weight), "grad_attn", 1, 6)


def head_of(pieces, group, h):
    part = pieces[-1].shape[2]
    parts = []
    for p in pieces:
        start = (group * EARLY * HDIM if p.shape[2] > part else 0) + h * HDIM
        parts.append([p[i, :, start : start + HDIM] for i in range(3)])
    return (jnp.concatenate(x, axis=0) for x in zip(*parts))


def span_forward(query, key, value, bias, live, weight_ref, inverse_ref, out_ref, heads_ref, h, span):
    cols = slice(h * HDIM, (h + 1) * HDIM)
    scores = dot(key, query[span], 1, 1) + bias
    peak = jnp.max(scores, axis=0, keepdims=True)
    weights = jnp.exp2((scores - peak) * (math.log2(math.e) / math.sqrt(HDIM))).astype(bf16)
    weight_ref[h, :, span] = weights
    inverse = 1.0 / jnp.sum(weights.astype(f32), axis=0, keepdims=True)
    inverse_ref[h, :, span] = inverse
    heads = dot(value, weights, 0, 0) * inverse
    out_ref[cols, span] = heads
    heads_ref[cols, span] = jnp.where(live, heads, 0.0).astype(bf16)


def forward_shapes(pieces):
    _, rows, width = pieces[-1].shape
    total = 4 * rows
    return [
        sds((width // HDIM, total, total), bf16),
        sds((width // HDIM, 1, total), f32),
        sds((width, total), f32),
        sds((width, total), bf16),
    ]


def forward_kernel(meta, p0, p1, p2, p3, weight_ref, inverse_ref, out_ref, heads_ref, bias_ref):
    pieces = (p0, p1, p2, p3)
    rows = p0.shape[1]
    total = 4 * rows
    query_live = token_pos((1, total), 1, meta[Z]) < meta[COUNT]
    key_live = token_pos((total, 1), 0, meta[Z]) < meta[COUNT]
    bias_ref[...] = jnp.where(key_live | ~query_live, 0.0, -jnp.inf)
    for h in range(p3.shape[2] // HDIM):
        query, key, value = head_of(pieces, 0, h)
        for t in range(2):
            span = slice(2 * rows * t, 2 * rows * (t + 1))
            outs = (weight_ref, inverse_ref, out_ref, heads_ref, h, span)
            span_forward(query, key, value, bias_ref[:, span], query_live[:, span], *outs)


def forward(meta, pieces):
    total = 4 * pieces[-1].shape[1]
    shapes = forward_shapes(pieces) + [sds((total, total), f32)]
    return whole(forward_kernel, shapes, (meta, *pieces), "attend_forward", 1, 8)


def span_gradients(query, key, value, grad, weights, inverse, outs):
    turned = grad.astype(f32).T
    row_delta = jnp.sum(outs * turned, axis=0, keepdims=True)
    grad_prob = dot(value, grad, 1, 1)
    factor = inverse * (1.0 / math.sqrt(HDIM))
    dscore = (weights.astype(f32) * ((grad_prob - row_delta) * factor)).astype(bf16)
    grad_query = dot(key, dscore, 0, 0).T.astype(bf16)
    grad_value = dot(weights, (turned * inverse).T.astype(bf16), 1, 0)
    return grad_query, dot(dscore, query, 1, 0), grad_value


def backward_early_kernel(*refs):
    pieces, (grad_ref, weight_ref, inverse_ref, out_ref, query_out, key_out, value_out) = refs[:4], refs[4:]
    early = grad_ref.shape[0]
    for h in range(pieces[-1].shape[2] // HDIM):
        cols = slice(h * HDIM, (h + 1) * HDIM)
        query, key, value = head_of(pieces, 0, h)
        grad_key = grad_value = 0.0
        for span in (slice(0, 2 * BLOCK), slice(2 * BLOCK, early)):
            grad_query, add_key, add_value = span_gradients(
                query[span], key, value, grad_ref[span, cols],
                weight_ref[h, :, span], inverse_ref[h, :, span], out_ref[cols, span],
            )
            query_out[span, cols] = grad_query
            grad_key += add_key
            grad_value += add_value
        key_out[:, cols] = grad_key
        value_out[:, cols] = grad_value


def backward_early(pieces, grad, saved):
    _, rows, part = pieces[-1].shape
    shapes = [sds((grad.shape[0], part), bf16), sds((4 * rows, part), f32), sds((4 * rows, part), f32)]
    return whole(backward_early_kernel, shapes, (*pieces, grad, *saved), "backward_early", 0, 8)


def backward_kernel(meta, own, near, far2a, far3a, far2b, far3b, early_ref, corner0, corner1, w_ref, *refs):
    saved, done, backs, late_ref = (refs[:3], refs[3:6]), refs[6:9], refs[9:13], refs[13]
    rows = own.shape[1]
    early, total = early_ref.shape[0], 4 * rows
    heads = own.shape[2] // HDIM
    sums = {}

    def head_span(n, span, grad):
        group, h = divmod(n, EARLY)
        query, key, value = head_of(((own, near, far2a, far3a), (own, near, far2b, far3b))[group], group, h)
        weight_ref, inverse_ref, out_ref = saved[group]
        here = slice(h * HDIM, (h + 1) * HDIM)
        cols = slice(n * HDIM, (n + 1) * HDIM)
        grad_query, add_key, add_value = span_gradients(
            query[span], key, value, grad, weight_ref[h, :, span], inverse_ref[h, :, span], out_ref[here, span]
        )
        for k in range(span.start // rows, span.stop // rows):
            at = k * rows - span.start
            backs[k][0, :, cols] = grad_query[at : at + rows]
        grad_key, grad_value = sums.get(n, (0.0, 0.0))
        sums[n] = (grad_key + add_key, grad_value + add_value)

    for n in range(EARLY, heads):
        head_span(n, slice(0, 2 * rows), early_ref[: 2 * rows, n * HDIM : (n + 1) * HDIM])
    corner = jnp.concatenate([corner0[...], corner1[...]], axis=0)
    live = token_pos((rows, 1), 0, meta[Z], early) < meta[COUNT]
    tile = 2 * HDIM
    for i in range(w_ref.shape[0] // tile):
        part = slice(i * tile, (i + 1) * tile)
        late_ref[:, part] = jnp.where(live, dot(corner, w_ref[part, :], 1, 1), 0.0).astype(bf16)
    for n in range(heads):
        cols = slice(n * HDIM, (n + 1) * HDIM)
        if n < EARLY:
            sums[n] = (done[1][:, cols], done[2][:, cols])
            for k in range(early // rows):
                backs[k][0, :, cols] = done[0][k * rows : (k + 1) * rows, cols]
            head_span(n, slice(early, total), late_ref[:, cols])
        else:
            grad = jnp.concatenate([early_ref[2 * rows :, cols], late_ref[:, cols]], axis=0)
            head_span(n, slice(2 * rows, total), grad)
        for k in range(4):
            mine = slice(k * rows, (k + 1) * rows)
            backs[k][1, :, cols] = sums[n][0][mine].astype(bf16)
            backs[k][2, :, cols] = sums[n][1][mine].astype(bf16)


def backward(meta, pieces, grad, corners, weight, saved, done):
    shapes = [sds(pieces[0].shape, bf16)] * 4
    operands = (meta, *pieces, grad, *corners, weight, *saved, *done)
    scratch = [pltpu.VMEM((pieces[0].shape[1], weight.shape[0]), bf16)]
    return whole(backward_kernel, shapes, operands, "attend_backward", 1, 10, scratch)


LINE = HDIM // 8


def line_at(meta, head, other, j):
    at = head * HDIM + ((meta[CORE] ^ other) * 4 + (meta[CHIP] ^ j)) * LINE
    return pl.ds(pl.multiple_of(at, LINE), LINE)


def lines_of(meta, heads_ref):
    lines = []
    for other in (1, 0):
        for j in range(4):
            lines += [heads_ref[line_at(meta, h, other, j), :] for h in range(heads_ref.shape[0] // HDIM)]
    return jnp.concatenate(lines, axis=0)


def weight_kernel(meta, p0, p1, p2, p3, bias_ref, heads_a, *refs):
    pieces, grads = (p0, p1, p2, p3), refs[:-6]
    weight_ref, inverse_ref, out_ref, send_ref, keep_ref, heads_b = refs[-6:]
    rows = p0.shape[1]
    query_live = token_pos((1, 4 * rows), 1, meta[Z]) < meta[COUNT]
    tile = 4 * HDIM
    tiles = send_ref.shape[1] // tile
    whole_size = send_ref.shape[0] // 4

    def product(lines, first, i):
        cols = slice(i * tile, (i + 1) * tile)
        result = dot(lines, jnp.concatenate([g[:, cols] for g in grads], axis=0), 1, 0)
        size = lines.shape[0] // 8
        for j in range(4):
            at = slice(j * whole_size + first, j * whole_size + first + size)
            send_ref[at, cols] = result[j * size : (j + 1) * size].astype(bf16)
            keep_ref[at, cols] = result[(4 + j) * size : (5 + j) * size]

    lines = lines_of(meta, heads_a)
    count = p3.shape[2] // HDIM
    for n in range(max(tiles, 2 * count)):
        if n < 2 * count:
            h, t = divmod(n, 2)
            query, key, value = head_of(pieces, 1, h)
            span = slice(2 * rows * t, 2 * rows * (t + 1))
            outs = (weight_ref, inverse_ref, out_ref, heads_b, h, span)
            span_forward(query, key, value, bias_ref[:, span], query_live[:, span], *outs)
        if n < tiles:
            product(lines, 0, n)
    lines_b = lines_of(meta, heads_b)
    for i in range(tiles):
        product(lines_b, lines.shape[0] // 8, i)


def weight_halves(meta, pieces, bias, heads, grads):
    forward_out = forward_shapes(pieces)
    width = heads.shape[0] + pieces[-1].shape[2]
    shape = (width // 2, grads[0].shape[1])
    shapes = forward_out[:3] + [sds(shape, bf16), sds(shape, f32)]
    scratch = [pltpu.VMEM(forward_out[3].shape, bf16)]
    return whole(weight_kernel, shapes, (meta, *pieces, bias, heads, *grads), "weight_halves", 1, 10, scratch)


def add_kernel(keep_ref, recv_ref, *outs):
    size = outs[0].shape[0]
    for j, out_ref in enumerate(outs):
        part = slice(j * size, (j + 1) * size)
        out_ref[...] = (keep_ref[part, :] + recv_ref[part, :].astype(f32)).astype(out_ref.dtype)


def add_parts(keep, recv):
    shape = (keep.shape[0] // 4, keep.shape[1])
    return whole(add_kernel, [sds(shape, f32)] + [sds(shape, bf16)] * 3, (keep, recv), "add_parts")


def total_kernel(scale, own_ref, r1, r2, r3, out_ref):
    total = own_ref[...] + r1[...].astype(f32) + r2[...].astype(f32) + r3[...].astype(f32)
    out_ref[...] = (total * scale).astype(bf16)


def total_of(own, recvs, scale):
    return whole(functools.partial(total_kernel, scale), sds(own.shape, bf16), (own, *recvs), "scene_mean")


def weight_copies(meta, parts, first, out_ref, sems):
    copies = []
    for p, ref in enumerate(parts, first):
        for h in range(ref.shape[0] // LINE):
            line = out_ref.at[line_at(meta, h, p // 4, p % 4), :]
            copies.append(pltpu.make_async_copy(ref.at[pl.ds(h * LINE, LINE), :], line, sems.at[len(copies)]))
    return copies


def head_copies(meta, pieces, outs, sems):
    copies = []
    for k, ref in pieces.items():
        width = ref.shape[2]
        start = pl.multiple_of((meta[Z] ^ k) * width, 128)
        for i, out_ref in enumerate(outs):
            part = out_ref.at[:, pl.ds(start, width)]
            copies.append(pltpu.make_async_copy(ref.at[i], part, sems.at[len(copies)]))
    return copies


def join(kernel, meta, parts, shapes, copies, name, outs=()):
    return pl.pallas_call(
        kernel,
        out_shape=shapes,
        in_specs=[pl.BlockSpec(memory_space=pltpu.SMEM)]
        + [pl.BlockSpec(memory_space=pltpu.VMEM)] * len(parts)
        + [pl.BlockSpec(memory_space=pl.ANY)] * len(outs),
        out_specs=[pl.BlockSpec(memory_space=pl.ANY)] * len(shapes),
        scratch_shapes=[pltpu.SemaphoreType.DMA((n,)) for n in copies],
        input_output_aliases={1 + len(parts) + i: i for i in range(len(outs))},
        compiler_params=params(),
        cost_estimate=NO_COST,
        name=name,
    )(meta, *parts, *outs)


def join_weight_kernel(meta, *refs):
    run_all(weight_copies(meta, refs[:4], 0, refs[4], refs[5]))


def join_weight(meta, near):
    size, outw = near[0].shape
    return join(join_weight_kernel, meta, near, [sds((8 * size, outw), bf16)], [4 * size // LINE], "join_weight")[0]


def join_heads_kernel(meta, own, back2, back3, *refs):
    run_all(head_copies(meta, {0: own, 2: back2, 3: back3}, refs[:3], refs[3]))


def join_heads(meta, own, back2, back3):
    _, rows, width = own.shape
    shapes = [sds((rows, 4 * width), bf16)] * 3
    return join(join_heads_kernel, meta, (own, back2, back3), shapes, [9], "join_heads")


def join_last_kernel(meta, *refs):
    far, back1, outs, sems = refs[:4], refs[4], refs[9:13], refs[13:]
    run_all(weight_copies(meta, far, 4, outs[3], sems[0]) + head_copies(meta, {1: back1}, outs[:3], sems[1]))


def join_last(meta, far, back1, outs):
    shapes = [sds(x.shape, x.dtype) for x in outs]
    return join(join_last_kernel, meta, (*far, back1), shapes, [4 * far[0].shape[0] // LINE, 3], "join_last", outs)


def dense_body(queries, keys_in, values, out_grad, out_weight, voxel_count):
    meta = jnp.stack([lax.axis_index("shard"), voxel_count[0], lax.axis_index("core"), lax.axis_index("chips")])
    meta = meta.astype(jnp.int32)

    def send(x, k, *earlier):
        return swap(after(x, *earlier) if earlier else x, "shard", 4, k)

    across = send(out_grad, 2)
    beside = send(out_grad, 1)
    own, near1, far2a, far2b, far3a, far3b = pack(meta, queries, keys_in, values)
    piece1 = send(near1, 1)
    piece3a = send(far3a, 3, beside)
    piece2a = send(far2a, 2, across)
    piece3b = send(far3b, 3, piece3a)
    piece2b = send(far2b, 2, piece2a)
    half = across.shape[0] * 5 // 8
    mine = hold(after(out_grad, across))
    grad_early = grad_attn(meta, (mine, beside, across), out_weight, 0)
    corners = [send(across[:half], 1), send(after(across, piece1, grad_early)[half:], 1)]

    *saved_a, heads_a, bias = forward(meta, (own, piece1, piece2a, piece3a))
    early = backward_early((own, piece1, piece2a, piece3a), grad_early, saved_a)
    heads_a, *early, piece2b, piece3b = lax.optimization_barrier((heads_a, *early, piece2b, piece3b))
    grad_early, piece2b, *corners = lax.optimization_barrier((grad_early, piece2b, *corners))
    grads = (mine, beside, across, *corners)

    *saved_b, out, keep = weight_halves(meta, (own, piece1, piece2b, piece3b), bias, heads_a, grads)
    recv = swap(out, "core", 2, 1)
    corners = after(grads[3:], out)
    pieces = (own, piece1, piece2a, piece3a, piece2b, piece3b)
    own0, *backs = backward(meta, pieces, grad_early, corners, out_weight, (*saved_a, *saved_b), early)
    own_part, *sends = add_parts(after(keep, own0), recv)
    recvs = [swap(x, "chips", 4, j + 1) for j, x in enumerate(sends)]
    back3, back2 = send(backs[2], 3), send(backs[1], 2)
    done = total_of(own_part, recvs, 1.0 / 8)
    near = [done] + [swap(done, "chips", 4, j) for j in (1, 2, 3)]
    back1 = send(backs[0], 1, near[1])
    weight = join_weight(meta, near)
    weight, *near, back2, back3 = lax.optimization_barrier((weight, *near, back2, back3))
    far = [swap(x, "core", 2, 1) for x in near]
    heads = join_heads(meta, own0, back2, back3)
    return tuple(join_last(meta, far, back1, (*heads, weight)))


def attend_listed(queries, keys_in, values, block_ids, live_count):
    row_count, width_all = queries.shape
    head_count = width_all // HDIM
    block_count = row_count // BLOCK
    score_scale = 1.0 / math.sqrt(HDIM)
    query_blk = queries.reshape(block_count, BLOCK, head_count, HDIM)
    key_blk = keys_in.reshape(block_count, BLOCK, head_count, HDIM)[block_ids].reshape(
        block_count, NB * BLOCK, head_count, HDIM
    )
    value_blk = values.reshape(block_count, BLOCK, head_count, HDIM)[block_ids].reshape(
        block_count, NB * BLOCK, head_count, HDIM
    )
    query_pos = jnp.arange(row_count, dtype=jnp.int32).reshape(block_count, BLOCK)
    key_pos = (
        block_ids[:, :, None] * BLOCK + jnp.arange(BLOCK, dtype=jnp.int32)[None, None, :]
    ).reshape(block_count, NB * BLOCK)
    allowed = (key_pos[:, None, :] < live_count) | (query_pos[:, :, None] >= live_count)
    scores = (
        jnp.einsum("bqhd,bkhd->bhqk", query_blk, key_blk, preferred_element_type=jnp.float32)
        * score_scale
    )
    scores = jnp.where(allowed[:, None], scores, -jnp.inf)
    peak = jnp.max(scores, axis=-1, keepdims=True)
    weights = jnp.exp(scores - peak)
    probs = weights / jnp.sum(weights, axis=-1, keepdims=True)
    return (query_blk, key_blk, value_blk, probs)


def listed_body(queries, keys_in, values, out_grad, out_weight, block_lists, voxel_count):
    local_rows = queries.shape[0]
    live_count = voxel_count[0]
    block_ids = block_lists[0]
    positions = lax.axis_index("shard") * local_rows + jnp.arange(local_rows, dtype=jnp.int32)
    grad_live = jnp.where((positions < live_count)[:, None], out_grad, jnp.zeros_like(out_grad))
    query_head, key_head, value_head = (
        lax.all_to_all(queries, "shard", split_axis=1, concat_axis=0, tiled=True),
        lax.all_to_all(keys_in, "shard", split_axis=1, concat_axis=0, tiled=True),
        lax.all_to_all(values, "shard", split_axis=1, concat_axis=0, tiled=True),
    )
    row_count, width_all = query_head.shape
    head_count = width_all // HDIM
    block_count = row_count // BLOCK
    score_scale = 1.0 / math.sqrt(HDIM)
    query_blk, key_blk, value_blk, probs = attend_listed(
        query_head, key_head, value_head, block_ids, live_count
    )
    prob_bf = probs.astype(jnp.bfloat16)
    heads_out = (
        jnp.einsum("bhqk,bkhd->bqhd", prob_bf, value_blk, preferred_element_type=jnp.float32)
        .reshape(row_count, width_all)
        .astype(jnp.bfloat16)
    )
    row_piece = lax.all_gather(grad_live, "shard", axis=0, tiled=True)
    acc_now = jnp.einsum("rw,ro->wo", heads_out, row_piece, preferred_element_type=jnp.float32)
    product = jnp.einsum("ro,wo->rw", row_piece, out_weight, preferred_element_type=jnp.float32)
    grad_o = product.astype(jnp.bfloat16).reshape(block_count, BLOCK, head_count, HDIM)
    grad_prob = jnp.einsum("bqhd,bkhd->bhqk", grad_o, value_blk, preferred_element_type=jnp.float32)
    row_delta = jnp.sum(probs * grad_prob, axis=-1, keepdims=True)
    dscore = (probs * (grad_prob - row_delta) * score_scale).astype(jnp.bfloat16)
    grad_query = (
        jnp.einsum("bhqk,bkhd->bqhd", dscore, key_blk, preferred_element_type=jnp.float32)
        .reshape(row_count, width_all)
        .astype(jnp.bfloat16)
    )
    onehot = (
        block_ids[:, :, None] == jnp.arange(block_count, dtype=jnp.int32)[None, None, :]
    ).astype(jnp.float32)
    key_parts = jnp.einsum(
        "bhqk,bqhd->bkhd", dscore, query_blk, preferred_element_type=jnp.float32
    ).reshape(block_count, NB, BLOCK, width_all)
    value_parts = jnp.einsum(
        "bhqk,bqhd->bkhd", prob_bf, grad_o, preferred_element_type=jnp.float32
    ).reshape(block_count, NB, BLOCK, width_all)
    grad_key = (
        jnp.einsum("bjc,bjrx->crx", onehot, key_parts, precision=lax.Precision.HIGHEST)
        .reshape(row_count, width_all)
        .astype(jnp.bfloat16)
    )
    grad_value = (
        jnp.einsum("bjc,bjrx->crx", onehot, value_parts, precision=lax.Precision.HIGHEST)
        .reshape(row_count, width_all)
        .astype(jnp.bfloat16)
    )
    query_back, key_back, value_back = (
        lax.all_to_all(grad_query, "shard", split_axis=0, concat_axis=1, tiled=True),
        lax.all_to_all(grad_key, "shard", split_axis=0, concat_axis=1, tiled=True),
        lax.all_to_all(grad_value, "shard", split_axis=0, concat_axis=1, tiled=True),
    )
    scene_total = lax.axis_size(DP)
    summed = lax.psum(acc_now, DP)
    grad_weight = (summed / scene_total).astype(jnp.bfloat16)
    return (query_back, key_back, value_back, grad_weight)


def body(queries, keys_in, values, out_grad, out_weight, block_lists, voxel_count):
    dense = block_lists.shape[1] == NB and queries.shape[0] == BLOCK
    if dense and lax.axis_size("shard") == 4 and lax.axis_size("chips") == 4:
        return dense_body(queries, keys_in, values, out_grad, out_weight, voxel_count)
    return listed_body(queries, keys_in, values, out_grad, out_weight, block_lists, voxel_count)


def solution(mesh):
    chips = mesh.shape["dp"] // 2
    mesh = jax.sharding.Mesh(mesh.devices.reshape(chips, 2, -1), ("chips", "core", "shard"))
    return jax.shard_map(
        body,
        mesh=mesh,
        in_specs=(
            P((*DP, "shard"), None),
            P((*DP, "shard"), None),
            P((*DP, "shard"), None),
            P((*DP, "shard"), None),
            P("shard", None),
            P(DP, None, None),
            P(DP),
        ),
        out_specs=(
            P((*DP, "shard"), None),
            P((*DP, "shard"), None),
            P((*DP, "shard"), None),
            P("shard", None),
        ),
        check_vma=False,
    )
```
